32 devices in a mesh: narrow: 2 (over y), wide: 16 (over z, x, core).
Axes of the slice: x: 2, y: 2, z: 4, core: 2. Of those that a mesh axis runs over, the one named last changes fastest.
Arguments:
- patches: bfloat16 [2, 11520, 512], P('narrow', 'wide'), may hold values from -6 to 6
- language: bfloat16 [2, 2464, 512], P('narrow', 'wide'), may hold values from -6 to 6
- w_lang: bfloat16 [512, 512], replicated, may hold values from -0.25 to 0.25
- w_attn: bfloat16 [2, 4, 512, 512], replicated, may hold values from -0.25 to 0.25
- w_up: bfloat16 [2, 512, 2048], replicated, may hold values from -0.25 to 0.25
- w_down: bfloat16 [2, 2048, 512], replicated, may hold values from -0.125 to 0.125
- norm_gain: float32 [2, 2, 512], replicated, may hold values from 0.5 to 1.5
- norm_bias: float32 [2, 2, 512], replicated, may hold values from -3 to 3
- ff_bias: float32 [2, 2048], replicated, may hold values from -3 to 3
- out_bias: float32 [2, 512], replicated, may hold values from -3 to 3
- cotangent: bfloat16 [2, 11520, 512], P('narrow', 'wide'), may hold values from -6 to 6
- classes: int32 [2, 8], P('narrow'), may hold values from 0 to 1
Outputs:
- grad_patches: float32 [2, 11520, 512], P('narrow', 'wide')
- grad_language: float32 [2, 2464, 512], P('narrow', 'wide')
- grad_w_lang: float32 [512, 512], P('wide')
- grad_w_attn: float32 [2, 4, 512, 512], P(None, None, 'wide')
- grad_w_up: float32 [2, 512, 2048], P(None, 'wide')
- grad_w_down: float32 [2, 2048, 512], P(None, 'wide')
- grad_norm_gain: float32 [2, 2, 512], P(None, None, 'wide')
- grad_norm_bias: float32 [2, 2, 512], P(None, None, 'wide')
- grad_ff_bias: float32 [2, 2048], P(None, 'wide')
- grad_out_bias: float32 [2, 512], P(None, 'wide')
The draws below stay inside these ranges and needn't reach their ends.
Inputs may be any that keep to these rules, and one draw needn't show every extreme that they name: classes[g, p] == 1: wide devices 2 p and 2 p + 1 of group g hold one item of 5 views of 288 patches in view order, its language in the first slot of device 2 p; 0: each of them holds two items of 5 views of 72 patches, one per language slot.
All inputs are finite; a program needn't handle non-finite values.
Results may differ from the reference program's by a relative error of at most 0.02.
Values may be sent and summed in bfloat16 or wider, within the bound.
No kernel may reach another device: no remote copies, remote signals or barrier semaphores. Data moves between devices by JAX's collectives and lax.ppermute only.
A program may use at most 320 MiB of HBM per device.

```python
import jax
import jax.numpy as jnp
from jax import lax

D = 512
HEADS = 8
HD = 64
FF = 2048
LANG = 77
VIEWS = 5
VB = 288
VS = 72
ROWS = 720
PAIRS = 8
GROUPS = 2
PROWS = 11520
LROWS = 2464


def plant(values, rng, low, top_value):
    longest = values.shape.index(max(values.shape))
    spots = []
    for shift in (0, 1):
        where = [jax.random.randint(jax.random.fold_in(rng, axis), (), 0, length) for axis, length in enumerate(values.shape)]
        where[longest] = (where[longest] + shift) % values.shape[longest]
        spots.append(tuple(where))
    return values.at[spots[0]].set(low).at[spots[1]].set(top_value)


def levels(stream_key, dims, pieces, low, high):
    def one(position, shards_of):
        steps = jax.random.uniform(jax.random.fold_in(jax.random.fold_in(stream_key, 6), position), (shards_of,), jnp.float32, low / len(pieces), high / len(pieces))
        return jnp.repeat(jnp.exp(steps), dims[position] // shards_of).reshape((-1,) + (1,) * (len(dims) - position - 1))

    level = one(*pieces[0])
    for cut in pieces[1:]:
        level = level * one(*cut)
    return level


def gaussian(own_key, dims, deviation, most, pieces=(), held_as=jnp.bfloat16):
    array = jax.random.normal(own_key, dims, jnp.float32) * deviation
    if len(pieces) > 0:
        array = levels(own_key, dims, pieces, -0.22, 0.18) * array
    return jnp.clip(array, min=-most, max=most).astype(held_as)


def setup_inputs(seed: int = 0) -> dict:
    streams_of = jax.random.split(jax.random.key(seed), 13)
    patches = gaussian(streams_of[0], (GROUPS, PROWS, D), 1.0, 6.0, ((0, 2), (1, 16)))
    language = gaussian(streams_of[1], (GROUPS, LROWS, D), 1.0, 6.0, ((0, 2), (1, 16)))
    w_lang = gaussian(streams_of[2], (D, D), D ** -0.5, 0.25)
    w_attn = gaussian(streams_of[3], (2, 4, D, D), D ** -0.5, 0.25)
    w_up = gaussian(streams_of[4], (2, D, FF), D ** -0.5, 0.25)
    w_down = gaussian(streams_of[5], (2, FF, D), FF ** -0.5, 0.125)
    norm_gain = jnp.clip(1.0 + 0.1 * jax.random.normal(streams_of[6], (2, 2, D), jnp.float32), 0.5, 1.5)
    norm_bias = gaussian(streams_of[7], (2, 2, D), 0.3, 3.0, (), jnp.float32)
    ff_bias = gaussian(streams_of[8], (2, FF), 0.3, 3.0, (), jnp.float32)
    out_bias = gaussian(streams_of[9], (2, D), 0.3, 3.0, (), jnp.float32)
    cotangent = gaussian(streams_of[10], (GROUPS, PROWS, D), 1.0, 6.0, ((0, 2), (1, 16)))
    classes = plant(jax.random.randint(streams_of[11], (GROUPS, PAIRS), 0, 2), jax.random.fold_in(streams_of[11], 1), 0, 1).astype(jnp.int32)
    return dict(patches=patches, language=language, w_lang=w_lang, w_attn=w_attn, w_up=w_up, w_down=w_down, norm_gain=norm_gain, norm_bias=norm_bias, ff_bias=ff_bias, out_bias=out_bias, cotangent=cotangent, classes=classes)


@jax.custom_vjp
def low(v):
    return lax.optimization_barrier(v.astype(jnp.bfloat16)).astype(jnp.float32)

@jax.custom_vjp
def low_back(v):
    return v

def low_keep(v):
    return (low(v), None)

def low_pass(kept, grad):
    return (grad,)

def back_keep(v):
    return (v, None)

def back_low(kept, grad):
    return (low(grad),)
low.defvjp(low_keep, low_pass)
low_back.defvjp(back_keep, back_low)
HIGH = lax.Precision.HIGHEST
epsilon = 1e-05
masked_out = -1e+30

def layer_norm(values, gain, bias):
    mean = lax.optimization_barrier(jnp.mean(values, axis=-1, keepdims=True))
    centered = values - mean
    variance = lax.optimization_barrier(jnp.mean(centered * centered, axis=-1, keepdims=True))
    return centered * lax.rsqrt(variance + epsilon) * gain + bias

def project(values, weight):
    return jnp.einsum('...d,de->...e', values, weight, precision=HIGH)

def pair_labels(klass):
    rows = jnp.arange(2 * ROWS, dtype=jnp.int32)
    side = rows // ROWS
    local = rows % ROWS
    half = ROWS // 2
    item = jnp.where(klass == 1, 0, side * 2 + local // half)
    view = jnp.where(klass == 1, rows // VB, local % half // VS)
    slots = jnp.arange(4 * LANG, dtype=jnp.int32) // LANG
    lang_item = jnp.where(klass == 1, jnp.where(slots == 0, 0, -1), slots)
    return (item, item * VIEWS + view, lang_item)

def split_heads(values):
    return values.reshape(values.shape[0], HEADS, HD)

def softmax_mix(query, keys, values, allowed):
    scores = low_back(jnp.einsum('qhe,khe->hqk', query, keys, precision=HIGH))
    scores = jnp.where(allowed[None], scores, masked_out)
    peak = lax.optimization_barrier(jnp.max(scores, axis=-1, keepdims=True))
    weights = jnp.exp(scores - peak)
    probs = low(weights / lax.optimization_barrier(jnp.sum(weights, axis=-1, keepdims=True)))
    mixed = jnp.einsum('hqk,khe->qhe', probs, values, precision=HIGH)
    return mixed.reshape(mixed.shape[0], HEADS * HD)

def view_pair(pack):
    query, keys, values, klass = pack
    item, view, lang_item = pair_labels(klass)
    allowed = view[:, None] == view[None, :]
    return softmax_mix(split_heads(query), split_heads(keys), split_heads(values), allowed)

def joint_pair(pack):
    query, keys, values, lang_keys, lang_values, klass = pack
    item, view, lang_item = pair_labels(klass)
    allowed = item[:, None] == jnp.concatenate([item, lang_item])[None, :]
    all_keys = jnp.concatenate([keys, lang_keys])
    all_values = jnp.concatenate([values, lang_values])
    return softmax_mix(split_heads(query), split_heads(all_keys), split_heads(all_values), allowed)

def forward(patches, language, w_lang, w_attn, w_up, w_down, norm_gain, norm_bias, ff_bias, out_bias, classes):
    flat_classes = classes.reshape(-1).astype(jnp.int32)

    def by_pair(values, per):
        return values.reshape(GROUPS * PAIRS, per, values.shape[-1])
    feats = low_back(project(language, w_lang))
    state = patches
    for layer in range(2):
        normed = low(layer_norm(state, norm_gain[layer, 0], norm_bias[layer, 0]))
        query = low_back(low(project(normed, w_attn[layer, 0]) * 0.125))
        keys = low_back(low(project(normed, w_attn[layer, 1])))
        values = low_back(low(project(normed, w_attn[layer, 2])))
        if layer == 0:
            mixed = lax.map(jax.checkpoint(view_pair), (by_pair(query, 2 * ROWS), by_pair(keys, 2 * ROWS), by_pair(values, 2 * ROWS), flat_classes))
        else:
            lang_normed = low(layer_norm(feats, norm_gain[1, 0], norm_bias[1, 0]))
            lang_keys = low_back(low(project(lang_normed, w_attn[1, 1])))
            lang_values = low_back(low(project(lang_normed, w_attn[1, 2])))
            mixed = lax.map(jax.checkpoint(joint_pair), (by_pair(query, 2 * ROWS), by_pair(keys, 2 * ROWS), by_pair(values, 2 * ROWS), by_pair(lang_keys, 4 * LANG), by_pair(lang_values, 4 * LANG), flat_classes))
        mixed = low_back(low(mixed.reshape(GROUPS, PROWS, D)))
        state = state + low_back(project(mixed, w_attn[layer, 3]))
        normed = low(layer_norm(state, norm_gain[layer, 1], norm_bias[layer, 1]))
        hidden = low_back(project(normed, w_up[layer]) + ff_bias[layer])
        active = low(jax.nn.gelu(hidden))
        state = state + low_back(project(active, w_down[layer]) + out_bias[layer])
    return state

def reference(patches, language, w_lang, w_attn, w_up, w_down, norm_gain, norm_bias, ff_bias, out_bias, cotangent, classes):
    floats = [a.astype(jnp.float32) for a in (patches, language, w_lang, w_attn, w_up, w_down, norm_gain, norm_bias, ff_bias, out_bias)]

    def run(p_in, l_in, wl, wa, wu, wd, ng, nb, fb, ob):
        return forward(p_in, l_in, wl, wa, wu, wd, ng, nb, fb, ob, classes)
    result, pullback = jax.vjp(run, *floats)
    grads = pullback(cotangent.astype(jnp.float32))
    return (grads[0], grads[1], grads[2], grads[3], grads[4], grads[5], grads[6], grads[7], grads[8], grads[9])
```

```python
import functools

import jax
import jax.numpy as jnp
from jax import lax
from jax.experimental import pallas as pl
from jax.experimental.pallas import tpu as pltpu
from jax.sharding import PartitionSpec as P

HEADS = 8
HD = 64
LANG = 77
VB = 288
VS = 72
ROWS = 720
EDGE = VB // 2
PADDED = ROWS + EDGE
LPAD = 160
LONE = 96
KEYS = 2 * ROWS + LONE
PAIR = 2 * HD
QT = 240
KT = 256
SLICES = 16

epsilon = 1e-05
masked_out = -1e30
BF = jnp.bfloat16
F32 = jnp.float32


def layer_norm(values, gain, bias):
    mean = jnp.mean(values, axis=-1, keepdims=True)
    centered = values - mean
    variance = jnp.mean(centered * centered, axis=-1, keepdims=True)
    return centered * lax.rsqrt(variance + epsilon) * gain + bias


def matmul(left, right):
    return jnp.dot(left, right, preferred_element_type=F32)


def mat_left(left, right):
    return lax.dot_general(left, right, (((0,), (0,)), ((), ())), preferred_element_type=F32)


def mat_right(left, right):
    return lax.dot_general(left, right, (((1,), (1,)), ((), ())), preferred_element_type=F32)


def lane_mask(head):
    lanes = lax.broadcasted_iota(jnp.int32, (1, PAIR), 1)
    return jnp.where(lanes // HD == head, 1.0, 0.0).astype(BF)


def in_half(shape):
    return lax.broadcasted_iota(jnp.int32, shape, 1) % HD


def row_of(shape):
    return lax.broadcasted_iota(jnp.int32, shape, 0)


def key_marks(allowed, items):
    lane = in_half(allowed.shape)
    marks = jnp.where(lane < items, jnp.where(allowed, 0.0, masked_out), 0.0)
    return jnp.where((lane >= 4) & (lane < 7), 1.0, marks).astype(BF)


def joint_key_marks(klass):
    shape = (KEYS, PAIR)
    row, lane = row_of(shape), in_half(shape)
    first = (row < ROWS // 2) | ((row >= ROWS) & (row < ROWS + LANG))
    second = ((row >= ROWS // 2) & (row < ROWS)) | ((row >= ROWS + LANG) & (row < ROWS + 2 * LANG))
    fine = jnp.where(row < 2 * ROWS + LANG, 1, 0)
    coarse = jnp.where(lane == 0, jnp.where(first, 1, 0), jnp.where(second, 1, 0))
    return key_marks(jnp.where(klass == 1, fine, coarse) == 1, 2)


def joint_row_marks():
    shape = (ROWS, PAIR)
    row, lane = row_of(shape), in_half(shape)
    return jnp.where(lane == row // (ROWS // 2), 1.0, 0.0).astype(BF)


def view_key_marks(klass):
    shape = (PADDED, PAIR)
    row, lane = row_of(shape), in_half(shape)
    same = jnp.where(lane == row % VB // VS, 1, 0)
    return key_marks(jnp.where(klass == 1, 1, same) == 1, 4)


def view_row_marks():
    shape = (PADDED, PAIR)
    row, lane = row_of(shape), in_half(shape)
    return jnp.where(lane == row % VB // VS, 1.0, 0.0).astype(BF)


def three_parts(values):
    high = values.astype(BF)
    rest = values - high.astype(F32)
    middle = rest.astype(BF)
    low = (rest - middle.astype(F32)).astype(BF)
    return (high.astype(F32), middle.astype(F32), low.astype(F32))


def with_parts(values, base):
    lane = in_half(values.shape)
    high, middle, low = three_parts(values)
    picked = jnp.where(lane == 4, -high, jnp.where(lane == 5, -middle, jnp.where(lane == 6, -low, base)))
    return picked.astype(BF)


def total_columns(shape, head):
    lanes = lax.broadcasted_iota(jnp.int32, shape, 1)
    return jnp.where(lanes // HD == head, 1.0, 0.0).astype(BF)


def attend_tile(query, marks, keys, values):
    lanes = lax.broadcasted_iota(jnp.int32, (1, PAIR), 1)
    out, peaks = None, []
    for head in range(2):
        mask = lane_mask(head)
        left = jnp.concatenate([query * mask, marks * mask], axis=1)
        scores = mat_right(left, keys)
        peak = jnp.max(scores, axis=1, keepdims=True)
        weights = jnp.exp(scores - peak).astype(BF)
        part = matmul(weights, values[head])
        out = part if out is None else out + part
        peaks.append(peak)
    total = out[:, PAIR:]
    mixed = (out[:, :PAIR] / total).astype(BF)
    logsum = jnp.where(lanes < HD, peaks[0], peaks[1]) + jnp.log(total)
    return (mixed, with_parts(logsum, marks.astype(F32)))


def put_values(block, first, second, rows):
    first[rows, :PAIR] = block * lane_mask(0)
    second[rows, :PAIR] = block * lane_mask(1)


def joint_place(klass, side, kv_ref, far_ref, lang_ref, put):
    put(slice(0, ROWS), kv_ref[...])

    @pl.when(klass == 1)
    def fine():
        put(slice(ROWS, 2 * ROWS), far_ref[:ROWS])

        @pl.when(side == 0)
        def own():
            put(slice(2 * ROWS, KEYS), lang_ref[:LONE])

        @pl.when(side == 1)
        def partner():
            put(slice(2 * ROWS, KEYS), far_ref[ROWS:])

    @pl.when(klass != 1)
    def coarse():
        put(slice(ROWS, ROWS + LPAD), lang_ref[...])


def joint_forward_kernel(
    flags, q_ref, kv_ref, far_ref, lang_ref, mixed_ref, ext_ref, keys, first, second, marks
):
    klass, side = flags[0], flags[1]

    @pl.when(pl.program_id(0) == 0)
    def prepare():
        keys[...] = jnp.zeros_like(keys)
        first[...] = jnp.zeros_like(first)
        second[...] = jnp.zeros_like(second)
        keys[:, PAIR:] = joint_key_marks(klass)
        first[:, PAIR:] = total_columns((KEYS, PAIR), 0)
        second[:, PAIR:] = total_columns((KEYS, PAIR), 1)
        marks[...] = joint_row_marks()

    def put(rows, block):
        keys[rows, :PAIR] = block[:, :PAIR]
        put_values(block[:, PAIR:], first, second, rows)

    joint_place(klass, side, kv_ref, far_ref, lang_ref, put)

    def tile(index, carry):
        rows = pl.ds(pl.multiple_of(index * QT, 16), QT)
        mixed, ext = attend_tile(
            q_ref[rows, :], marks[rows, :], keys[...], (first[...], second[...])
        )
        mixed_ref[rows, :] = mixed
        ext_ref[rows, :] = ext
        return carry

    lax.fori_loop(0, ROWS // QT, tile, 0)


def joint_forward(flags, query, kv, far, lang):
    rows = query.shape[0]
    return pl.pallas_call(
        joint_forward_kernel,
        grid_spec=pltpu.PrefetchScalarGridSpec(
            num_scalar_prefetch=1,
            grid=(HEADS // 2,),
            in_specs=[
                pl.BlockSpec((rows, PAIR), lambda i, f: (0, i)),
                pl.BlockSpec((rows, 2 * PAIR), lambda i, f: (0, i)),
                pl.BlockSpec((ROWS + LONE, 2 * PAIR), lambda i, f: (0, i)),
                pl.BlockSpec((LPAD, 2 * PAIR), lambda i, f: (0, i)),
            ],
            out_specs=[pl.BlockSpec((rows, PAIR), lambda i, f: (0, i))] * 2,
            scratch_shapes=[pltpu.VMEM((KEYS, 2 * PAIR), BF)] * 3 + [pltpu.VMEM((ROWS, PAIR), BF)],
        ),
        out_shape=[jax.ShapeDtypeStruct((rows, HEADS * HD), BF)] * 2,
        compiler_params=pltpu.CompilerParams(vmem_limit_bytes=48 * 2**20),
        cost_estimate=pl.CostEstimate(
            flops=8 * rows * KEYS * HEADS * HD * 2, bytes_accessed=8 * 2**20, transcendentals=0
        ),
        name="joint_forward",
    )(flags, query, kv, far, lang)


def inner_marks(grad, mixed):
    lanes = lax.broadcasted_iota(jnp.int32, (1, PAIR), 1)
    product = grad.astype(F32) * mixed.astype(F32)
    first = jnp.sum(jnp.where(lanes < HD, product, 0.0), axis=1, keepdims=True)
    second = jnp.sum(jnp.where(lanes < HD, 0.0, product), axis=1, keepdims=True)
    return with_parts(jnp.where(lanes < HD, first, second), jnp.zeros_like(product))


def attend_back_tile(keys, values, keys_across, left, grads):
    grad_keys, grad_values, across = None, None, []
    for head in range(2):
        probs = jnp.exp(mat_right(keys, left[head]))
        inner = mat_right(values, grads[head])
        grad_scores = (probs * inner).astype(BF)
        part_values = matmul(probs.astype(BF), grads[head][:, :PAIR])
        part_keys = matmul(grad_scores, left[head][:, :PAIR])
        grad_keys = part_keys if head == 0 else grad_keys + part_keys
        grad_values = part_values if head == 0 else grad_values + part_values
        across.append(matmul(keys_across[head * HD : (head + 1) * HD, :], grad_scores))
    return (grad_keys, grad_values, across)


def fill_rows(left, grads, rows, query, ext, grad, mixed):
    inner = inner_marks(grad, mixed)
    for head in range(2):
        mask = lane_mask(head)
        left[head, rows, :PAIR] = query * mask
        left[head, rows, PAIR:] = ext * mask
        grads[head, rows, :PAIR] = grad * mask
        grads[head, rows, PAIR:] = inner * mask


def joint_backward_kernel(
    flags, q_ref, ext_ref, kv_ref, far_ref, lang_ref, mixed_ref, grad_ref, dq_ref, dkv_ref,
    keys, values, across, left, grads, total,
):
    klass, side = flags[0], flags[1]

    @pl.when(pl.program_id(0) == 0)
    def prepare():
        keys[...] = jnp.zeros_like(keys)
        values[...] = jnp.zeros_like(values)
        shared = joint_key_marks(klass)
        keys[:, PAIR:] = shared
        values[:, PAIR:] = shared

    def put(rows, block):
        keys[rows, :PAIR] = block[:, :PAIR]
        values[rows, :PAIR] = block[:, PAIR:]

    joint_place(klass, side, kv_ref, far_ref, lang_ref, put)
    across[...] = keys[:, :PAIR].T
    fill_rows(left, grads, slice(0, ROWS), q_ref[...], ext_ref[...], grad_ref[...], mixed_ref[...])
    total[...] = jnp.zeros_like(total)

    def tile(index, carry):
        rows = pl.ds(pl.multiple_of(index * KT, KT), KT)
        grad_keys, grad_values, parts = attend_back_tile(
            keys[rows, :], values[rows, :], across[:, rows], left, grads
        )
        dkv_ref[rows, :PAIR] = grad_keys.astype(BF)
        dkv_ref[rows, PAIR:] = grad_values.astype(BF)
        for head in range(2):
            total[head * HD : (head + 1) * HD, :] += parts[head]
        return carry

    lax.fori_loop(0, KEYS // KT, tile, 0)
    dq_ref[...] = total[...].T.astype(BF)


def joint_backward(flags, query, ext, kv, far, lang, mixed, grad):
    rows = query.shape[0]
    one = pl.BlockSpec((rows, PAIR), lambda i, f: (0, i))
    return pl.pallas_call(
        joint_backward_kernel,
        grid_spec=pltpu.PrefetchScalarGridSpec(
            num_scalar_prefetch=1,
            grid=(HEADS // 2,),
            in_specs=[
                one,
                one,
                pl.BlockSpec((rows, 2 * PAIR), lambda i, f: (0, i)),
                pl.BlockSpec((ROWS + LONE, 2 * PAIR), lambda i, f: (0, i)),
                pl.BlockSpec((LPAD, 2 * PAIR), lambda i, f: (0, i)),
                one,
                one,
            ],
            out_specs=[one, pl.BlockSpec((KEYS, 2 * PAIR), lambda i, f: (0, i))],
            scratch_shapes=[
                pltpu.VMEM((KEYS, 2 * PAIR), BF),
                pltpu.VMEM((KEYS, 2 * PAIR), BF),
                pltpu.VMEM((PAIR, KEYS), BF),
                pltpu.VMEM((2, ROWS, 2 * PAIR), BF),
                pltpu.VMEM((2, ROWS, 2 * PAIR), BF),
                pltpu.VMEM((PAIR, ROWS), F32),
            ],
        ),
        out_shape=[
            jax.ShapeDtypeStruct((rows, HEADS * HD), BF),
            jax.ShapeDtypeStruct((KEYS, 2 * HEADS * HD), BF),
        ],
        compiler_params=pltpu.CompilerParams(vmem_limit_bytes=48 * 2**20),
        cost_estimate=pl.CostEstimate(
            flops=20 * rows * KEYS * HEADS * HD * 2, bytes_accessed=12 * 2**20, transcendentals=0
        ),
        name="joint_backward",
    )(flags, query, ext, kv, far, lang, mixed, grad)


def view_spots(side):
    own = pl.ds(pl.multiple_of(side * EDGE, 16), ROWS)
    far = pl.ds(pl.multiple_of((1 - side) * ROWS, 16), EDGE)
    return (own, far)


def view_forward_kernel(
    flags, q_ref, kv_ref, far_ref, mixed_ref, ext_ref, rows_q, keys, first, second, marks, out, ext_out
):
    klass, side = flags[0], flags[1]
    own, far = view_spots(side)

    @pl.when(pl.program_id(0) == 0)
    def prepare():
        rows_q[...] = jnp.zeros_like(rows_q)
        keys[:, PAIR:] = view_key_marks(klass)
        first[:, PAIR:] = total_columns((PADDED, PAIR), 0)
        second[:, PAIR:] = total_columns((PADDED, PAIR), 1)
        marks[...] = view_row_marks()

    rows_q[own, :] = q_ref[...]
    for rows, ref in ((own, kv_ref), (far, far_ref)):
        keys[rows, :PAIR] = ref[:, :PAIR]
        put_values(ref[:, PAIR:], first, second, rows)

    def tile(index, carry):
        rows = pl.ds(pl.multiple_of(index * VB, 16), VB)
        mixed, ext = attend_tile(
            rows_q[rows, :], marks[rows, :], keys[rows, :], (first[rows, :], second[rows, :])
        )
        out[rows, :] = mixed
        ext_out[rows, :] = ext
        return carry

    lax.fori_loop(0, PADDED // VB, tile, 0)
    mixed_ref[...] = out[own, :]
    ext_ref[...] = ext_out[own, :]


def view_forward(flags, query, kv, far):
    rows = query.shape[0]
    one = pl.BlockSpec((rows, PAIR), lambda i, f: (0, i))
    return pl.pallas_call(
        view_forward_kernel,
        grid_spec=pltpu.PrefetchScalarGridSpec(
            num_scalar_prefetch=1,
            grid=(HEADS // 2,),
            in_specs=[
                one,
                pl.BlockSpec((rows, 2 * PAIR), lambda i, f: (0, i)),
                pl.BlockSpec((EDGE, 2 * PAIR), lambda i, f: (0, i)),
            ],
            out_specs=[one] * 2,
            scratch_shapes=[pltpu.VMEM((PADDED, PAIR), BF)]
            + [pltpu.VMEM((PADDED, 2 * PAIR), BF)] * 3
            + [pltpu.VMEM((PADDED, PAIR), BF)] * 3,
        ),
        out_shape=[jax.ShapeDtypeStruct((rows, HEADS * HD), BF)] * 2,
        compiler_params=pltpu.CompilerParams(vmem_limit_bytes=48 * 2**20),
        cost_estimate=pl.CostEstimate(
            flops=8 * rows * VB * HEADS * HD * 2, bytes_accessed=6 * 2**20, transcendentals=0
        ),
        name="view_forward",
    )(flags, query, kv, far)


def view_backward_kernel(
    flags, q_ref, ext_ref, kv_ref, far_ref, mixed_ref, grad_ref, dq_ref, dkv_ref, dfar_ref,
    keys, values, across, left, grads, back, dkv,
):
    klass, side = flags[0], flags[1]
    own, far = view_spots(side)

    @pl.when(pl.program_id(0) == 0)
    def prepare():
        shared = view_key_marks(klass)
        keys[:, PAIR:] = shared
        values[:, PAIR:] = shared
        left[...] = jnp.zeros_like(left)
        grads[...] = jnp.zeros_like(grads)

    for rows, ref in ((own, kv_ref), (far, far_ref)):
        keys[rows, :PAIR] = ref[:, :PAIR]
        values[rows, :PAIR] = ref[:, PAIR:]
    fill_rows(left, grads, own, q_ref[...], ext_ref[...], grad_ref[...], mixed_ref[...])

    def tile(index, carry):
        rows = pl.ds(pl.multiple_of(index * VB, 16), VB)
        here = keys[rows, :]
        grad_keys, grad_values, parts = attend_back_tile(
            here,
            values[rows, :],
            here[:, :PAIR].T,
            [left[head, rows, :] for head in range(2)],
            [grads[head, rows, :] for head in range(2)],
        )
        dkv[rows, :PAIR] = grad_keys.astype(BF)
        dkv[rows, PAIR:] = grad_values.astype(BF)
        back[rows, :] = jnp.concatenate(parts, axis=0).T.astype(BF)
        return carry

    lax.fori_loop(0, PADDED // VB, tile, 0)
    dq_ref[...] = back[own, :]
    dkv_ref[...] = dkv[own, :]
    dfar_ref[...] = dkv[far, :]


def view_backward(flags, query, ext, kv, far, mixed, grad):
    rows = query.shape[0]
    one = pl.BlockSpec((rows, PAIR), lambda i, f: (0, i))
    two = pl.BlockSpec((rows, 2 * PAIR), lambda i, f: (0, i))
    edge = pl.BlockSpec((EDGE, 2 * PAIR), lambda i, f: (0, i))
    return pl.pallas_call(
        view_backward_kernel,
        grid_spec=pltpu.PrefetchScalarGridSpec(
            num_scalar_prefetch=1,
            grid=(HEADS // 2,),
            in_specs=[one, one, two, edge, one, one],
            out_specs=[one, two, edge],
            scratch_shapes=[
                pltpu.VMEM((PADDED, 2 * PAIR), BF),
                pltpu.VMEM((PADDED, 2 * PAIR), BF),
                pltpu.VMEM((PAIR, PADDED), BF),
                pltpu.VMEM((2, PADDED, 2 * PAIR), BF),
                pltpu.VMEM((2, PADDED, 2 * PAIR), BF),
                pltpu.VMEM((PADDED, PAIR), BF),
                pltpu.VMEM((PADDED, 2 * PAIR), BF),
            ],
        ),
        out_shape=[
            jax.ShapeDtypeStruct((rows, HEADS * HD), BF),
            jax.ShapeDtypeStruct((rows, 2 * HEADS * HD), BF),
            jax.ShapeDtypeStruct((EDGE, 2 * HEADS * HD), BF),
        ],
        compiler_params=pltpu.CompilerParams(vmem_limit_bytes=48 * 2**20),
        cost_estimate=pl.CostEstimate(
            flops=20 * rows * VB * HEADS * HD * 2, bytes_accessed=8 * 2**20, transcendentals=0
        ),
        name="view_backward",
    )(flags, query, ext, kv, far, mixed, grad)


def pair_swap(block):
    count = lax.axis_size("wide")
    return lax.ppermute(block, "wide", [(at, at ^ 1) for at in range(count)])


def interleave(keys, values):
    width = keys.shape[1]
    both = jnp.stack([keys.reshape(-1, width // PAIR, PAIR), values.reshape(-1, width // PAIR, PAIR)], axis=2)
    return both.reshape(-1, 2 * width)


def apart(both):
    width = both.shape[-1] // 2
    parts = both.reshape(both.shape[:-1] + (width // PAIR, 2, PAIR))
    return (
        parts[..., 0, :].reshape(both.shape[:-1] + (width,)),
        parts[..., 1, :].reshape(both.shape[:-1] + (width,)),
    )


def mlp_forward(state, gain, bias, w_in, b_in):
    normed = layer_norm(state, gain, bias).astype(BF)
    hidden = matmul(normed, w_in) + b_in
    active = jax.nn.gelu(hidden).astype(BF)
    return (normed, hidden, active)


def mlp_backward(grad, state, normed, hidden, active, gain, bias, w_in, w_out):
    grad_low = grad.astype(BF)
    grad_outb = jnp.sum(grad_low.astype(F32), axis=0)
    grad_down = mat_left(active, grad_low).astype(BF)
    grad_active = mat_right(grad_low, w_out)
    unused, gelu_back = jax.vjp(jax.nn.gelu, hidden)
    grad_hidden = gelu_back(grad_active)[0].astype(BF)
    grad_ffb = jnp.sum(grad_hidden.astype(F32), axis=0)
    grad_up = mat_left(normed, grad_hidden).astype(BF)
    grad_normed = mat_right(grad_hidden, w_in)
    unused, norm_back = jax.vjp(layer_norm, state, gain, bias)
    grad_state, grad_gain, grad_bias = norm_back(grad_normed)
    return (grad + grad_state, (grad_down, grad_outb, grad_ffb, grad_up, grad_gain, grad_bias))


def reduce_slices(part, order):
    count = lax.axis_size("wide")
    position = lax.axis_index("wide")
    low = count // SLICES
    bits = SLICES.bit_length() - 1
    high = position // low
    buffer = part.reshape((2,) * bits + part.shape[1:])
    held = list(range(bits - 1, -1, -1))
    for bit in order:
        at = held.index(bit)
        mine = high >> bit & 1
        send = lax.dynamic_index_in_dim(buffer, 1 - mine, at, keepdims=False)
        keep = lax.dynamic_index_in_dim(buffer, mine, at, keepdims=False)
        held.remove(bit)
        stride = low << bit
        got = lax.ppermute(send, "wide", [(p, p ^ stride) for p in range(count)])
        buffer = keep + got
    half = low
    while half > 1:
        half //= 2
        mine = position // half % 2
        size = buffer.shape[0] // 2
        send = lax.dynamic_slice_in_dim(buffer, (1 - mine) * size, size, 0)
        keep = lax.dynamic_slice_in_dim(buffer, mine * size, size, 0)
        got = lax.ppermute(send, "wide", [(p, p ^ half) for p in range(count)])
        buffer = keep + got
    if lax.axis_size("narrow") == 2:
        got = lax.ppermute(buffer, "narrow", [(0, 1), (1, 0)])
        return buffer.astype(F32) + got.astype(F32)
    return lax.psum(buffer, "narrow").astype(F32)


def sliced(grad):
    return grad.reshape((SLICES, grad.shape[0] // SLICES) + grad.shape[1:])


def body(
    patches,
    language,
    w_lang,
    w_attn,
    w_up,
    w_down,
    norm_gain,
    norm_bias,
    ff_bias,
    out_bias,
    cotangent,
    classes,
):
    position = lax.axis_index("wide")
    side = position % 2
    klass = lax.dynamic_index_in_dim(classes[0], position // 2, 0, keepdims=False)
    flags = jnp.stack([klass, side]).astype(jnp.int32)
    fine = klass == 1
    width = w_lang.shape[0]
    start = patches[0].astype(F32)
    lang_low = jnp.pad(language[0], ((0, LPAD - language.shape[1]), (0, 0)))
    w_query = [w_attn[layer, 0] * jnp.asarray(0.125, BF) for layer in range(2)]
    w_kv = [interleave(w_attn[layer, 1], w_attn[layer, 2]) for layer in range(2)]

    normed_a = layer_norm(start, norm_gain[0, 0], norm_bias[0, 0]).astype(BF)
    kv_a = matmul(normed_a, w_kv[0]).astype(BF)
    far_a = pair_swap(jnp.where(side == 0, kv_a[ROWS - EDGE :], kv_a[:EDGE]))
    query_a = matmul(normed_a, w_query[0]).astype(BF)
    mixed_a, ext_a = view_forward(flags, query_a, kv_a, far_a)
    after_a = start + matmul(mixed_a, w_attn[0, 3])
    normed_b, hidden_b, active_b = mlp_forward(
        after_a, norm_gain[0, 1], norm_bias[0, 1], w_up[0], ff_bias[0]
    )
    state_b = after_a + matmul(active_b, w_down[0]) + out_bias[0]

    feats = matmul(lang_low, w_lang)
    lang_normed = layer_norm(feats, norm_gain[1, 0], norm_bias[1, 0]).astype(BF)
    lang_kv = matmul(lang_normed, w_kv[1]).astype(BF)
    normed_c = layer_norm(state_b, norm_gain[1, 0], norm_bias[1, 0]).astype(BF)
    kv_c = matmul(normed_c, w_kv[1]).astype(BF)
    far_c = pair_swap(jnp.concatenate([kv_c, lang_kv[:LONE]]))
    query_c = matmul(normed_c, w_query[1]).astype(BF)
    mixed_c, ext_c = joint_forward(flags, query_c, kv_c, far_c, lang_kv)
    after_c = state_b + matmul(mixed_c, w_attn[1, 3])
    normed_d, hidden_d, active_d = mlp_forward(
        after_c, norm_gain[1, 1], norm_bias[1, 1], w_up[1], ff_bias[1]
    )

    grad = cotangent[0].astype(F32)
    grad, mlp_two = mlp_backward(
        grad, after_c, normed_d, hidden_d, active_d, norm_gain[1, 1], norm_bias[1, 1], w_up[1], w_down[1]
    )
    down_two = reduce_slices(sliced(mlp_two[0]), (0, 1, 2, 3))
    up_two = reduce_slices(sliced(mlp_two[3]), (0, 2, 3, 1))
    grad_low_c = grad.astype(BF)
    wout_two = mat_left(mixed_c, grad_low_c).astype(BF)
    grad_mixed_c = mat_right(grad_low_c, w_attn[1, 3]).astype(BF)
    dq_c, dkv_c = joint_backward(flags, query_c, ext_c, kv_c, far_c, lang_kv, mixed_c, grad_mixed_c)
    back_c = pair_swap(dkv_c[ROWS:]).astype(F32)
    own_kv = (dkv_c[:ROWS].astype(F32) + jnp.where(fine, back_c[:ROWS], 0.0)).astype(BF)
    lone = jnp.where(side == 0, dkv_c[2 * ROWS :].astype(F32) + back_c[ROWS:], 0.0)
    lang_dkv = jnp.where(
        fine,
        jnp.pad(lone, ((0, LPAD - LONE), (0, 0))),
        dkv_c[ROWS : ROWS + LPAD].astype(F32),
    ).astype(BF)
    grad_normed_c = mat_right(dq_c, w_query[1]) + mat_right(own_kv, w_kv[1])
    dwq_two = mat_left(normed_c, dq_c) * 0.125
    dwkv_two = mat_left(normed_c, own_kv) + mat_left(lang_normed, lang_dkv)
    unused, norm_back_c = jax.vjp(layer_norm, state_b, norm_gain[1, 0], norm_bias[1, 0])
    grad_state_c, gain_c, bias_c = norm_back_c(grad_normed_c)
    grad = grad + grad_state_c

    unused, lang_back = jax.vjp(layer_norm, feats, norm_gain[1, 0], norm_bias[1, 0])
    grad_feats, gain_lang, bias_lang = lang_back(mat_right(lang_dkv, w_kv[1]))
    feats_low = grad_feats.astype(BF)
    dw_lang = mat_left(lang_low, feats_low).astype(BF)
    grad_language = mat_right(feats_low, w_lang)[: language.shape[1]]
    attn_two = reduce_slices(
        sliced(jnp.concatenate([dwq_two.astype(BF), dwkv_two.astype(BF), wout_two, dw_lang], axis=1)),
        (0, 1, 2, 3),
    )

    grad, mlp_one = mlp_backward(
        grad, after_a, normed_b, hidden_b, active_b, norm_gain[0, 1], norm_bias[0, 1], w_up[0], w_down[0]
    )
    down_one = reduce_slices(sliced(mlp_one[0]), (0, 1, 2, 3))
    up_one = reduce_slices(sliced(mlp_one[3]), (0, 2, 3, 1))
    grad_low_a = grad.astype(BF)
    wout_one = mat_left(mixed_a, grad_low_a).astype(BF)
    grad_mixed_a = mat_right(grad_low_a, w_attn[0, 3]).astype(BF)
    dq_a, dkv_a, dfar_a = view_backward(flags, query_a, ext_a, kv_a, far_a, mixed_a, grad_mixed_a)
    back_a = pair_swap(dfar_a)
    spread = jnp.where(
        side == 0,
        jnp.pad(back_a, ((ROWS - EDGE, 0), (0, 0))),
        jnp.pad(back_a, ((0, ROWS - EDGE), (0, 0))),
    )
    own_kv_a = (dkv_a.astype(F32) + spread.astype(F32)).astype(BF)
    grad_normed_a = mat_right(dq_a, w_query[0]) + mat_right(own_kv_a, w_kv[0])
    dwq_one = (mat_left(normed_a, dq_a) * 0.125).astype(BF)
    dwkv_one = mat_left(normed_a, own_kv_a).astype(BF)
    unused, norm_back_a = jax.vjp(layer_norm, start, norm_gain[0, 0], norm_bias[0, 0])
    grad_state_a, gain_a, bias_a = norm_back_a(grad_normed_a)
    grad = grad + grad_state_a

    wide = lax.axis_size("wide")
    vectors = [
        jnp.stack([gain_a, mlp_one[4], gain_c + gain_lang, mlp_two[4]]),
        jnp.stack([bias_a, mlp_one[5], bias_c + bias_lang, mlp_two[5]]),
        jnp.stack([mlp_one[2], mlp_two[2]]),
        jnp.stack([mlp_one[1], mlp_two[1]]),
    ]
    rows_each = width // SLICES
    per = width // wide
    small = []
    for vector in vectors:
        share = vector.reshape(vector.shape[0], width, -1)
        small.append(jnp.transpose(share, (1, 0, 2)).reshape(width, -1))
    small = jnp.concatenate(small, axis=1).astype(BF)
    used = small.shape[1]
    small = jnp.pad(small, ((0, 0), (0, 128 - used)))
    attn_one = reduce_slices(
        sliced(jnp.concatenate([dwq_one, dwkv_one, wout_one, small], axis=1)), (0, 1, 2, 3)
    )

    def attention_grads(reduced):
        key, value = apart(reduced[:, width : 3 * width])
        return jnp.stack([reduced[:, :width], key, value, reduced[:, 3 * width : 4 * width]])

    grad_w_attn = jnp.stack([attention_grads(attn_one), attention_grads(attn_two)])
    small = attn_one[:, 4 * width : 4 * width + used]
    shares, at = [], 0
    for vector in vectors:
        size = vector.shape[0] * (vector.shape[1] // width)
        share = small[:, at : at + size].reshape(per, vector.shape[0], -1)
        shares.append(jnp.transpose(share, (1, 0, 2)).reshape(vector.shape[0], -1))
        at += size
    return (
        grad[None],
        grad_language[None],
        attn_two[:, 4 * width :],
        grad_w_attn,
        jnp.stack([up_one, up_two]),
        jnp.stack([down_one, down_two]),
        shares[0].reshape(2, 2, -1),
        shares[1].reshape(2, 2, -1),
        shares[2],
        shares[3],
    )


def solution(mesh):
    in_specs = (
        P("narrow", "wide", None),
        P("narrow", "wide", None),
        P(),
        P(),
        P(),
        P(),
        P(),
        P(),
        P(),
        P(),
        P("narrow", "wide", None),
        P("narrow", None),
    )
    out_specs = (
        P("narrow", "wide", None),
        P("narrow", "wide", None),
        P("wide", None),
        P(None, None, "wide", None),
        P(None, "wide", None),
        P(None, "wide", None),
        P(None, None, "wide"),
        P(None, None, "wide"),
        P(None, "wide"),
        P(None, "wide"),
    )
    return jax.shard_map(body, mesh=mesh, in_specs=in_specs, out_specs=out_specs, check_vma=False)
```

```python
import functools

import jax
import jax.numpy as jnp
from jax import lax
from jax.experimental import pallas as pl
from jax.experimental.pallas import tpu as pltpu
from jax.sharding import PartitionSpec as P

HEADS = 8
HD = 64
LANG = 77
VB = 288
VS = 72
ROWS = 720
EDGE = VB // 2
PADDED = ROWS + EDGE
LPAD = 160
LONE = 96
KEYS = 2 * ROWS + LONE
PAIR = 2 * HD
SLICES = 16
LONG, SHORT = 60.0, 0.5
JOINT_VMEM = 60 * 2**20
JOINT_BACK_VMEM = 60 * 2**20
VIEW_VMEM = 60 * 2**20
DENSE_VMEM = 60 * 2**20
NEAR_VMEM = 16 * 2**20

epsilon = 1e-05
masked_out = -1e30
BF = jnp.bfloat16
F32 = jnp.float32


def matmul(left, right):
    return jnp.dot(left, right, preferred_element_type=F32)


def mat_left(left, right):
    return lax.dot_general(left, right, (((0,), (0,)), ((), ())), preferred_element_type=F32)


def mat_right(left, right):
    return lax.dot_general(left, right, (((1,), (1,)), ((), ())), preferred_element_type=F32)


def cost_of(microseconds):
    return pl.CostEstimate(flops=int(microseconds * 1e9), bytes_accessed=1, transcendentals=0)


def waiting(kernel, inputs, more):
    if not more:
        return kernel

    def without(*refs):
        return kernel(*refs[:inputs], *refs[inputs + more :])

    return without


def lane_mask(head):
    lanes = lax.broadcasted_iota(jnp.int32, (1, PAIR), 1)
    return jnp.where(lanes // HD == head, 1.0, 0.0).astype(BF)


def in_half(shape):
    return lax.broadcasted_iota(jnp.int32, shape, 1) % HD


def row_of(shape):
    return lax.broadcasted_iota(jnp.int32, shape, 0)


def key_marks(allowed, items):
    lane = in_half(allowed.shape)
    marks = jnp.where(lane < items, jnp.where(allowed, 0.0, masked_out), 0.0)
    return jnp.where((lane >= 4) & (lane < 7), 1.0, marks).astype(BF)


def joint_key_marks(klass):
    shape = (KEYS, PAIR)
    row, lane = row_of(shape), in_half(shape)
    first = (row < ROWS // 2) | ((row >= ROWS) & (row < ROWS + LANG))
    second = ((row >= ROWS // 2) & (row < ROWS)) | ((row >= ROWS + LANG) & (row < ROWS + 2 * LANG))
    fine = jnp.where(row < 2 * ROWS + LANG, 1, 0)
    coarse = jnp.where(lane == 0, jnp.where(first, 1, 0), jnp.where(second, 1, 0))
    return key_marks(jnp.where(klass == 1, fine, coarse) == 1, 2)


def joint_row_marks():
    shape = (ROWS, PAIR)
    row, lane = row_of(shape), in_half(shape)
    return jnp.where(lane == row // (ROWS // 2), 1.0, 0.0).astype(BF)


def view_key_marks(klass):
    shape = (PADDED, PAIR)
    row, lane = row_of(shape), in_half(shape)
    same = jnp.where(lane == row % VB // VS, 1, 0)
    return key_marks(jnp.where(klass == 1, 1, same) == 1, 4)


def view_row_marks():
    shape = (PADDED, PAIR)
    row, lane = row_of(shape), in_half(shape)
    return jnp.where(lane == row % VB // VS, 1.0, 0.0).astype(BF)


def with_parts(values):
    lane = in_half(values.shape)
    high = values.astype(BF).astype(F32)
    rest = values - high
    middle = rest.astype(BF).astype(F32)
    low = rest - middle
    picked = jnp.where(lane == 4, -high, jnp.where(lane == 5, -middle, jnp.where(lane == 6, -low, 0.0)))
    return picked.astype(BF)


def attend_heads(units):
    scores = [mat_right(keys, right) for right, keys, across in units]
    weights = [jnp.exp(part - jnp.max(part, axis=0, keepdims=True)).astype(BF) for part in scores]
    outs = [matmul(unit[2], part) for unit, part in zip(units, weights)]
    shares = [1.0 / out[HD : HD + 1] for out in outs]
    return [(part, out[:HD] * share, share) for part, out, share in zip(weights, outs, shares)]


def score_side(query, marks, head):
    mask = lane_mask(head)
    return jnp.concatenate([query * mask, marks * mask], axis=1)


def joint_place(klass, side, kv_ref, far_ref, lang_ref, put):
    put(slice(0, ROWS), kv_ref[...])

    @pl.when(klass == 1)
    def fine():
        put(slice(ROWS, 2 * ROWS), far_ref[:ROWS])

        @pl.when(side == 0)
        def own():
            put(slice(2 * ROWS, KEYS), lang_ref[:LONE])

        @pl.when(side == 1)
        def partner():
            put(slice(2 * ROWS, KEYS), far_ref[ROWS:])

    @pl.when(klass != 1)
    def coarse():
        put(slice(ROWS, ROWS + LPAD), lang_ref[...])


def joint_forward_kernel(
    flags, q_ref, kv_ref, far_ref, lang_ref, mixed_ref, weights_ref, share_ref, keys, values, across, marks
):
    klass, side = flags[0], flags[1]

    @pl.when(pl.program_id(0) == 0)
    def prepare():
        keys[...] = jnp.zeros_like(keys)
        values[...] = jnp.zeros_like(values)
        across[...] = jnp.ones_like(across)
        keys[:, PAIR:] = joint_key_marks(klass)
        marks[...] = joint_row_marks()

    def put(rows, block):
        keys[rows, :PAIR] = block[:, :PAIR]
        values[rows, :] = block[:, PAIR:]

    joint_place(klass, side, kv_ref, far_ref, lang_ref, put)
    turned = values[...].T
    for head in range(2):
        across[head, :HD, :] = turned[head * HD : (head + 1) * HD, :]

    units = [(score_side(q_ref[...], marks[...], head), keys[...], across[head]) for head in range(2)]
    done = attend_heads(units)
    for head in range(2):
        weights_ref[head] = done[head][0]
        share_ref[0, head : head + 1, :] = done[head][2]
    mixed_ref[...] = jnp.concatenate([done[0][1], done[1][1]], axis=0).T.astype(BF)


def joint_forward(flags, query, kv, far, lang):
    rows = query.shape[0]
    return pl.pallas_call(
        joint_forward_kernel,
        grid_spec=pltpu.PrefetchScalarGridSpec(
            num_scalar_prefetch=1,
            grid=(HEADS // 2,),
            in_specs=[
                pl.BlockSpec((rows, PAIR), lambda i, f: (0, i)),
                pl.BlockSpec((rows, 2 * PAIR), lambda i, f: (0, i)),
                pl.BlockSpec((ROWS + LONE, 2 * PAIR), lambda i, f: (0, i)),
                pl.BlockSpec((LPAD, 2 * PAIR), lambda i, f: (0, i)),
            ],
            out_specs=[
                pl.BlockSpec((rows, PAIR), lambda i, f: (0, i)),
                pl.BlockSpec((2, KEYS, rows), lambda i, f: (i, 0, 0)),
                pl.BlockSpec((1, 8, rows), lambda i, f: (i, 0, 0)),
            ],
            scratch_shapes=[
                pltpu.VMEM((KEYS, 2 * PAIR), BF),
                pltpu.VMEM((KEYS, PAIR), BF),
                pltpu.VMEM((2, HD + 16, KEYS), BF),
                pltpu.VMEM((ROWS, PAIR), BF),
            ],
        ),
        out_shape=[
            jax.ShapeDtypeStruct((rows, HEADS * HD), BF),
            jax.ShapeDtypeStruct((HEADS, KEYS, rows), BF),
            jax.ShapeDtypeStruct((HEADS // 2, 8, rows), F32),
        ],
        compiler_params=pltpu.CompilerParams(vmem_limit_bytes=JOINT_VMEM),
        cost_estimate=cost_of(20),
        name="joint_forward",
    )(flags, query, kv, far, lang)


def inner_marks(grad, mixed):
    lanes = lax.broadcasted_iota(jnp.int32, (1, PAIR), 1)
    product = grad.astype(F32) * mixed.astype(F32)
    first = jnp.sum(jnp.where(lanes < HD, product, 0.0), axis=1, keepdims=True)
    second = jnp.sum(jnp.where(lanes < HD, 0.0, product), axis=1, keepdims=True)
    return with_parts(jnp.where(lanes < HD, first, second))


def attend_back(units):
    inner = [mat_right(unit[0], unit[5]) for unit in units]
    probs = [unit[2].astype(F32) * unit[3] for unit in units]
    grad_scores = [(left * right).astype(BF) for left, right in zip(probs, inner)]
    grad_values = [matmul(part.astype(BF), unit[5][:, :PAIR]) for part, unit in zip(probs, units)]
    grad_keys = [matmul(part, unit[4]) for part, unit in zip(grad_scores, units)]
    across = [matmul(unit[1], part) for part, unit in zip(grad_scores, units)]
    return list(zip(grad_keys, grad_values, across))


def fill_rows(left, grads, rows, query, grad, mixed):
    inner = inner_marks(grad, mixed)
    for head in range(2):
        mask = lane_mask(head)
        left[head, rows, :] = query * mask
        grads[head, rows, :PAIR] = grad * mask
        grads[head, rows, PAIR:] = inner * mask


def joint_backward_kernel(
    flags, q_ref, kv_ref, far_ref, lang_ref, mixed_ref, weights_ref, share_ref, grad_ref, dq_ref, dkv_ref,
    dfar_key, dfar_value, keys, values, across, left, grads,
):
    klass, side = flags[0], flags[1]

    @pl.when(pl.program_id(0) == 0)
    def prepare():
        keys[...] = jnp.zeros_like(keys)
        values[...] = jnp.zeros_like(values)
        values[:, PAIR:] = joint_key_marks(klass)

    def put(rows, block):
        keys[rows, :] = block[:, :PAIR]
        values[rows, :PAIR] = block[:, PAIR:]

    joint_place(klass, side, kv_ref, far_ref, lang_ref, put)
    across[...] = keys[...].T
    fill_rows(left, grads, slice(0, ROWS), q_ref[...], grad_ref[...], mixed_ref[...])
    units = [
        (
            values[...],
            across[head * HD : (head + 1) * HD, :],
            weights_ref[head],
            share_ref[0, head : head + 1, :],
            left[head],
            grads[head],
        )
        for head in range(2)
    ]
    first, second = attend_back(units)
    for span, at, far in ((slice(0, PAIR), 0, dfar_key), (slice(PAIR, 2 * PAIR), 1, dfar_value)):
        both = (first[at] + second[at]).astype(BF)
        dkv_ref[:, span] = both[:ROWS]
        far[...] = both[ROWS:]
    dq_ref[...] = jnp.concatenate([first[2], second[2]], axis=0).T.astype(BF)


def joint_backward(flags, query, kv, far, lang, mixed, weights, share, grad, base, pairs, after=(), cost=LONG):
    rows = query.shape[0]
    one = pl.BlockSpec((rows, PAIR), lambda i, f: (0, i + base))
    return pl.pallas_call(
        waiting(joint_backward_kernel, 9, len(after)),
        grid_spec=pltpu.PrefetchScalarGridSpec(
            num_scalar_prefetch=1,
            grid=(pairs,),
            in_specs=[
                one,
                pl.BlockSpec((rows, 2 * PAIR), lambda i, f: (0, i + base)),
                pl.BlockSpec((ROWS + LONE, 2 * PAIR), lambda i, f: (0, i + base)),
                pl.BlockSpec((LPAD, 2 * PAIR), lambda i, f: (0, i + base)),
                one,
                pl.BlockSpec((2, KEYS, rows), lambda i, f: (i + base, 0, 0)),
                pl.BlockSpec((1, 8, rows), lambda i, f: (i + base, 0, 0)),
                one,
            ]
            + [pl.BlockSpec(memory_space=pl.ANY)] * len(after),
            out_specs=[
                pl.BlockSpec((rows, PAIR), lambda i, f: (0, i)),
                pl.BlockSpec((rows, 2 * PAIR), lambda i, f: (0, i)),
                pl.BlockSpec((ROWS + LONE, PAIR), lambda i, f: (0, i)),
                pl.BlockSpec((ROWS + LONE, PAIR), lambda i, f: (0, i)),
            ],
            scratch_shapes=[
                pltpu.VMEM((KEYS, PAIR), BF),
                pltpu.VMEM((KEYS, 2 * PAIR), BF),
                pltpu.VMEM((PAIR, KEYS), BF),
                pltpu.VMEM((2, ROWS, PAIR), BF),
                pltpu.VMEM((2, ROWS, 2 * PAIR), BF),
            ],
        ),
        out_shape=[
            jax.ShapeDtypeStruct((rows, pairs * PAIR), BF),
            jax.ShapeDtypeStruct((rows, 2 * pairs * PAIR), BF),
            jax.ShapeDtypeStruct((ROWS + LONE, pairs * PAIR), BF),
            jax.ShapeDtypeStruct((ROWS + LONE, pairs * PAIR), BF),
        ],
        compiler_params=pltpu.CompilerParams(vmem_limit_bytes=JOINT_BACK_VMEM),
        cost_estimate=cost_of(cost),
        name="joint_backward",
    )(flags, query, kv, far, lang, mixed, weights, share, grad, *after)


def view_spots(side):
    own = pl.ds(pl.multiple_of(side * EDGE, 16), ROWS)
    far = pl.ds(pl.multiple_of((1 - side) * ROWS, 16), EDGE)
    return (own, far)


def view_forward_kernel(
    flags, q_ref, kv_ref, edge_ref, gain, bias, w_key, w_value, mixed_ref, weights_ref, share_ref, far_ref,
    rows_q, keys, values, across, marks, out, edge,
):
    klass, side = flags[0], flags[1]
    own, far = view_spots(side)

    @pl.when(pl.program_id(0) == 0)
    def prepare():
        rows_q[...] = jnp.zeros_like(rows_q)
        across[...] = jnp.ones_like(across)
        keys[:, PAIR:] = view_key_marks(klass)
        marks[...] = view_row_marks()
        unit, scale = centre(edge_ref[...].astype(F32))
        edge[...] = (unit * gain[0, 0:1] + bias[0, 0:1]).astype(BF)

    far_ref[:, :PAIR] = matmul(edge[...], w_key[0, 0]).astype(BF)
    far_ref[:, PAIR:] = matmul(edge[...], w_value[0, 0]).astype(BF)
    rows_q[own, :] = q_ref[...]
    for rows, ref in ((own, kv_ref), (far, far_ref)):
        keys[rows, :PAIR] = ref[:, :PAIR]
        values[rows, :] = ref[:, PAIR:]

    units = []
    for index in range(PADDED // VB):
        rows = slice(index * VB, (index + 1) * VB)
        turned = values[rows, :].T
        for head in range(2):
            across[index, head, :HD, :] = turned[head * HD : (head + 1) * HD, :]
            right = score_side(rows_q[rows, :], marks[rows, :], head)
            units.append((right, keys[rows, :], across[index, head]))
    done = attend_heads(units)
    for index in range(PADDED // VB):
        rows = slice(index * VB, (index + 1) * VB)
        for head in range(2):
            weights_ref[index, head] = done[2 * index + head][0]
            share_ref[index, 0, head : head + 1, :] = done[2 * index + head][2]
        pair = [done[2 * index + head][1] for head in range(2)]
        out[rows, :] = jnp.concatenate(pair, axis=0).T.astype(BF)

    mixed_ref[...] = out[own, :]


def view_forward(flags, query, kv, edge, gain, bias, w_attn):
    rows, width = query.shape
    blocks = PADDED // VB
    one = pl.BlockSpec((rows, PAIR), lambda i, f: (0, i))
    whole = pl.BlockSpec(gain.shape, lambda i, f: (0, 0, 0))
    return pl.pallas_call(
        view_forward_kernel,
        grid_spec=pltpu.PrefetchScalarGridSpec(
            num_scalar_prefetch=1,
            grid=(HEADS // 2,),
            in_specs=[
                one,
                pl.BlockSpec((rows, 2 * PAIR), lambda i, f: (0, i)),
                pl.BlockSpec((EDGE, width), lambda i, f: (0, 0)),
                whole,
                whole,
                pl.BlockSpec((1, 1, width, PAIR), lambda i, f: (0, 1, 0, i)),
                pl.BlockSpec((1, 1, width, PAIR), lambda i, f: (0, 2, 0, i)),
            ],
            out_specs=[
                one,
                pl.BlockSpec((blocks, 2, VB, VB), lambda i, f: (0, i, 0, 0)),
                pl.BlockSpec((blocks, 1, 8, VB), lambda i, f: (0, i, 0, 0)),
                pl.BlockSpec((EDGE, 2 * PAIR), lambda i, f: (0, i)),
            ],
            scratch_shapes=[
                pltpu.VMEM((PADDED, PAIR), BF),
                pltpu.VMEM((PADDED, 2 * PAIR), BF),
                pltpu.VMEM((PADDED, PAIR), BF),
                pltpu.VMEM((blocks, 2, HD + 16, VB), BF),
                pltpu.VMEM((PADDED, PAIR), BF),
                pltpu.VMEM((PADDED, PAIR), BF),
                pltpu.VMEM((EDGE, width), BF),
            ],
        ),
        out_shape=[
            jax.ShapeDtypeStruct((rows, HEADS * HD), BF),
            jax.ShapeDtypeStruct((blocks, HEADS, VB, VB), BF),
            jax.ShapeDtypeStruct((blocks, HEADS // 2, 8, VB), F32),
            jax.ShapeDtypeStruct((EDGE, 2 * width), BF),
        ],
        compiler_params=pltpu.CompilerParams(vmem_limit_bytes=VIEW_VMEM),
        cost_estimate=cost_of(10),
        name="view_forward",
    )(flags, query, kv, edge, gain, bias, w_attn, w_attn)


def view_backward_kernel(
    flags, q_ref, kv_ref, far_ref, mixed_ref, weights_ref, share_ref, grad_ref, dq_ref, dkv_ref, dfar_ref,
    keys, values, left, grads, back, dkv,
):
    klass, side = flags[0], flags[1]
    own, far = view_spots(side)

    @pl.when(pl.program_id(0) == 0)
    def prepare():
        values[:, PAIR:] = view_key_marks(klass)
        left[...] = jnp.zeros_like(left)
        grads[...] = jnp.zeros_like(grads)

    for rows, ref in ((own, kv_ref), (far, far_ref)):
        keys[rows, :] = ref[:, :PAIR]
        values[rows, :PAIR] = ref[:, PAIR:]
    fill_rows(left, grads, own, q_ref[...], grad_ref[...], mixed_ref[...])

    units = []
    for index in range(PADDED // VB):
        rows = slice(index * VB, (index + 1) * VB)
        across = keys[rows, :].T
        for head in range(2):
            units.append(
                (
                    values[rows, :],
                    across[head * HD : (head + 1) * HD, :],
                    weights_ref[index, head],
                    share_ref[index, 0, head : head + 1, :],
                    left[head, rows, :],
                    grads[head, rows, :],
                )
            )
    done = attend_back(units)
    for index in range(PADDED // VB):
        rows = slice(index * VB, (index + 1) * VB)
        first, second = done[2 * index], done[2 * index + 1]
        dkv[rows, :PAIR] = (first[0] + second[0]).astype(BF)
        dkv[rows, PAIR:] = (first[1] + second[1]).astype(BF)
        back[rows, :] = jnp.concatenate([first[2], second[2]], axis=0).T.astype(BF)

    dq_ref[...] = back[own, :]
    dkv_ref[...] = dkv[own, :]
    dfar_ref[...] = dkv[far, :]


def view_backward(flags, query, kv, far, mixed, weights, share, grad, base, pairs, after=(), cost=LONG):
    rows = query.shape[0]
    blocks = PADDED // VB
    one = pl.BlockSpec((rows, PAIR), lambda i, f: (0, i + base))
    two = pl.BlockSpec((rows, 2 * PAIR), lambda i, f: (0, i + base))
    edge = pl.BlockSpec((EDGE, 2 * PAIR), lambda i, f: (0, i + base))
    return pl.pallas_call(
        waiting(view_backward_kernel, 8, len(after)),
        grid_spec=pltpu.PrefetchScalarGridSpec(
            num_scalar_prefetch=1,
            grid=(pairs,),
            in_specs=[
                one,
                two,
                edge,
                one,
                pl.BlockSpec((blocks, 2, VB, VB), lambda i, f: (0, i + base, 0, 0)),
                pl.BlockSpec((blocks, 1, 8, VB), lambda i, f: (0, i + base, 0, 0)),
                one,
            ]
            + [pl.BlockSpec(memory_space=pl.ANY)] * len(after),
            out_specs=[
                pl.BlockSpec((rows, PAIR), lambda i, f: (0, i)),
                pl.BlockSpec((rows, 2 * PAIR), lambda i, f: (0, i)),
                pl.BlockSpec((EDGE, 2 * PAIR), lambda i, f: (0, i)),
            ],
            scratch_shapes=[
                pltpu.VMEM((PADDED, PAIR), BF),
                pltpu.VMEM((PADDED, 2 * PAIR), BF),
                pltpu.VMEM((2, PADDED, PAIR), BF),
                pltpu.VMEM((2, PADDED, 2 * PAIR), BF),
                pltpu.VMEM((PADDED, PAIR), BF),
                pltpu.VMEM((PADDED, 2 * PAIR), BF),
            ],
        ),
        out_shape=[
            jax.ShapeDtypeStruct((rows, pairs * PAIR), BF),
            jax.ShapeDtypeStruct((rows, 2 * pairs * PAIR), BF),
            jax.ShapeDtypeStruct((EDGE, 2 * pairs * PAIR), BF),
        ],
        compiler_params=pltpu.CompilerParams(vmem_limit_bytes=VIEW_VMEM),
        cost_estimate=cost_of(cost),
        name="view_backward",
    )(flags, query, kv, far, mixed, weights, share, grad, *after)


CHUNK = 512
DOWN_ROWS = 128
BITS = SLICES.bit_length() - 1


class Route:
    def __init__(self, steps, halves):
        self.steps = steps
        self.halves = halves
        self.order = [bit for step in steps for bit in step]
        self.units = 1 << len(self.order)

    def unit(self, position):
        last = len(self.order) - 1
        return sum((position >> (last - at) & 1) << bit for at, bit in enumerate(self.order))

    def parts(self, step):
        return 1 << len(self.steps[step])

    def rows(self, rows):
        return rows // 2 if self.halves else rows


PLAIN = Route(((0,), (1,), (2,), (3,)), False)
SPLIT = Route(((1,), (0,), (2,), (3,), (4,)), True)
LAST = Route(((1,), (0,), (2,), (3, 4)), True)


def hand_out(held, parts, flags, route):
    each = route.units // len(parts)
    rows = route.rows(held.shape[1])
    for position in range(route.units):
        if route.halves:
            unit = jnp.bitwise_xor(route.unit(position), flags[2] * 2 + flags[3])
            block = held[unit // 2, pl.ds(pl.multiple_of(unit % 2 * rows, 16), rows), :]
        else:
            block = held[jnp.bitwise_xor(route.unit(position), flags[2])]
        parts[position // each][position % each] = block


def part_shapes(route, rows, width):
    each = route.units // route.parts(0)
    return [((each, route.rows(rows), width), BF)] * route.parts(0)


def centre(values):
    mean = jnp.mean(values, axis=-1, keepdims=True)
    centered = values - mean
    variance = jnp.mean(centered * centered, axis=-1, keepdims=True)
    scale = lax.rsqrt(variance + epsilon)
    return (centered * scale, scale)


def norm_back(grad, unit, scale, gain):
    grad_gain = jnp.sum(grad * unit, axis=0, keepdims=True)
    grad_bias = jnp.sum(grad, axis=0, keepdims=True)
    scaled = grad * gain
    level = jnp.mean(scaled, axis=-1, keepdims=True)
    along = jnp.mean(scaled * unit, axis=-1, keepdims=True)
    return ((scaled - level - unit * along) * scale, grad_gain, grad_bias)


def gelu_both(hidden):
    root, cubic = 0.7978845608028654, 0.044715
    square = hidden * hidden
    bend = jnp.tanh(hidden * (root + (root * cubic) * square))
    half = 0.5 + 0.5 * bend
    slope = (0.5 * hidden) * (1.0 - bend * bend) * (root + (3.0 * root * cubic) * square)
    return (hidden * half, half + slope)


def mix(keys, values):
    parts = []
    for at in range(0, keys.shape[1], PAIR):
        parts += [keys[:, at : at + PAIR], values[:, at : at + PAIR]]
    return jnp.concatenate(parts, axis=1)


def unmix(both):
    blocks = [both[:, at : at + PAIR] for at in range(0, both.shape[1], PAIR)]
    return (jnp.concatenate(blocks[0::2], axis=1), jnp.concatenate(blocks[1::2], axis=1))


def project(normed, w_qkv, query, kv):
    kv[: normed.shape[0]] = mix(matmul(normed, w_qkv[1]).astype(BF), matmul(normed, w_qkv[2]).astype(BF))
    kv.send()
    query[...] = (matmul(normed, w_qkv[0]) * 0.125).astype(BF)


class Fetch:
    def __init__(self, source, buffer, semaphore, more):
        self.copy = pltpu.make_async_copy(source, buffer, semaphore)
        self.buffer, self.more, self.here = buffer, more, False

    def ref(self):
        if not self.here:
            self.copy.wait()
            self.here = True
            self.more(2)
        return self.buffer

    def __getitem__(self, index):
        return self.ref()[index]


class Store:
    def __init__(self, buffer, target, semaphores, pieces):
        self.buffer, self.copies, self.gone = buffer, [], []
        for at, piece in enumerate(pieces):
            source = buffer if piece is None else buffer.at[piece]
            place = target if piece is None else target.at[piece]
            self.copies.append(pltpu.make_async_copy(source, place, semaphores.at[at]))
            self.gone.append(False)

    def __setitem__(self, index, value):
        self.buffer[index] = value

    def __getitem__(self, index):
        return self.buffer[index]

    def send(self, at=None):
        for place, copy in enumerate(self.copies):
            if not self.gone[place] and at in (None, place):
                copy.start()
                self.gone[place] = True


LEAD = 4


def dense_call(kernel, name, operands, fetches, outs, cost, scratch=(), flags=None, after=(), pieces=None, lead=LEAD):
    shapes = [
        jax.eval_shape(lambda array, index=index: array if index is None else array[index], operands[at])
        for at, index in fetches
    ]
    count, first = len(operands), 0 if flags is None else 1
    pieces = [(pieces or {}).get(at, (None,)) for at in range(len(outs))]

    def run(*refs):
        inputs = refs[first : first + count]
        rest = refs[first + count + len(after) :]
        targets, rest = rest[: len(outs)], rest[len(outs) :]
        buffers, rest = rest[: len(fetches)], rest[len(fetches) :]
        held, rest = rest[: len(outs)], rest[len(outs) :]
        came, went, own = rest[0], rest[1 : 1 + len(outs)], rest[1 + len(outs) :]
        fetched, started = [], [0]

        def more(number):
            for fetch in fetched[started[0] : started[0] + number]:
                fetch.copy.start()
            started[0] += number

        for place, (at, index) in enumerate(fetches):
            source = inputs[at] if index is None else inputs[at].at[index]
            fetched.append(Fetch(source, buffers[place], came.at[place], more))
        more(lead)
        stores = [Store(*parts) for parts in zip(held, targets, went, pieces)]
        kernel(*([refs[0]] if first else []), fetched, stores, *own)
        for fetch in fetched:
            fetch.ref()
        for store in stores:
            store.send()
        for store in stores:
            for copy in store.copies:
                copy.wait()

    anywhere = pl.BlockSpec(memory_space=pl.ANY)
    return pl.pallas_call(
        run,
        in_specs=[pl.BlockSpec(memory_space=pltpu.SMEM)] * first + [anywhere] * (count + len(after)),
        out_specs=[anywhere] * len(outs),
        out_shape=[jax.ShapeDtypeStruct(shape, kind) for shape, kind in outs],
        scratch_shapes=[pltpu.VMEM(part.shape, part.dtype) for part in shapes]
        + [pltpu.VMEM(shape, kind) for shape, kind in outs]
        + [pltpu.SemaphoreType.DMA((len(fetches),))]
        + [pltpu.SemaphoreType.DMA((len(piece),)) for piece in pieces]
        + list(scratch),
        compiler_params=pltpu.CompilerParams(vmem_limit_bytes=DENSE_VMEM),
        cost_estimate=cost_of(cost),
        name=name,
    )(*([flags] if first else []), *operands, *after)


def near_call(kernel, name, outs, args, scratch=(), flags=None, after=(), cost=SHORT):
    vmem = pl.BlockSpec(memory_space=pltpu.VMEM)
    specs = [vmem] * len(args)
    if flags is not None:
        specs = [pl.BlockSpec(memory_space=pltpu.SMEM)] + specs
        args = [flags] + list(args)
    return pl.pallas_call(
        waiting(kernel, len(args), len(after)),
        in_specs=specs + [pl.BlockSpec(memory_space=pl.ANY)] * len(after),
        out_specs=[vmem] * len(outs),
        out_shape=[jax.ShapeDtypeStruct(shape, kind) for shape, kind in outs],
        scratch_shapes=list(scratch),
        compiler_params=pltpu.CompilerParams(vmem_limit_bytes=NEAR_VMEM),
        cost_estimate=cost_of(cost),
        name=name,
    )(*args, *after)


QKV = slice(0, 3)


def enter_kernel(layer, fetched, stores):
    x, gain, bias, w_qkv = fetched
    normed, query, kv = stores
    unit, scale = centre(x[...].astype(F32))
    low = (unit * gain[layer, 0:1] + bias[layer, 0:1]).astype(BF)
    normed[...] = low
    normed.send()
    project(low, w_qkv, query, kv)


def enter(x, gain, bias, w_attn, layer):
    rows, width = x.shape
    return dense_call(
        functools.partial(enter_kernel, layer),
        "enter",
        (x, gain, bias, w_attn),
        [(0, None), (1, None), (2, None), (3, (layer, QKV))],
        [((rows, width), BF), ((rows, width), BF), ((rows, 2 * width), BF)],
        SHORT,
    )


def chunks(hidden):
    return [slice(at, at + CHUNK) for at in range(0, hidden, CHUNK)]


def wide_pieces(hidden):
    return [(slice(None), span) for span in chunks(hidden)]


def mlp_fetches(layer, up_at, down_at, hidden):
    found = []
    for span in chunks(hidden):
        found += [(up_at, (layer, slice(None), span)), (down_at, (layer, span))]
    return found


def middle_kernel(fetched, stores):
    x, mixed, w_out, gain, bias, ff_bias, out_bias = fetched[:7]
    mlp, (language, w_lang, w_qkv) = fetched[7:-3], fetched[-3:]
    after, normed, active, slope, state, next_normed, query, kv, feats, lang_normed, lang_kv = stores
    total = x[...].astype(F32) + matmul(mixed[...], w_out[...])
    after[...] = total
    after.send()
    unit, scale = centre(total)
    low = (unit * gain[0, 1:2] + bias[0, 1:2]).astype(BF)
    normed[...] = low
    normed.send()
    total = total + out_bias[0:1, :]
    for at in range(0, len(mlp), 2):
        span = slice(at // 2 * CHUNK, (at // 2 + 1) * CHUNK)
        value, rise = gelu_both(matmul(low, mlp[at][...]) + ff_bias[0:1, span])
        value = value.astype(BF)
        active[:, span] = value
        active.send(at // 2)
        slope[:, span] = rise.astype(BF)
        slope.send(at // 2)
        total = total + matmul(value, mlp[at + 1][...])
    found = matmul(language[...], w_lang[...])
    feats[...] = found
    feats.send()
    unit, scale = centre(found)
    low = (unit * gain[1, 0:1] + bias[1, 0:1]).astype(BF)
    lang_normed[...] = low
    lang_normed.send()
    both = mix(matmul(low, w_qkv[1]).astype(BF), matmul(low, w_qkv[2]).astype(BF))
    lang_kv[...] = both
    lang_kv.send()
    kv[ROWS:] = both[:LONE]
    state[...] = total
    state.send()
    unit, scale = centre(total)
    low = (unit * gain[1, 0:1] + bias[1, 0:1]).astype(BF)
    next_normed[...] = low
    next_normed.send()
    project(low, w_qkv, query, kv)


def middle(x, mixed, gain, bias, w_attn, w_up, ff_bias, w_down, out_bias, language, w_lang):
    rows, width = x.shape
    hidden = w_up.shape[2]
    return dense_call(
        middle_kernel,
        "middle",
        (x, mixed, gain, bias, w_attn, ff_bias, out_bias, w_up, w_down, language, w_lang),
        [(0, None), (1, None), (4, (0, 3)), (2, None), (3, None), (5, None), (6, None)]
        + mlp_fetches(0, 7, 8, hidden)
        + [(9, None), (10, None), (4, (1, QKV))],
        [
            ((rows, width), F32),
            ((rows, width), BF),
            ((rows, hidden), BF),
            ((rows, hidden), BF),
            ((rows, width), F32),
            ((rows, width), BF),
            ((rows, width), BF),
            ((rows + LONE, 2 * width), BF),
            ((LPAD, width), F32),
            ((LPAD, width), BF),
            ((LPAD, 2 * width), BF),
        ],
        LONG,
        pieces={2: wide_pieces(hidden), 3: wide_pieces(hidden)},
        lead=7,
    )


def put_up(held, at, grad):
    rows = grad.shape[0] // SLICES
    put_rows(held, at // CHUNK * rows, grad)


def put_down(held, at, start, grad):
    rows = DOWN_ROWS
    for piece in range(grad.shape[0] // rows):
        held[at // rows + piece, start : start + rows, :] = grad[piece * rows : (piece + 1) * rows]


def put_rows(held, place, grad):
    rows = grad.shape[0] // SLICES
    for piece in range(SLICES):
        held[piece, place : place + rows, :] = grad[piece * rows : (piece + 1) * rows]


def mlp_tail(layer, grad, grad_normed, unit, scale, gain, mixed, w_out, ups, place, out_grad, out_mixed, small):
    width = unit.shape[1]
    grad_state, grad_gain, grad_bias = norm_back(grad_normed, unit, scale, gain[layer, 1:2])
    grad = grad + grad_state
    out_grad[...] = grad
    out_grad.send()
    small[1:2, :width] = grad_gain
    small[1:2, width : 2 * width] = grad_bias
    low = grad.astype(BF)
    put_rows(ups, place, mat_left(mixed[...], low).astype(BF))
    out_mixed[...] = mat_right(low, w_out[...]).astype(BF)
    out_mixed.send()


def mlp_chunk(span, low, grad_low, slope, w_up, w_down, ups, small):
    grad_hidden = slope * mat_right(grad_low, w_down)
    hidden_low = grad_hidden.astype(BF)
    put_up(ups, span.start, mat_left(low, hidden_low).astype(BF))
    small[0:1, span] = jnp.sum(hidden_low.astype(F32), axis=0, keepdims=True)
    return mat_right(hidden_low, w_up)


def turn_kernel(flags, fetched, stores, weights):
    x, mixed, w_out, gain, bias, ff_bias, cotangent = fetched[:7]
    mlp = fetched[7:]
    out_grad, out_mixed, keep, send, small = stores
    small[...] = jnp.zeros(small.buffer.shape, F32)
    total = x[...] + matmul(mixed[...], w_out[...])
    width = total.shape[1]
    hidden = len(mlp) // 2 * CHUNK
    unit, scale = centre(total)
    low = (unit * gain[1, 1:2] + bias[1, 1:2]).astype(BF)
    grad_low = cotangent[...]
    grad = grad_low.astype(F32)
    small[1:2, 2 * width : 3 * width] = jnp.sum(grad, axis=0, keepdims=True)
    grad_normed = None
    for at, span in enumerate(chunks(hidden)):
        w_up, w_down = mlp[2 * at][...], mlp[2 * at + 1][...]
        value, rise = gelu_both(matmul(low, w_up) + ff_bias[1:2, span])
        part = mlp_chunk(span, low, grad_low, rise, w_up, w_down, weights, small)
        put_down(weights, span.start, DOWN_ROWS, mat_left(value.astype(BF), grad_low).astype(BF))
        grad_normed = part if grad_normed is None else grad_normed + part
    mlp_tail(
        1, grad, grad_normed, unit, scale, gain, mixed, w_out, weights, hidden // SLICES + DOWN_ROWS,
        out_grad, out_mixed, small,
    )
    hand_out(weights, (keep, send), flags, PLAIN)


def turn(flags, x, mixed, gain, bias, w_attn, w_up, ff_bias, w_down, cotangent):
    rows, width = x.shape
    hidden = w_up.shape[2]
    held = (2 * hidden + width) // SLICES
    done = dense_call(
        turn_kernel, "turn",
        (x, mixed, gain, bias, w_attn, ff_bias, cotangent, w_up, w_down),
        [(0, None), (1, None), (4, (1, 3)), (2, None), (3, None), (5, None), (6, None)]
        + mlp_fetches(1, 7, 8, hidden),
        [((rows, width), F32), ((rows, width), BF)] + part_shapes(PLAIN, held, width) + [((8, hidden), F32)],
        LONG,
        [pltpu.VMEM((SLICES, held, width), BF)],
        flags,
        lead=7,
    )
    return (done[0], done[1], done[2:4], done[4])


def beside(*blocks):
    return jnp.concatenate([block[...] for block in blocks], axis=1)


def leave_grad(unit, scale, gain, grad, grad_query, grad_key, grad_value, w_qkv):
    grad_normed = mat_right(grad_query, w_qkv[0]) * 0.125
    grad_normed = grad_normed + mat_right(grad_key, w_qkv[1]) + mat_right(grad_value, w_qkv[2])
    grad_state, grad_gain, grad_bias = norm_back(grad_normed, unit, scale, gain)
    return (grad + grad_state, grad_gain, grad_bias)


def leave_kernel(flags, fetched, stores, sums, held):
    query_one, query_two, normed, kv_one, kv_two, far_one, far_two, x, gain, w_qkv, grad = fetched[:11]
    out, keep, send, token = stores
    token[...] = jnp.zeros(token.buffer.shape, F32)
    grad_query = beside(query_one, query_two)
    low = normed[...]
    width = low.shape[1]
    place = width // SLICES
    put_rows(held, 0, (mat_left(low, grad_query) * 0.125).astype(BF))
    sums[...] = beside(kv_one, kv_two).astype(F32)
    rows = pl.ds(pl.multiple_of((1 - flags[1]) * (ROWS - EDGE), 16), EDGE)
    sums[rows, :] += beside(far_one, far_two).astype(F32)
    grad_key, grad_value = unmix(sums[...].astype(BF))
    put_rows(held, place, mat_left(low, grad_key).astype(BF))
    put_rows(held, 2 * place, mat_left(low, grad_value).astype(BF))
    unit, scale = centre(x[...].astype(F32))
    total, grad_gain, grad_bias = leave_grad(
        unit, scale, gain[0, 0:1], grad[...], grad_query, grad_key, grad_value, w_qkv
    )
    out[...] = total
    out.send()
    put_small(held, 3 * place, fetched[11:], grad_gain, grad_bias)
    hand_out(held, (keep, send), flags, LAST)


SMALL_ROWS = 32


def put_small(held, place, small, grad_gain, grad_bias):
    width = grad_gain.shape[1]
    rows = [grad_gain, small[0][1:2, :width], small[2][0:1, :width], small[1][1:2, :width]]
    rows += [grad_bias, small[0][1:2, width : 2 * width], small[2][0:1, width : 2 * width]]
    rows += [small[1][1:2, width : 2 * width]]
    rows += [small[at][1:2, 2 * width : 3 * width] for at in range(2)]
    block = jnp.concatenate(rows, axis=0)
    long = jnp.concatenate([small[at][0:1, :] for at in range(2)], axis=0)
    each, more = width // SLICES, long.shape[1] // SLICES
    for piece in range(SLICES):
        head = jnp.pad(block[:, piece * each : (piece + 1) * each], ((0, 0), (0, more - each)))
        tail = long[:, piece * more : (piece + 1) * more]
        rest = jnp.zeros((SMALL_ROWS - head.shape[0] - tail.shape[0], more), F32)
        both = jnp.concatenate([head, tail, rest], axis=0).astype(BF)
        held[piece, place : place + SMALL_ROWS, :] = jnp.pad(both, ((0, 0), (0, width - more)))


def leave(flags, x, gain, normed, grad, queries, kvs, fars, w_attn, smalls, after):
    rows, width = x.shape
    held = 3 * (width // SLICES) + SMALL_ROWS
    done = dense_call(
        leave_kernel, "leave",
        (*queries, normed, *kvs, *fars, x, gain, w_attn, grad, *smalls),
        [(at, None) for at in range(9)] + [(9, (0, QKV))] + [(at, None) for at in range(10, 14)],
        [((rows, width), F32)] + part_shapes(LAST, held, width) + [((8, PAIR), F32)],
        4.0,
        [pltpu.VMEM((rows, 2 * width), F32), pltpu.VMEM((SLICES, held, width), BF)],
        flags,
        after,
        lead=8,
    )
    return (done[0], done[1:3], done[3])


def put_sums(klass, side, sums, lang_sums, kv, here, far, own, there, span):
    @pl.when(klass == 1)
    def fine():
        sums[:, span] = (kv[:, here].astype(F32) + far[:ROWS, there].astype(F32)).astype(BF)

        @pl.when(side == 0)
        def owner():
            lang_sums[:LONE, span] = (own[ROWS:, there].astype(F32) + far[ROWS:, there].astype(F32)).astype(BF)

    @pl.when(klass != 1)
    def coarse():
        sums[:, span] = kv[:, here]
        lang_sums[:, span] = own[:LPAD, there]


def descend_kernel(flags, fetched, stores, sums, lang_sums, plain, split):
    query_one, query_two, normed, kv_one, kv_two = fetched[:5]
    fars, owns = (fetched[5:7], fetched[7:9]), (fetched[9:11], fetched[11:13])
    w_qkv, x, gain, grad, low_normed = fetched[13:18]
    mlp, (after, mixed, w_out, lang_normed, feats, language, w_lang) = fetched[18:-7], fetched[-7:]
    out_grad, out_mixed, grad_language, keep, send, split_keep, split_send, small, small_mid = stores
    klass, side = flags[0], flags[1]
    small[...] = jnp.zeros(small.buffer.shape, F32)
    small_mid[...] = jnp.zeros(small_mid.buffer.shape, F32)
    lang_sums[...] = jnp.zeros_like(lang_sums)
    fars = [[part.ref() for part in fars[at]] for at in range(2)]
    owns = [[part.ref() for part in owns[at]] for at in range(2)]
    at = 0
    for place, kv in enumerate((kv_one.ref(), kv_two.ref())):
        for pair in range(kv.shape[1] // PAIR // 2):
            for which in range(2):
                there = slice(pair * PAIR, (pair + 1) * PAIR)
                here = slice((2 * pair + which) * PAIR, (2 * pair + which + 1) * PAIR)
                span = slice(at, at + PAIR)
                at += PAIR
                put_sums(klass, side, sums, lang_sums, kv, here, fars[place][which], owns[place][which], there, span)

    grad_query, low = beside(query_one, query_two), normed[...]
    grad_key, grad_value = unmix(sums[...])
    width = low.shape[1]
    place = width // SLICES
    unit, scale = centre(x[...])
    grad, grad_gain, grad_bias = leave_grad(
        unit, scale, gain[1, 0:1], grad[...], grad_query, grad_key, grad_value, w_qkv
    )
    lang_key, lang_value = unmix(lang_sums[...])
    lang_low = lang_normed[...]
    hidden = len(mlp) // 4 * CHUNK
    up_rows = hidden // SLICES
    put_rows(plain, up_rows, (mat_left(low, grad_query) * 0.125).astype(BF))
    put_rows(plain, up_rows + place, (mat_left(low, grad_key) + mat_left(lang_low, lang_key)).astype(BF))
    put_rows(split, DOWN_ROWS, (mat_left(low, grad_value) + mat_left(lang_low, lang_value)).astype(BF))
    lang_grad = mat_right(lang_key, w_qkv[1]) + mat_right(lang_value, w_qkv[2])
    unit, scale = centre(feats[...])
    grad_feats, lang_gain, lang_bias = norm_back(lang_grad, unit, scale, gain[1, 0:1])
    feats_low = grad_feats.astype(BF)
    put_rows(split, DOWN_ROWS + place, mat_left(language[...], feats_low).astype(BF))
    grad_language[...] = mat_right(feats_low, w_lang[...])
    grad_language.send()
    small_mid[0:1, :width] = grad_gain + lang_gain
    small_mid[0:1, width : 2 * width] = grad_bias + lang_bias

    grad_low = grad.astype(BF)
    small[1:2, 2 * width : 3 * width] = jnp.sum(grad_low.astype(F32), axis=0, keepdims=True)
    low = low_normed[...]
    grad_normed = None
    for at, span in enumerate(chunks(hidden)):
        w_down, rise, w_up, active = [part[...] for part in mlp[4 * at : 4 * at + 4]]
        part = mlp_chunk(span, low, grad_low, rise.astype(F32), w_up, w_down, plain, small)
        put_down(split, span.start, 0, mat_left(active, grad_low).astype(BF))
        grad_normed = part if grad_normed is None else grad_normed + part
    unit, scale = centre(after[...])
    mlp_tail(
        0, grad, grad_normed, unit, scale, gain, mixed, w_out, split, DOWN_ROWS + 2 * place, out_grad, out_mixed, small
    )
    hand_out(plain, (keep, send), flags, PLAIN)
    send.send()
    hand_out(split, (split_keep, split_send), flags, SPLIT)


def descend(
    flags, state, gain, normed, grad, queries, kvs, fars, owns, w_attn, feats, lang_normed, language, w_lang,
    after, mixed, low_normed, active, slope, w_up, w_down, follows,
):
    rows, width = state.shape
    hidden = w_up.shape[2]
    place = width // SLICES
    plain, split = hidden // SLICES + 2 * place, DOWN_ROWS + 3 * place
    fetches = []
    for span in chunks(hidden):
        fetches += [(19, (0, span)), (20, (slice(None), span)), (18, (0, slice(None), span)), (21, (slice(None), span))]
    done = dense_call(
        descend_kernel, "descend",
        (*queries, normed, *kvs, *fars, *owns, w_attn, state, gain, grad, low_normed)
        + (w_up, w_down, slope, active, after, mixed, lang_normed, feats, language, w_lang),
        [(at, None) for at in range(13)]
        + [(13, (1, QKV))]
        + [(at, None) for at in range(14, 18)]
        + fetches
        + [(22, None), (23, None), (13, (0, 3)), (24, None), (25, None), (26, None), (27, None)],
        [((rows, width), F32), ((rows, width), BF), ((LPAD, width), F32)]
        + part_shapes(PLAIN, plain, width)
        + part_shapes(SPLIT, split, width)
        + [((8, hidden), F32), ((8, 2 * width), F32)],
        3.0,
        [
            pltpu.VMEM((rows, 2 * width), BF),
            pltpu.VMEM((LPAD, 2 * width), BF),
            pltpu.VMEM((SLICES, plain, width), BF),
            pltpu.VMEM((SLICES, split, width), BF),
        ],
        flags,
        follows,
        lead=18,
    )
    return (done[0], done[1], done[2], done[3:5], done[5:7], done[7], done[8])


def pair_swap(block):
    count = lax.axis_size("wide")
    return lax.ppermute(block, "wide", [(at, at ^ 1) for at in range(count)])


class Flow:
    def __init__(self, route, parts):
        self.route, self.step = route, 0
        self.units = route.units
        self.keep = [parts[0]]
        self.send(parts)

    def send(self, parts):
        self.got = []
        if self.step < len(self.route.steps):
            bits = self.route.steps[self.step]
            self.units //= 1 << len(bits)
            for at, part in enumerate(parts[1:], 1):
                found = [bit for place, bit in enumerate(bits) if at >> (len(bits) - 1 - place) & 1]
                self.got.append(self.move(part, found))
        else:
            self.keep = [parts[0]]
            self.got.append(self.move(parts[0], [0] if self.route.halves else None))

    def move(self, part, bits):
        shift = 1 if self.route.halves else 0
        if bits is None or bits == [0] and shift:
            return lax.ppermute(part, "narrow", [(0, 1), (1, 0)])
        count = lax.axis_size("wide")
        stride = sum((count // SLICES) << (bit - shift) for bit in bits)
        return lax.ppermute(part, "wide", [(p, p ^ stride) for p in range(count)])


def step_kernel(layout, ins, outs):
    at = 0
    for out, (count, rows) in zip(outs, layout):
        total = None
        for term in ins[at : at + count]:
            part = term[rows] if rows is not None else term[...]
            total = part.astype(F32) if total is None else total + part.astype(F32)
        out[...] = total.astype(BF)
        if isinstance(out, Store):
            out.send()
        at += count


def step(flows, after=(), near=False, cost=SHORT, lazy=False):
    operands, fetches, layout, outs, plan = [], [], [], [], []
    for flow in flows:
        flow.step += 1
        terms = flow.keep + flow.got
        last = flow.step == len(flow.route.steps)
        count = 1 if last else flow.route.parts(flow.step)
        each = flow.units // count
        made = [part for part in range(count) if part or last or not lazy]
        for part in reversed(made):
            rows = slice(part * each, (part + 1) * each)
            for term in terms:
                fetches.append((len(operands), rows))
                operands.append(term)
            layout.append((len(terms), rows))
            outs.append(((each,) + terms[0].shape[1:], BF))
        plan.append((flow, terms, count, made))
    if near:
        done = near_call(
            lambda *refs: step_kernel(layout, refs[: len(operands)], refs[len(operands) :]),
            "step", outs, operands, after=after, cost=cost,
        )
    else:
        done = dense_call(
            lambda ins, stores: step_kernel([(count, None) for count, rows in layout], ins, stores),
            "step", operands, fetches, outs, cost, after=after, lead=len(fetches),
        )
    at = 0
    for flow, terms, count, made in plan:
        parts = [None] * count
        for part in reversed(made):
            parts[part] = done[at]
            at += 1
        flow.keep = terms if parts[0] is None else [parts[0]]
        flow.send(parts)
    return done


def split_low(buffer):
    count = lax.axis_size("wide")
    position = lax.axis_index("wide")
    half = count // SLICES
    while half > 1:
        half //= 2
        mine = position // half % 2
        size = buffer.shape[0] // 2
        send = lax.dynamic_slice_in_dim(buffer, (1 - mine) * size, size, 0)
        keep = lax.dynamic_slice_in_dim(buffer, mine * size, size, 0)
        buffer = keep + lax.ppermute(send.astype(BF), "wide", [(p, p ^ half) for p in range(count)])
    return buffer


def finish_kernel(
    flags, first, first_got, plain, plain_got, split, split_got, attn_one, attn_one_got,
    lang, attn, ups, downs, gains, biases, ff_biases, out_biases, whole, last,
):
    rows, width = attn.shape[2:]
    up_rows, down_rows = ups.shape[2] // width * rows, downs.shape[1]

    def both(buffer, got):
        return buffer[0].astype(F32) + got[0].astype(F32)

    def put_ups(layer, found):
        for at in range(ups.shape[2] // width):
            ups[layer, :, at * width : (at + 1) * width] = found[at * rows : (at + 1) * rows]

    found = both(first, first_got)
    put_ups(1, found)
    downs[1] = found[up_rows : up_rows + down_rows]
    attn[1, 3] = found[up_rows + down_rows :]
    found = both(plain, plain_got)
    put_ups(0, found)
    attn[1, 0] = found[up_rows : up_rows + rows]
    attn[1, 1] = found[up_rows + rows :]
    whole[flags[3]] = split[0].astype(F32)
    whole[1 - flags[3]] = split_got[0].astype(F32)
    found = jnp.concatenate([whole[0], whole[1]], axis=0)
    downs[0] = found[:down_rows]
    attn[1, 2] = found[down_rows : down_rows + rows]
    lang[...] = found[down_rows + rows : down_rows + 2 * rows]
    attn[0, 3] = found[down_rows + 2 * rows :]
    last[flags[3]] = attn_one[0].astype(F32)
    last[1 - flags[3]] = attn_one_got[0].astype(F32)
    found = jnp.concatenate([last[0], last[1]], axis=0)
    for at in range(3):
        attn[0, at] = found[at * rows : (at + 1) * rows]
    small = found[3 * rows :]
    for layer in range(2):
        gains[layer] = small[2 * layer : 2 * layer + 2, :rows]
        biases[layer] = small[4 + 2 * layer : 6 + 2 * layer, :rows]
    out_biases[...] = small[8:10, :rows]
    ff_biases[...] = small[10:12, : ff_biases.shape[1]]


def finish(flags, flows, width, hidden):
    rows = width // SLICES
    args = []
    for flow in flows:
        args += flow.keep + flow.got
    return near_call(
        finish_kernel, "finish",
        [
            ((rows, width), F32),
            ((2, 4, rows, width), F32),
            ((2, rows, hidden), F32),
            ((2, hidden // SLICES, width), F32),
            ((2, 2, rows), F32),
            ((2, 2, rows), F32),
            ((2, hidden // SLICES), F32),
            ((2, rows), F32),
        ],
        args,
        [
            pltpu.VMEM((2, (DOWN_ROWS + 3 * rows) // 2, width), F32),
            pltpu.VMEM((2, (3 * rows + SMALL_ROWS) // 2, width), F32),
        ],
        flags,
    )


def body(
    patches,
    language,
    w_lang,
    w_attn,
    w_up,
    w_down,
    norm_gain,
    norm_bias,
    ff_bias,
    out_bias,
    cotangent,
    classes,
):
    position = lax.axis_index("wide")
    wide = lax.axis_size("wide")
    side = position % 2
    klass = lax.dynamic_index_in_dim(classes[0], position // 2, 0, keepdims=False)
    high = position // (wide // SLICES)
    flags = jnp.stack([klass, side, high, lax.axis_index("narrow")]).astype(jnp.int32)
    width = w_lang.shape[0]
    hidden = w_up.shape[2]
    start = patches[0]
    lang_low = jnp.pad(language[0], ((0, LPAD - language.shape[1]), (0, 0)))

    edge = pair_swap(jnp.where(side == 0, start[ROWS - EDGE :], start[:EDGE]))
    normed_a, query_a, kv_a = enter(start, norm_gain, norm_bias, w_attn, 0)
    mixed_a, weights_a, share_a, far_a = view_forward(flags, query_a, kv_a, edge, norm_gain, norm_bias, w_attn)
    after_a, normed_b, active_b, slope_b, state_b, normed_c, query_c, kv_c, feats, lang_normed, lang_kv = middle(
        start, mixed_a, norm_gain, norm_bias, w_attn, w_up, ff_bias, w_down, out_bias, lang_low, w_lang
    )
    far_c = pair_swap(kv_c)
    mixed_c, weights_c, share_c = joint_forward(flags, query_c, kv_c, far_c, lang_kv)

    grad, grad_mixed_c, parts, small_two = turn(
        flags, state_b, mixed_c, norm_gain, norm_bias, w_attn, w_up, ff_bias, w_down, cotangent[0]
    )
    first = Flow(PLAIN, parts)
    joint = (flags, query_c, kv_c, far_c, lang_kv, mixed_c, weights_c, share_c, grad_mixed_c)
    query_one, kv_one, *edge_one = joint_backward(*joint, 0, 1)
    far_one = [pair_swap(part) for part in edge_one]
    done = step([first], [query_one], lazy=True)
    query_two, kv_two, *edge_two = joint_backward(*joint, 1, HEADS // 2 - 1, done)
    far_two = [pair_swap(part) for part in edge_two]
    grad, grad_mixed_a, grad_language, plain_parts, split_parts, small_one, small_mid = descend(
        flags, state_b, norm_gain, normed_c, grad, (query_one, query_two), (kv_one, kv_two), (*far_one, *far_two),
        (*edge_one, *edge_two), w_attn, feats, lang_normed, lang_low, w_lang,
        after_a, mixed_a, normed_b, active_b, slope_b, w_up, w_down, (),
    )
    plain, split = Flow(PLAIN, plain_parts), Flow(SPLIT, split_parts)

    done = step([first], [small_mid], lazy=True)
    view = (flags, query_a, kv_a, far_a, mixed_a, weights_a, share_a, grad_mixed_a)
    half = HEADS // 4
    query_one, kv_one, edge_one = view_backward(*view, 0, half, done)
    far_one = pair_swap(edge_one)
    done = step([plain, split], [query_one])
    query_two, kv_two, edge_two = view_backward(*view, half, half, done, SHORT)
    far_two = pair_swap(edge_two)
    done = step([first], [query_two])
    grad, attn_parts, token = leave(
        flags, start, norm_gain, normed_a, grad, (query_one, query_two), (kv_one, kv_two), (far_one, far_two),
        w_attn, (small_one, small_two, small_mid), done,
    )
    attn_one = Flow(LAST, attn_parts)

    done = step([plain, split, first], [token], near=True, cost=LONG)
    done = step([attn_one], [done[0]], near=True)
    done = step([plain, split], [done[0]], near=True)
    done = step([attn_one], [done[0]], near=True)
    done = step([plain, split], [done[0]], near=True)
    done = step([attn_one], [done[0]], near=True)
    done = step([split], [done[0]], near=True)
    done = step([attn_one], [done[0]], near=True)
    flows = (first, plain, split, attn_one)
    grad_w_lang, grad_w_attn, grad_w_up, grad_w_down, *vectors = finish(flags, flows, width, hidden)
    gains, biases, ff_biases, out_biases = vectors

    def own(values, dim):
        if wide == SLICES:
            return values
        values = jnp.moveaxis(values, dim, 0)
        return jnp.moveaxis(split_low(values), 0, dim)

    return (
        grad[None],
        grad_language[None, : language.shape[1]],
        own(grad_w_lang, 0),
        own(grad_w_attn, 2),
        own(grad_w_up, 1),
        own(grad_w_down, 1),
        own(gains, 2),
        own(biases, 2),
        own(ff_biases, 1),
        own(out_biases, 1),
    )


def solution(mesh):
    in_specs = (
        P("narrow", "wide", None),
        P("narrow", "wide", None),
        P(),
        P(),
        P(),
        P(),
        P(),
        P(),
        P(),
        P(),
        P("narrow", "wide", None),
        P("narrow", None),
    )
    out_specs = (
        P("narrow", "wide", None),
        P("narrow", "wide", None),
        P("wide", None),
        P(None, None, "wide", None),
        P(None, "wide", None),
        P(None, "wide", None),
        P(None, None, "wide"),
        P(None, None, "wide"),
        P(None, "wide"),
        P(None, "wide"),
    )
    return jax.shard_map(body, mesh=mesh, in_specs=in_specs, out_specs=out_specs, check_vma=False)
```

```python
import functools

import jax
import jax.numpy as jnp
from jax import lax
from jax.experimental import pallas as pl
from jax.experimental.pallas import tpu as pltpu
from jax.sharding import PartitionSpec as P

HEADS = 8
HD = 64
LANG = 77
VB = 288
VS = 72
ROWS = 720
EDGE = VB // 2
PADDED = ROWS + EDGE
LPAD = 160
LONE = 96
KEYS = 2 * ROWS + LONE
PAIR = 2 * HD
SLICES = 16
ROWS_UP = 768
VB_UP = 384
STEP_VMEM = 20 * 2**20
LONG, SHORT = 60.0, 0.5
JOINT_VMEM = 60 * 2**20
JOINT_BACK_VMEM = 60 * 2**20
VIEW_VMEM = 60 * 2**20
DENSE_VMEM = 60 * 2**20
NEAR_VMEM = 16 * 2**20

epsilon = 1e-05
masked_out = -1e30
BF = jnp.bfloat16
F32 = jnp.float32


def matmul(left, right):
    return jnp.dot(left, right, preferred_element_type=F32)


def mat_left(left, right):
    return lax.dot_general(left, right, (((0,), (0,)), ((), ())), preferred_element_type=F32)


def mat_right(left, right):
    return lax.dot_general(left, right, (((1,), (1,)), ((), ())), preferred_element_type=F32)


def cost_of(microseconds):
    return pl.CostEstimate(flops=int(microseconds * 1e9), bytes_accessed=1, transcendentals=0)


def waiting(kernel, inputs, more):
    if not more:
        return kernel

    def without(*refs):
        return kernel(*refs[:inputs], *refs[inputs + more :])

    return without


def lane_mask(head):
    lanes = lax.broadcasted_iota(jnp.int32, (1, PAIR), 1)
    return jnp.where(lanes // HD == head, 1.0, 0.0).astype(BF)


def in_half(shape):
    return lax.broadcasted_iota(jnp.int32, shape, 1) % HD


def row_of(shape):
    return lax.broadcasted_iota(jnp.int32, shape, 0)


def key_marks(allowed, items):
    lane = in_half(allowed.shape)
    marks = jnp.where(lane < items, jnp.where(allowed, 0.0, masked_out), 0.0)
    return jnp.where((lane >= 4) & (lane < 7), 1.0, marks).astype(BF)


def joint_key_marks(klass):
    shape = (KEYS, PAIR)
    row, lane = row_of(shape), in_half(shape)
    first = (row < ROWS // 2) | ((row >= ROWS) & (row < ROWS + LANG))
    second = ((row >= ROWS // 2) & (row < ROWS)) | ((row >= ROWS + LANG) & (row < ROWS + 2 * LANG))
    fine = jnp.where(row < 2 * ROWS + LANG, 1, 0)
    coarse = jnp.where(lane == 0, jnp.where(first, 1, 0), jnp.where(second, 1, 0))
    return key_marks(jnp.where(klass == 1, fine, coarse) == 1, 2)


def joint_row_marks():
    shape = (ROWS, PAIR)
    row, lane = row_of(shape), in_half(shape)
    return jnp.where(lane == row // (ROWS // 2), 1.0, 0.0).astype(BF)


def view_key_marks(klass):
    shape = (PADDED, PAIR)
    row, lane = row_of(shape), in_half(shape)
    same = jnp.where(lane == row % VB // VS, 1, 0)
    return key_marks(jnp.where(klass == 1, 1, same) == 1, 4)


def view_row_marks():
    shape = (PADDED, PAIR)
    row, lane = row_of(shape), in_half(shape)
    return jnp.where(lane == row % VB // VS, 1.0, 0.0).astype(BF)


def with_parts(values):
    lane = in_half(values.shape)
    high = values.astype(BF).astype(F32)
    rest = values - high
    middle = rest.astype(BF).astype(F32)
    low = rest - middle
    picked = jnp.where(lane == 4, -high, jnp.where(lane == 5, -middle, jnp.where(lane == 6, -low, 0.0)))
    return picked.astype(BF)


def attend_heads(units):
    scores = [mat_right(keys, right) for right, keys, across in units]
    weights = [jnp.exp(part - jnp.max(part, axis=0, keepdims=True)).astype(BF) for part in scores]
    outs = [matmul(unit[2], part) for unit, part in zip(units, weights)]
    shares = [1.0 / out[HD : HD + 1] for out in outs]
    return [(part, out[:HD] * share, share) for part, out, share in zip(weights, outs, shares)]


def score_side(query, marks, head):
    mask = lane_mask(head)
    return jnp.concatenate([query * mask, marks * mask], axis=1)


def joint_place(klass, side, kv_ref, far_ref, lang_ref, put):
    put(slice(0, ROWS), kv_ref[:ROWS])

    @pl.when(klass == 1)
    def fine():
        put(slice(ROWS, 2 * ROWS), far_ref[:ROWS])

        @pl.when(side == 0)
        def own():
            put(slice(2 * ROWS, KEYS), lang_ref[:LONE])

        @pl.when(side == 1)
        def partner():
            put(slice(2 * ROWS, KEYS), far_ref[ROWS:])

    @pl.when(klass != 1)
    def coarse():
        put(slice(ROWS, ROWS + LPAD), lang_ref[...])


def inner_marks(grad, mixed):
    lanes = lax.broadcasted_iota(jnp.int32, (1, PAIR), 1)
    product = grad.astype(F32) * mixed.astype(F32)
    first = jnp.sum(jnp.where(lanes < HD, product, 0.0), axis=1, keepdims=True)
    second = jnp.sum(jnp.where(lanes < HD, 0.0, product), axis=1, keepdims=True)
    return with_parts(jnp.where(lanes < HD, first, second))


def attend_back(units):
    inner = [mat_right(unit[0], unit[5]) for unit in units]
    probs = [unit[2].astype(F32) * unit[3] for unit in units]
    grad_scores = [(left * right).astype(BF) for left, right in zip(probs, inner)]
    grad_values = [matmul(part.astype(BF), unit[5][:, :PAIR]) for part, unit in zip(probs, units)]
    grad_keys = [matmul(part, unit[4]) for part, unit in zip(grad_scores, units)]
    across = [matmul(unit[1], part) for part, unit in zip(grad_scores, units)]
    return list(zip(grad_keys, grad_values, across))


def fill_rows(left, grads, rows, query, grad, mixed):
    inner = inner_marks(grad, mixed)
    for head in range(2):
        mask = lane_mask(head)
        left[head, rows, :] = query * mask
        grads[head, rows, :PAIR] = grad * mask
        grads[head, rows, PAIR:] = inner * mask


def joint_backward_kernel(
    flags, q_ref, kv_ref, far_ref, lang_ref, mixed_ref, weights_ref, share_ref, grad_ref, dq_ref, dkv_ref,
    dfar_key, dfar_value, token, keys, values, across, left, grads,
):
    klass, side = flags[0], flags[1]

    @pl.when(pl.program_id(0) == 0)
    def prepare():
        keys[...] = jnp.zeros_like(keys)
        values[...] = jnp.zeros_like(values)
        values[:, PAIR:] = joint_key_marks(klass)

    def put(rows, block):
        keys[rows, :] = block[:, :PAIR]
        values[rows, :PAIR] = block[:, PAIR:]

    joint_place(klass, side, kv_ref, far_ref, lang_ref, put)
    token[...] = jnp.zeros_like(token)
    across[...] = keys[...].T
    fill_rows(left, grads, slice(0, ROWS), q_ref[...], grad_ref[...], mixed_ref[...])
    units = [
        (
            values[...],
            across[head * HD : (head + 1) * HD, :],
            weights_ref[head, :, :ROWS],
            share_ref[0, head : head + 1, :],
            left[head],
            grads[head],
        )
        for head in range(2)
    ]
    first, second = attend_back(units)
    for span, at, far in ((slice(0, PAIR), 0, dfar_key), (slice(PAIR, 2 * PAIR), 1, dfar_value)):
        both = (first[at] + second[at]).astype(BF)
        dkv_ref[:, span] = both[:ROWS]
        far[...] = both[ROWS:]
    dq_ref[...] = jnp.concatenate([first[2], second[2]], axis=0).T.astype(BF)


def joint_backward(flags, query, kv, far, lang, mixed, weights, share, grad, base, pairs, after=(), cost=LONG):
    rows = query.shape[0]
    one = pl.BlockSpec((rows, PAIR), lambda i, f: (0, i + base))
    return pl.pallas_call(
        waiting(joint_backward_kernel, 9, len(after)),
        grid_spec=pltpu.PrefetchScalarGridSpec(
            num_scalar_prefetch=1,
            grid=(pairs,),
            in_specs=[
                one,
                pl.BlockSpec((rows, 2 * PAIR), lambda i, f: (0, i + base)),
                pl.BlockSpec((ROWS + LONE, 2 * PAIR), lambda i, f: (0, i + base)),
                pl.BlockSpec((LPAD, 2 * PAIR), lambda i, f: (0, i + base)),
                one,
                pl.BlockSpec((2, KEYS, ROWS_UP), lambda i, f: (i + base, 0, 0)),
                pl.BlockSpec((1, 8, rows), lambda i, f: (i + base, 0, 0)),
                one,
            ]
            + [pl.BlockSpec(memory_space=pl.ANY)] * len(after),
            out_specs=[
                pl.BlockSpec((rows, PAIR), lambda i, f: (0, i)),
                pl.BlockSpec((rows, 2 * PAIR), lambda i, f: (0, i)),
                pl.BlockSpec((ROWS + LONE, PAIR), lambda i, f: (0, i)),
                pl.BlockSpec((ROWS + LONE, PAIR), lambda i, f: (0, i)),
                pl.BlockSpec((8, PAIR), lambda i, f: (0, 0)),
            ],
            scratch_shapes=[
                pltpu.VMEM((KEYS, PAIR), BF),
                pltpu.VMEM((KEYS, 2 * PAIR), BF),
                pltpu.VMEM((PAIR, KEYS), BF),
                pltpu.VMEM((2, ROWS, PAIR), BF),
                pltpu.VMEM((2, ROWS, 2 * PAIR), BF),
            ],
        ),
        out_shape=[
            jax.ShapeDtypeStruct((rows, pairs * PAIR), BF),
            jax.ShapeDtypeStruct((rows, 2 * pairs * PAIR), BF),
            jax.ShapeDtypeStruct((ROWS + LONE, pairs * PAIR), BF),
            jax.ShapeDtypeStruct((ROWS + LONE, pairs * PAIR), BF),
            jax.ShapeDtypeStruct((8, PAIR), F32),
        ],
        compiler_params=pltpu.CompilerParams(vmem_limit_bytes=JOINT_BACK_VMEM),
        cost_estimate=cost_of(cost),
        name="joint_backward",
    )(flags, query, kv, far, lang, mixed, weights, share, grad, *after)


def view_spots(side):
    own = pl.ds(pl.multiple_of(side * EDGE, 16), ROWS)
    far = pl.ds(pl.multiple_of((1 - side) * ROWS, 16), EDGE)
    return (own, far)


def view_backward_kernel(
    flags, q_ref, keys, value_ref, mixed_ref, weights_ref, share_ref, grad_ref, dq_ref, dkv_ref, dfar_ref,
    token, values, left, grads, back, dkv,
):
    klass, side = flags[0], flags[1]
    own, far = view_spots(side)

    @pl.when(pl.program_id(0) == 0)
    def prepare():
        values[:, PAIR:] = view_key_marks(klass)
        left[...] = jnp.zeros_like(left)
        grads[...] = jnp.zeros_like(grads)

    values[:, :PAIR] = value_ref[...]
    fill_rows(left, grads, own, q_ref[own, :], grad_ref[...], mixed_ref[...])

    units = []
    for index in range(PADDED // VB):
        rows = slice(index * VB, (index + 1) * VB)
        across = keys[rows, :].T
        for head in range(2):
            units.append(
                (
                    values[rows, :],
                    across[head * HD : (head + 1) * HD, :],
                    weights_ref[index, head, :, :VB],
                    share_ref[index, 0, head : head + 1, :],
                    left[head, rows, :],
                    grads[head, rows, :],
                )
            )
    done = attend_back(units)
    for index in range(PADDED // VB):
        rows = slice(index * VB, (index + 1) * VB)
        first, second = done[2 * index], done[2 * index + 1]
        dkv[rows, :PAIR] = (first[0] + second[0]).astype(BF)
        dkv[rows, PAIR:] = (first[1] + second[1]).astype(BF)
        back[rows, :] = jnp.concatenate([first[2], second[2]], axis=0).T.astype(BF)

    dq_ref[...] = back[own, :]
    dkv_ref[...] = dkv[own, :]
    dfar_ref[...] = dkv[far, :]
    token[...] = jnp.zeros_like(token)


def view_backward(flags, query, key, value, mixed, weights, share, grad, base, pairs, after=(), cost=LONG):
    rows = mixed.shape[0]
    blocks = PADDED // VB
    one = pl.BlockSpec((rows, PAIR), lambda i, f: (0, i + base))
    tall = pl.BlockSpec((PADDED, PAIR), lambda i, f: (0, i + base))
    return pl.pallas_call(
        waiting(view_backward_kernel, 8, len(after)),
        grid_spec=pltpu.PrefetchScalarGridSpec(
            num_scalar_prefetch=1,
            grid=(pairs,),
            in_specs=[
                tall,
                tall,
                tall,
                one,
                pl.BlockSpec((blocks, 2, VB, VB_UP), lambda i, f: (0, i + base, 0, 0)),
                pl.BlockSpec((blocks, 1, 8, VB), lambda i, f: (0, i + base, 0, 0)),
                one,
            ]
            + [pl.BlockSpec(memory_space=pl.ANY)] * len(after),
            out_specs=[
                pl.BlockSpec((rows, PAIR), lambda i, f: (0, i)),
                pl.BlockSpec((rows, 2 * PAIR), lambda i, f: (0, i)),
                pl.BlockSpec((EDGE, 2 * PAIR), lambda i, f: (0, i)),
                pl.BlockSpec((8, PAIR), lambda i, f: (0, 0)),
            ],
            scratch_shapes=[
                pltpu.VMEM((PADDED, 2 * PAIR), BF),
                pltpu.VMEM((2, PADDED, PAIR), BF),
                pltpu.VMEM((2, PADDED, 2 * PAIR), BF),
                pltpu.VMEM((PADDED, PAIR), BF),
                pltpu.VMEM((PADDED, 2 * PAIR), BF),
            ],
        ),
        out_shape=[
            jax.ShapeDtypeStruct((rows, pairs * PAIR), BF),
            jax.ShapeDtypeStruct((rows, 2 * pairs * PAIR), BF),
            jax.ShapeDtypeStruct((EDGE, 2 * pairs * PAIR), BF),
            jax.ShapeDtypeStruct((8, PAIR), F32),
        ],
        compiler_params=pltpu.CompilerParams(vmem_limit_bytes=VIEW_VMEM),
        cost_estimate=cost_of(cost),
        name="view_backward",
    )(flags, query, key, value, mixed, weights, share, grad, *after)


CHUNK = 512
DOWN_ROWS = 128
BITS = SLICES.bit_length() - 1


class Route:
    def __init__(self, steps, halves):
        self.steps = steps
        self.halves = halves
        self.order = [bit for step in steps for bit in step]
        self.units = 1 << len(self.order)

    def unit(self, position):
        last = len(self.order) - 1
        return sum((position >> (last - at) & 1) << bit for at, bit in enumerate(self.order))

    def parts(self, step):
        return 1 << len(self.steps[step])

    def rows(self, rows):
        return rows // 2 if self.halves else rows


PLAIN = Route(((0,), (1,), (2,), (3,)), False)
SPLIT = Route(((1,), (0,), (2,), (3,), (4,)), True)
LAST = Route(((1,), (0,), (2,), (3, 4)), True)


def hand_out(held, parts, flags, route, span=slice(None)):
    each = route.units // len(parts)
    rows = route.rows(held.shape[1])
    for position in range(route.units):
        if route.halves:
            unit = jnp.bitwise_xor(route.unit(position), flags[2] * 2 + flags[3])
            block = held[unit // 2, pl.ds(pl.multiple_of(unit % 2 * rows, 16), rows), :]
        else:
            block = held[jnp.bitwise_xor(route.unit(position), flags[2]), span]
        parts[position // each][position % each, span] = block


def part_shapes(route, rows, width):
    each = route.units // route.parts(0)
    return [((each, route.rows(rows), width), BF)] * route.parts(0)


def centre(values):
    mean = jnp.mean(values, axis=-1, keepdims=True)
    centered = values - mean
    variance = jnp.mean(centered * centered, axis=-1, keepdims=True)
    scale = lax.rsqrt(variance + epsilon)
    return (centered * scale, scale)


def norm_back(grad, unit, scale, gain):
    grad_gain = jnp.sum(grad * unit, axis=0, keepdims=True)
    grad_bias = jnp.sum(grad, axis=0, keepdims=True)
    scaled = grad * gain
    level = jnp.mean(scaled, axis=-1, keepdims=True)
    along = jnp.mean(scaled * unit, axis=-1, keepdims=True)
    return ((scaled - level - unit * along) * scale, grad_gain, grad_bias)


def gelu_both(hidden):
    root, cubic = 0.7978845608028654, 0.044715
    square = hidden * hidden
    bend = jnp.tanh(hidden * (root + (root * cubic) * square))
    half = 0.5 + 0.5 * bend
    slope = (0.5 * hidden) * (1.0 - bend * bend) * (root + (3.0 * root * cubic) * square)
    return (hidden * half, half + slope)


def mix(keys, values):
    parts = []
    for at in range(0, keys.shape[1], PAIR):
        parts += [keys[:, at : at + PAIR], values[:, at : at + PAIR]]
    return jnp.concatenate(parts, axis=1)


def unmix(both):
    blocks = [both[:, at : at + PAIR] for at in range(0, both.shape[1], PAIR)]
    return (jnp.concatenate(blocks[0::2], axis=1), jnp.concatenate(blocks[1::2], axis=1))


class Fetch:
    def __init__(self, source, buffer, semaphore, more):
        self.copy = pltpu.make_async_copy(source, buffer, semaphore)
        self.buffer, self.more, self.here = buffer, more, False

    def ref(self):
        if not self.here:
            self.copy.wait()
            self.here = True
            self.more(2)
        return self.buffer

    def __getitem__(self, index):
        return self.ref()[index]


class Store:
    def __init__(self, buffer, target, semaphores, pieces):
        self.buffer, self.copies, self.gone = buffer, [], []
        for at, piece in enumerate(pieces):
            source = buffer if piece is None else buffer.at[piece]
            place = target if piece is None else target.at[piece]
            self.copies.append(pltpu.make_async_copy(source, place, semaphores.at[at]))
            self.gone.append(False)

    def __setitem__(self, index, value):
        self.buffer[index] = value

    def __getitem__(self, index):
        return self.buffer[index]

    def send(self, at=None):
        for place, copy in enumerate(self.copies):
            if not self.gone[place] and at in (None, place):
                copy.start()
                self.gone[place] = True


LEAD = 4
QKV = slice(0, 3)


def dense_call(kernel, name, operands, fetches, outs, cost, scratch=(), flags=None, after=(), pieces=None, lead=LEAD, room=DENSE_VMEM, raw=()):
    shapes = [
        jax.eval_shape(lambda array, index=index: array if index is None else array[index], operands[at])
        for at, index in fetches
    ]
    count, first = len(operands), 0 if flags is None else 1
    pieces = [(pieces or {}).get(at, (None,)) for at in range(len(outs))]

    def run(*refs):
        inputs = refs[first : first + count]
        rest = refs[first + count + len(after) :]
        targets, rest = rest[: len(outs)], rest[len(outs) :]
        straight, rest = rest[: len(raw)], rest[len(raw) :]
        buffers, rest = rest[: len(fetches)], rest[len(fetches) :]
        held, rest = rest[: len(outs)], rest[len(outs) :]
        came, went, own = rest[0], rest[1 : 1 + len(outs)], rest[1 + len(outs) :]
        fetched, started = [], [0]

        def more(number):
            for fetch in fetched[started[0] : started[0] + number]:
                fetch.copy.start()
            started[0] += number

        for place, (at, index) in enumerate(fetches):
            source = inputs[at] if index is None else inputs[at].at[index]
            fetched.append(Fetch(source, buffers[place], came.at[place], more))
        more(lead)
        stores = [Store(*parts) for parts in zip(held, targets, went, pieces)]
        kernel(*([refs[0]] if first else []), fetched, stores, *straight, *own)
        for fetch in fetched:
            fetch.ref()
        for store in stores:
            store.send()
        for store in stores:
            for copy in store.copies:
                copy.wait()

    anywhere = pl.BlockSpec(memory_space=pl.ANY)
    return pl.pallas_call(
        run,
        in_specs=[pl.BlockSpec(memory_space=pltpu.SMEM)] * first + [anywhere] * (count + len(after)),
        out_specs=[anywhere] * (len(outs) + len(raw)),
        out_shape=[jax.ShapeDtypeStruct(shape, kind) for shape, kind in (*outs, *raw)],
        scratch_shapes=[pltpu.VMEM(part.shape, part.dtype) for part in shapes]
        + [pltpu.VMEM(shape, kind) for shape, kind in outs]
        + [pltpu.SemaphoreType.DMA((len(fetches),))]
        + [pltpu.SemaphoreType.DMA((len(piece),)) for piece in pieces]
        + list(scratch),
        compiler_params=pltpu.CompilerParams(vmem_limit_bytes=room),
        cost_estimate=cost_of(cost),
        name=name,
    )(*([flags] if first else []), *operands, *after)


def near_call(kernel, name, outs, args, scratch=(), flags=None, after=(), cost=SHORT):
    vmem = pl.BlockSpec(memory_space=pltpu.VMEM)
    specs = [vmem] * len(args)
    if flags is not None:
        specs = [pl.BlockSpec(memory_space=pltpu.SMEM)] + specs
        args = [flags] + list(args)
    return pl.pallas_call(
        waiting(kernel, len(args), len(after)),
        in_specs=specs + [pl.BlockSpec(memory_space=pl.ANY)] * len(after),
        out_specs=[vmem] * len(outs),
        out_shape=[jax.ShapeDtypeStruct(shape, kind) for shape, kind in outs],
        scratch_shapes=list(scratch),
        compiler_params=pltpu.CompilerParams(vmem_limit_bytes=NEAR_VMEM),
        cost_estimate=cost_of(cost),
        name=name,
    )(*args, *after)


QKV = slice(0, 3)


def chunks(hidden):
    return [slice(at, at + CHUNK) for at in range(0, hidden, CHUNK)]


def wide_pieces(hidden):
    return [(slice(None), span) for span in chunks(hidden)]


def mlp_fetches(layer, up_at, down_at, hidden):
    found = []
    for span in chunks(hidden):
        found += [(up_at, (layer, slice(None), span)), (down_at, (layer, span))]
    return found


def attend_views(p, query, key, value, row_marks, key_marks, weights, share, mixed):
    lanes = pl.ds(pl.multiple_of(p * PAIR, PAIR), PAIR)
    units = []
    for index in range(PADDED // VB):
        rows = slice(index * VB, (index + 1) * VB)
        keys = jnp.concatenate([key[rows, lanes], key_marks[rows, :]], axis=1)
        turned = value[rows, lanes].T
        for head in range(2):
            across = jnp.concatenate([turned[head * HD : (head + 1) * HD], jnp.ones((16, VB), BF)], axis=0)
            units.append((score_side(query[rows, lanes], row_marks[rows, :], head), keys, across))
    done = attend_heads(units)
    for index in range(PADDED // VB):
        rows = slice(index * VB, (index + 1) * VB)
        for head in range(2):
            weights[index, 2 * p + head, :, :VB] = done[2 * index + head][0]
            share[index, p, head : head + 1, :] = done[2 * index + head][2]
        pair = [done[2 * index + head][1] for head in range(2)]
        mixed[rows, lanes] = jnp.concatenate(pair, axis=0).T.astype(BF)


def climb_kernel(flags, fetched, stores, rows_all, mixed_all, row_marks, key_marks):
    x, edge, gain, bias, w_first, w_out, ff_bias, out_bias = fetched[:8]
    mlp, (language, w_lang, w_qkv) = fetched[8:-3], fetched[-3:]
    first, rest = stores[:7], stores[7:]
    normed_one, query_all, key_all, value_all, mixed, weights, share = first
    after, normed, active, slope, state, next_normed, query, kv, feats, lang_normed, lang_kv = rest
    klass, side = flags[0], flags[1]
    own, far = view_spots(side)
    rows_all[own, :] = x[...]
    rows_all[far, :] = edge[...]
    row_marks[...] = view_row_marks()
    key_marks[...] = view_key_marks(klass)
    unit, scale = centre(rows_all[...].astype(F32))
    low = (unit * gain[0, 0:1] + bias[0, 0:1]).astype(BF)
    key_all[...] = matmul(low, w_first[1]).astype(BF)
    key_all.send()
    value_all[...] = matmul(low, w_first[2]).astype(BF)
    value_all.send()
    query_all[...] = (matmul(low, w_first[0]) * 0.125).astype(BF)
    query_all.send()
    rows_all[...] = low
    normed_one[...] = rows_all[own, :]
    normed_one.send()

    def pair(p, carry):
        attend_views(
            p, query_all.buffer, key_all.buffer, value_all.buffer, row_marks, key_marks, weights.buffer,
            share.buffer, mixed_all,
        )
        return carry

    lax.fori_loop(0, HEADS // 2, pair, 0)
    weights.send()
    share.send()
    mixed[...] = mixed_all[own, :]
    mixed.send()

    total = x[...].astype(F32) + matmul(mixed[...], w_out[...])
    after[...] = total
    after.send()
    unit, scale = centre(total)
    low = (unit * gain[0, 1:2] + bias[0, 1:2]).astype(BF)
    normed[...] = low
    normed.send()
    total = total + out_bias[0:1, :]
    for at in range(0, len(mlp), 2):
        span = slice(at // 2 * CHUNK, (at // 2 + 1) * CHUNK)
        grown, rise = gelu_both(matmul(low, mlp[at][...]) + ff_bias[0:1, span])
        grown = grown.astype(BF)
        active[:, span] = grown
        active.send(at // 2)
        slope[:, span] = rise.astype(BF)
        slope.send(at // 2)
        total = total + matmul(grown, mlp[at + 1][...])
    found = matmul(language[...], w_lang[...])
    feats[...] = found
    feats.send()
    unit, scale = centre(found)
    low = (unit * gain[1, 0:1] + bias[1, 0:1]).astype(BF)
    lang_normed[...] = low
    lang_normed.send()
    both = mix(matmul(low, w_qkv[1]).astype(BF), matmul(low, w_qkv[2]).astype(BF))
    lang_kv[...] = both
    lang_kv.send()
    kv[ROWS:] = both[:LONE]
    state[...] = total
    state.send()
    unit, scale = centre(total)
    low = (unit * gain[1, 0:1] + bias[1, 0:1]).astype(BF)
    next_normed[...] = low
    next_normed.send()
    kv[:ROWS] = mix(matmul(low, w_qkv[1]).astype(BF), matmul(low, w_qkv[2]).astype(BF))
    kv.send()
    query[...] = (matmul(low, w_qkv[0]) * 0.125).astype(BF)


def climb(flags, x, edge, gain, bias, w_attn, w_up, ff_bias, w_down, out_bias, language, w_lang):
    rows, width = x.shape
    hidden = w_up.shape[2]
    blocks = PADDED // VB
    return dense_call(
        climb_kernel,
        "climb",
        (x, edge, gain, bias, w_attn, ff_bias, out_bias, w_up, w_down, language, w_lang),
        [(0, None), (1, None), (2, None), (3, None), (4, (0, QKV)), (4, (0, 3)), (5, None), (6, None)]
        + mlp_fetches(0, 7, 8, hidden)
        + [(9, None), (10, None), (4, (1, QKV))],
        [
            ((rows, width), BF),
            ((PADDED, width), BF),
            ((PADDED, width), BF),
            ((PADDED, width), BF),
            ((rows, width), BF),
            ((blocks, HEADS, VB, VB_UP), BF),
            ((blocks, HEADS // 2, 8, VB), F32),
            ((rows, width), F32),
            ((rows, width), BF),
            ((rows, hidden), BF),
            ((rows, hidden), BF),
            ((rows, width), F32),
            ((rows, width), BF),
            ((rows, width), BF),
            ((rows + LONE, 2 * width), BF),
            ((LPAD, width), F32),
            ((LPAD, width), BF),
            ((LPAD, 2 * width), BF),
        ],
        LONG,
        [
            pltpu.VMEM((PADDED, width), BF),
            pltpu.VMEM((PADDED, width), BF),
            pltpu.VMEM((PADDED, PAIR), BF),
            pltpu.VMEM((PADDED, PAIR), BF),
        ],
        flags,
        pieces={9: wide_pieces(hidden), 10: wide_pieces(hidden)},
        lead=5,
    )


def put_up(held, at, grad):
    rows = grad.shape[0] // SLICES
    put_rows(held, at // CHUNK * rows, grad)


def put_down(held, at, start, grad):
    rows = DOWN_ROWS
    for piece in range(grad.shape[0] // rows):
        held[at // rows + piece, start : start + rows, :] = grad[piece * rows : (piece + 1) * rows]


def put_rows(held, place, grad):
    rows = grad.shape[0] // SLICES
    for piece in range(SLICES):
        held[piece, place : place + rows, :] = grad[piece * rows : (piece + 1) * rows]


def mlp_tail(layer, grad, grad_normed, unit, scale, gain, mixed, w_out, ups, place, out_grad, out_mixed, small):
    width = unit.shape[1]
    grad_state, grad_gain, grad_bias = norm_back(grad_normed, unit, scale, gain[layer, 1:2])
    grad = grad + grad_state
    out_grad[...] = grad
    out_grad.send()
    small[1:2, :width] = grad_gain
    small[1:2, width : 2 * width] = grad_bias
    low = grad.astype(BF)
    put_rows(ups, place, mat_left(mixed[...], low).astype(BF))
    out_mixed[...] = mat_right(low, w_out[...]).astype(BF)
    out_mixed.send()


def mlp_chunk(span, low, grad_low, slope, w_up, w_down, ups, small):
    grad_hidden = slope * mat_right(grad_low, w_down)
    hidden_low = grad_hidden.astype(BF)
    put_up(ups, span.start, mat_left(low, hidden_low).astype(BF))
    small[0:1, span] = jnp.sum(hidden_low.astype(F32), axis=0, keepdims=True)
    return mat_right(hidden_low, w_up)


def joint_scores(query, marks, keys, key_marks, p, head):
    lanes = pl.ds(pl.multiple_of(p * PAIR, PAIR), PAIR)
    return mat_right(
        jnp.concatenate([keys[:, lanes], key_marks[...]], axis=1), score_side(query[:, lanes], marks[...], head)
    )


def crest_kernel(
    flags, fetched, stores, probs, weights, keys, values, key_marks, marks, scores, peaks, held, copied
):
    query, kv, far, lang, x, w_out, gain, bias, ff_bias, cotangent = fetched[:10]
    mlp = fetched[10:]
    mixed, share, out_grad, out_mixed, keep, send, small = stores
    klass, side = flags[0], flags[1]
    query, kv, far, lang = query.ref(), kv.ref(), far.ref(), lang.ref()
    x.more(len(fetched))

    keys[...] = jnp.zeros_like(keys)
    values[...] = jnp.zeros_like(values)
    key_marks[...] = joint_key_marks(klass)
    marks[...] = joint_row_marks()

    def put(rows, block):
        for p in range(HEADS // 2):
            lanes = slice(p * PAIR, (p + 1) * PAIR)
            keys[rows, lanes] = block[:, 2 * p * PAIR : (2 * p + 1) * PAIR]
            values[rows, lanes] = block[:, (2 * p + 1) * PAIR : (2 * p + 2) * PAIR]

    joint_place(klass, side, kv, far, lang, put)

    def copy_out(p, head):
        return pltpu.make_async_copy(held.at[head], probs.at[2 * p + head], copied.at[head])

    def one(p, head, turned):
        across = jnp.concatenate([turned[head * HD : (head + 1) * HD], jnp.ones((16, KEYS), BF)], axis=0)
        found = jnp.exp(scores[head, :, :ROWS] - peaks[head]).astype(BF)
        held[head, :, :ROWS] = found
        copy_out(p, head).start()
        out = matmul(across, found)
        part = 1.0 / out[HD : HD + 1]
        share[p, head : head + 1, :] = part
        return out[:HD] * part

    for head in range(2):
        held[head] = jnp.zeros(held.shape[1:], BF)
        copy_out(0, head).start()
    def form(p, head):
        found = joint_scores(query, marks, keys, key_marks, p, head)
        scores[head, :, :ROWS] = found
        peaks[head] = jnp.max(found, axis=0, keepdims=True)

    form(0, 0)

    def pair(p, carry):
        lanes = pl.ds(pl.multiple_of(p * PAIR, PAIR), PAIR)
        turned = values[:, lanes].T
        copy_out(p, 0).wait()
        form(p, 1)
        first = one(p, 0, turned)
        copy_out(p, 1).wait()
        form(jnp.minimum(p + 1, HEADS // 2 - 1), 0)
        second = one(p, 1, turned)
        mixed.buffer[:, lanes] = jnp.concatenate([first, second], axis=0).T.astype(BF)
        return carry

    lax.fori_loop(0, HEADS // 2, pair, 0)
    mixed.send()
    share.send()

    small[...] = jnp.zeros(small.buffer.shape, F32)
    total = x[...] + matmul(mixed[...], w_out[...])
    width = total.shape[1]
    hidden = len(mlp) // 2 * CHUNK
    unit, scale = centre(total)
    low = (unit * gain[1, 1:2] + bias[1, 1:2]).astype(BF)
    grad_low = cotangent[...]
    grad = grad_low.astype(F32)
    small[1:2, 2 * width : 3 * width] = jnp.sum(grad, axis=0, keepdims=True)
    grad_normed = None
    for at, span in enumerate(chunks(hidden)):
        w_up, w_down = mlp[2 * at][...], mlp[2 * at + 1][...]
        value, rise = gelu_both(matmul(low, w_up) + ff_bias[1:2, span])
        part = mlp_chunk(span, low, grad_low, rise, w_up, w_down, weights, small)
        put_down(weights, span.start, DOWN_ROWS, mat_left(value.astype(BF), grad_low).astype(BF))
        grad_normed = part if grad_normed is None else grad_normed + part
    hand_out(weights, (keep, send), flags, PLAIN, slice(0, hidden // SLICES + DOWN_ROWS))
    send.send(0)
    keep.send(0)
    mlp_tail(
        1, grad, grad_normed, unit, scale, gain, mixed, w_out, weights, hidden // SLICES + DOWN_ROWS,
        out_grad, out_mixed, small,
    )
    hand_out(weights, (keep, send), flags, PLAIN, slice(hidden // SLICES + DOWN_ROWS, weights.shape[1]))
    for head in range(2):
        copy_out(HEADS // 2 - 1, head).wait()


def crest(flags, query, kv, far, lang, x, gain, bias, w_attn, w_up, ff_bias, w_down, cotangent):
    rows, width = x.shape
    hidden = w_up.shape[2]
    held = (2 * hidden + width) // SLICES
    early = 2 * hidden // SLICES
    done = dense_call(
        crest_kernel, "crest",
        (query, kv, far, lang, x, w_attn, gain, bias, ff_bias, cotangent, w_up, w_down),
        [(0, None), (1, None), (2, None), (3, None), (4, None), (5, (1, 3))]
        + [(at, None) for at in range(6, 10)]
        + mlp_fetches(1, 10, 11, hidden),
        [((rows, width), BF), ((HEADS // 2, 8, rows), F32), ((rows, width), F32), ((rows, width), BF)]
        + part_shapes(PLAIN, held, width)
        + [((8, hidden), F32)],
        LONG,
        [
            pltpu.VMEM((SLICES, held, width), BF),
            pltpu.VMEM((KEYS, width), BF),
            pltpu.VMEM((KEYS, width), BF),
            pltpu.VMEM((KEYS, PAIR), BF),
            pltpu.VMEM((rows, PAIR), BF),
            pltpu.VMEM((2, KEYS, ROWS_UP), F32),
            pltpu.VMEM((2, 1, rows), F32),
            pltpu.VMEM((2, KEYS, ROWS_UP), BF),
            pltpu.SemaphoreType.DMA((2,)),
        ],
        flags,
        pieces={at: [(slice(None), slice(0, early)), (slice(None), slice(early, held))] for at in (4, 5)},
        lead=4,
        raw=[((HEADS, KEYS, ROWS_UP), BF)],
    )
    return (done[0], done[7], done[1], done[2], done[3], done[4:6], done[6])


def beside(*blocks):
    return jnp.concatenate([block[...] for block in blocks], axis=1)


def leave_grad(unit, scale, gain, grad, grad_query, grad_key, grad_value, w_qkv):
    grad_normed = mat_right(grad_query, w_qkv[0]) * 0.125
    grad_normed = grad_normed + mat_right(grad_key, w_qkv[1]) + mat_right(grad_value, w_qkv[2])
    grad_state, grad_gain, grad_bias = norm_back(grad_normed, unit, scale, gain)
    return (grad + grad_state, grad_gain, grad_bias)


def leave_kernel(flags, fetched, stores, sums, held):
    query_one, query_two, normed, kv_one, kv_two, far_one, far_two, x, gain, w_qkv, grad = fetched[:11]
    out, keep, send, token = stores
    token[...] = jnp.zeros(token.buffer.shape, F32)
    grad_query = beside(query_one, query_two)
    low = normed[...]
    width = low.shape[1]
    place = width // SLICES
    put_rows(held, 0, (mat_left(low, grad_query) * 0.125).astype(BF))
    sums[...] = beside(kv_one, kv_two).astype(F32)
    rows = pl.ds(pl.multiple_of((1 - flags[1]) * (ROWS - EDGE), 16), EDGE)
    sums[rows, :] += beside(far_one, far_two).astype(F32)
    grad_key, grad_value = unmix(sums[...].astype(BF))
    unit, scale = centre(x[...].astype(F32))
    total, grad_gain, grad_bias = leave_grad(
        unit, scale, gain[0, 0:1], grad[...], grad_query, grad_key, grad_value, w_qkv
    )
    out[...] = total
    out.send()
    put_rows(held, place, mat_left(low, grad_key).astype(BF))
    put_rows(held, 2 * place, mat_left(low, grad_value).astype(BF))
    put_small(held, 3 * place, fetched[11:], grad_gain, grad_bias)
    hand_out(held, (keep, send), flags, LAST)


SMALL_ROWS = 32


def put_small(held, place, small, grad_gain, grad_bias):
    width = grad_gain.shape[1]
    rows = [grad_gain, small[0][1:2, :width], small[2][0:1, :width], small[1][1:2, :width]]
    rows += [grad_bias, small[0][1:2, width : 2 * width], small[2][0:1, width : 2 * width]]
    rows += [small[1][1:2, width : 2 * width]]
    rows += [small[at][1:2, 2 * width : 3 * width] for at in range(2)]
    block = jnp.concatenate(rows, axis=0)
    long = jnp.concatenate([small[at][0:1, :] for at in range(2)], axis=0)
    each, more = width // SLICES, long.shape[1] // SLICES
    for piece in range(SLICES):
        head = jnp.pad(block[:, piece * each : (piece + 1) * each], ((0, 0), (0, more - each)))
        tail = long[:, piece * more : (piece + 1) * more]
        rest = jnp.zeros((SMALL_ROWS - head.shape[0] - tail.shape[0], more), F32)
        both = jnp.concatenate([head, tail, rest], axis=0).astype(BF)
        held[piece, place : place + SMALL_ROWS, :] = jnp.pad(both, ((0, 0), (0, width - more)))


def leave(flags, x, gain, normed, grad, queries, kvs, fars, w_attn, smalls, after):
    rows, width = x.shape
    held = 3 * (width // SLICES) + SMALL_ROWS
    done = dense_call(
        leave_kernel, "leave",
        (*queries, normed, *kvs, *fars, x, gain, w_attn, grad, *smalls),
        [(at, None) for at in range(9)] + [(9, (0, QKV))] + [(at, None) for at in range(10, 14)],
        [((rows, width), F32)] + part_shapes(LAST, held, width) + [((8, PAIR), F32)],
        4.0,
        [pltpu.VMEM((rows, 2 * width), F32), pltpu.VMEM((SLICES, held, width), BF)],
        flags,
        after,
        lead=8,
    )
    return (done[0], done[1:3], done[3])


def put_sums(klass, side, sums, lang_sums, kv, here, far, own, lone, there, span):
    @pl.when(klass == 1)
    def fine():
        sums[:, span] = (kv[:, here].astype(F32) + far[:ROWS, there].astype(F32)).astype(BF)

        @pl.when(side == 0)
        def owner():
            lang_sums[:LONE, span] = (lone[:, there].astype(F32) + far[ROWS:, there].astype(F32)).astype(BF)

    @pl.when(klass != 1)
    def coarse():
        sums[:, span] = kv[:, here]
        lang_sums[:, span] = own[:, there]


def descend_kernel(flags, fetched, stores, sums, lang_sums, plain, split):
    query_one, query_two, normed, x, kv_one, kv_two = fetched[:6]
    fars, owns, lones = (fetched[6:8], fetched[8:10]), (fetched[10:12], fetched[12:14]), (fetched[14:16], fetched[16:18])
    w_qkv, gain, grad, low_normed = fetched[18:22]
    mlp, (after, mixed, w_out, lang_normed, feats, language, w_lang) = fetched[22:-7], fetched[-7:]
    out_grad, out_mixed, grad_language, keep, send, split_keep, split_send, small, small_mid = stores
    klass, side = flags[0], flags[1]
    small[...] = jnp.zeros(small.buffer.shape, F32)
    small_mid[...] = jnp.zeros(small_mid.buffer.shape, F32)
    lang_sums[...] = jnp.zeros_like(lang_sums)
    grad_query, low = beside(query_one, query_two), normed[...]
    width = low.shape[1]
    place = width // SLICES
    hidden = len(mlp) // 4 * CHUNK
    up_rows = hidden // SLICES
    put_rows(plain, up_rows, (mat_left(low, grad_query) * 0.125).astype(BF))
    unit, scale = centre(x[...])
    fars = [[part.ref() for part in fars[at]] for at in range(2)]
    owns = [[part.ref() for part in owns[at]] for at in range(2)]
    lones = [[part.ref() for part in lones[at]] for at in range(2)]
    at = 0
    for half, kv in enumerate((kv_one.ref(), kv_two.ref())):
        for pair in range(kv.shape[1] // PAIR // 2):
            for which in range(2):
                there = slice(pair * PAIR, (pair + 1) * PAIR)
                here = slice((2 * pair + which) * PAIR, (2 * pair + which + 1) * PAIR)
                span = slice(at, at + PAIR)
                at += PAIR
                put_sums(
                    klass, side, sums, lang_sums, kv, here, fars[half][which], owns[half][which], lones[half][which],
                    there, span,
                )

    grad_key, grad_value = unmix(sums[...])
    grad, grad_gain, grad_bias = leave_grad(
        unit, scale, gain[1, 0:1], grad[...], grad_query, grad_key, grad_value, w_qkv
    )
    lang_key, lang_value = unmix(lang_sums[...])
    lang_low = lang_normed[...]
    put_rows(plain, up_rows + place, (mat_left(low, grad_key) + mat_left(lang_low, lang_key)).astype(BF))
    put_rows(split, DOWN_ROWS, (mat_left(low, grad_value) + mat_left(lang_low, lang_value)).astype(BF))
    lang_grad = mat_right(lang_key, w_qkv[1]) + mat_right(lang_value, w_qkv[2])
    unit, scale = centre(feats[...])
    grad_feats, lang_gain, lang_bias = norm_back(lang_grad, unit, scale, gain[1, 0:1])
    feats_low = grad_feats.astype(BF)
    put_rows(split, DOWN_ROWS + place, mat_left(language[...], feats_low).astype(BF))
    grad_language[...] = mat_right(feats_low, w_lang[...])
    grad_language.send()
    small_mid[0:1, :width] = grad_gain + lang_gain
    small_mid[0:1, width : 2 * width] = grad_bias + lang_bias

    grad_low = grad.astype(BF)
    small[1:2, 2 * width : 3 * width] = jnp.sum(grad_low.astype(F32), axis=0, keepdims=True)
    low = low_normed[...]
    grad_normed = None
    for at, span in enumerate(chunks(hidden)):
        w_down, rise, w_up, active = [part[...] for part in mlp[4 * at : 4 * at + 4]]
        part = mlp_chunk(span, low, grad_low, rise.astype(F32), w_up, w_down, plain, small)
        put_down(split, span.start, 0, mat_left(active, grad_low).astype(BF))
        grad_normed = part if grad_normed is None else grad_normed + part
    hand_out(plain, (keep, send), flags, PLAIN)
    send.send()
    keep.send()
    unit, scale = centre(after[...])
    mlp_tail(
        0, grad, grad_normed, unit, scale, gain, mixed, w_out, split, DOWN_ROWS + 2 * place, out_grad, out_mixed, small
    )
    hand_out(split, (split_keep, split_send), flags, SPLIT)


def descend(
    flags, state, gain, normed, grad, queries, kvs, fars, owns, w_attn, feats, lang_normed, language, w_lang,
    after, mixed, low_normed, active, slope, w_up, w_down, follows,
):
    rows, width = state.shape
    hidden = w_up.shape[2]
    place = width // SLICES
    plain, split = hidden // SLICES + 2 * place, DOWN_ROWS + 3 * place
    fetches = []
    for span in chunks(hidden):
        fetches += [(19, (0, span)), (20, (slice(None), span)), (18, (0, slice(None), span)), (21, (slice(None), span))]
    head, foot = slice(0, LPAD), slice(ROWS, ROWS + LONE)
    done = dense_call(
        descend_kernel, "descend",
        (*queries, normed, state, *kvs, *fars, *owns, w_attn, gain, grad, low_normed)
        + (w_up, w_down, slope, active, after, mixed, lang_normed, feats, language, w_lang),
        [(at, None) for at in range(10)]
        + [(at, (head,)) for at in range(10, 14)]
        + [(at, (foot,)) for at in range(10, 14)]
        + [(14, (1, QKV)), (15, None), (16, None), (17, None)]
        + fetches
        + [(22, None), (23, None), (14, (0, 3)), (24, None), (25, None), (26, None), (27, None)],
        [((rows, width), F32), ((rows, width), BF), ((LPAD, width), F32)]
        + part_shapes(PLAIN, plain, width)
        + part_shapes(SPLIT, split, width)
        + [((8, hidden), F32), ((8, 2 * width), F32)],
        3.0,
        [
            pltpu.VMEM((rows, 2 * width), BF),
            pltpu.VMEM((LPAD, 2 * width), BF),
            pltpu.VMEM((SLICES, plain, width), BF),
            pltpu.VMEM((SLICES, split, width), BF),
        ],
        flags,
        follows,
        lead=10,
    )
    return (done[0], done[1], done[2], done[3:5], done[5:7], done[7], done[8])


def pair_swap(block):
    count = lax.axis_size("wide")
    return lax.ppermute(block, "wide", [(at, at ^ 1) for at in range(count)])


class Flow:
    def __init__(self, route, parts):
        self.route, self.step = route, 0
        self.units = route.units
        self.keep = [parts[0]]
        self.send(parts)

    def send(self, parts):
        self.got = []
        if self.step < len(self.route.steps):
            bits = self.route.steps[self.step]
            self.units //= 1 << len(bits)
            for at, part in enumerate(parts[1:], 1):
                found = [bit for place, bit in enumerate(bits) if at >> (len(bits) - 1 - place) & 1]
                self.got.append(self.move(part, found))
        else:
            self.keep = [parts[0]]
            self.got.append(self.move(parts[0], [0] if self.route.halves else None))

    def move(self, part, bits):
        shift = 1 if self.route.halves else 0
        if bits is None or bits == [0] and shift:
            return lax.ppermute(part, "narrow", [(0, 1), (1, 0)])
        count = lax.axis_size("wide")
        stride = sum((count // SLICES) << (bit - shift) for bit in bits)
        return lax.ppermute(part, "wide", [(p, p ^ stride) for p in range(count)])


def step_kernel(layout, ins, outs):
    at = 0
    for out, (count, rows) in zip(outs, layout):
        total = None
        for term in ins[at : at + count]:
            part = term[rows] if rows is not None else term[...]
            total = part.astype(F32) if total is None else total + part.astype(F32)
        out[...] = total.astype(BF)
        if isinstance(out, Store):
            out.send()
        at += count


def step(flows, after=(), near=False, cost=SHORT, lazy=False):
    operands, fetches, layout, outs, plan = [], [], [], [], []
    for flow in flows:
        flow.step += 1
        terms = flow.keep + flow.got
        last = flow.step == len(flow.route.steps)
        count = 1 if last else flow.route.parts(flow.step)
        each = flow.units // count
        made = [part for part in range(count) if part or last or not lazy]
        for part in reversed(made):
            rows = slice(part * each, (part + 1) * each)
            for term in terms:
                fetches.append((len(operands), rows))
                operands.append(term)
            layout.append((len(terms), rows))
            outs.append(((each,) + terms[0].shape[1:], BF))
        plan.append((flow, terms, count, made))
    if near:
        done = near_call(
            lambda *refs: step_kernel(layout, refs[: len(operands)], refs[len(operands) :]),
            "step", outs, operands, after=after, cost=cost,
        )
    else:
        done = dense_call(
            lambda ins, stores: step_kernel([(count, None) for count, rows in layout], ins, stores),
            "step", operands, fetches, outs, cost, after=after, lead=len(fetches), room=STEP_VMEM,
        )
    at = 0
    for flow, terms, count, made in plan:
        parts = [None] * count
        for part in reversed(made):
            parts[part] = done[at]
            at += 1
        flow.keep = terms if parts[0] is None else [parts[0]]
        flow.send(parts)
    return done


def split_low(buffer):
    count = lax.axis_size("wide")
    position = lax.axis_index("wide")
    half = count // SLICES
    while half > 1:
        half //= 2
        mine = position // half % 2
        size = buffer.shape[0] // 2
        send = lax.dynamic_slice_in_dim(buffer, (1 - mine) * size, size, 0)
        keep = lax.dynamic_slice_in_dim(buffer, mine * size, size, 0)
        buffer = keep + lax.ppermute(send.astype(BF), "wide", [(p, p ^ half) for p in range(count)])
    return buffer


def finish_kernel(
    flags, first, first_got, plain, plain_got, split, split_got, attn_one, attn_one_got,
    lang, attn, ups, downs, gains, biases, ff_biases, out_biases, whole, last,
):
    rows, width = attn.shape[2:]
    up_rows, down_rows = ups.shape[2] // width * rows, downs.shape[1]

    def both(buffer, got):
        return buffer[0].astype(F32) + got[0].astype(F32)

    def put_ups(layer, found):
        for at in range(ups.shape[2] // width):
            ups[layer, :, at * width : (at + 1) * width] = found[at * rows : (at + 1) * rows]

    found = both(first, first_got)
    put_ups(1, found)
    downs[1] = found[up_rows : up_rows + down_rows]
    attn[1, 3] = found[up_rows + down_rows :]
    found = both(plain, plain_got)
    put_ups(0, found)
    attn[1, 0] = found[up_rows : up_rows + rows]
    attn[1, 1] = found[up_rows + rows :]
    whole[flags[3]] = split[0].astype(F32)
    whole[1 - flags[3]] = split_got[0].astype(F32)
    found = jnp.concatenate([whole[0], whole[1]], axis=0)
    downs[0] = found[:down_rows]
    attn[1, 2] = found[down_rows : down_rows + rows]
    lang[...] = found[down_rows + rows : down_rows + 2 * rows]
    attn[0, 3] = found[down_rows + 2 * rows :]
    last[flags[3]] = attn_one[0].astype(F32)
    last[1 - flags[3]] = attn_one_got[0].astype(F32)
    found = jnp.concatenate([last[0], last[1]], axis=0)
    for at in range(3):
        attn[0, at] = found[at * rows : (at + 1) * rows]
    small = found[3 * rows :]
    for layer in range(2):
        gains[layer] = small[2 * layer : 2 * layer + 2, :rows]
        biases[layer] = small[4 + 2 * layer : 6 + 2 * layer, :rows]
    out_biases[...] = small[8:10, :rows]
    ff_biases[...] = small[10:12, : ff_biases.shape[1]]


def finish(flags, flows, width, hidden):
    rows = width // SLICES
    args = []
    for flow in flows:
        args += flow.keep + flow.got
    return near_call(
        finish_kernel, "finish",
        [
            ((rows, width), F32),
            ((2, 4, rows, width), F32),
            ((2, rows, hidden), F32),
            ((2, hidden // SLICES, width), F32),
            ((2, 2, rows), F32),
            ((2, 2, rows), F32),
            ((2, hidden // SLICES), F32),
            ((2, rows), F32),
        ],
        args,
        [
            pltpu.VMEM((2, (DOWN_ROWS + 3 * rows) // 2, width), F32),
            pltpu.VMEM((2, (3 * rows + SMALL_ROWS) // 2, width), F32),
        ],
        flags,
    )


def body(
    patches,
    language,
    w_lang,
    w_attn,
    w_up,
    w_down,
    norm_gain,
    norm_bias,
    ff_bias,
    out_bias,
    cotangent,
    classes,
):
    position = lax.axis_index("wide")
    wide = lax.axis_size("wide")
    side = position % 2
    klass = lax.dynamic_index_in_dim(classes[0], position // 2, 0, keepdims=False)
    high = position // (wide // SLICES)
    flags = jnp.stack([klass, side, high, lax.axis_index("narrow")]).astype(jnp.int32)
    width = w_lang.shape[0]
    hidden = w_up.shape[2]
    start = patches[0]
    lang_low = jnp.pad(language[0], ((0, LPAD - language.shape[1]), (0, 0)))

    edge = pair_swap(jnp.where(side == 0, start[ROWS - EDGE :], start[:EDGE]))
    normed_a, query_a, key_a, value_a, mixed_a, weights_a, share_a, *rest = climb(
        flags, start, edge, norm_gain, norm_bias, w_attn, w_up, ff_bias, w_down, out_bias, lang_low, w_lang
    )
    after_a, normed_b, active_b, slope_b, state_b, normed_c, query_c, kv_c, feats, lang_normed, lang_kv = rest
    far_c = pair_swap(kv_c)
    mixed_c, weights_c, share_c, grad, grad_mixed_c, parts, small_two = crest(
        flags, query_c, kv_c, far_c, lang_kv, state_b, norm_gain, norm_bias, w_attn, w_up, ff_bias, w_down,
        cotangent[0],
    )
    first = Flow(PLAIN, parts)
    joint = (flags, query_c, kv_c, far_c, lang_kv, mixed_c, weights_c, share_c, grad_mixed_c)
    query_one, kv_one, *edge_one, token = joint_backward(*joint, 0, HEADS // 4)
    far_one = [pair_swap(part) for part in edge_one]
    done = step([first], [token], lazy=True)
    query_two, kv_two, *edge_two, token = joint_backward(*joint, HEADS // 4, HEADS // 4, done)
    far_two = [pair_swap(part) for part in edge_two]
    grad, grad_mixed_a, grad_language, plain_parts, split_parts, small_one, small_mid = descend(
        flags, state_b, norm_gain, normed_c, grad, (query_one, query_two), (kv_one, kv_two), (*far_one, *far_two),
        (*edge_one, *edge_two), w_attn, feats, lang_normed, lang_low, w_lang,
        after_a, mixed_a, normed_b, active_b, slope_b, w_up, w_down, (),
    )
    plain, split = Flow(PLAIN, plain_parts), Flow(SPLIT, split_parts)

    done = step([first], [small_mid], lazy=True)
    view = (flags, query_a, key_a, value_a, mixed_a, weights_a, share_a, grad_mixed_a)
    half = HEADS // 4
    query_one, kv_one, edge_one, token = view_backward(*view, 0, half, done)
    far_one = pair_swap(edge_one)
    done = step([plain, split], [token])
    query_two, kv_two, edge_two, token = view_backward(*view, half, half, done, SHORT)
    far_two = pair_swap(edge_two)
    done = step([first], [token])
    grad, attn_parts, token = leave(
        flags, start, norm_gain, normed_a, grad, (query_one, query_two), (kv_one, kv_two), (far_one, far_two),
        w_attn, (small_one, small_two, small_mid), done,
    )
    attn_one = Flow(LAST, attn_parts)

    done = step([plain, split, first], [token], near=True, cost=LONG)
    done = step([attn_one], [done[0]], near=True)
    done = step([plain, split], [done[0]], near=True)
    done = step([attn_one], [done[0]], near=True)
    done = step([plain, split], [done[0]], near=True)
    done = step([attn_one], [done[0]], near=True)
    done = step([split], [done[0]], near=True)
    done = step([attn_one], [done[0]], near=True)
    flows = (first, plain, split, attn_one)
    grad_w_lang, grad_w_attn, grad_w_up, grad_w_down, *vectors = finish(flags, flows, width, hidden)
    gains, biases, ff_biases, out_biases = vectors

    def own(values, dim):
        if wide == SLICES:
            return values
        values = jnp.moveaxis(values, dim, 0)
        return jnp.moveaxis(split_low(values), 0, dim)

    return (
        grad[None],
        grad_language[None, : language.shape[1]],
        own(grad_w_lang, 0),
        own(grad_w_attn, 2),
        own(grad_w_up, 1),
        own(grad_w_down, 1),
        own(gains, 2),
        own(biases, 2),
        own(ff_biases, 1),
        own(out_biases, 1),
    )


def solution(mesh):
    in_specs = (
        P("narrow", "wide", None),
        P("narrow", "wide", None),
        P(),
        P(),
        P(),
        P(),
        P(),
        P(),
        P(),
        P(),
        P("narrow", "wide", None),
        P("narrow", None),
    )
    out_specs = (
        P("narrow", "wide", None),
        P("narrow", "wide", None),
        P("wide", None),
        P(None, None, "wide", None),
        P(None, "wide", None),
        P(None, "wide", None),
        P(None, None, "wide"),
        P(None, None, "wide"),
        P(None, "wide"),
        P(None, "wide"),
    )
    return jax.shard_map(body, mesh=mesh, in_specs=in_specs, out_specs=out_specs, check_vma=False)
```

```python
import functools

import jax
import jax.numpy as jnp
from jax import lax
from jax.experimental import pallas as pl
from jax.experimental.pallas import tpu as pltpu
from jax.sharding import PartitionSpec as P

HEADS = 8
HD = 64
LANG = 77
VB = 288
VS = 72
ROWS = 720
EDGE = VB // 2
PADDED = ROWS + EDGE
LPAD = 160
LONE = 96
KEYS = 2 * ROWS + LONE
PAIR = 2 * HD
SLICES = 16
ROWS_UP = 768
VB_UP = 384
STEP_VMEM = 20 * 2**20
LONG, SHORT = 60.0, 0.5
JOINT_VMEM = 60 * 2**20
JOINT_BACK_VMEM = 60 * 2**20
VIEW_VMEM = 60 * 2**20
DENSE_VMEM = 60 * 2**20
NEAR_VMEM = 16 * 2**20

epsilon = 1e-05
masked_out = -1e30
BF = jnp.bfloat16
F32 = jnp.float32


def matmul(left, right):
    return jnp.dot(left, right, preferred_element_type=F32)


def mat_left(left, right):
    return lax.dot_general(left, right, (((0,), (0,)), ((), ())), preferred_element_type=F32)


def mat_right(left, right):
    return lax.dot_general(left, right, (((1,), (1,)), ((), ())), preferred_element_type=F32)


def cost_of(microseconds):
    return pl.CostEstimate(flops=int(microseconds * 1e9), bytes_accessed=1, transcendentals=0)


def waiting(kernel, inputs, more):
    if not more:
        return kernel

    def without(*refs):
        return kernel(*refs[:inputs], *refs[inputs + more :])

    return without


def lane_mask(head):
    lanes = lax.broadcasted_iota(jnp.int32, (1, PAIR), 1)
    return jnp.where(lanes // HD == head, 1.0, 0.0).astype(BF)


def in_half(shape):
    return lax.broadcasted_iota(jnp.int32, shape, 1) % HD


def row_of(shape):
    return lax.broadcasted_iota(jnp.int32, shape, 0)


def key_marks(allowed, items):
    lane = in_half(allowed.shape)
    marks = jnp.where(lane < items, jnp.where(allowed, 0.0, masked_out), 0.0)
    return jnp.where((lane >= 4) & (lane < 7), 1.0, marks).astype(BF)


def joint_key_marks(klass):
    shape = (KEYS, PAIR)
    row, lane = row_of(shape), in_half(shape)
    first = (row < ROWS // 2) | ((row >= ROWS) & (row < ROWS + LANG))
    second = ((row >= ROWS // 2) & (row < ROWS)) | ((row >= ROWS + LANG) & (row < ROWS + 2 * LANG))
    fine = jnp.where(row < 2 * ROWS + LANG, 1, 0)
    coarse = jnp.where(lane == 0, jnp.where(first, 1, 0), jnp.where(second, 1, 0))
    return key_marks(jnp.where(klass == 1, fine, coarse) == 1, 2)


def joint_row_marks():
    shape = (ROWS, PAIR)
    row, lane = row_of(shape), in_half(shape)
    return jnp.where(lane == row // (ROWS // 2), 1.0, 0.0).astype(BF)


def view_key_marks(klass):
    shape = (PADDED, PAIR)
    row, lane = row_of(shape), in_half(shape)
    same = jnp.where(lane == row % VB // VS, 1, 0)
    return key_marks(jnp.where(klass == 1, 1, same) == 1, 4)


def view_row_marks():
    shape = (PADDED, PAIR)
    row, lane = row_of(shape), in_half(shape)
    return jnp.where(lane == row % VB // VS, 1.0, 0.0).astype(BF)


def with_parts(values):
    lane = in_half(values.shape)
    high = values.astype(BF).astype(F32)
    rest = values - high
    middle = rest.astype(BF).astype(F32)
    low = rest - middle
    picked = jnp.where(lane == 4, -high, jnp.where(lane == 5, -middle, jnp.where(lane == 6, -low, 0.0)))
    return picked.astype(BF)


def attend_heads(units):
    scores = [mat_right(keys, right) for right, keys, across in units]
    weights = [jnp.exp(part - jnp.max(part, axis=0, keepdims=True)).astype(BF) for part in scores]
    outs = [matmul(unit[2], part) for unit, part in zip(units, weights)]
    shares = [1.0 / out[HD : HD + 1] for out in outs]
    return [(part, out[:HD] * share, share) for part, out, share in zip(weights, outs, shares)]


def score_side(query, marks, head):
    mask = lane_mask(head)
    return jnp.concatenate([query * mask, marks * mask], axis=1)


def joint_place(klass, side, kv_ref, far_ref, lang_ref, put):
    put(slice(0, ROWS), kv_ref[:ROWS])

    @pl.when(klass == 1)
    def fine():
        put(slice(ROWS, 2 * ROWS), far_ref[:ROWS])

        @pl.when(side == 0)
        def own():
            put(slice(2 * ROWS, KEYS), lang_ref[:LONE])

        @pl.when(side == 1)
        def partner():
            put(slice(2 * ROWS, KEYS), far_ref[ROWS:])

    @pl.when(klass != 1)
    def coarse():
        put(slice(ROWS, ROWS + LPAD), lang_ref[...])


def inner_marks(grad, mixed):
    lanes = lax.broadcasted_iota(jnp.int32, (1, PAIR), 1)
    product = grad.astype(F32) * mixed.astype(F32)
    first = jnp.sum(jnp.where(lanes < HD, product, 0.0), axis=1, keepdims=True)
    second = jnp.sum(jnp.where(lanes < HD, 0.0, product), axis=1, keepdims=True)
    return with_parts(jnp.where(lanes < HD, first, second))


def attend_back(units):
    inner = [mat_right(unit[0], unit[5]) for unit in units]
    probs = [unit[2].astype(F32) * unit[3] for unit in units]
    grad_scores = [(left * right).astype(BF) for left, right in zip(probs, inner)]
    grad_values = [matmul(part.astype(BF), unit[5][:, :PAIR]) for part, unit in zip(probs, units)]
    grad_keys = [matmul(part, unit[4]) for part, unit in zip(grad_scores, units)]
    across = [matmul(unit[1], part) for part, unit in zip(grad_scores, units)]
    return list(zip(grad_keys, grad_values, across))


def fill_rows(left, grads, rows, query, grad, mixed):
    inner = inner_marks(grad, mixed)
    for head in range(2):
        mask = lane_mask(head)
        left[head, rows, :] = query * mask
        grads[head, rows, :PAIR] = grad * mask
        grads[head, rows, PAIR:] = inner * mask


def joint_backward_kernel(
    flags, q_ref, kv_ref, far_ref, lang_ref, mixed_ref, weights_ref, share_ref, grad_ref, dq_ref, dkv_ref,
    dfar_key, dfar_value, token, keys, values, across, left, grads,
):
    klass, side = flags[0], flags[1]

    @pl.when(pl.program_id(0) == 0)
    def prepare():
        keys[...] = jnp.zeros_like(keys)
        values[...] = jnp.zeros_like(values)
        values[:, PAIR:] = joint_key_marks(klass)

    def put(rows, block):
        keys[rows, :] = block[:, :PAIR]
        values[rows, :PAIR] = block[:, PAIR:]

    joint_place(klass, side, kv_ref, far_ref, lang_ref, put)
    token[...] = jnp.zeros_like(token)
    across[...] = keys[...].T
    fill_rows(left, grads, slice(0, ROWS), q_ref[...], grad_ref[...], mixed_ref[...])
    units = [
        (
            values[...],
            across[head * HD : (head + 1) * HD, :],
            weights_ref[head, :, :ROWS],
            share_ref[0, head : head + 1, :],
            left[head],
            grads[head],
        )
        for head in range(2)
    ]
    first, second = attend_back(units)
    for span, at, far in ((slice(0, PAIR), 0, dfar_key), (slice(PAIR, 2 * PAIR), 1, dfar_value)):
        both = (first[at] + second[at]).astype(BF)
        dkv_ref[:, span] = both[:ROWS]
        far[...] = both[ROWS:]
    dq_ref[...] = jnp.concatenate([first[2], second[2]], axis=0).T.astype(BF)


def joint_backward(flags, query, kv, far, lang, mixed, weights, share, grad, base, pairs, after=(), cost=LONG):
    rows = query.shape[0]
    one = pl.BlockSpec((rows, PAIR), lambda i, f: (0, i + base))
    return pl.pallas_call(
        waiting(joint_backward_kernel, 9, len(after)),
        grid_spec=pltpu.PrefetchScalarGridSpec(
            num_scalar_prefetch=1,
            grid=(pairs,),
            in_specs=[
                one,
                pl.BlockSpec((rows, 2 * PAIR), lambda i, f: (0, i + base)),
                pl.BlockSpec((ROWS + LONE, 2 * PAIR), lambda i, f: (0, i + base)),
                pl.BlockSpec((LPAD, 2 * PAIR), lambda i, f: (0, i + base)),
                one,
                pl.BlockSpec((2, KEYS, ROWS_UP), lambda i, f: (i + base, 0, 0)),
                pl.BlockSpec((1, 8, rows), lambda i, f: (i + base, 0, 0)),
                one,
            ]
            + [pl.BlockSpec(memory_space=pl.ANY)] * len(after),
            out_specs=[
                pl.BlockSpec((rows, PAIR), lambda i, f: (0, i)),
                pl.BlockSpec((rows, 2 * PAIR), lambda i, f: (0, i)),
                pl.BlockSpec((ROWS + LONE, PAIR), lambda i, f: (0, i)),
                pl.BlockSpec((ROWS + LONE, PAIR), lambda i, f: (0, i)),
                pl.BlockSpec((8, PAIR), lambda i, f: (0, 0)),
            ],
            scratch_shapes=[
                pltpu.VMEM((KEYS, PAIR), BF),
                pltpu.VMEM((KEYS, 2 * PAIR), BF),
                pltpu.VMEM((PAIR, KEYS), BF),
                pltpu.VMEM((2, ROWS, PAIR), BF),
                pltpu.VMEM((2, ROWS, 2 * PAIR), BF),
            ],
        ),
        out_shape=[
            jax.ShapeDtypeStruct((rows, pairs * PAIR), BF),
            jax.ShapeDtypeStruct((rows, 2 * pairs * PAIR), BF),
            jax.ShapeDtypeStruct((ROWS + LONE, pairs * PAIR), BF),
            jax.ShapeDtypeStruct((ROWS + LONE, pairs * PAIR), BF),
            jax.ShapeDtypeStruct((8, PAIR), F32),
        ],
        compiler_params=pltpu.CompilerParams(vmem_limit_bytes=JOINT_BACK_VMEM),
        cost_estimate=cost_of(cost),
        name="joint_backward",
    )(flags, query, kv, far, lang, mixed, weights, share, grad, *after)


def view_spots(side):
    own = pl.ds(pl.multiple_of(side * EDGE, 16), ROWS)
    far = pl.ds(pl.multiple_of((1 - side) * ROWS, 16), EDGE)
    return (own, far)


def view_backward_kernel(
    flags, q_ref, keys, value_ref, mixed_ref, weights_ref, share_ref, grad_ref, dq_ref, dkv_ref, dfar_ref,
    token, values, left, grads, back, dkv,
):
    klass, side = flags[0], flags[1]
    own, far = view_spots(side)

    @pl.when(pl.program_id(0) == 0)
    def prepare():
        values[:, PAIR:] = view_key_marks(klass)
        left[...] = jnp.zeros_like(left)
        grads[...] = jnp.zeros_like(grads)

    values[:, :PAIR] = value_ref[...]
    fill_rows(left, grads, own, q_ref[own, :], grad_ref[...], mixed_ref[...])

    units = []
    for index in range(PADDED // VB):
        rows = slice(index * VB, (index + 1) * VB)
        across = keys[rows, :].T
        for head in range(2):
            units.append(
                (
                    values[rows, :],
                    across[head * HD : (head + 1) * HD, :],
                    weights_ref[index, head, :, :VB],
                    share_ref[index, 0, head : head + 1, :],
                    left[head, rows, :],
                    grads[head, rows, :],
                )
            )
    done = attend_back(units)
    for index in range(PADDED // VB):
        rows = slice(index * VB, (index + 1) * VB)
        first, second = done[2 * index], done[2 * index + 1]
        dkv[rows, :PAIR] = (first[0] + second[0]).astype(BF)
        dkv[rows, PAIR:] = (first[1] + second[1]).astype(BF)
        back[rows, :] = jnp.concatenate([first[2], second[2]], axis=0).T.astype(BF)

    dq_ref[...] = back[own, :]
    dkv_ref[...] = dkv[own, :]
    dfar_ref[...] = dkv[far, :]
    token[...] = jnp.zeros_like(token)


def view_backward(flags, query, key, value, mixed, weights, share, grad, base, pairs, after=(), cost=LONG):
    rows = mixed.shape[0]
    blocks = PADDED // VB
    one = pl.BlockSpec((rows, PAIR), lambda i, f: (0, i + base))
    tall = pl.BlockSpec((PADDED, PAIR), lambda i, f: (0, i + base))
    return pl.pallas_call(
        waiting(view_backward_kernel, 8, len(after)),
        grid_spec=pltpu.PrefetchScalarGridSpec(
            num_scalar_prefetch=1,
            grid=(pairs,),
            in_specs=[
                tall,
                tall,
                tall,
                one,
                pl.BlockSpec((blocks, 2, VB, VB_UP), lambda i, f: (0, i + base, 0, 0)),
                pl.BlockSpec((blocks, 1, 8, VB), lambda i, f: (0, i + base, 0, 0)),
                one,
            ]
            + [pl.BlockSpec(memory_space=pl.ANY)] * len(after),
            out_specs=[
                pl.BlockSpec((rows, PAIR), lambda i, f: (0, i)),
                pl.BlockSpec((rows, 2 * PAIR), lambda i, f: (0, i)),
                pl.BlockSpec((EDGE, 2 * PAIR), lambda i, f: (0, i)),
                pl.BlockSpec((8, PAIR), lambda i, f: (0, 0)),
            ],
            scratch_shapes=[
                pltpu.VMEM((PADDED, 2 * PAIR), BF),
                pltpu.VMEM((2, PADDED, PAIR), BF),
                pltpu.VMEM((2, PADDED, 2 * PAIR), BF),
                pltpu.VMEM((PADDED, PAIR), BF),
                pltpu.VMEM((PADDED, 2 * PAIR), BF),
            ],
        ),
        out_shape=[
            jax.ShapeDtypeStruct((rows, pairs * PAIR), BF),
            jax.ShapeDtypeStruct((rows, 2 * pairs * PAIR), BF),
            jax.ShapeDtypeStruct((EDGE, 2 * pairs * PAIR), BF),
            jax.ShapeDtypeStruct((8, PAIR), F32),
        ],
        compiler_params=pltpu.CompilerParams(vmem_limit_bytes=VIEW_VMEM),
        cost_estimate=cost_of(cost),
        name="view_backward",
    )(flags, query, key, value, mixed, weights, share, grad, *after)


CHUNK = 512
DOWN_ROWS = 128
BITS = SLICES.bit_length() - 1


class Route:
    def __init__(self, steps, halves):
        self.steps = steps
        self.halves = halves
        self.order = [bit for step in steps for bit in step]
        self.units = 1 << len(self.order)

    def unit(self, position):
        last = len(self.order) - 1
        return sum((position >> (last - at) & 1) << bit for at, bit in enumerate(self.order))

    def parts(self, step):
        return 1 << len(self.steps[step])

    def rows(self, rows):
        return rows // 2 if self.halves else rows


PLAIN = Route(((0,), (1,), (2,), (3,)), False)
SPLIT = Route(((1,), (0,), (2,), (3,), (4,)), True)
LAST = Route(((1,), (0,), (2,), (3, 4)), True)


def hand_out(held, parts, flags, route, span=slice(None)):
    each = route.units // len(parts)
    rows = route.rows(held.shape[1])
    for position in range(route.units):
        if route.halves:
            unit = jnp.bitwise_xor(route.unit(position), flags[2] * 2 + flags[3])
            block = held[unit // 2, pl.ds(pl.multiple_of(unit % 2 * rows, 16), rows), :]
        else:
            block = held[jnp.bitwise_xor(route.unit(position), flags[2]), span]
        parts[position // each][position % each, span] = block


def part_shapes(route, rows, width):
    each = route.units // route.parts(0)
    return [((each, route.rows(rows), width), BF)] * route.parts(0)


def centre(values):
    mean = jnp.mean(values, axis=-1, keepdims=True)
    centered = values - mean
    variance = jnp.mean(centered * centered, axis=-1, keepdims=True)
    scale = lax.rsqrt(variance + epsilon)
    return (centered * scale, scale)


def norm_back(grad, unit, scale, gain):
    grad_gain = jnp.sum(grad * unit, axis=0, keepdims=True)
    grad_bias = jnp.sum(grad, axis=0, keepdims=True)
    scaled = grad * gain
    level = jnp.mean(scaled, axis=-1, keepdims=True)
    along = jnp.mean(scaled * unit, axis=-1, keepdims=True)
    return ((scaled - level - unit * along) * scale, grad_gain, grad_bias)


def gelu_both(hidden):
    root, cubic = 0.7978845608028654, 0.044715
    square = hidden * hidden
    bend = jnp.tanh(hidden * (root + (root * cubic) * square))
    half = 0.5 + 0.5 * bend
    slope = (0.5 * hidden) * (1.0 - bend * bend) * (root + (3.0 * root * cubic) * square)
    return (hidden * half, half + slope)


def mix(keys, values):
    parts = []
    for at in range(0, keys.shape[1], PAIR):
        parts += [keys[:, at : at + PAIR], values[:, at : at + PAIR]]
    return jnp.concatenate(parts, axis=1)


def unmix(both):
    blocks = [both[:, at : at + PAIR] for at in range(0, both.shape[1], PAIR)]
    return (jnp.concatenate(blocks[0::2], axis=1), jnp.concatenate(blocks[1::2], axis=1))


class Fetch:
    def __init__(self, source, buffer, semaphore, more):
        self.copy = pltpu.make_async_copy(source, buffer, semaphore)
        self.buffer, self.more, self.here = buffer, more, False

    def ref(self):
        if not self.here:
            self.more(0, self)
            self.copy.wait()
            self.here = True
            self.more(2)
        return self.buffer

    def __getitem__(self, index):
        return self.ref()[index]


class Store:
    def __init__(self, buffer, target, semaphores, pieces):
        self.buffer, self.copies, self.gone = buffer, [], []
        for at, piece in enumerate(pieces):
            source = buffer if piece is None else buffer.at[piece]
            place = target if piece is None else target.at[piece]
            self.copies.append(pltpu.make_async_copy(source, place, semaphores.at[at]))
            self.gone.append(False)

    def __setitem__(self, index, value):
        self.buffer[index] = value

    def __getitem__(self, index):
        return self.buffer[index]

    def send(self, at=None):
        for place, copy in enumerate(self.copies):
            if not self.gone[place] and at in (None, place):
                copy.start()
                self.gone[place] = True


LEAD = 4
QKV = slice(0, 3)


def dense_call(kernel, name, operands, fetches, outs, cost, scratch=(), flags=None, after=(), pieces=None, lead=LEAD, room=DENSE_VMEM, raw=()):
    shapes = [
        jax.eval_shape(lambda array, index=index: array if index is None else array[index], operands[at])
        for at, index in fetches
    ]
    count, first = len(operands), 0 if flags is None else 1
    pieces = [(pieces or {}).get(at, (None,)) for at in range(len(outs))]

    def run(*refs):
        inputs = refs[first : first + count]
        rest = refs[first + count + len(after) :]
        targets, rest = rest[: len(outs)], rest[len(outs) :]
        straight, rest = rest[: len(raw)], rest[len(raw) :]
        buffers, rest = rest[: len(fetches)], rest[len(fetches) :]
        held, rest = rest[: len(outs)], rest[len(outs) :]
        came, went, own = rest[0], rest[1 : 1 + len(outs)], rest[1 + len(outs) :]
        fetched, started = [], [0]

        def more(number, wanted=None):
            if wanted is not None:
                number = fetched.index(wanted) + 1 - started[0]
            for fetch in fetched[started[0] : started[0] + max(number, 0)]:
                fetch.copy.start()
            started[0] += max(number, 0)

        for place, (at, index) in enumerate(fetches):
            source = inputs[at] if index is None else inputs[at].at[index]
            fetched.append(Fetch(source, buffers[place], came.at[place], more))
        more(lead)
        stores = [Store(*parts) for parts in zip(held, targets, went, pieces)]
        kernel(*([refs[0]] if first else []), fetched, stores, *straight, *own)
        for fetch in fetched:
            fetch.ref()
        for store in stores:
            store.send()
        for store in stores:
            for copy in store.copies:
                copy.wait()

    anywhere = pl.BlockSpec(memory_space=pl.ANY)
    return pl.pallas_call(
        run,
        in_specs=[pl.BlockSpec(memory_space=pltpu.SMEM)] * first + [anywhere] * (count + len(after)),
        out_specs=[anywhere] * (len(outs) + len(raw)),
        out_shape=[jax.ShapeDtypeStruct(shape, kind) for shape, kind in (*outs, *raw)],
        scratch_shapes=[pltpu.VMEM(part.shape, part.dtype) for part in shapes]
        + [pltpu.VMEM(shape, kind) for shape, kind in outs]
        + [pltpu.SemaphoreType.DMA((len(fetches),))]
        + [pltpu.SemaphoreType.DMA((len(piece),)) for piece in pieces]
        + list(scratch),
        compiler_params=pltpu.CompilerParams(vmem_limit_bytes=room),
        cost_estimate=cost_of(cost),
        name=name,
    )(*([flags] if first else []), *operands, *after)


def near_call(kernel, name, outs, args, scratch=(), flags=None, after=(), cost=SHORT):
    vmem = pl.BlockSpec(memory_space=pltpu.VMEM)
    specs = [vmem] * len(args)
    if flags is not None:
        specs = [pl.BlockSpec(memory_space=pltpu.SMEM)] + specs
        args = [flags] + list(args)
    return pl.pallas_call(
        waiting(kernel, len(args), len(after)),
        in_specs=specs + [pl.BlockSpec(memory_space=pl.ANY)] * len(after),
        out_specs=[vmem] * len(outs),
        out_shape=[jax.ShapeDtypeStruct(shape, kind) for shape, kind in outs],
        scratch_shapes=list(scratch),
        compiler_params=pltpu.CompilerParams(vmem_limit_bytes=NEAR_VMEM),
        cost_estimate=cost_of(cost),
        name=name,
    )(*args, *after)


QKV = slice(0, 3)


def chunks(hidden):
    return [slice(at, at + CHUNK) for at in range(0, hidden, CHUNK)]


def wide_pieces(hidden):
    return [(slice(None), span) for span in chunks(hidden)]


def mlp_fetches(layer, up_at, down_at, hidden):
    found = []
    for span in chunks(hidden):
        found += [(up_at, (layer, slice(None), span)), (down_at, (layer, span))]
    return found


def attend_views(p, query, key, value, row_marks, key_marks, weights, share, mixed):
    lanes = pl.ds(pl.multiple_of(p * PAIR, PAIR), PAIR)
    units = []
    for index in range(PADDED // VB):
        rows = slice(index * VB, (index + 1) * VB)
        keys = jnp.concatenate([key[rows, lanes], key_marks[rows, :]], axis=1)
        turned = value[rows, lanes].T
        for head in range(2):
            across = jnp.concatenate([turned[head * HD : (head + 1) * HD], jnp.ones((16, VB), BF)], axis=0)
            units.append((score_side(query[rows, lanes], row_marks[rows, :], head), keys, across))
    done = attend_heads(units)
    for index in range(PADDED // VB):
        rows = slice(index * VB, (index + 1) * VB)
        for head in range(2):
            weights[index, 2 * p + head, :, :VB] = done[2 * index + head][0]
            share[index, p, head : head + 1, :] = done[2 * index + head][2]
        pair = [done[2 * index + head][1] for head in range(2)]
        mixed[rows, lanes] = jnp.concatenate(pair, axis=0).T.astype(BF)


def climb_kernel(flags, fetched, stores, rows_all, mixed_all, row_marks, key_marks):
    x, edge, gain, bias, w_first, w_out, ff_bias, out_bias = fetched[:8]
    mlp, (language, w_lang, w_qkv) = fetched[8:-3], fetched[-3:]
    first, rest = stores[:7], stores[7:]
    normed_one, query_all, key_all, value_all, mixed, weights, share = first
    after, normed, active, slope, state, next_normed, query, kv, feats, lang_normed, lang_kv = rest
    klass, side = flags[0], flags[1]
    own, far = view_spots(side)
    rows_all[own, :] = x[...]
    rows_all[far, :] = edge[...]
    row_marks[...] = view_row_marks()
    key_marks[...] = view_key_marks(klass)
    unit, scale = centre(rows_all[...].astype(F32))
    low = (unit * gain[0, 0:1] + bias[0, 0:1]).astype(BF)
    key_all[...] = matmul(low, w_first[1]).astype(BF)
    key_all.send()
    value_all[...] = matmul(low, w_first[2]).astype(BF)
    value_all.send()
    query_all[...] = (matmul(low, w_first[0]) * 0.125).astype(BF)
    query_all.send()
    rows_all[...] = low
    normed_one[...] = rows_all[own, :]
    normed_one.send()

    def pair(p, carry):
        attend_views(
            p, query_all.buffer, key_all.buffer, value_all.buffer, row_marks, key_marks, weights.buffer,
            share.buffer, mixed_all,
        )
        return carry

    lax.fori_loop(0, HEADS // 2, pair, 0)
    weights.send()
    share.send()
    mixed[...] = mixed_all[own, :]
    mixed.send()

    total = x[...].astype(F32) + matmul(mixed[...], w_out[...])
    after[...] = total
    after.send()
    unit, scale = centre(total)
    low = (unit * gain[0, 1:2] + bias[0, 1:2]).astype(BF)
    normed[...] = low
    normed.send()
    total = total + out_bias[0:1, :]
    for at in range(0, len(mlp), 2):
        span = slice(at // 2 * CHUNK, (at // 2 + 1) * CHUNK)
        grown, rise = gelu_both(matmul(low, mlp[at][...]) + ff_bias[0:1, span])
        grown = grown.astype(BF)
        active[:, span] = grown
        active.send(at // 2)
        slope[:, span] = rise.astype(BF)
        slope.send(at // 2)
        total = total + matmul(grown, mlp[at + 1][...])
    found = matmul(language[...], w_lang[...])
    feats[...] = found
    feats.send()
    unit, scale = centre(found)
    low = (unit * gain[1, 0:1] + bias[1, 0:1]).astype(BF)
    lang_normed[...] = low
    lang_normed.send()
    both = mix(matmul(low, w_qkv[1]).astype(BF), matmul(low, w_qkv[2]).astype(BF))
    lang_kv[...] = both
    lang_kv.send()
    kv[ROWS:] = both[:LONE]
    state[...] = total
    state.send()
    unit, scale = centre(total)
    low = (unit * gain[1, 0:1] + bias[1, 0:1]).astype(BF)
    next_normed[...] = low
    next_normed.send()
    kv[:ROWS] = mix(matmul(low, w_qkv[1]).astype(BF), matmul(low, w_qkv[2]).astype(BF))
    kv.send()
    query[...] = (matmul(low, w_qkv[0]) * 0.125).astype(BF)


def climb(flags, x, edge, gain, bias, w_attn, w_up, ff_bias, w_down, out_bias, language, w_lang):
    rows, width = x.shape
    hidden = w_up.shape[2]
    blocks = PADDED // VB
    return dense_call(
        climb_kernel,
        "climb",
        (x, edge, gain, bias, w_attn, ff_bias, out_bias, w_up, w_down, language, w_lang),
        [(0, None), (1, None), (2, None), (3, None), (4, (0, QKV)), (4, (0, 3)), (5, None), (6, None)]
        + mlp_fetches(0, 7, 8, hidden)
        + [(9, None), (10, None), (4, (1, QKV))],
        [
            ((rows, width), BF),
            ((PADDED, width), BF),
            ((PADDED, width), BF),
            ((PADDED, width), BF),
            ((rows, width), BF),
            ((blocks, HEADS, VB, VB_UP), BF),
            ((blocks, HEADS // 2, 8, VB), F32),
            ((rows, width), F32),
            ((rows, width), BF),
            ((rows, hidden), BF),
            ((rows, hidden), BF),
            ((rows, width), F32),
            ((rows, width), BF),
            ((rows, width), BF),
            ((rows + LONE, 2 * width), BF),
            ((LPAD, width), F32),
            ((LPAD, width), BF),
            ((LPAD, 2 * width), BF),
        ],
        LONG,
        [
            pltpu.VMEM((PADDED, width), BF),
            pltpu.VMEM((PADDED, width), BF),
            pltpu.VMEM((PADDED, PAIR), BF),
            pltpu.VMEM((PADDED, PAIR), BF),
        ],
        flags,
        pieces={9: wide_pieces(hidden), 10: wide_pieces(hidden)},
        lead=5,
    )


def put_up(held, at, grad):
    rows = grad.shape[0] // SLICES
    put_rows(held, at // CHUNK * rows, grad)


def put_down(held, at, start, grad):
    rows = DOWN_ROWS
    for piece in range(grad.shape[0] // rows):
        held[at // rows + piece, start : start + rows, :] = grad[piece * rows : (piece + 1) * rows]


def put_rows(held, place, grad):
    rows = grad.shape[0] // SLICES
    for piece in range(SLICES):
        held[piece, place : place + rows, :] = grad[piece * rows : (piece + 1) * rows]


def mlp_tail(layer, grad, grad_normed, unit, scale, gain, mixed, w_out, ups, place, out_grad, out_mixed, small):
    width = unit.shape[1]
    grad_state, grad_gain, grad_bias = norm_back(grad_normed, unit, scale, gain[layer, 1:2])
    grad = grad + grad_state
    out_grad[...] = grad
    out_grad.send()
    small[1:2, :width] = grad_gain
    small[1:2, width : 2 * width] = grad_bias
    low = grad.astype(BF)
    put_rows(ups, place, mat_left(mixed[...], low).astype(BF))
    out_mixed[...] = mat_right(low, w_out[...]).astype(BF)
    out_mixed.send()


def mlp_chunk(span, low, grad_low, slope, w_up, w_down, ups, small):
    grad_hidden = slope * mat_right(grad_low, w_down)
    hidden_low = grad_hidden.astype(BF)
    put_up(ups, span.start, mat_left(low, hidden_low).astype(BF))
    small[0:1, span] = jnp.sum(hidden_low.astype(F32), axis=0, keepdims=True)
    return mat_right(hidden_low, w_up)


def joint_scores(query, marks, keys, key_marks, p, head):
    lanes = pl.ds(pl.multiple_of(p * PAIR, PAIR), PAIR)
    return mat_right(
        jnp.concatenate([keys[:, lanes], key_marks[...]], axis=1), score_side(query[:, lanes], marks[...], head)
    )


def crest_kernel(
    flags, fetched, stores, probs, weights, keys, values, key_marks, marks, scores, peaks, held, copied
):
    query, kv, far, lang, x, w_out, gain, bias, ff_bias, cotangent = fetched[:10]
    mlp = fetched[10:]
    mixed, share, out_grad, out_mixed, keep, send, small = stores
    klass, side = flags[0], flags[1]
    query, kv, far, lang = query.ref(), kv.ref(), far.ref(), lang.ref()
    x.more(len(fetched))

    keys[...] = jnp.zeros_like(keys)
    values[...] = jnp.zeros_like(values)
    key_marks[...] = joint_key_marks(klass)
    marks[...] = joint_row_marks()

    def put(rows, block):
        for p in range(HEADS // 2):
            lanes = slice(p * PAIR, (p + 1) * PAIR)
            keys[rows, lanes] = block[:, 2 * p * PAIR : (2 * p + 1) * PAIR]
            values[rows, lanes] = block[:, (2 * p + 1) * PAIR : (2 * p + 2) * PAIR]

    joint_place(klass, side, kv, far, lang, put)

    def copy_out(p, head):
        return pltpu.make_async_copy(held.at[head], probs.at[2 * p + head], copied.at[head])

    def one(p, head, turned):
        across = jnp.concatenate([turned[head * HD : (head + 1) * HD], jnp.ones((16, KEYS), BF)], axis=0)
        found = jnp.exp(scores[head, :, :ROWS] - peaks[head]).astype(BF)
        held[head, :, :ROWS] = found
        copy_out(p, head).start()
        out = matmul(across, found)
        part = 1.0 / out[HD : HD + 1]
        share[p, head : head + 1, :] = part
        return out[:HD] * part

    for head in range(2):
        held[head] = jnp.zeros(held.shape[1:], BF)
        copy_out(0, head).start()
    def form(p, head):
        found = joint_scores(query, marks, keys, key_marks, p, head)
        scores[head, :, :ROWS] = found
        peaks[head] = jnp.max(found, axis=0, keepdims=True)

    form(0, 0)

    def pair(p, carry):
        lanes = pl.ds(pl.multiple_of(p * PAIR, PAIR), PAIR)
        turned = values[:, lanes].T
        copy_out(p, 0).wait()
        form(p, 1)
        first = one(p, 0, turned)
        copy_out(p, 1).wait()
        form(jnp.minimum(p + 1, HEADS // 2 - 1), 0)
        second = one(p, 1, turned)
        mixed.buffer[:, lanes] = jnp.concatenate([first, second], axis=0).T.astype(BF)
        return carry

    lax.fori_loop(0, HEADS // 2, pair, 0)
    mixed.send()
    share.send()

    small[...] = jnp.zeros(small.buffer.shape, F32)
    total = x[...] + matmul(mixed[...], w_out[...])
    width = total.shape[1]
    hidden = len(mlp) // 2 * CHUNK
    unit, scale = centre(total)
    low = (unit * gain[1, 1:2] + bias[1, 1:2]).astype(BF)
    grad_low = cotangent[...]
    grad = grad_low.astype(F32)
    small[1:2, 2 * width : 3 * width] = jnp.sum(grad, axis=0, keepdims=True)
    grad_normed = None
    for at, span in enumerate(chunks(hidden)):
        w_up, w_down = mlp[2 * at][...], mlp[2 * at + 1][...]
        value, rise = gelu_both(matmul(low, w_up) + ff_bias[1:2, span])
        part = mlp_chunk(span, low, grad_low, rise, w_up, w_down, weights, small)
        put_down(weights, span.start, DOWN_ROWS, mat_left(value.astype(BF), grad_low).astype(BF))
        grad_normed = part if grad_normed is None else grad_normed + part
    hand_out(weights, (keep, send), flags, PLAIN, slice(0, hidden // SLICES + DOWN_ROWS))
    send.send(0)
    keep.send(0)
    mlp_tail(
        1, grad, grad_normed, unit, scale, gain, mixed, w_out, weights, hidden // SLICES + DOWN_ROWS,
        out_grad, out_mixed, small,
    )
    hand_out(weights, (keep, send), flags, PLAIN, slice(hidden // SLICES + DOWN_ROWS, weights.shape[1]))
    for head in range(2):
        copy_out(HEADS // 2 - 1, head).wait()


def crest(flags, query, kv, far, lang, x, gain, bias, w_attn, w_up, ff_bias, w_down, cotangent):
    rows, width = x.shape
    hidden = w_up.shape[2]
    held = (2 * hidden + width) // SLICES
    early = 2 * hidden // SLICES
    done = dense_call(
        crest_kernel, "crest",
        (query, kv, far, lang, x, w_attn, gain, bias, ff_bias, cotangent, w_up, w_down),
        [(0, None), (1, None), (2, None), (3, None), (4, None), (5, (1, 3))]
        + [(at, None) for at in range(6, 10)]
        + mlp_fetches(1, 10, 11, hidden),
        [((rows, width), BF), ((HEADS // 2, 8, rows), F32), ((rows, width), F32), ((rows, width), BF)]
        + part_shapes(PLAIN, held, width)
        + [((8, hidden), F32)],
        LONG,
        [
            pltpu.VMEM((SLICES, held, width), BF),
            pltpu.VMEM((KEYS, width), BF),
            pltpu.VMEM((KEYS, width), BF),
            pltpu.VMEM((KEYS, PAIR), BF),
            pltpu.VMEM((rows, PAIR), BF),
            pltpu.VMEM((2, KEYS, ROWS_UP), F32),
            pltpu.VMEM((2, 1, rows), F32),
            pltpu.VMEM((2, KEYS, ROWS_UP), BF),
            pltpu.SemaphoreType.DMA((2,)),
        ],
        flags,
        pieces={at: [(slice(None), slice(0, early)), (slice(None), slice(early, held))] for at in (4, 5)},
        lead=4,
        raw=[((HEADS, KEYS, ROWS_UP), BF)],
    )
    return (done[0], done[7], done[1], done[2], done[3], done[4:6], done[6])


def leave_grad(unit, scale, gain, grad, grad_query, grad_key, grad_value, w_qkv):
    grad_normed = mat_right(grad_query, w_qkv[0]) * 0.125
    grad_normed = grad_normed + mat_right(grad_key, w_qkv[1]) + mat_right(grad_value, w_qkv[2])
    grad_state, grad_gain, grad_bias = norm_back(grad_normed, unit, scale, gain)
    return (grad + grad_state, grad_gain, grad_bias)


def leave_kernel(flags, fetched, stores, sums, held):
    query, normed, kv, far, x, gain, w_qkv, grad = fetched[:8]
    out, keep, send, token = stores
    token[...] = jnp.zeros(token.buffer.shape, F32)
    grad_query, low = query[...], normed[...]
    width = low.shape[1]
    place = width // SLICES
    put_rows(held, 0, (mat_left(low, grad_query) * 0.125).astype(BF))
    sums[...] = kv[...].astype(F32)
    rows = pl.ds(pl.multiple_of((1 - flags[1]) * (ROWS - EDGE), 16), EDGE)
    sums[rows, :] += far[...].astype(F32)
    grad_key, grad_value = unmix(sums[...].astype(BF))
    unit, scale = centre(x[...].astype(F32))
    total, grad_gain, grad_bias = leave_grad(
        unit, scale, gain[0, 0:1], grad[...], grad_query, grad_key, grad_value, w_qkv
    )
    out[...] = total
    out.send()
    put_rows(held, place, mat_left(low, grad_key).astype(BF))
    put_rows(held, 2 * place, mat_left(low, grad_value).astype(BF))
    put_small(held, 3 * place, fetched[8:], grad_gain, grad_bias)
    hand_out(held, (keep, send), flags, LAST)


SMALL_ROWS = 32


def put_small(held, place, small, grad_gain, grad_bias):
    width = grad_gain.shape[1]
    rows = [grad_gain, small[0][1:2, :width], small[2][0:1, :width], small[1][1:2, :width]]
    rows += [grad_bias, small[0][1:2, width : 2 * width], small[2][0:1, width : 2 * width]]
    rows += [small[1][1:2, width : 2 * width]]
    rows += [small[at][1:2, 2 * width : 3 * width] for at in range(2)]
    block = jnp.concatenate(rows, axis=0)
    long = jnp.concatenate([small[at][0:1, :] for at in range(2)], axis=0)
    each, more = width // SLICES, long.shape[1] // SLICES
    for piece in range(SLICES):
        head = jnp.pad(block[:, piece * each : (piece + 1) * each], ((0, 0), (0, more - each)))
        tail = long[:, piece * more : (piece + 1) * more]
        rest = jnp.zeros((SMALL_ROWS - head.shape[0] - tail.shape[0], more), F32)
        both = jnp.concatenate([head, tail, rest], axis=0).astype(BF)
        held[piece, place : place + SMALL_ROWS, :] = jnp.pad(both, ((0, 0), (0, width - more)))


def leave(flags, x, gain, normed, grad, query, kv, far, w_attn, smalls, after):
    rows, width = x.shape
    held = 3 * (width // SLICES) + SMALL_ROWS
    done = dense_call(
        leave_kernel, "leave",
        (query, normed, kv, far, x, gain, w_attn, grad, *smalls),
        [(at, None) for at in range(6)] + [(6, (0, QKV))] + [(at, None) for at in range(7, 11)],
        [((rows, width), F32)] + part_shapes(LAST, held, width) + [((8, PAIR), F32)],
        4.0,
        [pltpu.VMEM((rows, 2 * width), F32), pltpu.VMEM((SLICES, held, width), BF)],
        flags,
        after,
        lead=8,
    )
    return (done[0], done[1:3], done[3])


def put_sums(klass, side, sums, lang_sums, kv, here, far, own, lone, there):
    @pl.when(klass == 1)
    def fine():
        sums[:, here] = (kv[:, here].astype(F32) + far[:ROWS, there].astype(F32)).astype(BF)

        @pl.when(side == 0)
        def owner():
            lang_sums[:LONE, here] = (lone[:, there].astype(F32) + far[ROWS:, there].astype(F32)).astype(BF)

    @pl.when(klass != 1)
    def coarse():
        sums[:, here] = kv[:, here]
        lang_sums[:, here] = own[:, there]


def descend_kernel(flags, fetched, stores, sums, lang_sums, plain, split):
    query, normed, x, kv = fetched[:4]
    fars, owns, lones = fetched[4:6], fetched[6:8], fetched[8:10]
    w_qkv, gain, grad, low_normed = fetched[10:14]
    mlp, (after, mixed, w_out, lang_normed, feats, language, w_lang) = fetched[14:-7], fetched[-7:]
    out_grad, out_mixed, grad_language, keep, send, split_keep, split_send, small, small_mid = stores
    klass, side = flags[0], flags[1]
    small[...] = jnp.zeros(small.buffer.shape, F32)
    small_mid[...] = jnp.zeros(small_mid.buffer.shape, F32)
    lang_sums[...] = jnp.zeros_like(lang_sums)
    grad_query, low = query[...], normed[...]
    width = low.shape[1]
    place = width // SLICES
    hidden = len(mlp) // 4 * CHUNK
    up_rows = hidden // SLICES
    put_rows(plain, up_rows, (mat_left(low, grad_query) * 0.125).astype(BF))
    unit, scale = centre(x[...])
    kv = kv.ref()
    fars, owns, lones = [[part.ref() for part in parts] for parts in (fars, owns, lones)]
    for pair in range(HEADS // 2):
        for which in range(2):
            there = slice(pair * PAIR, (pair + 1) * PAIR)
            here = slice((2 * pair + which) * PAIR, (2 * pair + which + 1) * PAIR)
            put_sums(klass, side, sums, lang_sums, kv, here, fars[which], owns[which], lones[which], there)

    grad_key, grad_value = unmix(sums[...])
    grad, grad_gain, grad_bias = leave_grad(
        unit, scale, gain[1, 0:1], grad[...], grad_query, grad_key, grad_value, w_qkv
    )
    lang_key, lang_value = unmix(lang_sums[...])
    lang_low = lang_normed[...]
    put_rows(plain, up_rows + place, (mat_left(low, grad_key) + mat_left(lang_low, lang_key)).astype(BF))
    put_rows(split, DOWN_ROWS, (mat_left(low, grad_value) + mat_left(lang_low, lang_value)).astype(BF))
    lang_grad = mat_right(lang_key, w_qkv[1]) + mat_right(lang_value, w_qkv[2])
    unit, scale = centre(feats[...])
    grad_feats, lang_gain, lang_bias = norm_back(lang_grad, unit, scale, gain[1, 0:1])
    feats_low = grad_feats.astype(BF)
    put_rows(split, DOWN_ROWS + place, mat_left(language[...], feats_low).astype(BF))
    grad_language[...] = mat_right(feats_low, w_lang[...])
    grad_language.send()
    small_mid[0:1, :width] = grad_gain + lang_gain
    small_mid[0:1, width : 2 * width] = grad_bias + lang_bias

    grad_low = grad.astype(BF)
    small[1:2, 2 * width : 3 * width] = jnp.sum(grad_low.astype(F32), axis=0, keepdims=True)
    low = low_normed[...]
    grad_normed = None
    for at, span in enumerate(chunks(hidden)):
        w_down, rise, w_up, active = [part[...] for part in mlp[4 * at : 4 * at + 4]]
        part = mlp_chunk(span, low, grad_low, rise.astype(F32), w_up, w_down, plain, small)
        put_down(split, span.start, 0, mat_left(active, grad_low).astype(BF))
        grad_normed = part if grad_normed is None else grad_normed + part
    hand_out(plain, (keep, send), flags, PLAIN)
    send.send()
    keep.send()
    unit, scale = centre(after[...])
    mlp_tail(
        0, grad, grad_normed, unit, scale, gain, mixed, w_out, split, DOWN_ROWS + 2 * place, out_grad, out_mixed, small
    )
    hand_out(split, (split_keep, split_send), flags, SPLIT)


def descend(
    flags, state, gain, normed, grad, query, kv, fars, owns, w_attn, feats, lang_normed, language, w_lang,
    after, mixed, low_normed, active, slope, w_up, w_down, follows,
):
    rows, width = state.shape
    hidden = w_up.shape[2]
    place = width // SLICES
    plain, split = hidden // SLICES + 2 * place, DOWN_ROWS + 3 * place
    fetches = []
    for span in chunks(hidden):
        fetches += [(13, (0, span)), (14, (slice(None), span)), (12, (0, slice(None), span)), (15, (slice(None), span))]
    head, foot = slice(0, LPAD), slice(ROWS, ROWS + LONE)
    done = dense_call(
        descend_kernel, "descend",
        (query, normed, state, kv, *fars, *owns, w_attn, gain, grad, low_normed)
        + (w_up, w_down, slope, active, after, mixed, lang_normed, feats, language, w_lang),
        [(at, None) for at in range(6)]
        + [(at, (head,)) for at in range(6, 8)]
        + [(at, (foot,)) for at in range(6, 8)]
        + [(8, (1, QKV)), (9, None), (10, None), (11, None)]
        + fetches
        + [(16, None), (17, None), (8, (0, 3)), (18, None), (19, None), (20, None), (21, None)],
        [((rows, width), F32), ((rows, width), BF), ((LPAD, width), F32)]
        + part_shapes(PLAIN, plain, width)
        + part_shapes(SPLIT, split, width)
        + [((8, hidden), F32), ((8, 2 * width), F32)],
        LONG,
        [
            pltpu.VMEM((rows, 2 * width), BF),
            pltpu.VMEM((LPAD, 2 * width), BF),
            pltpu.VMEM((SLICES, plain, width), BF),
            pltpu.VMEM((SLICES, split, width), BF),
        ],
        flags,
        follows,
        lead=6,
    )
    return (done[0], done[1], done[2], done[3:5], done[5:7], done[7], done[8])


def pair_swap(block):
    count = lax.axis_size("wide")
    return lax.ppermute(block, "wide", [(at, at ^ 1) for at in range(count)])


class Flow:
    def __init__(self, route, parts):
        self.route, self.step = route, 0
        self.units = route.units
        self.keep = [parts[0]]
        self.send(parts)

    def send(self, parts):
        self.got = []
        if self.step < len(self.route.steps):
            bits = self.route.steps[self.step]
            self.units //= 1 << len(bits)
            for at, part in enumerate(parts[1:], 1):
                found = [bit for place, bit in enumerate(bits) if at >> (len(bits) - 1 - place) & 1]
                self.got.append(self.move(part, found))
        else:
            self.keep = [parts[0]]
            self.got.append(self.move(parts[0], [0] if self.route.halves else None))

    def move(self, part, bits):
        shift = 1 if self.route.halves else 0
        if bits is None or bits == [0] and shift:
            return lax.ppermute(part, "narrow", [(0, 1), (1, 0)])
        count = lax.axis_size("wide")
        stride = sum((count // SLICES) << (bit - shift) for bit in bits)
        return lax.ppermute(part, "wide", [(p, p ^ stride) for p in range(count)])


def step_kernel(layout, ins, outs):
    at = 0
    for out, (count, rows) in zip(outs, layout):
        total = None
        for term in ins[at : at + count]:
            part = term[rows] if rows is not None else term[...]
            total = part.astype(F32) if total is None else total + part.astype(F32)
        out[...] = total.astype(BF)
        if isinstance(out, Store):
            out.send()
        at += count


def step(flows, after=(), near=False, cost=SHORT, lazy=False):
    operands, fetches, layout, outs, plan = [], [], [], [], []
    for flow in flows:
        flow.step += 1
        terms = flow.keep + flow.got
        last = flow.step == len(flow.route.steps)
        count = 1 if last else flow.route.parts(flow.step)
        each = flow.units // count
        made = [part for part in range(count) if part or last or not lazy]
        for part in reversed(made):
            rows = slice(part * each, (part + 1) * each)
            for term in terms:
                fetches.append((len(operands), rows))
                operands.append(term)
            layout.append((len(terms), rows))
            outs.append(((each,) + terms[0].shape[1:], BF))
        plan.append((flow, terms, count, made))
    if near:
        done = near_call(
            lambda *refs: step_kernel(layout, refs[: len(operands)], refs[len(operands) :]),
            "step", outs, operands, after=after, cost=cost,
        )
    else:
        done = dense_call(
            lambda ins, stores: step_kernel([(count, None) for count, rows in layout], ins, stores),
            "step", operands, fetches, outs, cost, after=after, lead=len(fetches), room=STEP_VMEM,
        )
    at = 0
    for flow, terms, count, made in plan:
        parts = [None] * count
        for part in reversed(made):
            parts[part] = done[at]
            at += 1
        flow.keep = terms if parts[0] is None else [parts[0]]
        flow.send(parts)
    return done


def split_low(buffer):
    count = lax.axis_size("wide")
    position = lax.axis_index("wide")
    half = count // SLICES
    while half > 1:
        half //= 2
        mine = position // half % 2
        size = buffer.shape[0] // 2
        send = lax.dynamic_slice_in_dim(buffer, (1 - mine) * size, size, 0)
        keep = lax.dynamic_slice_in_dim(buffer, mine * size, size, 0)
        buffer = keep + lax.ppermute(send.astype(BF), "wide", [(p, p ^ half) for p in range(count)])
    return buffer


def finish_kernel(
    flags, first, first_got, plain, plain_got, split, split_got, attn_one, attn_one_got,
    lang, attn, ups, downs, gains, biases, ff_biases, out_biases, whole, last,
):
    rows, width = attn.shape[2:]
    up_rows, down_rows = ups.shape[2] // width * rows, downs.shape[1]

    def both(buffer, got):
        return buffer[0].astype(F32) + got[0].astype(F32)

    def put_ups(layer, found):
        for at in range(ups.shape[2] // width):
            ups[layer, :, at * width : (at + 1) * width] = found[at * rows : (at + 1) * rows]

    found = both(first, first_got)
    put_ups(1, found)
    downs[1] = found[up_rows : up_rows + down_rows]
    attn[1, 3] = found[up_rows + down_rows :]
    found = both(plain, plain_got)
    put_ups(0, found)
    attn[1, 0] = found[up_rows : up_rows + rows]
    attn[1, 1] = found[up_rows + rows :]
    whole[flags[3]] = split[0].astype(F32)
    whole[1 - flags[3]] = split_got[0].astype(F32)
    found = jnp.concatenate([whole[0], whole[1]], axis=0)
    downs[0] = found[:down_rows]
    attn[1, 2] = found[down_rows : down_rows + rows]
    lang[...] = found[down_rows + rows : down_rows + 2 * rows]
    attn[0, 3] = found[down_rows + 2 * rows :]
    last[flags[3]] = attn_one[0].astype(F32)
    last[1 - flags[3]] = attn_one_got[0].astype(F32)
    found = jnp.concatenate([last[0], last[1]], axis=0)
    for at in range(3):
        attn[0, at] = found[at * rows : (at + 1) * rows]
    small = found[3 * rows :]
    for layer in range(2):
        gains[layer] = small[2 * layer : 2 * layer + 2, :rows]
        biases[layer] = small[4 + 2 * layer : 6 + 2 * layer, :rows]
    out_biases[...] = small[8:10, :rows]
    ff_biases[...] = small[10:12, : ff_biases.shape[1]]


def finish(flags, flows, width, hidden):
    rows = width // SLICES
    args = []
    for flow in flows:
        args += flow.keep + flow.got
    return near_call(
        finish_kernel, "finish",
        [
            ((rows, width), F32),
            ((2, 4, rows, width), F32),
            ((2, rows, hidden), F32),
            ((2, hidden // SLICES, width), F32),
            ((2, 2, rows), F32),
            ((2, 2, rows), F32),
            ((2, hidden // SLICES), F32),
            ((2, rows), F32),
        ],
        args,
        [
            pltpu.VMEM((2, (DOWN_ROWS + 3 * rows) // 2, width), F32),
            pltpu.VMEM((2, (3 * rows + SMALL_ROWS) // 2, width), F32),
        ],
        flags,
    )


def body(
    patches,
    language,
    w_lang,
    w_attn,
    w_up,
    w_down,
    norm_gain,
    norm_bias,
    ff_bias,
    out_bias,
    cotangent,
    classes,
):
    position = lax.axis_index("wide")
    wide = lax.axis_size("wide")
    side = position % 2
    klass = lax.dynamic_index_in_dim(classes[0], position // 2, 0, keepdims=False)
    high = position // (wide // SLICES)
    flags = jnp.stack([klass, side, high, lax.axis_index("narrow")]).astype(jnp.int32)
    width = w_lang.shape[0]
    hidden = w_up.shape[2]
    start = patches[0]
    lang_low = jnp.pad(language[0], ((0, LPAD - language.shape[1]), (0, 0)))

    edge = pair_swap(jnp.where(side == 0, start[ROWS - EDGE :], start[:EDGE]))
    normed_a, query_a, key_a, value_a, mixed_a, weights_a, share_a, *rest = climb(
        flags, start, edge, norm_gain, norm_bias, w_attn, w_up, ff_bias, w_down, out_bias, lang_low, w_lang
    )
    after_a, normed_b, active_b, slope_b, state_b, normed_c, query_c, kv_c, feats, lang_normed, lang_kv = rest
    far_c = pair_swap(kv_c)
    mixed_c, weights_c, share_c, grad, grad_mixed_c, parts, small_two = crest(
        flags, query_c, kv_c, far_c, lang_kv, state_b, norm_gain, norm_bias, w_attn, w_up, ff_bias, w_down,
        cotangent[0],
    )
    first = Flow(PLAIN, parts)
    joint = (flags, query_c, kv_c, far_c, lang_kv, mixed_c, weights_c, share_c, grad_mixed_c)
    query, kv, *edges, token = joint_backward(*joint, 0, HEADS // 2)
    fars = [pair_swap(part) for part in edges]
    done = step([first], [token], lazy=True)
    grad, grad_mixed_a, grad_language, plain_parts, split_parts, small_one, small_mid = descend(
        flags, state_b, norm_gain, normed_c, grad, query, kv, fars, edges, w_attn, feats, lang_normed, lang_low,
        w_lang, after_a, mixed_a, normed_b, active_b, slope_b, w_up, w_down, done,
    )
    plain, split = Flow(PLAIN, plain_parts), Flow(SPLIT, split_parts)

    done = step([first], [small_mid], lazy=True, cost=30.0)
    done = step([plain, split], [done[0]])
    view = (flags, query_a, key_a, value_a, mixed_a, weights_a, share_a, grad_mixed_a)
    query, kv, edge, token = view_backward(*view, 0, HEADS // 2, done)
    far = pair_swap(edge)
    done = step([first], [token])
    grad, attn_parts, token = leave(
        flags, start, norm_gain, normed_a, grad, query, kv, far, w_attn, (small_one, small_two, small_mid), done
    )
    attn_one = Flow(LAST, attn_parts)

    done = step([plain, split, first], [token], near=True, cost=LONG)
    done = step([attn_one], [done[0]], near=True)
    done = step([plain, split], [done[0]], near=True)
    done = step([attn_one], [done[0]], near=True)
    done = step([plain, split], [done[0]], near=True)
    done = step([attn_one], [done[0]], near=True)
    done = step([split], [done[0]], near=True)
    done = step([attn_one], [done[0]], near=True)
    flows = (first, plain, split, attn_one)
    grad_w_lang, grad_w_attn, grad_w_up, grad_w_down, *vectors = finish(flags, flows, width, hidden)
    gains, biases, ff_biases, out_biases = vectors

    def own(values, dim):
        if wide == SLICES:
            return values
        values = jnp.moveaxis(values, dim, 0)
        return jnp.moveaxis(split_low(values), 0, dim)

    return (
        grad[None],
        grad_language[None, : language.shape[1]],
        own(grad_w_lang, 0),
        own(grad_w_attn, 2),
        own(grad_w_up, 1),
        own(grad_w_down, 1),
        own(gains, 2),
        own(biases, 2),
        own(ff_biases, 1),
        own(out_biases, 1),
    )


def solution(mesh):
    in_specs = (
        P("narrow", "wide", None),
        P("narrow", "wide", None),
        P(),
        P(),
        P(),
        P(),
        P(),
        P(),
        P(),
        P(),
        P("narrow", "wide", None),
        P("narrow", None),
    )
    out_specs = (
        P("narrow", "wide", None),
        P("narrow", "wide", None),
        P("wide", None),
        P(None, None, "wide", None),
        P(None, "wide", None),
        P(None, "wide", None),
        P(None, None, "wide"),
        P(None, None, "wide"),
        P(None, "wide"),
        P(None, "wide"),
    )
    return jax.shard_map(body, mesh=mesh, in_specs=in_specs, out_specs=out_specs, check_vma=False)
```

```python
import functools

import jax
import jax.numpy as jnp
from jax import lax
from jax.experimental import pallas as pl
from jax.experimental.pallas import tpu as pltpu
from jax.sharding import PartitionSpec as P

HEADS = 8
HD = 64
LANG = 77
VB = 288
VS = 72
ROWS = 720
EDGE = VB // 2
PADDED = ROWS + EDGE
LPAD = 160
LONE = 96
KEYS = 2 * ROWS + LONE
PAIR = 2 * HD
SLICES = 16
ROWS_UP = 768
VB_UP = 384
STEP_VMEM = 20 * 2**20
LONG, SHORT = 60.0, 0.5
JOINT_VMEM = 60 * 2**20
JOINT_BACK_VMEM = 60 * 2**20
VIEW_VMEM = 24 * 2**20
DENSE_VMEM = 60 * 2**20
NEAR_VMEM = 16 * 2**20

epsilon = 1e-05
masked_out = -1e30
BF = jnp.bfloat16
F32 = jnp.float32


def matmul(left, right):
    return jnp.dot(left, right, preferred_element_type=F32)


def mat_left(left, right):
    return lax.dot_general(left, right, (((0,), (0,)), ((), ())), preferred_element_type=F32)


def mat_right(left, right):
    return lax.dot_general(left, right, (((1,), (1,)), ((), ())), preferred_element_type=F32)


def cost_of(microseconds):
    return pl.CostEstimate(flops=int(microseconds * 1e9), bytes_accessed=1, transcendentals=0)


def waiting(kernel, inputs, more):
    if not more:
        return kernel

    def without(*refs):
        return kernel(*refs[:inputs], *refs[inputs + more :])

    return without


def lane_mask(head):
    lanes = lax.broadcasted_iota(jnp.int32, (1, PAIR), 1)
    return jnp.where(lanes // HD == head, 1.0, 0.0).astype(BF)


def in_half(shape):
    return lax.broadcasted_iota(jnp.int32, shape, 1) % HD


def row_of(shape):
    return lax.broadcasted_iota(jnp.int32, shape, 0)


def key_marks(allowed, items):
    lane = in_half(allowed.shape)
    marks = jnp.where(lane < items, jnp.where(allowed, 0.0, masked_out), 0.0)
    return jnp.where((lane >= 4) & (lane < 7), 1.0, marks).astype(BF)


def joint_key_marks(klass):
    shape = (KEYS, PAIR)
    row, lane = row_of(shape), in_half(shape)
    first = (row < ROWS // 2) | ((row >= ROWS) & (row < ROWS + LANG))
    second = ((row >= ROWS // 2) & (row < ROWS)) | ((row >= ROWS + LANG) & (row < ROWS + 2 * LANG))
    fine = jnp.where(row < 2 * ROWS + LANG, 1, 0)
    coarse = jnp.where(lane == 0, jnp.where(first, 1, 0), jnp.where(second, 1, 0))
    return key_marks(jnp.where(klass == 1, fine, coarse) == 1, 2)


def joint_row_marks():
    shape = (ROWS, PAIR)
    row, lane = row_of(shape), in_half(shape)
    return jnp.where(lane == row // (ROWS // 2), 1.0, 0.0).astype(BF)


def view_key_marks(klass):
    shape = (PADDED, PAIR)
    row, lane = row_of(shape), in_half(shape)
    same = jnp.where(lane == row % VB // VS, 1, 0)
    return key_marks(jnp.where(klass == 1, 1, same) == 1, 4)


def view_row_marks():
    shape = (PADDED, PAIR)
    row, lane = row_of(shape), in_half(shape)
    return jnp.where(lane == row % VB // VS, 1.0, 0.0).astype(BF)


def with_parts(values):
    lane = in_half(values.shape)
    high = values.astype(BF).astype(F32)
    rest = values - high
    middle = rest.astype(BF).astype(F32)
    low = rest - middle
    picked = jnp.where(lane == 4, -high, jnp.where(lane == 5, -middle, jnp.where(lane == 6, -low, 0.0)))
    return picked.astype(BF)


def attend_heads(units):
    scores = [mat_right(keys, right) for right, keys, across in units]
    weights = [jnp.exp(part - jnp.max(part, axis=0, keepdims=True)).astype(BF) for part in scores]
    outs = [matmul(unit[2], part) for unit, part in zip(units, weights)]
    shares = [1.0 / out[HD : HD + 1] for out in outs]
    return [(part, out[:HD] * share, share) for part, out, share in zip(weights, outs, shares)]


def score_side(query, marks, head):
    mask = lane_mask(head)
    return jnp.concatenate([query * mask, marks * mask], axis=1)


def joint_place(klass, side, kv_ref, far_ref, lang_ref, put):
    put(slice(0, ROWS), kv_ref[:ROWS])

    @pl.when(klass == 1)
    def fine():
        put(slice(ROWS, 2 * ROWS), far_ref[:ROWS])

        @pl.when(side == 0)
        def own():
            put(slice(2 * ROWS, KEYS), lang_ref[:LONE])

        @pl.when(side == 1)
        def partner():
            put(slice(2 * ROWS, KEYS), far_ref[ROWS:])

    @pl.when(klass != 1)
    def coarse():
        put(slice(ROWS, ROWS + LPAD), lang_ref[...])


def inner_marks(grad, mixed):
    lanes = lax.broadcasted_iota(jnp.int32, (1, PAIR), 1)
    product = grad.astype(F32) * mixed.astype(F32)
    first = jnp.sum(jnp.where(lanes < HD, product, 0.0), axis=1, keepdims=True)
    second = jnp.sum(jnp.where(lanes < HD, 0.0, product), axis=1, keepdims=True)
    return with_parts(jnp.where(lanes < HD, first, second))


def attend_back(units):
    inner = [mat_right(unit[0], unit[5]) for unit in units]
    probs = [unit[2].astype(F32) * unit[3] for unit in units]
    grad_scores = [(left * right).astype(BF) for left, right in zip(probs, inner)]
    grad_values = [matmul(part.astype(BF), unit[5][:, :PAIR]) for part, unit in zip(probs, units)]
    grad_keys = [matmul(part, unit[4]) for part, unit in zip(grad_scores, units)]
    across = [matmul(unit[1], part) for part, unit in zip(grad_scores, units)]
    return list(zip(grad_keys, grad_values, across))


def fill_rows(left, grads, rows, query, grad, mixed):
    inner = inner_marks(grad, mixed)
    for head in range(2):
        mask = lane_mask(head)
        left[head, rows, :] = query * mask
        grads[head, rows, :PAIR] = grad * mask
        grads[head, rows, PAIR:] = inner * mask


def joint_backward_kernel(
    flags, q_ref, kv_ref, far_ref, lang_ref, mixed_ref, weights_ref, share_ref, grad_ref, dq_ref, dkv_ref,
    dfar_key, dfar_value, token, keys, values, across, left, grads,
):
    klass, side = flags[0], flags[1]

    @pl.when(pl.program_id(0) == 0)
    def prepare():
        keys[...] = jnp.zeros_like(keys)
        values[...] = jnp.zeros_like(values)
        values[:, PAIR:] = joint_key_marks(klass)

    def put(rows, block):
        keys[rows, :] = block[:, :PAIR]
        values[rows, :PAIR] = block[:, PAIR:]

    joint_place(klass, side, kv_ref, far_ref, lang_ref, put)
    token[...] = jnp.zeros_like(token)
    across[...] = keys[...].T
    fill_rows(left, grads, slice(0, ROWS), q_ref[...], grad_ref[...], mixed_ref[...])
    units = [
        (
            values[...],
            across[head * HD : (head + 1) * HD, :],
            weights_ref[head, :, :ROWS],
            share_ref[0, head : head + 1, :],
            left[head],
            grads[head],
        )
        for head in range(2)
    ]
    first, second = attend_back(units)
    for span, at, far in ((slice(0, PAIR), 0, dfar_key), (slice(PAIR, 2 * PAIR), 1, dfar_value)):
        both = (first[at] + second[at]).astype(BF)
        dkv_ref[:, span] = both[:ROWS]
        far[...] = both[ROWS:]
    dq_ref[...] = jnp.concatenate([first[2], second[2]], axis=0).T.astype(BF)


def joint_backward(flags, query, kv, far, lang, mixed, weights, share, grad, base, pairs, after=(), cost=LONG):
    rows = query.shape[0]
    one = pl.BlockSpec((rows, PAIR), lambda i, f: (0, i + base))
    return pl.pallas_call(
        waiting(joint_backward_kernel, 9, len(after)),
        grid_spec=pltpu.PrefetchScalarGridSpec(
            num_scalar_prefetch=1,
            grid=(pairs,),
            in_specs=[
                one,
                pl.BlockSpec((rows, 2 * PAIR), lambda i, f: (0, i + base)),
                pl.BlockSpec((ROWS + LONE, 2 * PAIR), lambda i, f: (0, i + base)),
                pl.BlockSpec((LPAD, 2 * PAIR), lambda i, f: (0, i + base)),
                one,
                pl.BlockSpec((2, KEYS, ROWS_UP), lambda i, f: (i + base, 0, 0)),
                pl.BlockSpec((1, 8, rows), lambda i, f: (i + base, 0, 0)),
                one,
            ]
            + [pl.BlockSpec(memory_space=pltpu.HBM)] * len(after),
            out_specs=[
                pl.BlockSpec((rows, PAIR), lambda i, f: (0, i)),
                pl.BlockSpec((rows, 2 * PAIR), lambda i, f: (0, i)),
                pl.BlockSpec((ROWS + LONE, PAIR), lambda i, f: (0, i)),
                pl.BlockSpec((ROWS + LONE, PAIR), lambda i, f: (0, i)),
                pl.BlockSpec((8, PAIR), lambda i, f: (0, 0)),
            ],
            scratch_shapes=[
                pltpu.VMEM((KEYS, PAIR), BF),
                pltpu.VMEM((KEYS, 2 * PAIR), BF),
                pltpu.VMEM((PAIR, KEYS), BF),
                pltpu.VMEM((2, ROWS, PAIR), BF),
                pltpu.VMEM((2, ROWS, 2 * PAIR), BF),
            ],
        ),
        out_shape=[
            jax.ShapeDtypeStruct((rows, pairs * PAIR), BF),
            jax.ShapeDtypeStruct((rows, 2 * pairs * PAIR), BF),
            jax.ShapeDtypeStruct((ROWS + LONE, pairs * PAIR), BF),
            jax.ShapeDtypeStruct((ROWS + LONE, pairs * PAIR), BF),
            jax.ShapeDtypeStruct((8, PAIR), F32),
        ],
        compiler_params=pltpu.CompilerParams(vmem_limit_bytes=JOINT_BACK_VMEM),
        cost_estimate=cost_of(cost),
        name="joint_backward",
    )(flags, query, kv, far, lang, mixed, weights, share, grad, *after)


def view_spots(side):
    own = pl.ds(pl.multiple_of(side * EDGE, 16), ROWS)
    far = pl.ds(pl.multiple_of((1 - side) * ROWS, 16), EDGE)
    return (own, far)


def view_backward_kernel(
    flags, q_ref, keys, value_ref, mixed_ref, weights_ref, share_ref, grad_ref, dq_ref, dkv_ref, dfar_ref,
    token, values, left, grads, back, dkv,
):
    klass, side = flags[0], flags[1]
    own, far = view_spots(side)

    @pl.when(pl.program_id(0) == 0)
    def prepare():
        values[:, PAIR:] = view_key_marks(klass)
        left[...] = jnp.zeros_like(left)
        grads[...] = jnp.zeros_like(grads)

    values[:, :PAIR] = value_ref[...]
    fill_rows(left, grads, own, q_ref[own, :], grad_ref[...], mixed_ref[...])

    units = []
    for index in range(PADDED // VB):
        rows = slice(index * VB, (index + 1) * VB)
        across = keys[rows, :].T
        for head in range(2):
            units.append(
                (
                    values[rows, :],
                    across[head * HD : (head + 1) * HD, :],
                    weights_ref[index, head, :, :VB],
                    share_ref[index, 0, head : head + 1, :],
                    left[head, rows, :],
                    grads[head, rows, :],
                )
            )
    done = attend_back(units)
    for index in range(PADDED // VB):
        rows = slice(index * VB, (index + 1) * VB)
        first, second = done[2 * index], done[2 * index + 1]
        dkv[rows, :PAIR] = (first[0] + second[0]).astype(BF)
        dkv[rows, PAIR:] = (first[1] + second[1]).astype(BF)
        back[rows, :] = jnp.concatenate([first[2], second[2]], axis=0).T.astype(BF)

    dq_ref[...] = back[own, :]
    dkv_ref[...] = dkv[own, :]
    dfar_ref[...] = dkv[far, :]
    token[...] = jnp.zeros_like(token)


def view_backward(flags, query, key, value, mixed, weights, share, grad, base, pairs, after=(), cost=LONG):
    rows = mixed.shape[0]
    blocks = PADDED // VB
    one = pl.BlockSpec((rows, PAIR), lambda i, f: (0, i + base))
    tall = pl.BlockSpec((PADDED, PAIR), lambda i, f: (0, i + base))
    return pl.pallas_call(
        waiting(view_backward_kernel, 8, len(after)),
        grid_spec=pltpu.PrefetchScalarGridSpec(
            num_scalar_prefetch=1,
            grid=(pairs,),
            in_specs=[
                tall,
                tall,
                tall,
                one,
                pl.BlockSpec((blocks, 2, VB, VB_UP), lambda i, f: (0, i + base, 0, 0)),
                pl.BlockSpec((blocks, 1, 8, VB), lambda i, f: (0, i + base, 0, 0)),
                one,
            ]
            + [pl.BlockSpec(memory_space=pltpu.HBM)] * len(after),
            out_specs=[
                pl.BlockSpec((rows, PAIR), lambda i, f: (0, i)),
                pl.BlockSpec((rows, 2 * PAIR), lambda i, f: (0, i)),
                pl.BlockSpec((EDGE, 2 * PAIR), lambda i, f: (0, i)),
                pl.BlockSpec((8, PAIR), lambda i, f: (0, 0)),
            ],
            scratch_shapes=[
                pltpu.VMEM((PADDED, 2 * PAIR), BF),
                pltpu.VMEM((2, PADDED, PAIR), BF),
                pltpu.VMEM((2, PADDED, 2 * PAIR), BF),
                pltpu.VMEM((PADDED, PAIR), BF),
                pltpu.VMEM((PADDED, 2 * PAIR), BF),
            ],
        ),
        out_shape=[
            jax.ShapeDtypeStruct((rows, pairs * PAIR), BF),
            jax.ShapeDtypeStruct((rows, 2 * pairs * PAIR), BF),
            jax.ShapeDtypeStruct((EDGE, 2 * pairs * PAIR), BF),
            jax.ShapeDtypeStruct((8, PAIR), F32),
        ],
        compiler_params=pltpu.CompilerParams(vmem_limit_bytes=VIEW_VMEM),
        cost_estimate=cost_of(cost),
        name="view_backward",
    )(flags, query, key, value, mixed, weights, share, grad, *after)


CHUNK = 512
DOWN_ROWS = 128
BITS = SLICES.bit_length() - 1


class Route:
    def __init__(self, steps, halves):
        self.steps = steps
        self.halves = halves
        self.order = [bit for step in steps for bit in step]
        self.units = 1 << len(self.order)

    def unit(self, position):
        last = len(self.order) - 1
        return sum((position >> (last - at) & 1) << bit for at, bit in enumerate(self.order))

    def parts(self, step):
        return 1 << len(self.steps[step])

    def rows(self, rows):
        return rows // 2 if self.halves else rows


PLAIN = Route(((0,), (1,), (2,), (3,)), False)
SPLIT = Route(((1,), (0,), (2,), (3,), (4,)), True)
LAST = Route(((1,), (0,), (2,), (3, 4)), True)


def hand_out(held, parts, flags, route, span=slice(None)):
    each = route.units // len(parts)
    rows = route.rows(held.shape[1])
    for position in range(route.units):
        if route.halves:
            unit = jnp.bitwise_xor(route.unit(position), flags[2] * 2 + flags[3])
            block = held[unit // 2, pl.ds(pl.multiple_of(unit % 2 * rows, 16), rows), :]
        else:
            block = held[jnp.bitwise_xor(route.unit(position), flags[2]), span]
        parts[position // each][position % each, span] = block


def part_shapes(route, rows, width):
    each = route.units // route.parts(0)
    return [((each, route.rows(rows), width), BF)] * route.parts(0)


def centre(values):
    mean = jnp.mean(values, axis=-1, keepdims=True)
    centered = values - mean
    variance = jnp.mean(centered * centered, axis=-1, keepdims=True)
    scale = lax.rsqrt(variance + epsilon)
    return (centered * scale, scale)


def norm_back(grad, unit, scale, gain):
    grad_gain = jnp.sum(grad * unit, axis=0, keepdims=True)
    grad_bias = jnp.sum(grad, axis=0, keepdims=True)
    scaled = grad * gain
    level = jnp.mean(scaled, axis=-1, keepdims=True)
    along = jnp.mean(scaled * unit, axis=-1, keepdims=True)
    return ((scaled - level - unit * along) * scale, grad_gain, grad_bias)


def gelu_both(hidden):
    root, cubic = 0.7978845608028654, 0.044715
    square = hidden * hidden
    bend = jnp.tanh(hidden * (root + (root * cubic) * square))
    half = 0.5 + 0.5 * bend
    slope = (0.5 * hidden) * (1.0 - bend * bend) * (root + (3.0 * root * cubic) * square)
    return (hidden * half, half + slope)


def mix(keys, values):
    parts = []
    for at in range(0, keys.shape[1], PAIR):
        parts += [keys[:, at : at + PAIR], values[:, at : at + PAIR]]
    return jnp.concatenate(parts, axis=1)


def unmix(both):
    blocks = [both[:, at : at + PAIR] for at in range(0, both.shape[1], PAIR)]
    return (jnp.concatenate(blocks[0::2], axis=1), jnp.concatenate(blocks[1::2], axis=1))


class Fetch:
    def __init__(self, source, buffer, semaphore, more):
        self.copy = pltpu.make_async_copy(source, buffer, semaphore)
        self.buffer, self.more, self.here = buffer, more, False

    def ref(self):
        if not self.here:
            self.more(0, self)
            self.copy.wait()
            self.here = True
            self.more(2)
        return self.buffer

    def __getitem__(self, index):
        return self.ref()[index]


class Store:
    def __init__(self, buffer, target, semaphores, pieces):
        self.buffer, self.copies, self.gone = buffer, [], []
        for at, piece in enumerate(pieces):
            source = buffer if piece is None else buffer.at[piece]
            place = target if piece is None else target.at[piece]
            self.copies.append(pltpu.make_async_copy(source, place, semaphores.at[at]))
            self.gone.append(False)

    def __setitem__(self, index, value):
        self.buffer[index] = value

    def __getitem__(self, index):
        return self.buffer[index]

    def send(self, at=None):
        for place, copy in enumerate(self.copies):
            if not self.gone[place] and at in (None, place):
                copy.start()
                self.gone[place] = True


LEAD = 4
QKV = slice(0, 3)


def dense_call(kernel, name, operands, fetches, outs, cost, scratch=(), flags=None, after=(), pieces=None, lead=LEAD, room=DENSE_VMEM, raw=()):
    shapes = [
        jax.eval_shape(lambda array, index=index: array[:EDGE] if callable(index) else array[index or ...], operands[at])
        for at, index in fetches
    ]
    count, first = len(operands), 0 if flags is None else 1
    pieces = [(pieces or {}).get(at, (None,)) for at in range(len(outs))]

    def run(*refs):
        inputs = refs[first : first + count]
        rest = refs[first + count + len(after) :]
        targets, rest = rest[: len(outs)], rest[len(outs) :]
        straight, rest = rest[: len(raw)], rest[len(raw) :]
        buffers, rest = rest[: len(fetches)], rest[len(fetches) :]
        held, rest = rest[: len(outs)], rest[len(outs) :]
        came, went, own = rest[0], rest[1 : 1 + len(outs)], rest[1 + len(outs) :]
        fetched, started = [], [0]

        def more(number, wanted=None):
            if wanted is not None:
                number = fetched.index(wanted) + 1 - started[0]
            for fetch in fetched[started[0] : started[0] + max(number, 0)]:
                fetch.copy.start()
            started[0] += max(number, 0)

        for place, (at, index) in enumerate(fetches):
            index = index(refs[0]) if callable(index) else index
            source = inputs[at] if index is None else inputs[at].at[index]
            fetched.append(Fetch(source, buffers[place], came.at[place], more))
        more(lead)
        stores = [Store(*parts) for parts in zip(held, targets, went, pieces)]
        kernel(*([refs[0]] if first else []), fetched, stores, *straight, *own)
        for fetch in fetched:
            fetch.ref()
        for store in stores:
            store.send()
        for store in stores:
            for copy in store.copies:
                copy.wait()

    anywhere = pl.BlockSpec(memory_space=pl.ANY)
    return pl.pallas_call(
        run,
        in_specs=[pl.BlockSpec(memory_space=pltpu.SMEM)] * first
        + [anywhere] * count
        + [pl.BlockSpec(memory_space=pltpu.HBM)] * len(after),
        out_specs=[anywhere] * (len(outs) + len(raw)),
        out_shape=[jax.ShapeDtypeStruct(shape, kind) for shape, kind in (*outs, *raw)],
        scratch_shapes=[pltpu.VMEM(part.shape, part.dtype) for part in shapes]
        + [pltpu.VMEM(shape, kind) for shape, kind in outs]
        + [pltpu.SemaphoreType.DMA((len(fetches),))]
        + [pltpu.SemaphoreType.DMA((len(piece),)) for piece in pieces]
        + list(scratch),
        compiler_params=pltpu.CompilerParams(vmem_limit_bytes=room),
        cost_estimate=cost_of(cost),
        name=name,
    )(*([flags] if first else []), *operands, *after)


def near_call(kernel, name, outs, args, scratch=(), flags=None, after=(), cost=SHORT):
    vmem = pl.BlockSpec(memory_space=pltpu.VMEM)
    specs = [vmem] * len(args)
    if flags is not None:
        specs = [pl.BlockSpec(memory_space=pltpu.SMEM)] + specs
        args = [flags] + list(args)
    return pl.pallas_call(
        waiting(kernel, len(args), len(after)),
        in_specs=specs + [pl.BlockSpec(memory_space=pl.ANY)] * len(after),
        out_specs=[vmem] * len(outs),
        out_shape=[jax.ShapeDtypeStruct(shape, kind) for shape, kind in outs],
        scratch_shapes=list(scratch),
        compiler_params=pltpu.CompilerParams(vmem_limit_bytes=NEAR_VMEM),
        cost_estimate=cost_of(cost),
        name=name,
    )(*args, *after)


QKV = slice(0, 3)


def chunks(hidden):
    return [slice(at, at + CHUNK) for at in range(0, hidden, CHUNK)]


def wide_pieces(hidden):
    return [(slice(None), span) for span in chunks(hidden)]


def mlp_fetches(layer, up_at, down_at, hidden):
    found = []
    for span in chunks(hidden):
        found += [(up_at, (layer, slice(None), span)), (down_at, (layer, span))]
    return found


def attend_views(pairs, query, key, value, row_marks, key_marks, weights, share, mixed):
    places = [(p, index) for p in pairs for index in range(PADDED // VB)]
    units = []
    for p, index in places:
        lanes = pl.ds(pl.multiple_of(p * PAIR, PAIR), PAIR)
        rows = slice(index * VB, (index + 1) * VB)
        keys = jnp.concatenate([key[rows, lanes], key_marks[rows, :]], axis=1)
        turned = value[rows, lanes].T
        for head in range(2):
            across = jnp.concatenate([turned[head * HD : (head + 1) * HD], jnp.ones((16, VB), BF)], axis=0)
            units.append((score_side(query[rows, lanes], row_marks[rows, :], head), keys, across))
    done = attend_heads(units)
    for at, (p, index) in enumerate(places):
        lanes = pl.ds(pl.multiple_of(p * PAIR, PAIR), PAIR)
        rows = slice(index * VB, (index + 1) * VB)
        for head in range(2):
            weights[index, 2 * p + head, :, :VB] = done[2 * at + head][0]
            share[index, p, head : head + 1, :] = done[2 * at + head][2]
        pair = [done[2 * at + head][1] for head in range(2)]
        mixed[rows, lanes] = jnp.concatenate(pair, axis=0).T.astype(BF)


def climb_kernel(flags, fetched, stores, rows_all, mixed_all, row_marks, key_marks):
    x, edge, gain, bias, w_first, w_out, ff_bias, out_bias = fetched[:8]
    mlp, (language, w_lang, w_qkv) = fetched[8:-3], fetched[-3:]
    first, rest = stores[:7], stores[7:]
    normed_one, query_all, key_all, value_all, mixed, weights, share = first
    after, normed, active, slope, state, next_normed, query, kv, feats, lang_normed, lang_kv = rest
    klass, side = flags[0], flags[1]
    own, far = view_spots(side)
    rows_all[own, :] = x[...]
    rows_all[far, :] = edge[...]
    row_marks[...] = view_row_marks()
    key_marks[...] = view_key_marks(klass)
    unit, scale = centre(rows_all[...].astype(F32))
    low = (unit * gain[0, 0:1] + bias[0, 0:1]).astype(BF)
    key_all[...] = matmul(low, w_first[1]).astype(BF)
    key_all.send()
    value_all[...] = matmul(low, w_first[2]).astype(BF)
    value_all.send()
    query_all[...] = (matmul(low, w_first[0]) * 0.125).astype(BF)
    query_all.send()
    rows_all[...] = low
    normed_one[...] = rows_all[own, :]
    normed_one.send()

    def pair(p, carry):
        attend_views(
            (2 * p, 2 * p + 1), query_all.buffer, key_all.buffer, value_all.buffer, row_marks, key_marks, weights.buffer,
            share.buffer, mixed_all,
        )
        return carry

    lax.fori_loop(0, HEADS // 4, pair, 0)
    weights.send()
    share.send()
    mixed[...] = mixed_all[own, :]
    mixed.send()

    total = x[...].astype(F32) + matmul(mixed[...], w_out[...])
    after[...] = total
    after.send()
    unit, scale = centre(total)
    low = (unit * gain[0, 1:2] + bias[0, 1:2]).astype(BF)
    normed[...] = low
    normed.send()
    total = total + out_bias[0:1, :]
    for at in range(0, len(mlp), 2):
        span = slice(at // 2 * CHUNK, (at // 2 + 1) * CHUNK)
        grown, rise = gelu_both(matmul(low, mlp[at][...]) + ff_bias[0:1, span])
        grown = grown.astype(BF)
        active[:, span] = grown
        active.send(at // 2)
        slope[:, span] = rise.astype(BF)
        slope.send(at // 2)
        total = total + matmul(grown, mlp[at + 1][...])
    found = matmul(language[...], w_lang[...])
    feats[...] = found
    feats.send()
    unit, scale = centre(found)
    low = (unit * gain[1, 0:1] + bias[1, 0:1]).astype(BF)
    lang_normed[...] = low
    lang_normed.send()
    both = mix(matmul(low, w_qkv[1]).astype(BF), matmul(low, w_qkv[2]).astype(BF))
    lang_kv[...] = both
    lang_kv.send()
    kv[ROWS:] = both[:LONE]
    state[...] = total
    state.send()
    unit, scale = centre(total)
    low = (unit * gain[1, 0:1] + bias[1, 0:1]).astype(BF)
    next_normed[...] = low
    next_normed.send()
    kv[:ROWS] = mix(matmul(low, w_qkv[1]).astype(BF), matmul(low, w_qkv[2]).astype(BF))
    kv.send()
    query[...] = (matmul(low, w_qkv[0]) * 0.125).astype(BF)


def far_rows(flags):
    return (pl.ds(pl.multiple_of(flags[1] * (ROWS - EDGE), 16), EDGE),)


def climb(flags, x, edge, gain, bias, w_attn, w_up, ff_bias, w_down, out_bias, language, w_lang):
    rows, width = x.shape
    hidden = w_up.shape[2]
    blocks = PADDED // VB
    return dense_call(
        climb_kernel,
        "climb",
        (x, edge, gain, bias, w_attn, ff_bias, out_bias, w_up, w_down, language, w_lang),
        [(0, None), (1, far_rows), (2, None), (3, None), (4, (0, QKV)), (4, (0, 3)), (5, None), (6, None)]
        + mlp_fetches(0, 7, 8, hidden)
        + [(9, None), (10, None), (4, (1, QKV))],
        [
            ((rows, width), BF),
            ((PADDED, width), BF),
            ((PADDED, width), BF),
            ((PADDED, width), BF),
            ((rows, width), BF),
            ((blocks, HEADS, VB, VB_UP), BF),
            ((blocks, HEADS // 2, 8, VB), F32),
            ((rows, width), F32),
            ((rows, width), BF),
            ((rows, hidden), BF),
            ((rows, hidden), BF),
            ((rows, width), F32),
            ((rows, width), BF),
            ((rows, width), BF),
            ((rows + LONE, 2 * width), BF),
            ((LPAD, width), F32),
            ((LPAD, width), BF),
            ((LPAD, 2 * width), BF),
        ],
        LONG,
        [
            pltpu.VMEM((PADDED, width), BF),
            pltpu.VMEM((PADDED, width), BF),
            pltpu.VMEM((PADDED, PAIR), BF),
            pltpu.VMEM((PADDED, PAIR), BF),
        ],
        flags,
        pieces={9: wide_pieces(hidden), 10: wide_pieces(hidden)},
        lead=5,
        room=DENSE_VMEM,
    )


def put_up(held, at, grad):
    rows = grad.shape[0] // SLICES
    put_rows(held, at // CHUNK * rows, grad)


def put_down(held, at, start, grad):
    rows = DOWN_ROWS
    for piece in range(grad.shape[0] // rows):
        held[at // rows + piece, start : start + rows, :] = grad[piece * rows : (piece + 1) * rows]


def put_rows(held, place, grad):
    rows = grad.shape[0] // SLICES
    for piece in range(SLICES):
        held[piece, place : place + rows, :] = grad[piece * rows : (piece + 1) * rows]


def mlp_tail(layer, grad, grad_normed, unit, scale, gain, mixed, w_out, ups, place, out_grad, out_mixed, small):
    width = unit.shape[1]
    grad_state, grad_gain, grad_bias = norm_back(grad_normed, unit, scale, gain[layer, 1:2])
    grad = grad + grad_state
    out_grad[...] = grad
    out_grad.send()
    small[1:2, :width] = grad_gain
    small[1:2, width : 2 * width] = grad_bias
    low = grad.astype(BF)
    put_rows(ups, place, mat_left(mixed[...], low).astype(BF))
    out_mixed[...] = mat_right(low, w_out[...]).astype(BF)
    out_mixed.send()


def mlp_chunk(span, low, grad_low, slope, w_up, w_down, ups, small):
    grad_hidden = slope * mat_right(grad_low, w_down)
    hidden_low = grad_hidden.astype(BF)
    put_up(ups, span.start, mat_left(low, hidden_low).astype(BF))
    small[0:1, span] = jnp.sum(hidden_low.astype(F32), axis=0, keepdims=True)
    return mat_right(hidden_low, w_up)


def joint_scores(query, marks, keys, key_marks, p, head):
    lanes = pl.ds(pl.multiple_of(p * PAIR, PAIR), PAIR)
    return mat_right(
        jnp.concatenate([keys[:, lanes], key_marks[...]], axis=1), score_side(query[:, lanes], marks[...], head)
    )


def crest_kernel(
    flags, fetched, stores, probs, weights, keys, values, key_marks, marks, scores, peaks, held, copied
):
    query, kv, far, lang, x, w_out, gain, bias, ff_bias, cotangent = fetched[:10]
    mlp = fetched[10:]
    mixed, share, out_grad, out_mixed, keep, send, small = stores
    klass, side = flags[0], flags[1]
    query, kv, far, lang = query.ref(), kv.ref(), far.ref(), lang.ref()
    x.more(len(fetched))

    keys[...] = jnp.zeros_like(keys)
    values[...] = jnp.zeros_like(values)
    key_marks[...] = joint_key_marks(klass)
    marks[...] = joint_row_marks()

    def put(rows, block):
        for p in range(HEADS // 2):
            lanes = slice(p * PAIR, (p + 1) * PAIR)
            keys[rows, lanes] = block[:, 2 * p * PAIR : (2 * p + 1) * PAIR]
            values[rows, lanes] = block[:, (2 * p + 1) * PAIR : (2 * p + 2) * PAIR]

    joint_place(klass, side, kv, far, lang, put)

    def copy_out(p, head):
        return pltpu.make_async_copy(held.at[head], probs.at[2 * p + head], copied.at[head])

    def one(p, head, turned):
        across = jnp.concatenate([turned[head * HD : (head + 1) * HD], jnp.ones((16, KEYS), BF)], axis=0)
        found = jnp.exp(scores[head, :, :ROWS] - peaks[head]).astype(BF)
        held[head, :, :ROWS] = found
        copy_out(p, head).start()
        out = matmul(across, found)
        part = 1.0 / out[HD : HD + 1]
        share[p, head : head + 1, :] = part
        return out[:HD] * part

    for head in range(2):
        held[head] = jnp.zeros(held.shape[1:], BF)
        copy_out(0, head).start()
    def form(p, head):
        found = joint_scores(query, marks, keys, key_marks, p, head)
        scores[head, :, :ROWS] = found
        peaks[head] = jnp.max(found, axis=0, keepdims=True)

    form(0, 0)

    def pair(p, carry):
        lanes = pl.ds(pl.multiple_of(p * PAIR, PAIR), PAIR)
        turned = values[:, lanes].T
        copy_out(p, 0).wait()
        form(p, 1)
        first = one(p, 0, turned)
        copy_out(p, 1).wait()
        form(jnp.minimum(p + 1, HEADS // 2 - 1), 0)
        second = one(p, 1, turned)
        mixed.buffer[:, lanes] = jnp.concatenate([first, second], axis=0).T.astype(BF)
        return carry

    lax.fori_loop(0, HEADS // 2, pair, 0)
    mixed.send()
    share.send()

    small[...] = jnp.zeros(small.buffer.shape, F32)
    total = x[...] + matmul(mixed[...], w_out[...])
    width = total.shape[1]
    hidden = len(mlp) // 2 * CHUNK
    unit, scale = centre(total)
    low = (unit * gain[1, 1:2] + bias[1, 1:2]).astype(BF)
    grad_low = cotangent[...]
    grad = grad_low.astype(F32)
    small[1:2, 2 * width : 3 * width] = jnp.sum(grad, axis=0, keepdims=True)
    grad_normed = None
    for at, span in enumerate(chunks(hidden)):
        w_up, w_down = mlp[2 * at][...], mlp[2 * at + 1][...]
        value, rise = gelu_both(matmul(low, w_up) + ff_bias[1:2, span])
        part = mlp_chunk(span, low, grad_low, rise, w_up, w_down, weights, small)
        put_down(weights, span.start, DOWN_ROWS, mat_left(value.astype(BF), grad_low).astype(BF))
        grad_normed = part if grad_normed is None else grad_normed + part
    hand_out(weights, (keep, send), flags, PLAIN, slice(0, hidden // SLICES + DOWN_ROWS))
    send.send(0)
    keep.send(0)
    mlp_tail(
        1, grad, grad_normed, unit, scale, gain, mixed, w_out, weights, hidden // SLICES + DOWN_ROWS,
        out_grad, out_mixed, small,
    )
    hand_out(weights, (keep, send), flags, PLAIN, slice(hidden // SLICES + DOWN_ROWS, weights.shape[1]))
    for head in range(2):
        copy_out(HEADS // 2 - 1, head).wait()


def crest(flags, query, kv, far, lang, x, gain, bias, w_attn, w_up, ff_bias, w_down, cotangent):
    rows, width = x.shape
    hidden = w_up.shape[2]
    held = (2 * hidden + width) // SLICES
    early = 2 * hidden // SLICES
    done = dense_call(
        crest_kernel, "crest",
        (query, kv, far, lang, x, w_attn, gain, bias, ff_bias, cotangent, w_up, w_down),
        [(0, None), (1, None), (2, None), (3, None), (4, None), (5, (1, 3))]
        + [(at, None) for at in range(6, 10)]
        + mlp_fetches(1, 10, 11, hidden),
        [((rows, width), BF), ((HEADS // 2, 8, rows), F32), ((rows, width), F32), ((rows, width), BF)]
        + part_shapes(PLAIN, held, width)
        + [((8, hidden), F32)],
        LONG,
        [
            pltpu.VMEM((SLICES, held, width), BF),
            pltpu.VMEM((KEYS, width), BF),
            pltpu.VMEM((KEYS, width), BF),
            pltpu.VMEM((KEYS, PAIR), BF),
            pltpu.VMEM((rows, PAIR), BF),
            pltpu.VMEM((2, KEYS, ROWS_UP), F32),
            pltpu.VMEM((2, 1, rows), F32),
            pltpu.VMEM((2, KEYS, ROWS_UP), BF),
            pltpu.SemaphoreType.DMA((2,)),
        ],
        flags,
        pieces={at: [(slice(None), slice(0, early)), (slice(None), slice(early, held))] for at in (4, 5)},
        lead=4,
        room=DENSE_VMEM,
        raw=[((HEADS, KEYS, ROWS_UP), BF)],
    )
    return (done[0], done[7], done[1], done[2], done[3], done[4:6], done[6])


def leave_grad(unit, scale, gain, grad, grad_query, grad_key, grad_value, w_qkv):
    grad_normed = mat_right(grad_query, w_qkv[0]) * 0.125
    grad_normed = grad_normed + mat_right(grad_key, w_qkv[1]) + mat_right(grad_value, w_qkv[2])
    grad_state, grad_gain, grad_bias = norm_back(grad_normed, unit, scale, gain)
    return (grad + grad_state, grad_gain, grad_bias)


def leave_kernel(flags, fetched, stores, sums, held):
    query, normed, kv, far, x, gain, w_qkv, grad = fetched[:8]
    out, keep, send, token = stores
    token[...] = jnp.zeros(token.buffer.shape, F32)
    grad_query, low = query[...], normed[...]
    width = low.shape[1]
    place = width // SLICES
    put_rows(held, 0, (mat_left(low, grad_query) * 0.125).astype(BF))
    sums[...] = kv[...].astype(F32)
    rows = pl.ds(pl.multiple_of((1 - flags[1]) * (ROWS - EDGE), 16), EDGE)
    sums[rows, :] += far[...].astype(F32)
    grad_key, grad_value = unmix(sums[...].astype(BF))
    unit, scale = centre(x[...].astype(F32))
    total, grad_gain, grad_bias = leave_grad(
        unit, scale, gain[0, 0:1], grad[...], grad_query, grad_key, grad_value, w_qkv
    )
    out[...] = total
    out.send()
    put_rows(held, place, mat_left(low, grad_key).astype(BF))
    put_rows(held, 2 * place, mat_left(low, grad_value).astype(BF))
    put_small(held, 3 * place, fetched[8:], grad_gain, grad_bias)
    hand_out(held, (keep, send), flags, LAST)


SMALL_ROWS = 32


def put_small(held, place, small, grad_gain, grad_bias):
    width = grad_gain.shape[1]
    rows = [grad_gain, small[0][1:2, :width], small[2][0:1, :width], small[1][1:2, :width]]
    rows += [grad_bias, small[0][1:2, width : 2 * width], small[2][0:1, width : 2 * width]]
    rows += [small[1][1:2, width : 2 * width]]
    rows += [small[at][1:2, 2 * width : 3 * width] for at in range(2)]
    block = jnp.concatenate(rows, axis=0)
    long = jnp.concatenate([small[at][0:1, :] for at in range(2)], axis=0)
    each, more = width // SLICES, long.shape[1] // SLICES
    for piece in range(SLICES):
        head = jnp.pad(block[:, piece * each : (piece + 1) * each], ((0, 0), (0, more - each)))
        tail = long[:, piece * more : (piece + 1) * more]
        rest = jnp.zeros((SMALL_ROWS - head.shape[0] - tail.shape[0], more), F32)
        both = jnp.concatenate([head, tail, rest], axis=0).astype(BF)
        held[piece, place : place + SMALL_ROWS, :] = jnp.pad(both, ((0, 0), (0, width - more)))


def leave(flags, x, gain, normed, grad, query, kv, far, w_attn, smalls, after):
    rows, width = x.shape
    held = 3 * (width // SLICES) + SMALL_ROWS
    done = dense_call(
        leave_kernel, "leave",
        (query, normed, kv, far, x, gain, w_attn, grad, *smalls),
        [(at, None) for at in range(6)] + [(6, (0, QKV))] + [(at, None) for at in range(7, 11)],
        [((rows, width), F32)] + part_shapes(LAST, held, width) + [((8, PAIR), F32)],
        4.0,
        [pltpu.VMEM((rows, 2 * width), F32), pltpu.VMEM((SLICES, held, width), BF)],
        flags,
        after,
        lead=8,
        room=30 * 2**20,
    )
    return (done[0], done[1:3], done[3])


def put_sums(klass, side, sums, lang_sums, kv, here, far, own, lone, there):
    @pl.when(klass == 1)
    def fine():
        sums[:, here] = (kv[:, here].astype(F32) + far[:ROWS, there].astype(F32)).astype(BF)

        @pl.when(side == 0)
        def owner():
            lang_sums[:LONE, here] = (lone[:, there].astype(F32) + far[ROWS:, there].astype(F32)).astype(BF)

    @pl.when(klass != 1)
    def coarse():
        sums[:, here] = kv[:, here]
        lang_sums[:, here] = own[:, there]


def descend_kernel(flags, fetched, stores, sums, lang_sums, plain, split):
    query, normed, x, kv = fetched[:4]
    fars, owns, lones = fetched[4:6], fetched[6:8], fetched[8:10]
    w_qkv, gain, grad, low_normed = fetched[10:14]
    mlp, (after, mixed, w_out, lang_normed, feats, language, w_lang) = fetched[14:-7], fetched[-7:]
    out_grad, out_mixed, grad_language, keep, send, split_keep, split_send, small, small_mid = stores
    klass, side = flags[0], flags[1]
    small[...] = jnp.zeros(small.buffer.shape, F32)
    small_mid[...] = jnp.zeros(small_mid.buffer.shape, F32)
    lang_sums[...] = jnp.zeros_like(lang_sums)
    grad_query, low = query[...], normed[...]
    width = low.shape[1]
    place = width // SLICES
    hidden = len(mlp) // 4 * CHUNK
    up_rows = hidden // SLICES
    put_rows(plain, up_rows, (mat_left(low, grad_query) * 0.125).astype(BF))
    unit, scale = centre(x[...])
    kv = kv.ref()
    fars, owns, lones = [[part.ref() for part in parts] for parts in (fars, owns, lones)]
    for pair in range(HEADS // 2):
        for which in range(2):
            there = slice(pair * PAIR, (pair + 1) * PAIR)
            here = slice((2 * pair + which) * PAIR, (2 * pair + which + 1) * PAIR)
            put_sums(klass, side, sums, lang_sums, kv, here, fars[which], owns[which], lones[which], there)

    grad_key, grad_value = unmix(sums[...])
    grad, grad_gain, grad_bias = leave_grad(
        unit, scale, gain[1, 0:1], grad[...], grad_query, grad_key, grad_value, w_qkv
    )
    lang_key, lang_value = unmix(lang_sums[...])
    lang_low = lang_normed[...]
    put_rows(plain, up_rows + place, (mat_left(low, grad_key) + mat_left(lang_low, lang_key)).astype(BF))
    put_rows(split, DOWN_ROWS, (mat_left(low, grad_value) + mat_left(lang_low, lang_value)).astype(BF))
    lang_grad = mat_right(lang_key, w_qkv[1]) + mat_right(lang_value, w_qkv[2])
    unit, scale = centre(feats[...])
    grad_feats, lang_gain, lang_bias = norm_back(lang_grad, unit, scale, gain[1, 0:1])
    feats_low = grad_feats.astype(BF)
    put_rows(split, DOWN_ROWS + place, mat_left(language[...], feats_low).astype(BF))
    grad_language[...] = mat_right(feats_low, w_lang[...])
    grad_language.send()
    small_mid[0:1, :width] = grad_gain + lang_gain
    small_mid[0:1, width : 2 * width] = grad_bias + lang_bias

    grad_low = grad.astype(BF)
    small[1:2, 2 * width : 3 * width] = jnp.sum(grad_low.astype(F32), axis=0, keepdims=True)
    low = low_normed[...]
    grad_normed = None
    for at, span in enumerate(chunks(hidden)):
        w_down, rise, w_up, active = [part[...] for part in mlp[4 * at : 4 * at + 4]]
        part = mlp_chunk(span, low, grad_low, rise.astype(F32), w_up, w_down, plain, small)
        put_down(split, span.start, 0, mat_left(active, grad_low).astype(BF))
        grad_normed = part if grad_normed is None else grad_normed + part
    hand_out(plain, (keep, send), flags, PLAIN)
    send.send()
    keep.send()
    unit, scale = centre(after[...])
    mlp_tail(
        0, grad, grad_normed, unit, scale, gain, mixed, w_out, split, DOWN_ROWS + 2 * place, out_grad, out_mixed, small
    )
    hand_out(split, (split_keep, split_send), flags, SPLIT)


def descend(
    flags, state, gain, normed, grad, query, kv, fars, owns, w_attn, feats, lang_normed, language, w_lang,
    after, mixed, low_normed, active, slope, w_up, w_down, follows,
):
    rows, width = state.shape
    hidden = w_up.shape[2]
    place = width // SLICES
    plain, split = hidden // SLICES + 2 * place, DOWN_ROWS + 3 * place
    fetches = []
    for span in chunks(hidden):
        fetches += [(13, (0, span)), (14, (slice(None), span)), (12, (0, slice(None), span)), (15, (slice(None), span))]
    head, foot = slice(0, LPAD), slice(ROWS, ROWS + LONE)
    done = dense_call(
        descend_kernel, "descend",
        (query, normed, state, kv, *fars, *owns, w_attn, gain, grad, low_normed)
        + (w_up, w_down, slope, active, after, mixed, lang_normed, feats, language, w_lang),
        [(at, None) for at in range(6)]
        + [(at, (head,)) for at in range(6, 8)]
        + [(at, (foot,)) for at in range(6, 8)]
        + [(8, (1, QKV)), (9, None), (10, None), (11, None)]
        + fetches
        + [(16, None), (17, None), (8, (0, 3)), (18, None), (19, None), (20, None), (21, None)],
        [((rows, width), F32), ((rows, width), BF), ((LPAD, width), F32)]
        + part_shapes(PLAIN, plain, width)
        + part_shapes(SPLIT, split, width)
        + [((8, hidden), F32), ((8, 2 * width), F32)],
        LONG,
        [
            pltpu.VMEM((rows, 2 * width), BF),
            pltpu.VMEM((LPAD, 2 * width), BF),
            pltpu.VMEM((SLICES, plain, width), BF),
            pltpu.VMEM((SLICES, split, width), BF),
        ],
        flags,
        follows,
        lead=6,
    )
    return (done[0], done[1], done[2], done[3:5], done[5:7], done[7], done[8])


def pair_swap(block):
    count = lax.axis_size("wide")
    return lax.ppermute(block, "wide", [(at, at ^ 1) for at in range(count)])


class Flow:
    def __init__(self, route, parts):
        self.route, self.step = route, 0
        self.units = route.units
        self.keep = [parts[0]]
        self.send(parts)

    def send(self, parts):
        self.got = []
        if self.step < len(self.route.steps):
            bits = self.route.steps[self.step]
            self.units //= 1 << len(bits)
            for at, part in enumerate(parts[1:], 1):
                found = [bit for place, bit in enumerate(bits) if at >> (len(bits) - 1 - place) & 1]
                self.got.append(self.move(part, found))
        else:
            self.keep = [parts[0]]
            self.got.append(self.move(parts[0], [0] if self.route.halves else None))

    def move(self, part, bits):
        shift = 1 if self.route.halves else 0
        if bits is None or bits == [0] and shift:
            return lax.ppermute(part, "narrow", [(0, 1), (1, 0)])
        count = lax.axis_size("wide")
        stride = sum((count // SLICES) << (bit - shift) for bit in bits)
        return lax.ppermute(part, "wide", [(p, p ^ stride) for p in range(count)])


def step_kernel(layout, ins, outs):
    at = 0
    for out, (count, rows) in zip(outs, layout):
        total = None
        for term in ins[at : at + count]:
            part = term[rows] if rows is not None else term[...]
            total = part.astype(F32) if total is None else total + part.astype(F32)
        out[...] = total.astype(BF)
        if isinstance(out, Store):
            out.send()
        at += count


def step(flows, after=(), near=False, cost=SHORT, lazy=False):
    operands, fetches, layout, outs, plan = [], [], [], [], []
    for flow in flows:
        flow.step += 1
        terms = flow.keep + flow.got
        last = flow.step == len(flow.route.steps)
        count = 1 if last else flow.route.parts(flow.step)
        each = flow.units // count
        made = [part for part in range(count) if part or last or not lazy]
        for part in reversed(made):
            rows = slice(part * each, (part + 1) * each)
            for term in terms:
                fetches.append((len(operands), rows))
                operands.append(term)
            layout.append((len(terms), rows))
            outs.append(((each,) + terms[0].shape[1:], BF))
        plan.append((flow, terms, count, made))
    if near:
        done = near_call(
            lambda *refs: step_kernel(layout, refs[: len(operands)], refs[len(operands) :]),
            "step", outs, operands, after=after, cost=cost,
        )
    else:
        done = dense_call(
            lambda ins, stores: step_kernel([(count, None) for count, rows in layout], ins, stores),
            "step", operands, fetches, outs, cost, after=after, lead=len(fetches), room=STEP_VMEM,
        )
    at = 0
    for flow, terms, count, made in plan:
        parts = [None] * count
        for part in reversed(made):
            parts[part] = done[at]
            at += 1
        flow.keep = terms if parts[0] is None else [parts[0]]
        flow.send(parts)
    return done


def split_low(buffer):
    count = lax.axis_size("wide")
    position = lax.axis_index("wide")
    half = count // SLICES
    while half > 1:
        half //= 2
        mine = position // half % 2
        size = buffer.shape[0] // 2
        send = lax.dynamic_slice_in_dim(buffer, (1 - mine) * size, size, 0)
        keep = lax.dynamic_slice_in_dim(buffer, mine * size, size, 0)
        buffer = keep + lax.ppermute(send.astype(BF), "wide", [(p, p ^ half) for p in range(count)])
    return buffer


def finish_kernel(
    flags, first, first_got, plain, plain_got, split, split_got, attn_one, attn_one_got,
    lang, attn, ups, downs, gains, biases, ff_biases, out_biases, whole, last,
):
    rows, width = attn.shape[2:]
    up_rows, down_rows = ups.shape[2] // width * rows, downs.shape[1]

    def both(buffer, got):
        return buffer[0].astype(F32) + got[0].astype(F32)

    def put_ups(layer, found):
        for at in range(ups.shape[2] // width):
            ups[layer, :, at * width : (at + 1) * width] = found[at * rows : (at + 1) * rows]

    found = both(first, first_got)
    put_ups(1, found)
    downs[1] = found[up_rows : up_rows + down_rows]
    attn[1, 3] = found[up_rows + down_rows :]
    found = both(plain, plain_got)
    put_ups(0, found)
    attn[1, 0] = found[up_rows : up_rows + rows]
    attn[1, 1] = found[up_rows + rows :]
    whole[flags[3]] = split[0].astype(F32)
    whole[1 - flags[3]] = split_got[0].astype(F32)
    found = jnp.concatenate([whole[0], whole[1]], axis=0)
    downs[0] = found[:down_rows]
    attn[1, 2] = found[down_rows : down_rows + rows]
    lang[...] = found[down_rows + rows : down_rows + 2 * rows]
    attn[0, 3] = found[down_rows + 2 * rows :]
    last[flags[3]] = attn_one[0].astype(F32)
    last[1 - flags[3]] = attn_one_got[0].astype(F32)
    found = jnp.concatenate([last[0], last[1]], axis=0)
    for at in range(3):
        attn[0, at] = found[at * rows : (at + 1) * rows]
    small = found[3 * rows :]
    for layer in range(2):
        gains[layer] = small[2 * layer : 2 * layer + 2, :rows]
        biases[layer] = small[4 + 2 * layer : 6 + 2 * layer, :rows]
    out_biases[...] = small[8:10, :rows]
    ff_biases[...] = small[10:12, : ff_biases.shape[1]]


def finish(flags, flows, width, hidden):
    rows = width // SLICES
    args = []
    for flow in flows:
        args += flow.keep + flow.got
    return near_call(
        finish_kernel, "finish",
        [
            ((rows, width), F32),
            ((2, 4, rows, width), F32),
            ((2, rows, hidden), F32),
            ((2, hidden // SLICES, width), F32),
            ((2, 2, rows), F32),
            ((2, 2, rows), F32),
            ((2, hidden // SLICES), F32),
            ((2, rows), F32),
        ],
        args,
        [
            pltpu.VMEM((2, (DOWN_ROWS + 3 * rows) // 2, width), F32),
            pltpu.VMEM((2, (3 * rows + SMALL_ROWS) // 2, width), F32),
        ],
        flags,
    )


def body(
    patches,
    language,
    w_lang,
    w_attn,
    w_up,
    w_down,
    norm_gain,
    norm_bias,
    ff_bias,
    out_bias,
    cotangent,
    classes,
):
    position = lax.axis_index("wide")
    wide = lax.axis_size("wide")
    side = position % 2
    klass = lax.dynamic_index_in_dim(classes[0], position // 2, 0, keepdims=False)
    high = position // (wide // SLICES)
    flags = jnp.stack([klass, side, high, lax.axis_index("narrow")]).astype(jnp.int32)
    width = w_lang.shape[0]
    hidden = w_up.shape[2]
    start = patches[0]
    lang_low = jnp.pad(language[0], ((0, LPAD - language.shape[1]), (0, 0)))

    other = pair_swap(start)
    normed_a, query_a, key_a, value_a, mixed_a, weights_a, share_a, *rest = climb(
        flags, start, other, norm_gain, norm_bias, w_attn, w_up, ff_bias, w_down, out_bias, lang_low, w_lang
    )
    after_a, normed_b, active_b, slope_b, state_b, normed_c, query_c, kv_c, feats, lang_normed, lang_kv = rest
    far_c = pair_swap(kv_c)
    mixed_c, weights_c, share_c, grad, grad_mixed_c, parts, small_two = crest(
        flags, query_c, kv_c, far_c, lang_kv, state_b, norm_gain, norm_bias, w_attn, w_up, ff_bias, w_down,
        cotangent[0],
    )
    first = Flow(PLAIN, parts)
    joint = (flags, query_c, kv_c, far_c, lang_kv, mixed_c, weights_c, share_c, grad_mixed_c)
    query, kv, *edges, token = joint_backward(*joint, 0, HEADS // 2)
    fars = [pair_swap(part) for part in edges]
    done = step([first], [token], lazy=True)
    grad, grad_mixed_a, grad_language, plain_parts, split_parts, small_one, small_mid = descend(
        flags, state_b, norm_gain, normed_c, grad, query, kv, fars, edges, w_attn, feats, lang_normed, lang_low,
        w_lang, after_a, mixed_a, normed_b, active_b, slope_b, w_up, w_down, done,
    )
    plain, split = Flow(PLAIN, plain_parts), Flow(SPLIT, split_parts)

    done = step([first], [small_mid], lazy=True, cost=30.0)
    done = step([plain, split], [done[0]])
    view = (flags, query_a, key_a, value_a, mixed_a, weights_a, share_a, grad_mixed_a)
    query, kv, edge, token = view_backward(*view, 0, HEADS // 2, done)
    far = pair_swap(edge)
    done = step([first], [token])
    grad, attn_parts, token = leave(
        flags, start, norm_gain, normed_a, grad, query, kv, far, w_attn, (small_one, small_two, small_mid), done
    )
    attn_one = Flow(LAST, attn_parts)

    done = step([plain, split], [token], near=True, cost=LONG)
    done = step([attn_one], [done[0]], near=True)
    done = step([first], [done[0]], near=True, cost=5.0)
    done = step([plain, split], [done[0]], near=True)
    done = step([attn_one], [done[0]], near=True)
    done = step([plain, split], [done[0], first.got[0]], near=True)
    done = step([attn_one], [done[0]], near=True)
    done = step([split], [done[0]], near=True)
    done = step([attn_one], [done[0], plain.got[0]], near=True)
    flows = (first, plain, split, attn_one)
    grad_w_lang, grad_w_attn, grad_w_up, grad_w_down, *vectors = finish(flags, flows, width, hidden)
    gains, biases, ff_biases, out_biases = vectors

    def own(values, dim):
        if wide == SLICES:
            return values
        values = jnp.moveaxis(values, dim, 0)
        return jnp.moveaxis(split_low(values), 0, dim)

    return (
        grad[None],
        grad_language[None, : language.shape[1]],
        own(grad_w_lang, 0),
        own(grad_w_attn, 2),
        own(grad_w_up, 1),
        own(grad_w_down, 1),
        own(gains, 2),
        own(biases, 2),
        own(ff_biases, 1),
        own(out_biases, 1),
    )


def solution(mesh):
    in_specs = (
        P("narrow", "wide", None),
        P("narrow", "wide", None),
        P(),
        P(),
        P(),
        P(),
        P(),
        P(),
        P(),
        P(),
        P("narrow", "wide", None),
        P("narrow", None),
    )
    out_specs = (
        P("narrow", "wide", None),
        P("narrow", "wide", None),
        P("wide", None),
        P(None, None, "wide", None),
        P(None, "wide", None),
        P(None, "wide", None),
        P(None, None, "wide"),
        P(None, None, "wide"),
        P(None, "wide"),
        P(None, "wide"),
    )
    return jax.shard_map(body, mesh=mesh, in_specs=in_specs, out_specs=out_specs, check_vma=False)
```

```python
import functools

import jax
import jax.numpy as jnp
from jax import lax
from jax.experimental import pallas as pl
from jax.experimental.pallas import tpu as pltpu
from jax.sharding import PartitionSpec as P

HEADS = 8
HD = 64
LANG = 77
VB = 288
VS = 72
ROWS = 720
EDGE = VB // 2
PADDED = ROWS + EDGE
LPAD = 160
LONE = 96
KEYS = 2 * ROWS + LONE
PAIR = 2 * HD
SLICES = 16
ROWS_UP = 768
VB_UP = 384
STEP_VMEM = 20 * 2**20
LONG, SHORT = 60.0, 0.5
JOINT_VMEM = 60 * 2**20
JOINT_BACK_VMEM = 60 * 2**20
VIEW_VMEM = 36 * 2**20
DENSE_VMEM = 60 * 2**20
NEAR_VMEM = 16 * 2**20

epsilon = 1e-05
masked_out = -1e30
BF = jnp.bfloat16
F32 = jnp.float32


def matmul(left, right):
    return jnp.dot(left, right, preferred_element_type=F32)


def mat_left(left, right):
    return lax.dot_general(left, right, (((0,), (0,)), ((), ())), preferred_element_type=F32)


def mat_right(left, right):
    return lax.dot_general(left, right, (((1,), (1,)), ((), ())), preferred_element_type=F32)


def cost_of(microseconds):
    return pl.CostEstimate(flops=int(microseconds * 1e9), bytes_accessed=1, transcendentals=0)


def waiting(kernel, inputs, more):
    if not more:
        return kernel

    def without(*refs):
        return kernel(*refs[:inputs], *refs[inputs + more :])

    return without


def lane_mask(head):
    lanes = lax.broadcasted_iota(jnp.int32, (1, PAIR), 1)
    return jnp.where(lanes // HD == head, 1.0, 0.0).astype(BF)


def in_half(shape):
    return lax.broadcasted_iota(jnp.int32, shape, 1) % HD


def row_of(shape):
    return lax.broadcasted_iota(jnp.int32, shape, 0)


def key_marks(allowed, items):
    lane = in_half(allowed.shape)
    marks = jnp.where(lane < items, jnp.where(allowed, 0.0, masked_out), 0.0)
    return jnp.where((lane >= 4) & (lane < 7), 1.0, marks).astype(BF)


def joint_key_marks(klass):
    shape = (KEYS, PAIR)
    row, lane = row_of(shape), in_half(shape)
    first = (row < ROWS // 2) | ((row >= ROWS) & (row < ROWS + LANG))
    second = ((row >= ROWS // 2) & (row < ROWS)) | ((row >= ROWS + LANG) & (row < ROWS + 2 * LANG))
    fine = jnp.where(row < 2 * ROWS + LANG, 1, 0)
    coarse = jnp.where(lane == 0, jnp.where(first, 1, 0), jnp.where(second, 1, 0))
    return key_marks(jnp.where(klass == 1, fine, coarse) == 1, 2)


def joint_row_marks():
    shape = (ROWS, PAIR)
    row, lane = row_of(shape), in_half(shape)
    return jnp.where(lane == row // (ROWS // 2), 1.0, 0.0).astype(BF)


def view_key_marks(klass):
    shape = (PADDED, PAIR)
    row, lane = row_of(shape), in_half(shape)
    same = jnp.where(lane == row % VB // VS, 1, 0)
    return key_marks(jnp.where(klass == 1, 1, same) == 1, 4)


def view_row_marks():
    shape = (PADDED, PAIR)
    row, lane = row_of(shape), in_half(shape)
    return jnp.where(lane == row % VB // VS, 1.0, 0.0).astype(BF)


def with_parts(values):
    lane = in_half(values.shape)
    high = values.astype(BF).astype(F32)
    rest = values - high
    middle = rest.astype(BF).astype(F32)
    low = rest - middle
    picked = jnp.where(lane == 4, -high, jnp.where(lane == 5, -middle, jnp.where(lane == 6, -low, 0.0)))
    return picked.astype(BF)


def attend_heads(units):
    scores = [mat_right(keys, right) for right, keys, across in units]
    weights = [jnp.exp(part - jnp.max(part, axis=0, keepdims=True)).astype(BF) for part in scores]
    outs = [matmul(unit[2], part) for unit, part in zip(units, weights)]
    shares = [1.0 / out[HD : HD + 1] for out in outs]
    return [(part, out[:HD] * share, share) for part, out, share in zip(weights, outs, shares)]


def score_side(query, marks, head):
    mask = lane_mask(head)
    return jnp.concatenate([query * mask, marks * mask], axis=1)


def joint_place(klass, side, kv_ref, far_ref, lang_ref, put):
    put(slice(0, ROWS), kv_ref[:ROWS])

    @pl.when(klass == 1)
    def fine():
        put(slice(ROWS, 2 * ROWS), far_ref[:ROWS])

        @pl.when(side == 0)
        def own():
            put(slice(2 * ROWS, KEYS), lang_ref[:LONE])

        @pl.when(side == 1)
        def partner():
            put(slice(2 * ROWS, KEYS), far_ref[ROWS:])

    @pl.when(klass != 1)
    def coarse():
        put(slice(ROWS, ROWS + LPAD), lang_ref[...])


def inner_marks(grad, mixed):
    lanes = lax.broadcasted_iota(jnp.int32, (1, PAIR), 1)
    product = grad.astype(F32) * mixed.astype(F32)
    first = jnp.sum(jnp.where(lanes < HD, product, 0.0), axis=1, keepdims=True)
    second = jnp.sum(jnp.where(lanes < HD, 0.0, product), axis=1, keepdims=True)
    return with_parts(jnp.where(lanes < HD, first, second))


def attend_back(units):
    inner = [mat_right(unit[0], unit[5]) for unit in units]
    probs = [unit[2].astype(F32) * unit[3] for unit in units]
    grad_scores = [(left * right).astype(BF) for left, right in zip(probs, inner)]
    grad_values = [matmul(part.astype(BF), unit[5][:, :PAIR]) for part, unit in zip(probs, units)]
    grad_keys = [matmul(part, unit[4]) for part, unit in zip(grad_scores, units)]
    across = [matmul(unit[1], part) for part, unit in zip(grad_scores, units)]
    return list(zip(grad_keys, grad_values, across))


def fill_rows(left, grads, rows, query, grad, mixed):
    inner = inner_marks(grad, mixed)
    for head in range(2):
        mask = lane_mask(head)
        left[head, rows, :] = query * mask
        grads[head, rows, :PAIR] = grad * mask
        grads[head, rows, PAIR:] = inner * mask


def joint_backward_kernel(
    flags, q_ref, kv_ref, far_ref, lang_ref, mixed_ref, weights_ref, share_ref, grad_ref, dq_ref, dkv_ref,
    dfar_key, dfar_value, token, keys, values, across, left, grads,
):
    klass, side = flags[0], flags[1]

    @pl.when(pl.program_id(0) == 0)
    def prepare():
        keys[...] = jnp.zeros_like(keys)
        values[...] = jnp.zeros_like(values)
        values[:, PAIR:] = joint_key_marks(klass)

    def put(rows, block):
        keys[rows, :] = block[:, :PAIR]
        values[rows, :PAIR] = block[:, PAIR:]

    joint_place(klass, side, kv_ref, far_ref, lang_ref, put)
    token[...] = jnp.zeros_like(token)
    across[...] = keys[...].T
    fill_rows(left, grads, slice(0, ROWS), q_ref[...], grad_ref[...], mixed_ref[...])
    units = [
        (
            values[...],
            across[head * HD : (head + 1) * HD, :],
            weights_ref[head, :, :ROWS],
            share_ref[0, head : head + 1, :],
            left[head],
            grads[head],
        )
        for head in range(2)
    ]
    first, second = attend_back(units)
    for span, at, far in ((slice(0, PAIR), 0, dfar_key), (slice(PAIR, 2 * PAIR), 1, dfar_value)):
        both = (first[at] + second[at]).astype(BF)
        dkv_ref[:, span] = both[:ROWS]
        far[...] = both[ROWS:]
    dq_ref[...] = jnp.concatenate([first[2], second[2]], axis=0).T.astype(BF)


def joint_backward(flags, query, kv, far, lang, mixed, weights, share, grad, base, pairs, after=(), cost=LONG):
    rows = query.shape[0]
    one = pl.BlockSpec((rows, PAIR), lambda i, f: (0, i + base))
    return pl.pallas_call(
        waiting(joint_backward_kernel, 9, len(after)),
        grid_spec=pltpu.PrefetchScalarGridSpec(
            num_scalar_prefetch=1,
            grid=(pairs,),
            in_specs=[
                one,
                pl.BlockSpec((rows, 2 * PAIR), lambda i, f: (0, i + base)),
                pl.BlockSpec((ROWS + LONE, 2 * PAIR), lambda i, f: (0, i + base)),
                pl.BlockSpec((LPAD, 2 * PAIR), lambda i, f: (0, i + base)),
                one,
                pl.BlockSpec((2, KEYS, ROWS_UP), lambda i, f: (i + base, 0, 0)),
                pl.BlockSpec((1, 8, rows), lambda i, f: (i + base, 0, 0)),
                one,
            ]
            + [pl.BlockSpec(memory_space=pltpu.HBM)] * len(after),
            out_specs=[
                pl.BlockSpec((rows, PAIR), lambda i, f: (0, i)),
                pl.BlockSpec((rows, 2 * PAIR), lambda i, f: (0, i)),
                pl.BlockSpec((ROWS + LONE, PAIR), lambda i, f: (0, i)),
                pl.BlockSpec((ROWS + LONE, PAIR), lambda i, f: (0, i)),
                pl.BlockSpec((8, PAIR), lambda i, f: (0, 0)),
            ],
            scratch_shapes=[
                pltpu.VMEM((KEYS, PAIR), BF),
                pltpu.VMEM((KEYS, 2 * PAIR), BF),
                pltpu.VMEM((PAIR, KEYS), BF),
                pltpu.VMEM((2, ROWS, PAIR), BF),
                pltpu.VMEM((2, ROWS, 2 * PAIR), BF),
            ],
        ),
        out_shape=[
            jax.ShapeDtypeStruct((rows, pairs * PAIR), BF),
            jax.ShapeDtypeStruct((rows, 2 * pairs * PAIR), BF),
            jax.ShapeDtypeStruct((ROWS + LONE, pairs * PAIR), BF),
            jax.ShapeDtypeStruct((ROWS + LONE, pairs * PAIR), BF),
            jax.ShapeDtypeStruct((8, PAIR), F32),
        ],
        compiler_params=pltpu.CompilerParams(vmem_limit_bytes=JOINT_BACK_VMEM),
        cost_estimate=cost_of(cost),
        name="joint_backward",
    )(flags, query, kv, far, lang, mixed, weights, share, grad, *after)


def view_spots(side):
    own = pl.ds(pl.multiple_of(side * EDGE, 16), ROWS)
    far = pl.ds(pl.multiple_of((1 - side) * ROWS, 16), EDGE)
    return (own, far)


def view_backward_kernel(
    flags, q_ref, key_ref, value_ref, mixed_ref, weights_ref, share_ref, grad_ref, dq_ref, dkv_ref, dfar_ref,
    token, values, left, grads, back, dkv,
):
    klass, side = flags[0], flags[1]
    own, far = view_spots(side)

    @pl.when(pl.program_id(0) == 0)
    def prepare():
        for p in range(2):
            values[p, :, PAIR:] = view_key_marks(klass)
        left[...] = jnp.zeros_like(left)
        grads[...] = jnp.zeros_like(grads)

    units = []
    for p in range(2):
        lanes = slice(p * PAIR, (p + 1) * PAIR)
        values[p, :, :PAIR] = value_ref[:, lanes]
        fill_rows(left.at[p], grads.at[p], own, q_ref[own, lanes], grad_ref[:, lanes], mixed_ref[:, lanes])
    for p in range(2):
        lanes = slice(p * PAIR, (p + 1) * PAIR)
        for index in range(PADDED // VB):
            rows = slice(index * VB, (index + 1) * VB)
            across = key_ref[rows, lanes].T
            for head in range(2):
                units.append(
                    (
                        values[p, rows, :],
                        across[head * HD : (head + 1) * HD, :],
                        weights_ref[index, 2 * p + head, :, :VB],
                        share_ref[index, p, head : head + 1, :],
                        left[p, head, rows, :],
                        grads[p, head, rows, :],
                    )
                )
    done = attend_back(units)
    for p in range(2):
        for index in range(PADDED // VB):
            rows = slice(index * VB, (index + 1) * VB)
            at = 2 * (p * (PADDED // VB) + index)
            first, second = done[at], done[at + 1]
            dkv[rows, 2 * p * PAIR : (2 * p + 1) * PAIR] = (first[0] + second[0]).astype(BF)
            dkv[rows, (2 * p + 1) * PAIR : (2 * p + 2) * PAIR] = (first[1] + second[1]).astype(BF)
            back[rows, p * PAIR : (p + 1) * PAIR] = jnp.concatenate([first[2], second[2]], axis=0).T.astype(BF)

    dq_ref[...] = back[own, :]
    dkv_ref[...] = dkv[own, :]
    dfar_ref[...] = dkv[far, :]
    token[...] = jnp.zeros_like(token)


def view_backward(flags, query, key, value, mixed, weights, share, grad, base, pairs, after=(), cost=LONG):
    rows = mixed.shape[0]
    blocks = PADDED // VB
    one = pl.BlockSpec((rows, 2 * PAIR), lambda i, f: (0, i + base))
    tall = pl.BlockSpec((PADDED, 2 * PAIR), lambda i, f: (0, i + base))
    return pl.pallas_call(
        waiting(view_backward_kernel, 8, len(after)),
        grid_spec=pltpu.PrefetchScalarGridSpec(
            num_scalar_prefetch=1,
            grid=(pairs // 2,),
            in_specs=[
                tall,
                tall,
                tall,
                one,
                pl.BlockSpec((blocks, 4, VB, VB_UP), lambda i, f: (0, i + base, 0, 0)),
                pl.BlockSpec((blocks, 2, 8, VB), lambda i, f: (0, i + base, 0, 0)),
                one,
            ]
            + [pl.BlockSpec(memory_space=pltpu.HBM)] * len(after),
            out_specs=[
                pl.BlockSpec((rows, 2 * PAIR), lambda i, f: (0, i)),
                pl.BlockSpec((rows, 4 * PAIR), lambda i, f: (0, i)),
                pl.BlockSpec((EDGE, 4 * PAIR), lambda i, f: (0, i)),
                pl.BlockSpec((8, PAIR), lambda i, f: (0, 0)),
            ],
            scratch_shapes=[
                pltpu.VMEM((2, PADDED, 2 * PAIR), BF),
                pltpu.VMEM((2, 2, PADDED, PAIR), BF),
                pltpu.VMEM((2, 2, PADDED, 2 * PAIR), BF),
                pltpu.VMEM((PADDED, 2 * PAIR), BF),
                pltpu.VMEM((PADDED, 4 * PAIR), BF),
            ],
        ),
        out_shape=[
            jax.ShapeDtypeStruct((rows, pairs * PAIR), BF),
            jax.ShapeDtypeStruct((rows, 2 * pairs * PAIR), BF),
            jax.ShapeDtypeStruct((EDGE, 2 * pairs * PAIR), BF),
            jax.ShapeDtypeStruct((8, PAIR), F32),
        ],
        compiler_params=pltpu.CompilerParams(vmem_limit_bytes=VIEW_VMEM),
        cost_estimate=cost_of(cost),
        name="view_backward",
    )(flags, query, key, value, mixed, weights, share, grad, *after)


CHUNK = 512
DOWN_ROWS = 128
BITS = SLICES.bit_length() - 1


class Route:
    def __init__(self, steps, halves):
        self.steps = steps
        self.halves = halves
        self.order = [bit for step in steps for bit in step]
        self.units = 1 << len(self.order)

    def unit(self, position):
        last = len(self.order) - 1
        return sum((position >> (last - at) & 1) << bit for at, bit in enumerate(self.order))

    def parts(self, step):
        return 1 << len(self.steps[step])

    def rows(self, rows):
        return rows // 2 if self.halves else rows


PLAIN = Route(((0,), (1,), (2,), (3,)), False)
SPLIT = Route(((1,), (0,), (2,), (3,), (4,)), True)
LAST = Route(((1,), (0,), (2,), (3, 4)), True)


def hand_out(held, parts, flags, route, span=slice(None)):
    each = route.units // len(parts)
    rows = route.rows(held.shape[1])
    for position in range(route.units):
        if route.halves:
            unit = jnp.bitwise_xor(route.unit(position), flags[2] * 2 + flags[3])
            block = held[unit // 2, pl.ds(pl.multiple_of(unit % 2 * rows, 16), rows), :]
        else:
            block = held[jnp.bitwise_xor(route.unit(position), flags[2]), span]
        parts[position // each][position % each, span] = block


def part_shapes(route, rows, width):
    each = route.units // route.parts(0)
    return [((each, route.rows(rows), width), BF)] * route.parts(0)


def centre(values):
    mean = jnp.mean(values, axis=-1, keepdims=True)
    centered = values - mean
    variance = jnp.mean(centered * centered, axis=-1, keepdims=True)
    scale = lax.rsqrt(variance + epsilon)
    return (centered * scale, scale)


def norm_back(grad, unit, scale, gain):
    grad_gain = jnp.sum(grad * unit, axis=0, keepdims=True)
    grad_bias = jnp.sum(grad, axis=0, keepdims=True)
    scaled = grad * gain
    level = jnp.mean(scaled, axis=-1, keepdims=True)
    along = jnp.mean(scaled * unit, axis=-1, keepdims=True)
    return ((scaled - level - unit * along) * scale, grad_gain, grad_bias)


def gelu_both(hidden):
    root, cubic = 0.7978845608028654, 0.044715
    square = hidden * hidden
    bend = jnp.tanh(hidden * (root + (root * cubic) * square))
    half = 0.5 + 0.5 * bend
    slope = (0.5 * hidden) * (1.0 - bend * bend) * (root + (3.0 * root * cubic) * square)
    return (hidden * half, half + slope)


def mix(keys, values):
    parts = []
    for at in range(0, keys.shape[1], PAIR):
        parts += [keys[:, at : at + PAIR], values[:, at : at + PAIR]]
    return jnp.concatenate(parts, axis=1)


def unmix(both):
    blocks = [both[:, at : at + PAIR] for at in range(0, both.shape[1], PAIR)]
    return (jnp.concatenate(blocks[0::2], axis=1), jnp.concatenate(blocks[1::2], axis=1))


class Fetch:
    def __init__(self, source, buffer, semaphore, more):
        self.copy = pltpu.make_async_copy(source, buffer, semaphore)
        self.buffer, self.more, self.here = buffer, more, False

    def ref(self):
        if not self.here:
            self.more(0, self)
            self.copy.wait()
            self.here = True
            self.more(2)
        return self.buffer

    def __getitem__(self, index):
        return self.ref()[index]


class Store:
    def __init__(self, buffer, target, semaphores, pieces):
        self.buffer, self.copies, self.gone = buffer, [], []
        for at, piece in enumerate(pieces):
            source = buffer if piece is None else buffer.at[piece]
            place = target if piece is None else target.at[piece]
            self.copies.append(pltpu.make_async_copy(source, place, semaphores.at[at]))
            self.gone.append(False)

    def __setitem__(self, index, value):
        self.buffer[index] = value

    def __getitem__(self, index):
        return self.buffer[index]

    def send(self, at=None):
        for place, copy in enumerate(self.copies):
            if not self.gone[place] and at in (None, place):
                copy.start()
                self.gone[place] = True


LEAD = 4
QKV = slice(0, 3)


def dense_call(kernel, name, operands, fetches, outs, cost, scratch=(), flags=None, after=(), pieces=None, lead=LEAD, room=DENSE_VMEM, raw=()):
    shapes = [
        jax.eval_shape(lambda array, index=index: array[:EDGE] if callable(index) else array[index or ...], operands[at])
        for at, index in fetches
    ]
    count, first = len(operands), 0 if flags is None else 1
    pieces = [(pieces or {}).get(at, (None,)) for at in range(len(outs))]

    def run(*refs):
        inputs = refs[first : first + count]
        rest = refs[first + count + len(after) :]
        targets, rest = rest[: len(outs)], rest[len(outs) :]
        straight, rest = rest[: len(raw)], rest[len(raw) :]
        buffers, rest = rest[: len(fetches)], rest[len(fetches) :]
        held, rest = rest[: len(outs)], rest[len(outs) :]
        came, went, own = rest[0], rest[1 : 1 + len(outs)], rest[1 + len(outs) :]
        fetched, started = [], [0]

        def more(number, wanted=None):
            if wanted is not None:
                number = fetched.index(wanted) + 1 - started[0]
            for fetch in fetched[started[0] : started[0] + max(number, 0)]:
                fetch.copy.start()
            started[0] += max(number, 0)

        for place, (at, index) in enumerate(fetches):
            index = index(refs[0]) if callable(index) else index
            source = inputs[at] if index is None else inputs[at].at[index]
            fetched.append(Fetch(source, buffers[place], came.at[place], more))
        more(lead)
        stores = [Store(*parts) for parts in zip(held, targets, went, pieces)]
        kernel(*([refs[0]] if first else []), fetched, stores, *straight, *own)
        for fetch in fetched:
            fetch.ref()
        for store in stores:
            store.send()
        for store in stores:
            for copy in store.copies:
                copy.wait()

    anywhere = pl.BlockSpec(memory_space=pl.ANY)
    return pl.pallas_call(
        run,
        in_specs=[pl.BlockSpec(memory_space=pltpu.SMEM)] * first
        + [anywhere] * count
        + [pl.BlockSpec(memory_space=pltpu.HBM)] * len(after),
        out_specs=[anywhere] * (len(outs) + len(raw)),
        out_shape=[jax.ShapeDtypeStruct(shape, kind) for shape, kind in (*outs, *raw)],
        scratch_shapes=[pltpu.VMEM(part.shape, part.dtype) for part in shapes]
        + [pltpu.VMEM(shape, kind) for shape, kind in outs]
        + [pltpu.SemaphoreType.DMA((len(fetches),))]
        + [pltpu.SemaphoreType.DMA((len(piece),)) for piece in pieces]
        + list(scratch),
        compiler_params=pltpu.CompilerParams(vmem_limit_bytes=room),
        cost_estimate=cost_of(cost),
        name=name,
    )(*([flags] if first else []), *operands, *after)


def near_call(kernel, name, outs, args, scratch=(), flags=None, after=(), cost=SHORT):
    vmem = pl.BlockSpec(memory_space=pltpu.VMEM)
    specs = [vmem] * len(args)
    if flags is not None:
        specs = [pl.BlockSpec(memory_space=pltpu.SMEM)] + specs
        args = [flags] + list(args)
    return pl.pallas_call(
        waiting(kernel, len(args), len(after)),
        in_specs=specs + [pl.BlockSpec(memory_space=pl.ANY)] * len(after),
        out_specs=[vmem] * len(outs),
        out_shape=[jax.ShapeDtypeStruct(shape, kind) for shape, kind in outs],
        scratch_shapes=list(scratch),
        compiler_params=pltpu.CompilerParams(vmem_limit_bytes=NEAR_VMEM),
        cost_estimate=cost_of(cost),
        name=name,
    )(*args, *after)


QKV = slice(0, 3)


def chunks(hidden):
    return [slice(at, at + CHUNK) for at in range(0, hidden, CHUNK)]


def wide_pieces(hidden):
    return [(slice(None), span) for span in chunks(hidden)]


def mlp_fetches(layer, up_at, down_at, hidden):
    found = []
    for span in chunks(hidden):
        found += [(up_at, (layer, slice(None), span)), (down_at, (layer, span))]
    return found


def attend_views(pairs, query, key, value, row_marks, key_marks, weights, share, mixed):
    places = [(p, index) for p in pairs for index in range(PADDED // VB)]
    units = []
    for p, index in places:
        lanes = pl.ds(pl.multiple_of(p * PAIR, PAIR), PAIR)
        rows = slice(index * VB, (index + 1) * VB)
        keys = jnp.concatenate([key[rows, lanes], key_marks[rows, :]], axis=1)
        turned = value[rows, lanes].T
        for head in range(2):
            across = jnp.concatenate([turned[head * HD : (head + 1) * HD], jnp.ones((16, VB), BF)], axis=0)
            units.append((score_side(query[rows, lanes], row_marks[rows, :], head), keys, across))
    done = attend_heads(units)
    for at, (p, index) in enumerate(places):
        lanes = pl.ds(pl.multiple_of(p * PAIR, PAIR), PAIR)
        rows = slice(index * VB, (index + 1) * VB)
        for head in range(2):
            weights[index, 2 * p + head, :, :VB] = done[2 * at + head][0]
            share[index, p, head : head + 1, :] = done[2 * at + head][2]
        pair = [done[2 * at + head][1] for head in range(2)]
        mixed[rows, lanes] = jnp.concatenate(pair, axis=0).T.astype(BF)


def climb_kernel(flags, fetched, stores, rows_all, mixed_all, row_marks, key_marks):
    x, edge, gain, bias, w_first, w_out, ff_bias, out_bias = fetched[:8]
    mlp, (language, w_lang, w_qkv) = fetched[8:-3], fetched[-3:]
    first, rest = stores[:7], stores[7:]
    normed_one, query_all, key_all, value_all, mixed, weights, share = first
    after, normed, active, slope, state, next_normed, query, kv, feats, lang_normed, lang_kv = rest
    klass, side = flags[0], flags[1]
    own, far = view_spots(side)
    rows_all[own, :] = x[...]
    rows_all[far, :] = edge[...]
    row_marks[...] = view_row_marks()
    key_marks[...] = view_key_marks(klass)
    unit, scale = centre(rows_all[...].astype(F32))
    low = (unit * gain[0, 0:1] + bias[0, 0:1]).astype(BF)
    key_all[...] = matmul(low, w_first[1]).astype(BF)
    key_all.send()
    value_all[...] = matmul(low, w_first[2]).astype(BF)
    value_all.send()
    query_all[...] = (matmul(low, w_first[0]) * 0.125).astype(BF)
    query_all.send()
    rows_all[...] = low
    normed_one[...] = rows_all[own, :]
    normed_one.send()

    def pair(p, carry):
        attend_views(
            (2 * p, 2 * p + 1), query_all.buffer, key_all.buffer, value_all.buffer, row_marks, key_marks, weights.buffer,
            share.buffer, mixed_all,
        )
        return carry

    lax.fori_loop(0, HEADS // 4, pair, 0)
    weights.send()
    share.send()
    mixed[...] = mixed_all[own, :]
    mixed.send()

    total = x[...].astype(F32) + matmul(mixed[...], w_out[...])
    after[...] = total
    after.send()
    unit, scale = centre(total)
    low = (unit * gain[0, 1:2] + bias[0, 1:2]).astype(BF)
    normed[...] = low
    normed.send()
    total = total + out_bias[0:1, :]
    for at in range(0, len(mlp), 2):
        span = slice(at // 2 * CHUNK, (at // 2 + 1) * CHUNK)
        grown, rise = gelu_both(matmul(low, mlp[at][...]) + ff_bias[0:1, span])
        grown = grown.astype(BF)
        active[:, span] = grown
        active.send(at // 2)
        slope[:, span] = rise.astype(BF)
        slope.send(at // 2)
        total = total + matmul(grown, mlp[at + 1][...])
    found = matmul(language[...], w_lang[...])
    feats[...] = found
    feats.send()
    unit, scale = centre(found)
    low = (unit * gain[1, 0:1] + bias[1, 0:1]).astype(BF)
    lang_normed[...] = low
    lang_normed.send()
    both = mix(matmul(low, w_qkv[1]).astype(BF), matmul(low, w_qkv[2]).astype(BF))
    lang_kv[...] = both
    lang_kv.send()
    kv[ROWS:] = both[:LONE]
    state[...] = total
    state.send()
    unit, scale = centre(total)
    low = (unit * gain[1, 0:1] + bias[1, 0:1]).astype(BF)
    next_normed[...] = low
    next_normed.send()
    kv[:ROWS] = mix(matmul(low, w_qkv[1]).astype(BF), matmul(low, w_qkv[2]).astype(BF))
    kv.send()
    query[...] = (matmul(low, w_qkv[0]) * 0.125).astype(BF)


def far_rows(flags):
    return (pl.ds(pl.multiple_of(flags[1] * (ROWS - EDGE), 16), EDGE),)


def climb(flags, x, edge, gain, bias, w_attn, w_up, ff_bias, w_down, out_bias, language, w_lang):
    rows, width = x.shape
    hidden = w_up.shape[2]
    blocks = PADDED // VB
    return dense_call(
        climb_kernel,
        "climb",
        (x, edge, gain, bias, w_attn, ff_bias, out_bias, w_up, w_down, language, w_lang),
        [(0, None), (1, far_rows), (2, None), (3, None), (4, (0, QKV)), (4, (0, 3)), (5, None), (6, None)]
        + mlp_fetches(0, 7, 8, hidden)
        + [(9, None), (10, None), (4, (1, QKV))],
        [
            ((rows, width), BF),
            ((PADDED, width), BF),
            ((PADDED, width), BF),
            ((PADDED, width), BF),
            ((rows, width), BF),
            ((blocks, HEADS, VB, VB_UP), BF),
            ((blocks, HEADS // 2, 8, VB), F32),
            ((rows, width), F32),
            ((rows, width), BF),
            ((rows, hidden), BF),
            ((rows, hidden), BF),
            ((rows, width), F32),
            ((rows, width), BF),
            ((rows, width), BF),
            ((rows + LONE, 2 * width), BF),
            ((LPAD, width), F32),
            ((LPAD, width), BF),
            ((LPAD, 2 * width), BF),
        ],
        LONG,
        [
            pltpu.VMEM((PADDED, width), BF),
            pltpu.VMEM((PADDED, width), BF),
            pltpu.VMEM((PADDED, PAIR), BF),
            pltpu.VMEM((PADDED, PAIR), BF),
        ],
        flags,
        pieces={9: wide_pieces(hidden), 10: wide_pieces(hidden)},
        lead=5,
        room=DENSE_VMEM,
    )


def put_up(held, at, grad):
    rows = grad.shape[0] // SLICES
    put_rows(held, at // CHUNK * rows, grad)


def put_down(held, at, start, grad):
    rows = DOWN_ROWS
    for piece in range(grad.shape[0] // rows):
        held[at // rows + piece, start : start + rows, :] = grad[piece * rows : (piece + 1) * rows]


def put_rows(held, place, grad):
    rows = grad.shape[0] // SLICES
    for piece in range(SLICES):
        held[piece, place : place + rows, :] = grad[piece * rows : (piece + 1) * rows]


def mlp_tail(layer, grad, grad_normed, unit, scale, gain, mixed, w_out, ups, place, out_grad, out_mixed, small):
    width = unit.shape[1]
    grad_state, grad_gain, grad_bias = norm_back(grad_normed, unit, scale, gain[layer, 1:2])
    grad = grad + grad_state
    out_grad[...] = grad
    out_grad.send()
    small[1:2, :width] = grad_gain
    small[1:2, width : 2 * width] = grad_bias
    low = grad.astype(BF)
    put_rows(ups, place, mat_left(mixed[...], low).astype(BF))
    out_mixed[...] = mat_right(low, w_out[...]).astype(BF)
    out_mixed.send()


def mlp_chunk(span, low, grad_low, slope, w_up, w_down, ups, small):
    grad_hidden = slope * mat_right(grad_low, w_down)
    hidden_low = grad_hidden.astype(BF)
    put_up(ups, span.start, mat_left(low, hidden_low).astype(BF))
    small[0:1, span] = jnp.sum(hidden_low.astype(F32), axis=0, keepdims=True)
    return mat_right(hidden_low, w_up)


def joint_scores(query, marks, keys, key_marks, p, head):
    lanes = pl.ds(pl.multiple_of(p * PAIR, PAIR), PAIR)
    return mat_right(
        jnp.concatenate([keys[:, lanes], key_marks[...]], axis=1), score_side(query[:, lanes], marks[...], head)
    )


def crest_kernel(
    flags, fetched, stores, probs, weights, keys, values, key_marks, marks, scores, peaks, held, copied
):
    query, kv, far, lang, x, w_out, gain, bias, ff_bias, cotangent = fetched[:10]
    mlp = fetched[10:]
    mixed, share, out_grad, out_mixed, keep, send, small, outs = stores
    klass, side = flags[0], flags[1]
    query, kv, far, lang = query.ref(), kv.ref(), far.ref(), lang.ref()
    x.more(len(fetched))

    @pl.when(klass != 1)
    def empty():
        keys[ROWS:] = jnp.zeros((KEYS - ROWS, keys.shape[1]), BF)
        values[ROWS:] = jnp.zeros((KEYS - ROWS, values.shape[1]), BF)

    key_marks[...] = joint_key_marks(klass)
    marks[...] = joint_row_marks()

    def put(rows, block):
        for p in range(HEADS // 2):
            lanes = slice(p * PAIR, (p + 1) * PAIR)
            keys[rows, lanes] = block[:, 2 * p * PAIR : (2 * p + 1) * PAIR]
            values[rows, lanes] = block[:, (2 * p + 1) * PAIR : (2 * p + 2) * PAIR]

    joint_place(klass, side, kv, far, lang, put)

    def copy_out(p, head):
        return pltpu.make_async_copy(held.at[head], probs.at[2 * p + head], copied.at[head])

    def one(p, head, turned):
        across = jnp.concatenate([turned[head * HD : (head + 1) * HD], jnp.ones((16, KEYS), BF)], axis=0)
        found = jnp.exp(scores[head, :, :ROWS] - peaks[head]).astype(BF)
        held[head, :, :ROWS] = found
        copy_out(p, head).start()
        out = matmul(across, found)
        part = 1.0 / out[HD : HD + 1]
        share[p, head : head + 1, :] = part
        return out[:HD] * part

    for head in range(2):
        copy_out(0, head).start()
    def form(p, head):
        found = joint_scores(query, marks, keys, key_marks, p, head)
        scores[head, :, :ROWS] = found
        peaks[head] = jnp.max(found, axis=0, keepdims=True)

    form(0, 0)

    def pair(p, carry):
        lanes = pl.ds(pl.multiple_of(p * PAIR, PAIR), PAIR)
        turned = values[:, lanes].T
        copy_out(p, 0).wait()
        form(p, 1)
        first = one(p, 0, turned)
        copy_out(p, 1).wait()
        form(jnp.minimum(p + 1, HEADS // 2 - 1), 0)
        second = one(p, 1, turned)
        mixed.buffer[:, lanes] = jnp.concatenate([first, second], axis=0).T.astype(BF)
        return carry

    lax.fori_loop(0, HEADS // 2, pair, 0)
    mixed.send()
    share.send()

    small[...] = jnp.zeros(small.buffer.shape, F32)
    total = x[...] + matmul(mixed[...], w_out[...])
    width = total.shape[1]
    hidden = len(mlp) // 2 * CHUNK
    unit, scale = centre(total)
    low = (unit * gain[1, 1:2] + bias[1, 1:2]).astype(BF)
    grad_low = cotangent[...]
    grad = grad_low.astype(F32)
    small[1:2, 2 * width : 3 * width] = jnp.sum(grad, axis=0, keepdims=True)
    grad_normed = None
    for at, span in enumerate(chunks(hidden)):
        w_up, w_down = mlp[2 * at][...], mlp[2 * at + 1][...]
        value, rise = gelu_both(matmul(low, w_up) + ff_bias[1:2, span])
        part = mlp_chunk(span, low, grad_low, rise, w_up, w_down, weights, small)
        put_down(weights, span.start, DOWN_ROWS, mat_left(value.astype(BF), grad_low).astype(BF))
        grad_normed = part if grad_normed is None else grad_normed + part
    hand_out(weights, (keep, send), flags, PLAIN)
    send.send()
    keep.send()
    mlp_tail(1, grad, grad_normed, unit, scale, gain, mixed, w_out, outs.buffer, 0, out_grad, out_mixed, small)
    for head in range(2):
        copy_out(HEADS // 2 - 1, head).wait()


def crest(flags, query, kv, far, lang, x, gain, bias, w_attn, w_up, ff_bias, w_down, cotangent):
    rows, width = x.shape
    hidden = w_up.shape[2]
    held = 2 * hidden // SLICES
    done = dense_call(
        crest_kernel, "crest",
        (query, kv, far, lang, x, w_attn, gain, bias, ff_bias, cotangent, w_up, w_down),
        [(0, None), (1, None), (2, None), (3, None), (4, None), (5, (1, 3))]
        + [(at, None) for at in range(6, 10)]
        + mlp_fetches(1, 10, 11, hidden),
        [((rows, width), BF), ((HEADS // 2, 8, rows), F32), ((rows, width), F32), ((rows, width), BF)]
        + part_shapes(PLAIN, held, width)
        + [((8, hidden), F32), ((SLICES, width // SLICES, width), BF)],
        LONG,
        [
            pltpu.VMEM((SLICES, held, width), BF),
            pltpu.VMEM((KEYS, width), BF),
            pltpu.VMEM((KEYS, width), BF),
            pltpu.VMEM((KEYS, PAIR), BF),
            pltpu.VMEM((rows, PAIR), BF),
            pltpu.VMEM((2, KEYS, ROWS_UP), F32),
            pltpu.VMEM((2, 1, rows), F32),
            pltpu.VMEM((2, KEYS, ROWS_UP), BF),
            pltpu.SemaphoreType.DMA((2,)),
        ],
        flags,
        lead=4,
        room=DENSE_VMEM,
        raw=[((HEADS, KEYS, ROWS_UP), BF)],
    )
    return (done[0], done[8], done[1], done[2], done[3], done[4:6], done[6], done[7])


def leave_grad(unit, scale, gain, grad, grad_query, grad_key, grad_value, w_qkv):
    grad_normed = mat_right(grad_query, w_qkv[0]) * 0.125
    grad_normed = grad_normed + mat_right(grad_key, w_qkv[1]) + mat_right(grad_value, w_qkv[2])
    grad_state, grad_gain, grad_bias = norm_back(grad_normed, unit, scale, gain)
    return (grad + grad_state, grad_gain, grad_bias)


def leave_kernel(flags, fetched, stores, sums, held):
    query, normed, kv, far, x, gain, w_qkv, grad = fetched[:8]
    out, keep, send, token = stores
    token[...] = jnp.zeros(token.buffer.shape, F32)
    grad_query, low = query[...], normed[...]
    width = low.shape[1]
    place = width // SLICES
    put_rows(held, 0, (mat_left(low, grad_query) * 0.125).astype(BF))
    sums[...] = kv[...].astype(F32)
    rows = pl.ds(pl.multiple_of((1 - flags[1]) * (ROWS - EDGE), 16), EDGE)
    sums[rows, :] += far[...].astype(F32)
    grad_key, grad_value = unmix(sums[...].astype(BF))
    unit, scale = centre(x[...].astype(F32))
    total, grad_gain, grad_bias = leave_grad(
        unit, scale, gain[0, 0:1], grad[...], grad_query, grad_key, grad_value, w_qkv
    )
    out[...] = total
    out.send()
    put_rows(held, place, mat_left(low, grad_key).astype(BF))
    put_rows(held, 2 * place, mat_left(low, grad_value).astype(BF))
    put_small(held, 3 * place, fetched[8:], grad_gain, grad_bias)
    hand_out(held, (keep, send), flags, LAST)


SMALL_ROWS = 32


def put_small(held, place, small, grad_gain, grad_bias):
    width = grad_gain.shape[1]
    rows = [grad_gain, small[0][1:2, :width], small[2][0:1, :width], small[1][1:2, :width]]
    rows += [grad_bias, small[0][1:2, width : 2 * width], small[2][0:1, width : 2 * width]]
    rows += [small[1][1:2, width : 2 * width]]
    rows += [small[at][1:2, 2 * width : 3 * width] for at in range(2)]
    block = jnp.concatenate(rows, axis=0)
    long = jnp.concatenate([small[at][0:1, :] for at in range(2)], axis=0)
    each, more = width // SLICES, long.shape[1] // SLICES
    for piece in range(SLICES):
        head = jnp.pad(block[:, piece * each : (piece + 1) * each], ((0, 0), (0, more - each)))
        tail = long[:, piece * more : (piece + 1) * more]
        rest = jnp.zeros((SMALL_ROWS - head.shape[0] - tail.shape[0], more), F32)
        both = jnp.concatenate([head, tail, rest], axis=0).astype(BF)
        held[piece, place : place + SMALL_ROWS, :] = jnp.pad(both, ((0, 0), (0, width - more)))


def leave(flags, x, gain, normed, grad, query, kv, far, w_attn, smalls, after):
    rows, width = x.shape
    held = 3 * (width // SLICES) + SMALL_ROWS
    done = dense_call(
        leave_kernel, "leave",
        (query, normed, kv, far, x, gain, w_attn, grad, *smalls),
        [(at, None) for at in range(6)] + [(6, (0, QKV))] + [(at, None) for at in range(7, 11)],
        [((rows, width), F32)] + part_shapes(LAST, held, width) + [((8, PAIR), F32)],
        4.0,
        [pltpu.VMEM((rows, 2 * width), F32), pltpu.VMEM((SLICES, held, width), BF)],
        flags,
        after,
        lead=8,
        room=30 * 2**20,
    )
    return (done[0], done[1:3], done[3])


def put_sums(klass, side, sums, lang_sums, kv, here, far, own, lone, there):
    @pl.when(klass == 1)
    def fine():
        sums[:, here] = (kv[:, here].astype(F32) + far[:ROWS, there].astype(F32)).astype(BF)

        @pl.when(side == 0)
        def owner():
            lang_sums[:LONE, here] = (lone[:, there].astype(F32) + far[ROWS:, there].astype(F32)).astype(BF)

    @pl.when(klass != 1)
    def coarse():
        sums[:, here] = kv[:, here]
        lang_sums[:, here] = own[:, there]


def descend_kernel(flags, fetched, stores, sums, lang_sums, plain, split):
    query, normed, x, kv = fetched[:4]
    fars, owns, lones = fetched[4:6], fetched[6:8], fetched[8:10]
    w_qkv, gain, grad, low_normed = fetched[10:14]
    mlp, (after, mixed, w_out, lang_normed, feats, language, w_lang, later) = fetched[14:-8], fetched[-8:]
    out_grad, out_mixed, grad_language, keep, send, split_keep, split_send, small, small_mid = stores
    klass, side = flags[0], flags[1]
    small[...] = jnp.zeros(small.buffer.shape, F32)
    small_mid[...] = jnp.zeros(small_mid.buffer.shape, F32)
    lang_sums[...] = jnp.zeros_like(lang_sums)
    grad_query, low = query[...], normed[...]
    width = low.shape[1]
    place = width // SLICES
    hidden = len(mlp) // 4 * CHUNK
    up_rows = hidden // SLICES
    put_rows(plain, up_rows, (mat_left(low, grad_query) * 0.125).astype(BF))
    unit, scale = centre(x[...])
    kv = kv.ref()
    fars, owns, lones = [[part.ref() for part in parts] for parts in (fars, owns, lones)]
    for pair in range(HEADS // 2):
        for which in range(2):
            there = slice(pair * PAIR, (pair + 1) * PAIR)
            here = slice((2 * pair + which) * PAIR, (2 * pair + which + 1) * PAIR)
            put_sums(klass, side, sums, lang_sums, kv, here, fars[which], owns[which], lones[which], there)

    grad_key, grad_value = unmix(sums[...])
    grad, grad_gain, grad_bias = leave_grad(
        unit, scale, gain[1, 0:1], grad[...], grad_query, grad_key, grad_value, w_qkv
    )
    lang_key, lang_value = unmix(lang_sums[...])
    lang_low = lang_normed[...]
    put_rows(plain, up_rows + place, (mat_left(low, grad_key) + mat_left(lang_low, lang_key)).astype(BF))
    put_rows(split, DOWN_ROWS, (mat_left(low, grad_value) + mat_left(lang_low, lang_value)).astype(BF))
    lang_grad = mat_right(lang_key, w_qkv[1]) + mat_right(lang_value, w_qkv[2])
    unit, scale = centre(feats[...])
    grad_feats, lang_gain, lang_bias = norm_back(lang_grad, unit, scale, gain[1, 0:1])
    feats_low = grad_feats.astype(BF)
    put_rows(split, DOWN_ROWS + place, mat_left(language[...], feats_low).astype(BF))
    grad_language[...] = mat_right(feats_low, w_lang[...])
    grad_language.send()
    small_mid[0:1, :width] = grad_gain + lang_gain
    small_mid[0:1, width : 2 * width] = grad_bias + lang_bias

    grad_low = grad.astype(BF)
    small[1:2, 2 * width : 3 * width] = jnp.sum(grad_low.astype(F32), axis=0, keepdims=True)
    low = low_normed[...]
    grad_normed = None
    for at, span in enumerate(chunks(hidden)):
        w_down, rise, w_up, active = [part[...] for part in mlp[4 * at : 4 * at + 4]]
        part = mlp_chunk(span, low, grad_low, rise.astype(F32), w_up, w_down, plain, small)
        put_down(split, span.start, 0, mat_left(active, grad_low).astype(BF))
        grad_normed = part if grad_normed is None else grad_normed + part
    hand_out(plain, (keep, send), flags, PLAIN)
    send.send()
    keep.send()
    unit, scale = centre(after[...])
    mlp_tail(
        0, grad, grad_normed, unit, scale, gain, mixed, w_out, split, DOWN_ROWS + 2 * place, out_grad, out_mixed, small
    )
    split[:, DOWN_ROWS + 3 * place :, :] = later[...]
    hand_out(split, (split_keep, split_send), flags, SPLIT)


def descend(
    flags, state, gain, normed, grad, query, kv, fars, owns, w_attn, feats, lang_normed, language, w_lang,
    after, mixed, low_normed, active, slope, w_up, w_down, later, follows,
):
    rows, width = state.shape
    hidden = w_up.shape[2]
    place = width // SLICES
    plain, split = hidden // SLICES + 2 * place, DOWN_ROWS + 4 * place
    fetches = []
    for span in chunks(hidden):
        fetches += [(13, (0, span)), (14, (slice(None), span)), (12, (0, slice(None), span)), (15, (slice(None), span))]
    head, foot = slice(0, LPAD), slice(ROWS, ROWS + LONE)
    done = dense_call(
        descend_kernel, "descend",
        (query, normed, state, kv, *fars, *owns, w_attn, gain, grad, low_normed)
        + (w_up, w_down, slope, active, after, mixed, lang_normed, feats, language, w_lang, later),
        [(at, None) for at in range(6)]
        + [(at, (head,)) for at in range(6, 8)]
        + [(at, (foot,)) for at in range(6, 8)]
        + [(8, (1, QKV)), (9, None), (10, None), (11, None)]
        + fetches
        + [(16, None), (17, None), (8, (0, 3)), (18, None), (19, None), (20, None), (21, None), (22, None)],
        [((rows, width), F32), ((rows, width), BF), ((LPAD, width), F32)]
        + part_shapes(PLAIN, plain, width)
        + part_shapes(SPLIT, split, width)
        + [((8, hidden), F32), ((8, 2 * width), F32)],
        LONG,
        [
            pltpu.VMEM((rows, 2 * width), BF),
            pltpu.VMEM((LPAD, 2 * width), BF),
            pltpu.VMEM((SLICES, plain, width), BF),
            pltpu.VMEM((SLICES, split, width), BF),
        ],
        flags,
        follows,
        lead=6,
    )
    return (done[0], done[1], done[2], done[3:5], done[5:7], done[7], done[8])


def pair_swap(block):
    count = lax.axis_size("wide")
    return lax.ppermute(block, "wide", [(at, at ^ 1) for at in range(count)])


class Flow:
    def __init__(self, route, parts):
        self.route, self.step = route, 0
        self.units = route.units
        self.keep = [parts[0]]
        self.send(parts)

    def send(self, parts):
        self.got = []
        if self.step < len(self.route.steps):
            bits = self.route.steps[self.step]
            self.units //= 1 << len(bits)
            for at, part in enumerate(parts[1:], 1):
                found = [bit for place, bit in enumerate(bits) if at >> (len(bits) - 1 - place) & 1]
                self.got.append(self.move(part, found))
        else:
            self.keep = [parts[0]]
            self.got.append(self.move(parts[0], [0] if self.route.halves else None))

    def move(self, part, bits):
        shift = 1 if self.route.halves else 0
        if bits is None or bits == [0] and shift:
            return lax.ppermute(part, "narrow", [(0, 1), (1, 0)])
        count = lax.axis_size("wide")
        stride = sum((count // SLICES) << (bit - shift) for bit in bits)
        return lax.ppermute(part, "wide", [(p, p ^ stride) for p in range(count)])


def step_kernel(layout, ins, outs):
    at = 0
    for out, (count, rows) in zip(outs, layout):
        total = None
        for term in ins[at : at + count]:
            part = term[rows] if rows is not None else term[...]
            total = part.astype(F32) if total is None else total + part.astype(F32)
        out[...] = total.astype(BF)
        if isinstance(out, Store):
            out.send()
        at += count


def step(flows, after=(), near=False, cost=SHORT, lazy=False):
    operands, fetches, layout, outs, plan = [], [], [], [], []
    for flow in flows:
        flow.step += 1
        terms = flow.keep + flow.got
        last = flow.step == len(flow.route.steps)
        count = 1 if last else flow.route.parts(flow.step)
        each = flow.units // count
        made = [part for part in range(count) if part or last or not lazy]
        for part in reversed(made):
            rows = slice(part * each, (part + 1) * each)
            for term in terms:
                fetches.append((len(operands), rows))
                operands.append(term)
            layout.append((len(terms), rows))
            outs.append(((each,) + terms[0].shape[1:], BF))
        plan.append((flow, terms, count, made))
    if near:
        done = near_call(
            lambda *refs: step_kernel(layout, refs[: len(operands)], refs[len(operands) :]),
            "step", outs, operands, after=after, cost=cost,
        )
    else:
        done = dense_call(
            lambda ins, stores: step_kernel([(count, None) for count, rows in layout], ins, stores),
            "step", operands, fetches, outs, cost, after=after, lead=len(fetches), room=STEP_VMEM,
        )
    at = 0
    for flow, terms, count, made in plan:
        parts = [None] * count
        for part in reversed(made):
            parts[part] = done[at]
            at += 1
        flow.keep = terms if parts[0] is None else [parts[0]]
        flow.send(parts)
    return done


def split_low(buffer):
    count = lax.axis_size("wide")
    position = lax.axis_index("wide")
    half = count // SLICES
    while half > 1:
        half //= 2
        mine = position // half % 2
        size = buffer.shape[0] // 2
        send = lax.dynamic_slice_in_dim(buffer, (1 - mine) * size, size, 0)
        keep = lax.dynamic_slice_in_dim(buffer, mine * size, size, 0)
        buffer = keep + lax.ppermute(send.astype(BF), "wide", [(p, p ^ half) for p in range(count)])
    return buffer


def finish_kernel(
    flags, first, first_got, plain, plain_got, split, split_got, attn_one, attn_one_got,
    lang, attn, ups, downs, gains, biases, ff_biases, out_biases, whole, last,
):
    rows, width = attn.shape[2:]
    up_rows, down_rows = ups.shape[2] // width * rows, downs.shape[1]

    def both(buffer, got):
        return buffer[0].astype(F32) + got[0].astype(F32)

    def put_ups(layer, found):
        for at in range(ups.shape[2] // width):
            ups[layer, :, at * width : (at + 1) * width] = found[at * rows : (at + 1) * rows]

    found = both(first, first_got)
    put_ups(1, found)
    downs[1] = found[up_rows:]
    found = both(plain, plain_got)
    put_ups(0, found)
    attn[1, 0] = found[up_rows : up_rows + rows]
    attn[1, 1] = found[up_rows + rows :]
    whole[flags[3]] = split[0].astype(F32)
    whole[1 - flags[3]] = split_got[0].astype(F32)
    found = jnp.concatenate([whole[0], whole[1]], axis=0)
    downs[0] = found[:down_rows]
    attn[1, 2] = found[down_rows : down_rows + rows]
    lang[...] = found[down_rows + rows : down_rows + 2 * rows]
    attn[0, 3] = found[down_rows + 2 * rows : down_rows + 3 * rows]
    attn[1, 3] = found[down_rows + 3 * rows :]
    last[flags[3]] = attn_one[0].astype(F32)
    last[1 - flags[3]] = attn_one_got[0].astype(F32)
    found = jnp.concatenate([last[0], last[1]], axis=0)
    for at in range(3):
        attn[0, at] = found[at * rows : (at + 1) * rows]
    small = found[3 * rows :]
    for layer in range(2):
        gains[layer] = small[2 * layer : 2 * layer + 2, :rows]
        biases[layer] = small[4 + 2 * layer : 6 + 2 * layer, :rows]
    out_biases[...] = small[8:10, :rows]
    ff_biases[...] = small[10:12, : ff_biases.shape[1]]


def finish(flags, flows, width, hidden):
    rows = width // SLICES
    args = []
    for flow in flows:
        args += flow.keep + flow.got
    return near_call(
        finish_kernel, "finish",
        [
            ((rows, width), F32),
            ((2, 4, rows, width), F32),
            ((2, rows, hidden), F32),
            ((2, hidden // SLICES, width), F32),
            ((2, 2, rows), F32),
            ((2, 2, rows), F32),
            ((2, hidden // SLICES), F32),
            ((2, rows), F32),
        ],
        args,
        [
            pltpu.VMEM((2, (DOWN_ROWS + 4 * rows) // 2, width), F32),
            pltpu.VMEM((2, (3 * rows + SMALL_ROWS) // 2, width), F32),
        ],
        flags,
    )


def body(
    patches,
    language,
    w_lang,
    w_attn,
    w_up,
    w_down,
    norm_gain,
    norm_bias,
    ff_bias,
    out_bias,
    cotangent,
    classes,
):
    position = lax.axis_index("wide")
    wide = lax.axis_size("wide")
    side = position % 2
    klass = lax.dynamic_index_in_dim(classes[0], position // 2, 0, keepdims=False)
    high = position // (wide // SLICES)
    flags = jnp.stack([klass, side, high, lax.axis_index("narrow")]).astype(jnp.int32)
    width = w_lang.shape[0]
    hidden = w_up.shape[2]
    start = patches[0]
    lang_low = jnp.pad(language[0], ((0, LPAD - language.shape[1]), (0, 0)))

    other = pair_swap(start)
    normed_a, query_a, key_a, value_a, mixed_a, weights_a, share_a, *rest = climb(
        flags, start, other, norm_gain, norm_bias, w_attn, w_up, ff_bias, w_down, out_bias, lang_low, w_lang
    )
    after_a, normed_b, active_b, slope_b, state_b, normed_c, query_c, kv_c, feats, lang_normed, lang_kv = rest
    far_c = pair_swap(kv_c)
    mixed_c, weights_c, share_c, grad, grad_mixed_c, parts, small_two, outs_two = crest(
        flags, query_c, kv_c, far_c, lang_kv, state_b, norm_gain, norm_bias, w_attn, w_up, ff_bias, w_down,
        cotangent[0],
    )
    first = Flow(PLAIN, parts)
    joint = (flags, query_c, kv_c, far_c, lang_kv, mixed_c, weights_c, share_c, grad_mixed_c)
    query, kv, *edges, token = joint_backward(*joint, 0, HEADS // 2)
    fars = [pair_swap(part) for part in edges]
    done = step([first], [token], lazy=True)
    grad, grad_mixed_a, grad_language, plain_parts, split_parts, small_one, small_mid = descend(
        flags, state_b, norm_gain, normed_c, grad, query, kv, fars, edges, w_attn, feats, lang_normed, lang_low,
        w_lang, after_a, mixed_a, normed_b, active_b, slope_b, w_up, w_down, outs_two, done,
    )
    plain, split = Flow(PLAIN, plain_parts), Flow(SPLIT, split_parts)

    done = step([first], [small_mid], lazy=True, cost=30.0)
    done = step([plain, split], [done[0]])
    view = (flags, query_a, key_a, value_a, mixed_a, weights_a, share_a, grad_mixed_a)
    query, kv, edge, token = view_backward(*view, 0, HEADS // 2, done)
    far = pair_swap(edge)
    done = step([first], [token])
    grad, attn_parts, token = leave(
        flags, start, norm_gain, normed_a, grad, query, kv, far, w_attn, (small_one, small_two, small_mid), done
    )
    attn_one = Flow(LAST, attn_parts)

    done = step([plain, split], [token], near=True, cost=LONG)
    done = step([attn_one], [done[0]], near=True)
    done = step([first], [done[0]], near=True, cost=5.0)
    done = step([plain, split], [done[0]], near=True)
    done = step([attn_one], [done[0]], near=True)
    done = step([plain, split], [done[0], first.got[0]], near=True)
    done = step([attn_one], [done[0]], near=True)
    done = step([split], [done[0]], near=True)
    done = step([attn_one], [done[0], plain.got[0]], near=True)
    flows = (first, plain, split, attn_one)
    grad_w_lang, grad_w_attn, grad_w_up, grad_w_down, *vectors = finish(flags, flows, width, hidden)
    gains, biases, ff_biases, out_biases = vectors

    def own(values, dim):
        if wide == SLICES:
            return values
        values = jnp.moveaxis(values, dim, 0)
        return jnp.moveaxis(split_low(values), 0, dim)

    return (
        grad[None],
        grad_language[None, : language.shape[1]],
        own(grad_w_lang, 0),
        own(grad_w_attn, 2),
        own(grad_w_up, 1),
        own(grad_w_down, 1),
        own(gains, 2),
        own(biases, 2),
        own(ff_biases, 1),
        own(out_biases, 1),
    )


def solution(mesh):
    in_specs = (
        P("narrow", "wide", None),
        P("narrow", "wide", None),
        P(),
        P(),
        P(),
        P(),
        P(),
        P(),
        P(),
        P(),
        P("narrow", "wide", None),
        P("narrow", None),
    )
    out_specs = (
        P("narrow", "wide", None),
        P("narrow", "wide", None),
        P("wide", None),
        P(None, None, "wide", None),
        P(None, "wide", None),
        P(None, "wide", None),
        P(None, None, "wide"),
        P(None, None, "wide"),
        P(None, "wide"),
        P(None, "wide"),
    )
    return jax.shard_map(body, mesh=mesh, in_specs=in_specs, out_specs=out_specs, check_vma=False)
```

```python
import functools

import jax
import jax.numpy as jnp
from jax import lax
from jax.experimental import pallas as pl
from jax.experimental.pallas import tpu as pltpu
from jax.sharding import PartitionSpec as P

HEADS = 8
HD = 64
LANG = 77
VB = 288
VS = 72
ROWS = 720
EDGE = VB // 2
PADDED = ROWS + EDGE
LPAD = 160
LONE = 96
KEYS = 2 * ROWS + LONE
PAIR = 2 * HD
SLICES = 16
ROWS_UP = 768
VB_UP = 384
STEP_VMEM = 20 * 2**20
LONG, SHORT = 60.0, 0.5
JOINT_VMEM = 60 * 2**20
JOINT_BACK_VMEM = 60 * 2**20
VIEW_VMEM = 36 * 2**20
DENSE_VMEM = 60 * 2**20
NEAR_VMEM = 16 * 2**20

epsilon = 1e-05
masked_out = -1e30
BF = jnp.bfloat16
F32 = jnp.float32


def matmul(left, right):
    return jnp.dot(left, right, preferred_element_type=F32)


def mat_left(left, right):
    return lax.dot_general(left, right, (((0,), (0,)), ((), ())), preferred_element_type=F32)


def mat_right(left, right):
    return lax.dot_general(left, right, (((1,), (1,)), ((), ())), preferred_element_type=F32)


def cost_of(microseconds):
    return pl.CostEstimate(flops=int(microseconds * 1e9), bytes_accessed=1, transcendentals=0)


def waiting(kernel, inputs, more):
    if not more:
        return kernel

    def without(*refs):
        return kernel(*refs[:inputs], *refs[inputs + more :])

    return without


def lane_mask(head):
    lanes = lax.broadcasted_iota(jnp.int32, (1, PAIR), 1)
    return jnp.where(lanes // HD == head, 1.0, 0.0).astype(BF)


def in_half(shape):
    return lax.broadcasted_iota(jnp.int32, shape, 1) % HD


def row_of(shape):
    return lax.broadcasted_iota(jnp.int32, shape, 0)


def key_marks(allowed, items):
    lane = in_half(allowed.shape)
    marks = jnp.where(lane < items, jnp.where(allowed, 0.0, masked_out), 0.0)
    return jnp.where((lane >= 4) & (lane < 7), 1.0, marks).astype(BF)


def joint_key_marks(klass):
    shape = (KEYS, PAIR)
    row, lane = row_of(shape), in_half(shape)
    first = (row < ROWS // 2) | ((row >= ROWS) & (row < ROWS + LANG))
    second = ((row >= ROWS // 2) & (row < ROWS)) | ((row >= ROWS + LANG) & (row < ROWS + 2 * LANG))
    fine = jnp.where(row < 2 * ROWS + LANG, 1, 0)
    coarse = jnp.where(lane == 0, jnp.where(first, 1, 0), jnp.where(second, 1, 0))
    return key_marks(jnp.where(klass == 1, fine, coarse) == 1, 2)


def joint_row_marks():
    shape = (ROWS, PAIR)
    row, lane = row_of(shape), in_half(shape)
    return jnp.where(lane == row // (ROWS // 2), 1.0, 0.0).astype(BF)


def view_key_marks(klass):
    shape = (PADDED, PAIR)
    row, lane = row_of(shape), in_half(shape)
    same = jnp.where(lane == row % VB // VS, 1, 0)
    return key_marks(jnp.where(klass == 1, 1, same) == 1, 4)


def view_row_marks():
    shape = (PADDED, PAIR)
    row, lane = row_of(shape), in_half(shape)
    return jnp.where(lane == row % VB // VS, 1.0, 0.0).astype(BF)


def with_parts(values):
    lane = in_half(values.shape)
    high = values.astype(BF).astype(F32)
    rest = values - high
    middle = rest.astype(BF).astype(F32)
    low = rest - middle
    picked = jnp.where(lane == 4, -high, jnp.where(lane == 5, -middle, jnp.where(lane == 6, -low, 0.0)))
    return picked.astype(BF)


def attend_heads(units):
    scores = [mat_right(keys, right) for right, keys, across in units]
    weights = [jnp.exp(part - jnp.max(part, axis=0, keepdims=True)).astype(BF) for part in scores]
    outs = [matmul(unit[2], part) for unit, part in zip(units, weights)]
    shares = [1.0 / out[HD : HD + 1] for out in outs]
    return [(part, out[:HD] * share, share) for part, out, share in zip(weights, outs, shares)]


def score_side(query, marks, head):
    mask = lane_mask(head)
    return jnp.concatenate([query * mask, marks * mask], axis=1)


def joint_place(klass, side, kv_ref, far_ref, lang_ref, put):
    put(slice(0, ROWS), kv_ref[:ROWS])

    @pl.when(klass == 1)
    def fine():
        put(slice(ROWS, 2 * ROWS), far_ref[:ROWS])

        @pl.when(side == 0)
        def own():
            put(slice(2 * ROWS, KEYS), lang_ref[:LONE])

        @pl.when(side == 1)
        def partner():
            put(slice(2 * ROWS, KEYS), far_ref[ROWS:])

    @pl.when(klass != 1)
    def coarse():
        put(slice(ROWS, ROWS + LPAD), lang_ref[...])


def inner_marks(grad, mixed):
    lanes = lax.broadcasted_iota(jnp.int32, (1, PAIR), 1)
    product = grad.astype(F32) * mixed.astype(F32)
    first = jnp.sum(jnp.where(lanes < HD, product, 0.0), axis=1, keepdims=True)
    second = jnp.sum(jnp.where(lanes < HD, 0.0, product), axis=1, keepdims=True)
    return with_parts(jnp.where(lanes < HD, first, second))


def attend_back(units):
    inner = [mat_right(unit[0], unit[5]) for unit in units]
    probs = [unit[2].astype(F32) * unit[3] for unit in units]
    grad_scores = [(left * right).astype(BF) for left, right in zip(probs, inner)]
    grad_values = [matmul(part.astype(BF), unit[5][:, :PAIR]) for part, unit in zip(probs, units)]
    grad_keys = [matmul(part, unit[4]) for part, unit in zip(grad_scores, units)]
    across = [matmul(unit[1], part) for part, unit in zip(grad_scores, units)]
    return list(zip(grad_keys, grad_values, across))


def fill_rows(left, grads, rows, query, grad, mixed):
    inner = inner_marks(grad, mixed)
    for head in range(2):
        mask = lane_mask(head)
        left[head, rows, :] = query * mask
        grads[head, rows, :PAIR] = grad * mask
        grads[head, rows, PAIR:] = inner * mask


def joint_backward_kernel(
    flags, q_ref, kv_ref, far_ref, lang_ref, mixed_ref, weights_ref, share_ref, grad_ref, dq_ref, dkv_ref,
    dfar_key, dfar_value, token, keys, values, across, left, grads,
):
    klass, side = flags[0], flags[1]

    @pl.when(pl.program_id(0) == 0)
    def prepare():
        keys[...] = jnp.zeros_like(keys)
        values[...] = jnp.zeros_like(values)
        values[:, PAIR:] = joint_key_marks(klass)

    def put(rows, block):
        keys[rows, :] = block[:, :PAIR]
        values[rows, :PAIR] = block[:, PAIR:]

    joint_place(klass, side, kv_ref, far_ref, lang_ref, put)
    token[...] = jnp.zeros_like(token)
    across[...] = keys[...].T
    fill_rows(left, grads, slice(0, ROWS), q_ref[...], grad_ref[...], mixed_ref[...])
    units = [
        (
            values[...],
            across[head * HD : (head + 1) * HD, :],
            weights_ref[head, :, :ROWS],
            share_ref[0, head : head + 1, :],
            left[head],
            grads[head],
        )
        for head in range(2)
    ]
    first, second = attend_back(units)
    for span, at, far in ((slice(0, PAIR), 0, dfar_key), (slice(PAIR, 2 * PAIR), 1, dfar_value)):
        both = (first[at] + second[at]).astype(BF)
        dkv_ref[:, span] = both[:ROWS]
        far[...] = both[ROWS:]
    dq_ref[...] = jnp.concatenate([first[2], second[2]], axis=0).T.astype(BF)


def joint_backward(flags, query, kv, far, lang, mixed, weights, share, grad, base, pairs, after=(), cost=LONG):
    rows = query.shape[0]
    one = pl.BlockSpec((rows, PAIR), lambda i, f: (0, i + base))
    return pl.pallas_call(
        waiting(joint_backward_kernel, 9, len(after)),
        grid_spec=pltpu.PrefetchScalarGridSpec(
            num_scalar_prefetch=1,
            grid=(pairs,),
            in_specs=[
                one,
                pl.BlockSpec((rows, 2 * PAIR), lambda i, f: (0, i + base)),
                pl.BlockSpec((ROWS + LONE, 2 * PAIR), lambda i, f: (0, i + base)),
                pl.BlockSpec((LPAD, 2 * PAIR), lambda i, f: (0, i + base)),
                one,
                pl.BlockSpec((2, KEYS, ROWS_UP), lambda i, f: (i + base, 0, 0)),
                pl.BlockSpec((1, 8, rows), lambda i, f: (i + base, 0, 0)),
                one,
            ]
            + [pl.BlockSpec(memory_space=pltpu.HBM)] * len(after),
            out_specs=[
                pl.BlockSpec((rows, PAIR), lambda i, f: (0, i)),
                pl.BlockSpec((rows, 2 * PAIR), lambda i, f: (0, i)),
                pl.BlockSpec((ROWS + LONE, PAIR), lambda i, f: (0, i)),
                pl.BlockSpec((ROWS + LONE, PAIR), lambda i, f: (0, i)),
                pl.BlockSpec((8, PAIR), lambda i, f: (0, 0)),
            ],
            scratch_shapes=[
                pltpu.VMEM((KEYS, PAIR), BF),
                pltpu.VMEM((KEYS, 2 * PAIR), BF),
                pltpu.VMEM((PAIR, KEYS), BF),
                pltpu.VMEM((2, ROWS, PAIR), BF),
                pltpu.VMEM((2, ROWS, 2 * PAIR), BF),
            ],
        ),
        out_shape=[
            jax.ShapeDtypeStruct((rows, pairs * PAIR), BF),
            jax.ShapeDtypeStruct((rows, 2 * pairs * PAIR), BF),
            jax.ShapeDtypeStruct((ROWS + LONE, pairs * PAIR), BF),
            jax.ShapeDtypeStruct((ROWS + LONE, pairs * PAIR), BF),
            jax.ShapeDtypeStruct((8, PAIR), F32),
        ],
        compiler_params=pltpu.CompilerParams(vmem_limit_bytes=JOINT_BACK_VMEM),
        cost_estimate=cost_of(cost),
        name="joint_backward",
    )(flags, query, kv, far, lang, mixed, weights, share, grad, *after)


def view_spots(side):
    own = pl.ds(pl.multiple_of(side * EDGE, 16), ROWS)
    far = pl.ds(pl.multiple_of((1 - side) * ROWS, 16), EDGE)
    return (own, far)


def view_backward_kernel(
    flags, q_ref, key_ref, value_ref, mixed_ref, weights_ref, share_ref, grad_ref, dq_ref, dkv_ref, dfar_ref,
    token, values, left, grads, back, dkv,
):
    klass, side = flags[0], flags[1]
    own, far = view_spots(side)

    @pl.when(pl.program_id(0) == 0)
    def prepare():
        for p in range(2):
            values[p, :, PAIR:] = view_key_marks(klass)
        left[...] = jnp.zeros_like(left)
        grads[...] = jnp.zeros_like(grads)

    units = []
    for p in range(2):
        lanes = slice(p * PAIR, (p + 1) * PAIR)
        values[p, :, :PAIR] = value_ref[:, lanes]
        fill_rows(left.at[p], grads.at[p], own, q_ref[own, lanes], grad_ref[:, lanes], mixed_ref[:, lanes])
    for p in range(2):
        lanes = slice(p * PAIR, (p + 1) * PAIR)
        for index in range(PADDED // VB):
            rows = slice(index * VB, (index + 1) * VB)
            across = key_ref[rows, lanes].T
            for head in range(2):
                units.append(
                    (
                        values[p, rows, :],
                        across[head * HD : (head + 1) * HD, :],
                        weights_ref[index, 2 * p + head, :, :VB],
                        share_ref[index, p, head : head + 1, :],
                        left[p, head, rows, :],
                        grads[p, head, rows, :],
                    )
                )
    done = attend_back(units)
    for p in range(2):
        for index in range(PADDED // VB):
            rows = slice(index * VB, (index + 1) * VB)
            at = 2 * (p * (PADDED // VB) + index)
            first, second = done[at], done[at + 1]
            dkv[rows, 2 * p * PAIR : (2 * p + 1) * PAIR] = (first[0] + second[0]).astype(BF)
            dkv[rows, (2 * p + 1) * PAIR : (2 * p + 2) * PAIR] = (first[1] + second[1]).astype(BF)
            back[rows, p * PAIR : (p + 1) * PAIR] = jnp.concatenate([first[2], second[2]], axis=0).T.astype(BF)

    dq_ref[...] = back[own, :]
    dkv_ref[...] = dkv[own, :]
    dfar_ref[...] = dkv[far, :]
    token[...] = jnp.zeros_like(token)


def view_backward(flags, query, key, value, mixed, weights, share, grad, base, pairs, after=(), cost=LONG):
    rows = mixed.shape[0]
    blocks = PADDED // VB
    one = pl.BlockSpec((rows, 2 * PAIR), lambda i, f: (0, i + base))
    tall = pl.BlockSpec((PADDED, 2 * PAIR), lambda i, f: (0, i + base))
    return pl.pallas_call(
        waiting(view_backward_kernel, 8, len(after)),
        grid_spec=pltpu.PrefetchScalarGridSpec(
            num_scalar_prefetch=1,
            grid=(pairs // 2,),
            in_specs=[
                tall,
                tall,
                tall,
                one,
                pl.BlockSpec((blocks, 4, VB, VB_UP), lambda i, f: (0, i + base, 0, 0)),
                pl.BlockSpec((blocks, 2, 8, VB), lambda i, f: (0, i + base, 0, 0)),
                one,
            ]
            + [pl.BlockSpec(memory_space=pltpu.HBM)] * len(after),
            out_specs=[
                pl.BlockSpec((rows, 2 * PAIR), lambda i, f: (0, i)),
                pl.BlockSpec((rows, 4 * PAIR), lambda i, f: (0, i)),
                pl.BlockSpec((EDGE, 4 * PAIR), lambda i, f: (0, i)),
                pl.BlockSpec((8, PAIR), lambda i, f: (0, 0)),
            ],
            scratch_shapes=[
                pltpu.VMEM((2, PADDED, 2 * PAIR), BF),
                pltpu.VMEM((2, 2, PADDED, PAIR), BF),
                pltpu.VMEM((2, 2, PADDED, 2 * PAIR), BF),
                pltpu.VMEM((PADDED, 2 * PAIR), BF),
                pltpu.VMEM((PADDED, 4 * PAIR), BF),
            ],
        ),
        out_shape=[
            jax.ShapeDtypeStruct((rows, pairs * PAIR), BF),
            jax.ShapeDtypeStruct((rows, 2 * pairs * PAIR), BF),
            jax.ShapeDtypeStruct((EDGE, 2 * pairs * PAIR), BF),
            jax.ShapeDtypeStruct((8, PAIR), F32),
        ],
        compiler_params=pltpu.CompilerParams(vmem_limit_bytes=VIEW_VMEM),
        cost_estimate=cost_of(cost),
        name="view_backward",
    )(flags, query, key, value, mixed, weights, share, grad, *after)


CHUNK = 1024
SHORT_CHUNK = 512
DOWN_ROWS = 128
BITS = SLICES.bit_length() - 1


class Route:
    def __init__(self, steps, halves):
        self.steps = steps
        self.halves = halves
        self.order = [bit for step in steps for bit in step]
        self.units = 1 << len(self.order)

    def unit(self, position):
        last = len(self.order) - 1
        return sum((position >> (last - at) & 1) << bit for at, bit in enumerate(self.order))

    def parts(self, step):
        return 1 << len(self.steps[step])

    def rows(self, rows):
        return rows // 2 if self.halves else rows


PLAIN = Route(((0,), (1,), (2,), (3,)), False)
SPLIT = Route(((1,), (0,), (2,), (3,), (4,)), True)
LAST = Route(((1,), (0,), (2,), (3, 4)), True)


def hand_out(held, parts, flags, route, span=slice(None)):
    each = route.units // len(parts)
    rows = route.rows(held.shape[1])
    for position in range(route.units):
        if route.halves:
            unit = jnp.bitwise_xor(route.unit(position), flags[2] * 2 + flags[3])
            block = held[unit // 2, pl.ds(pl.multiple_of(unit % 2 * rows, 16), rows), :]
        else:
            block = held[jnp.bitwise_xor(route.unit(position), flags[2]), span]
        parts[position // each][position % each, span] = block


def part_shapes(route, rows, width):
    each = route.units // route.parts(0)
    return [((each, route.rows(rows), width), BF)] * route.parts(0)


def centre(values):
    mean = jnp.mean(values, axis=-1, keepdims=True)
    centered = values - mean
    variance = jnp.mean(centered * centered, axis=-1, keepdims=True)
    scale = lax.rsqrt(variance + epsilon)
    return (centered * scale, scale)


def norm_back(grad, unit, scale, gain):
    grad_gain = jnp.sum(grad * unit, axis=0, keepdims=True)
    grad_bias = jnp.sum(grad, axis=0, keepdims=True)
    scaled = grad * gain
    level = jnp.mean(scaled, axis=-1, keepdims=True)
    along = jnp.mean(scaled * unit, axis=-1, keepdims=True)
    return ((scaled - level - unit * along) * scale, grad_gain, grad_bias)


def gelu_both(hidden):
    root, cubic = 0.7978845608028654, 0.044715
    square = hidden * hidden
    bend = jnp.tanh(hidden * (root + (root * cubic) * square))
    half = 0.5 + 0.5 * bend
    slope = (0.5 * hidden) * (1.0 - bend * bend) * (root + (3.0 * root * cubic) * square)
    return (hidden * half, half + slope)


def mix(keys, values):
    parts = []
    for at in range(0, keys.shape[1], PAIR):
        parts += [keys[:, at : at + PAIR], values[:, at : at + PAIR]]
    return jnp.concatenate(parts, axis=1)


def unmix(both):
    blocks = [both[:, at : at + PAIR] for at in range(0, both.shape[1], PAIR)]
    return (jnp.concatenate(blocks[0::2], axis=1), jnp.concatenate(blocks[1::2], axis=1))


class Fetch:
    def __init__(self, source, buffer, semaphore, more):
        self.copy = pltpu.make_async_copy(source, buffer, semaphore)
        self.buffer, self.more, self.here = buffer, more, False

    def ref(self):
        if not self.here:
            self.more(0, self)
            self.copy.wait()
            self.here = True
            self.more(2)
        return self.buffer

    def __getitem__(self, index):
        return self.ref()[index]


class Store:
    def __init__(self, buffer, target, semaphores, pieces):
        self.buffer, self.copies, self.gone = buffer, [], []
        for at, piece in enumerate(pieces):
            source = buffer if piece is None else buffer.at[piece]
            place = target if piece is None else target.at[piece]
            self.copies.append(pltpu.make_async_copy(source, place, semaphores.at[at]))
            self.gone.append(False)

    def __setitem__(self, index, value):
        self.buffer[index] = value

    def __getitem__(self, index):
        return self.buffer[index]

    def send(self, at=None):
        for place, copy in enumerate(self.copies):
            if not self.gone[place] and at in (None, place):
                copy.start()
                self.gone[place] = True


LEAD = 4
QKV = slice(0, 3)


def dense_call(kernel, name, operands, fetches, outs, cost, scratch=(), flags=None, after=(), pieces=None, lead=LEAD, room=DENSE_VMEM, raw=()):
    shapes = [
        jax.eval_shape(lambda array, index=index: array[:EDGE] if callable(index) else array[index or ...], operands[at])
        for at, index in fetches
    ]
    count, first = len(operands), 0 if flags is None else 1
    pieces = [(pieces or {}).get(at, (None,)) for at in range(len(outs))]

    def run(*refs):
        inputs = refs[first : first + count]
        rest = refs[first + count + len(after) :]
        targets, rest = rest[: len(outs)], rest[len(outs) :]
        straight, rest = rest[: len(raw)], rest[len(raw) :]
        buffers, rest = rest[: len(fetches)], rest[len(fetches) :]
        held, rest = rest[: len(outs)], rest[len(outs) :]
        came, went, own = rest[0], rest[1 : 1 + len(outs)], rest[1 + len(outs) :]
        fetched, started = [], [0]

        def more(number, wanted=None):
            if wanted is not None:
                number = fetched.index(wanted) + 1 - started[0]
            for fetch in fetched[started[0] : started[0] + max(number, 0)]:
                fetch.copy.start()
            started[0] += max(number, 0)

        for place, (at, index) in enumerate(fetches):
            index = index(refs[0]) if callable(index) else index
            source = inputs[at] if index is None else inputs[at].at[index]
            fetched.append(Fetch(source, buffers[place], came.at[place], more))
        more(lead)
        stores = [Store(*parts) for parts in zip(held, targets, went, pieces)]
        kernel(*([refs[0]] if first else []), fetched, stores, *straight, *own)
        for fetch in fetched:
            fetch.ref()
        for store in stores:
            store.send()
        for store in stores:
            for copy in store.copies:
                copy.wait()

    anywhere = pl.BlockSpec(memory_space=pl.ANY)
    return pl.pallas_call(
        run,
        in_specs=[pl.BlockSpec(memory_space=pltpu.SMEM)] * first
        + [anywhere] * count
        + [pl.BlockSpec(memory_space=pltpu.HBM)] * len(after),
        out_specs=[anywhere] * (len(outs) + len(raw)),
        out_shape=[jax.ShapeDtypeStruct(shape, kind) for shape, kind in (*outs, *raw)],
        scratch_shapes=[pltpu.VMEM(part.shape, part.dtype) for part in shapes]
        + [pltpu.VMEM(shape, kind) for shape, kind in outs]
        + [pltpu.SemaphoreType.DMA((len(fetches),))]
        + [pltpu.SemaphoreType.DMA((len(piece),)) for piece in pieces]
        + list(scratch),
        compiler_params=pltpu.CompilerParams(vmem_limit_bytes=room),
        cost_estimate=cost_of(cost),
        name=name,
    )(*([flags] if first else []), *operands, *after)


def near_call(kernel, name, outs, args, scratch=(), flags=None, after=(), cost=SHORT):
    vmem = pl.BlockSpec(memory_space=pltpu.VMEM)
    specs = [vmem] * len(args)
    if flags is not None:
        specs = [pl.BlockSpec(memory_space=pltpu.SMEM)] + specs
        args = [flags] + list(args)
    return pl.pallas_call(
        waiting(kernel, len(args), len(after)),
        in_specs=specs + [pl.BlockSpec(memory_space=pl.ANY)] * len(after),
        out_specs=[vmem] * len(outs),
        out_shape=[jax.ShapeDtypeStruct(shape, kind) for shape, kind in outs],
        scratch_shapes=list(scratch),
        compiler_params=pltpu.CompilerParams(vmem_limit_bytes=NEAR_VMEM),
        cost_estimate=cost_of(cost),
        name=name,
    )(*args, *after)


QKV = slice(0, 3)


def chunks(hidden, size=CHUNK):
    return [slice(at, at + size) for at in range(0, hidden, size)]


def wide_pieces(hidden):
    return [(slice(None), span) for span in chunks(hidden)]


def mlp_fetches(layer, up_at, down_at, hidden, size=CHUNK):
    found = []
    for span in chunks(hidden, size):
        found += [(up_at, (layer, slice(None), span)), (down_at, (layer, span))]
    return found


def attend_views(pairs, query, key, value, row_marks, key_marks, weights, share, mixed):
    places = [(p, index) for p in pairs for index in range(PADDED // VB)]
    units = []
    for p, index in places:
        lanes = pl.ds(pl.multiple_of(p * PAIR, PAIR), PAIR)
        rows = slice(index * VB, (index + 1) * VB)
        keys = jnp.concatenate([key[rows, lanes], key_marks[rows, :]], axis=1)
        turned = value[rows, lanes].T
        for head in range(2):
            across = jnp.concatenate([turned[head * HD : (head + 1) * HD], jnp.ones((16, VB), BF)], axis=0)
            units.append((score_side(query[rows, lanes], row_marks[rows, :], head), keys, across))
    done = attend_heads(units)
    for at, (p, index) in enumerate(places):
        lanes = pl.ds(pl.multiple_of(p * PAIR, PAIR), PAIR)
        rows = slice(index * VB, (index + 1) * VB)
        for head in range(2):
            weights[index, 2 * p + head, :, :VB] = done[2 * at + head][0]
            share[index, p, head : head + 1, :] = done[2 * at + head][2]
        pair = [done[2 * at + head][1] for head in range(2)]
        mixed[rows, lanes] = jnp.concatenate(pair, axis=0).T.astype(BF)


def climb_kernel(flags, fetched, stores, rows_all, mixed_all, row_marks, key_marks):
    x, edge, gain, bias, w_first, w_out, ff_bias, out_bias = fetched[:8]
    mlp, (language, w_lang, w_qkv) = fetched[8:-3], fetched[-3:]
    first, rest = stores[:7], stores[7:]
    normed_one, query_all, key_all, value_all, mixed, weights, share = first
    after, normed, active, slope, state, next_normed, query, kv, feats, lang_normed, lang_kv = rest
    klass, side = flags[0], flags[1]
    own, far = view_spots(side)
    rows_all[own, :] = x[...]
    rows_all[far, :] = edge[...]
    row_marks[...] = view_row_marks()
    key_marks[...] = view_key_marks(klass)
    unit, scale = centre(rows_all[...].astype(F32))
    low = (unit * gain[0, 0:1] + bias[0, 0:1]).astype(BF)
    key_all[...] = matmul(low, w_first[1]).astype(BF)
    key_all.send()
    value_all[...] = matmul(low, w_first[2]).astype(BF)
    value_all.send()
    query_all[...] = (matmul(low, w_first[0]) * 0.125).astype(BF)
    query_all.send()
    rows_all[...] = low
    normed_one[...] = rows_all[own, :]
    normed_one.send()

    def pair(p, carry):
        attend_views(
            (2 * p, 2 * p + 1), query_all.buffer, key_all.buffer, value_all.buffer, row_marks, key_marks, weights.buffer,
            share.buffer, mixed_all,
        )
        return carry

    lax.fori_loop(0, HEADS // 4, pair, 0)
    weights.send()
    share.send()
    mixed[...] = mixed_all[own, :]
    mixed.send()

    total = x[...].astype(F32) + matmul(mixed[...], w_out[...])
    after[...] = total
    after.send()
    unit, scale = centre(total)
    low = (unit * gain[0, 1:2] + bias[0, 1:2]).astype(BF)
    normed[...] = low
    normed.send()
    total = total + out_bias[0:1, :]
    for at in range(0, len(mlp), 2):
        span = slice(at // 2 * CHUNK, (at // 2 + 1) * CHUNK)
        grown, rise = gelu_both(matmul(low, mlp[at][...]) + ff_bias[0:1, span])
        grown = grown.astype(BF)
        active[:, span] = grown
        active.send(at // 2)
        slope[:, span] = rise.astype(BF)
        slope.send(at // 2)
        total = total + matmul(grown, mlp[at + 1][...])
    found = matmul(language[...], w_lang[...])
    feats[...] = found
    feats.send()
    unit, scale = centre(found)
    low = (unit * gain[1, 0:1] + bias[1, 0:1]).astype(BF)
    lang_normed[...] = low
    lang_normed.send()
    both = mix(matmul(low, w_qkv[1]).astype(BF), matmul(low, w_qkv[2]).astype(BF))
    lang_kv[...] = both
    lang_kv.send()
    kv[ROWS:] = both[:LONE]
    state[...] = total
    state.send()
    unit, scale = centre(total)
    low = (unit * gain[1, 0:1] + bias[1, 0:1]).astype(BF)
    next_normed[...] = low
    next_normed.send()
    kv[:ROWS] = mix(matmul(low, w_qkv[1]).astype(BF), matmul(low, w_qkv[2]).astype(BF))
    kv.send()
    query[...] = (matmul(low, w_qkv[0]) * 0.125).astype(BF)


def far_rows(flags):
    return (pl.ds(pl.multiple_of(flags[1] * (ROWS - EDGE), 16), EDGE),)


def climb(flags, x, edge, gain, bias, w_attn, w_up, ff_bias, w_down, out_bias, language, w_lang):
    rows, width = x.shape
    hidden = w_up.shape[2]
    blocks = PADDED // VB
    return dense_call(
        climb_kernel,
        "climb",
        (x, edge, gain, bias, w_attn, ff_bias, out_bias, w_up, w_down, language, w_lang),
        [(0, None), (1, far_rows), (2, None), (3, None), (4, (0, QKV)), (4, (0, 3)), (5, None), (6, None)]
        + mlp_fetches(0, 7, 8, hidden)
        + [(9, None), (10, None), (4, (1, QKV))],
        [
            ((rows, width), BF),
            ((PADDED, width), BF),
            ((PADDED, width), BF),
            ((PADDED, width), BF),
            ((rows, width), BF),
            ((blocks, HEADS, VB, VB_UP), BF),
            ((blocks, HEADS // 2, 8, VB), F32),
            ((rows, width), F32),
            ((rows, width), BF),
            ((rows, hidden), BF),
            ((rows, hidden), BF),
            ((rows, width), F32),
            ((rows, width), BF),
            ((rows, width), BF),
            ((rows + LONE, 2 * width), BF),
            ((LPAD, width), F32),
            ((LPAD, width), BF),
            ((LPAD, 2 * width), BF),
        ],
        LONG,
        [
            pltpu.VMEM((PADDED, width), BF),
            pltpu.VMEM((PADDED, width), BF),
            pltpu.VMEM((PADDED, PAIR), BF),
            pltpu.VMEM((PADDED, PAIR), BF),
        ],
        flags,
        pieces={9: wide_pieces(hidden), 10: wide_pieces(hidden)},
        lead=5,
        room=DENSE_VMEM,
    )


def put_up(held, at, grad):
    width = grad.shape[0]
    rows = width // SLICES
    for place in range(0, grad.shape[1], width):
        put_rows(held, (at + place) // width * rows, grad[:, place : place + width])


def put_down(held, at, start, grad):
    rows = DOWN_ROWS
    for piece in range(grad.shape[0] // rows):
        held[at // rows + piece, start : start + rows, :] = grad[piece * rows : (piece + 1) * rows]


def put_rows(held, place, grad):
    rows = grad.shape[0] // SLICES
    for piece in range(SLICES):
        held[piece, place : place + rows, :] = grad[piece * rows : (piece + 1) * rows]


def mlp_tail(layer, grad, grad_normed, unit, scale, gain, mixed, w_out, ups, place, out_grad, out_mixed, small):
    width = unit.shape[1]
    grad_state, grad_gain, grad_bias = norm_back(grad_normed, unit, scale, gain[layer, 1:2])
    grad = grad + grad_state
    out_grad[...] = grad
    out_grad.send()
    small[1:2, :width] = grad_gain
    small[1:2, width : 2 * width] = grad_bias
    low = grad.astype(BF)
    put_rows(ups, place, mat_left(mixed[...], low).astype(BF))
    out_mixed[...] = mat_right(low, w_out[...]).astype(BF)
    out_mixed.send()


def mlp_chunk(span, low, grad_low, slope, w_up, w_down, ups, small):
    grad_hidden = slope * mat_right(grad_low, w_down)
    hidden_low = grad_hidden.astype(BF)
    put_up(ups, span.start, mat_left(low, hidden_low).astype(BF))
    small[0:1, span] = jnp.sum(hidden_low.astype(F32), axis=0, keepdims=True)
    return mat_right(hidden_low, w_up)


def joint_scores(query, marks, keys, key_marks, p, head):
    lanes = pl.ds(pl.multiple_of(p * PAIR, PAIR), PAIR)
    return mat_right(
        jnp.concatenate([keys[:, lanes], key_marks[...]], axis=1), score_side(query[:, lanes], marks[...], head)
    )


def crest_kernel(
    flags, fetched, stores, probs, weights, keys, values, key_marks, marks, scores, peaks, held, copied
):
    query, kv, far, lang, x, w_out, gain, bias, ff_bias, cotangent = fetched[:10]
    mlp = fetched[10:]
    mixed, share, out_grad, out_mixed, keep, send, small, outs = stores
    klass, side = flags[0], flags[1]
    query, kv, far, lang = query.ref(), kv.ref(), far.ref(), lang.ref()
    x.more(len(fetched))

    @pl.when(klass != 1)
    def empty():
        keys[ROWS:] = jnp.zeros((KEYS - ROWS, keys.shape[1]), BF)
        values[ROWS:] = jnp.zeros((KEYS - ROWS, values.shape[1]), BF)

    key_marks[...] = joint_key_marks(klass)
    marks[...] = joint_row_marks()

    def put(rows, block):
        for p in range(HEADS // 2):
            lanes = slice(p * PAIR, (p + 1) * PAIR)
            keys[rows, lanes] = block[:, 2 * p * PAIR : (2 * p + 1) * PAIR]
            values[rows, lanes] = block[:, (2 * p + 1) * PAIR : (2 * p + 2) * PAIR]

    joint_place(klass, side, kv, far, lang, put)

    def copy_out(p, head):
        return pltpu.make_async_copy(held.at[head], probs.at[2 * p + head], copied.at[head])

    def one(p, head, turned):
        across = jnp.concatenate([turned[head * HD : (head + 1) * HD], jnp.ones((16, KEYS), BF)], axis=0)
        found = jnp.exp(scores[head, :, :ROWS] - peaks[head]).astype(BF)
        held[head, :, :ROWS] = found
        copy_out(p, head).start()
        out = matmul(across, found)
        part = 1.0 / out[HD : HD + 1]
        share[p, head : head + 1, :] = part
        return out[:HD] * part

    for head in range(2):
        copy_out(0, head).start()
    def form(p, head):
        found = joint_scores(query, marks, keys, key_marks, p, head)
        scores[head, :, :ROWS] = found
        peaks[head] = jnp.max(found, axis=0, keepdims=True)

    form(0, 0)

    def pair(p, carry, last=False):
        lanes = pl.ds(pl.multiple_of(p * PAIR, PAIR), PAIR)
        turned = values[:, lanes].T
        copy_out(p, 0).wait()
        form(p, 1)
        first = one(p, 0, turned)
        copy_out(p, 1).wait()
        if not last:
            form(p + 1, 0)
        second = one(p, 1, turned)
        mixed.buffer[:, lanes] = jnp.concatenate([first, second], axis=0).T.astype(BF)
        return carry

    lax.fori_loop(0, HEADS // 2 - 1, pair, 0)
    pair(HEADS // 2 - 1, 0, True)
    mixed.send()
    share.send()

    small[...] = jnp.zeros(small.buffer.shape, F32)
    total = x[...] + matmul(mixed[...], w_out[...])
    width = total.shape[1]
    hidden = len(mlp) // 2 * SHORT_CHUNK
    unit, scale = centre(total)
    low = (unit * gain[1, 1:2] + bias[1, 1:2]).astype(BF)
    grad_low = cotangent[...]
    grad = grad_low.astype(F32)
    small[1:2, 2 * width : 3 * width] = jnp.sum(grad, axis=0, keepdims=True)
    grad_normed = None
    for at, span in enumerate(chunks(hidden, SHORT_CHUNK)):
        w_up, w_down = mlp[2 * at][...], mlp[2 * at + 1][...]
        value, rise = gelu_both(matmul(low, w_up) + ff_bias[1:2, span])
        part = mlp_chunk(span, low, grad_low, rise, w_up, w_down, weights, small)
        put_down(weights, span.start, DOWN_ROWS, mat_left(value.astype(BF), grad_low).astype(BF))
        grad_normed = part if grad_normed is None else grad_normed + part
    hand_out(weights, (keep, send), flags, PLAIN)
    send.send()
    keep.send()
    mlp_tail(1, grad, grad_normed, unit, scale, gain, mixed, w_out, outs.buffer, 0, out_grad, out_mixed, small)
    for head in range(2):
        copy_out(HEADS // 2 - 1, head).wait()


def crest(flags, query, kv, far, lang, x, gain, bias, w_attn, w_up, ff_bias, w_down, cotangent):
    rows, width = x.shape
    hidden = w_up.shape[2]
    held = 2 * hidden // SLICES
    done = dense_call(
        crest_kernel, "crest",
        (query, kv, far, lang, x, w_attn, gain, bias, ff_bias, cotangent, w_up, w_down),
        [(0, None), (1, None), (2, None), (3, None), (4, None), (5, (1, 3))]
        + [(at, None) for at in range(6, 10)]
        + mlp_fetches(1, 10, 11, hidden, SHORT_CHUNK),
        [((rows, width), BF), ((HEADS // 2, 8, rows), F32), ((rows, width), F32), ((rows, width), BF)]
        + part_shapes(PLAIN, held, width)
        + [((8, hidden), F32), ((SLICES, width // SLICES, width), BF)],
        LONG,
        [
            pltpu.VMEM((SLICES, held, width), BF),
            pltpu.VMEM((KEYS, width), BF),
            pltpu.VMEM((KEYS, width), BF),
            pltpu.VMEM((KEYS, PAIR), BF),
            pltpu.VMEM((rows, PAIR), BF),
            pltpu.VMEM((2, KEYS, ROWS_UP), F32),
            pltpu.VMEM((2, 1, rows), F32),
            pltpu.VMEM((2, KEYS, ROWS_UP), BF),
            pltpu.SemaphoreType.DMA((2,)),
        ],
        flags,
        lead=4,
        room=DENSE_VMEM,
        raw=[((HEADS, KEYS, ROWS_UP), BF)],
    )
    return (done[0], done[8], done[1], done[2], done[3], done[4:6], done[6], done[7])


def leave_grad(unit, scale, gain, grad, grad_query, grad_key, grad_value, w_qkv):
    grad_normed = mat_right(grad_query, w_qkv[0]) * 0.125
    grad_normed = grad_normed + mat_right(grad_key, w_qkv[1]) + mat_right(grad_value, w_qkv[2])
    grad_state, grad_gain, grad_bias = norm_back(grad_normed, unit, scale, gain)
    return (grad + grad_state, grad_gain, grad_bias)


def leave_kernel(flags, fetched, stores, sums, held):
    query, normed, kv, far, x, gain, w_qkv, grad = fetched[:8]
    out, keep, send, token = stores
    token[...] = jnp.zeros(token.buffer.shape, F32)
    grad_query, low = query[...], normed[...]
    width = low.shape[1]
    place = width // SLICES
    put_rows(held, 0, (mat_left(low, grad_query) * 0.125).astype(BF))
    sums[...] = kv[...].astype(F32)
    rows = pl.ds(pl.multiple_of((1 - flags[1]) * (ROWS - EDGE), 16), EDGE)
    sums[rows, :] += far[...].astype(F32)
    grad_key, grad_value = unmix(sums[...].astype(BF))
    unit, scale = centre(x[...].astype(F32))
    total, grad_gain, grad_bias = leave_grad(
        unit, scale, gain[0, 0:1], grad[...], grad_query, grad_key, grad_value, w_qkv
    )
    out[...] = total
    out.send()
    put_rows(held, place, mat_left(low, grad_key).astype(BF))
    put_rows(held, 2 * place, mat_left(low, grad_value).astype(BF))
    put_small(held, 3 * place, fetched[8:], grad_gain, grad_bias)
    hand_out(held, (keep, send), flags, LAST)


SMALL_ROWS = 32


def put_small(held, place, small, grad_gain, grad_bias):
    width = grad_gain.shape[1]
    rows = [grad_gain, small[0][1:2, :width], small[2][0:1, :width], small[1][1:2, :width]]
    rows += [grad_bias, small[0][1:2, width : 2 * width], small[2][0:1, width : 2 * width]]
    rows += [small[1][1:2, width : 2 * width]]
    rows += [small[at][1:2, 2 * width : 3 * width] for at in range(2)]
    block = jnp.concatenate(rows, axis=0)
    long = jnp.concatenate([small[at][0:1, :] for at in range(2)], axis=0)
    each, more = width // SLICES, long.shape[1] // SLICES
    for piece in range(SLICES):
        head = jnp.pad(block[:, piece * each : (piece + 1) * each], ((0, 0), (0, more - each)))
        tail = long[:, piece * more : (piece + 1) * more]
        rest = jnp.zeros((SMALL_ROWS - head.shape[0] - tail.shape[0], more), F32)
        both = jnp.concatenate([head, tail, rest], axis=0).astype(BF)
        held[piece, place : place + SMALL_ROWS, :] = jnp.pad(both, ((0, 0), (0, width - more)))


def leave(flags, x, gain, normed, grad, query, kv, far, w_attn, smalls, after):
    rows, width = x.shape
    held = 3 * (width // SLICES) + SMALL_ROWS
    done = dense_call(
        leave_kernel, "leave",
        (query, normed, kv, far, x, gain, w_attn, grad, *smalls),
        [(at, None) for at in range(6)] + [(6, (0, QKV))] + [(at, None) for at in range(7, 11)],
        [((rows, width), F32)] + part_shapes(LAST, held, width) + [((8, PAIR), F32)],
        4.0,
        [pltpu.VMEM((rows, 2 * width), F32), pltpu.VMEM((SLICES, held, width), BF)],
        flags,
        after,
        lead=8,
        room=30 * 2**20,
    )
    return (done[0], done[1:3], done[3])


def put_sums(klass, side, sums, lang_sums, kv, here, far, own, lone, there):
    @pl.when(klass == 1)
    def fine():
        sums[:, here] = (kv[:, here].astype(F32) + far[:ROWS, there].astype(F32)).astype(BF)

        @pl.when(side == 0)
        def owner():
            lang_sums[:LONE, here] = (lone[:, there].astype(F32) + far[ROWS:, there].astype(F32)).astype(BF)

    @pl.when(klass != 1)
    def coarse():
        sums[:, here] = kv[:, here]
        lang_sums[:, here] = own[:, there]


def descend_kernel(flags, fetched, stores, sums, lang_sums, plain, split):
    query, normed, x, kv = fetched[:4]
    fars, owns, lones = fetched[4:6], fetched[6:8], fetched[8:10]
    w_qkv, gain, grad, low_normed = fetched[10:14]
    mlp, (after, mixed, w_out, lang_normed, feats, language, w_lang, later) = fetched[14:-8], fetched[-8:]
    out_grad, out_mixed, grad_language, keep, send, split_keep, split_send, small, small_mid = stores
    klass, side = flags[0], flags[1]
    small[...] = jnp.zeros(small.buffer.shape, F32)
    small_mid[...] = jnp.zeros(small_mid.buffer.shape, F32)
    lang_sums[...] = jnp.zeros_like(lang_sums)
    grad_query, low = query[...], normed[...]
    width = low.shape[1]
    place = width // SLICES
    hidden = len(mlp) // 4 * CHUNK
    up_rows = hidden // SLICES
    put_rows(plain, up_rows, (mat_left(low, grad_query) * 0.125).astype(BF))
    unit, scale = centre(x[...])
    kv = kv.ref()
    fars, owns, lones = [[part.ref() for part in parts] for parts in (fars, owns, lones)]
    for pair in range(HEADS // 2):
        for which in range(2):
            there = slice(pair * PAIR, (pair + 1) * PAIR)
            here = slice((2 * pair + which) * PAIR, (2 * pair + which + 1) * PAIR)
            put_sums(klass, side, sums, lang_sums, kv, here, fars[which], owns[which], lones[which], there)

    grad_key, grad_value = unmix(sums[...])
    grad, grad_gain, grad_bias = leave_grad(
        unit, scale, gain[1, 0:1], grad[...], grad_query, grad_key, grad_value, w_qkv
    )
    lang_key, lang_value = unmix(lang_sums[...])
    lang_low = lang_normed[...]
    put_rows(plain, up_rows + place, (mat_left(low, grad_key) + mat_left(lang_low, lang_key)).astype(BF))
    put_rows(split, DOWN_ROWS, (mat_left(low, grad_value) + mat_left(lang_low, lang_value)).astype(BF))
    lang_grad = mat_right(lang_key, w_qkv[1]) + mat_right(lang_value, w_qkv[2])
    unit, scale = centre(feats[...])
    grad_feats, lang_gain, lang_bias = norm_back(lang_grad, unit, scale, gain[1, 0:1])
    feats_low = grad_feats.astype(BF)
    put_rows(split, DOWN_ROWS + place, mat_left(language[...], feats_low).astype(BF))
    grad_language[...] = mat_right(feats_low, w_lang[...])
    grad_language.send()
    small_mid[0:1, :width] = grad_gain + lang_gain
    small_mid[0:1, width : 2 * width] = grad_bias + lang_bias

    grad_low = grad.astype(BF)
    small[1:2, 2 * width : 3 * width] = jnp.sum(grad_low.astype(F32), axis=0, keepdims=True)
    low = low_normed[...]
    grad_normed = None
    for at, span in enumerate(chunks(hidden)):
        w_down, rise, w_up, active = [part[...] for part in mlp[4 * at : 4 * at + 4]]
        part = mlp_chunk(span, low, grad_low, rise.astype(F32), w_up, w_down, plain, small)
        put_down(split, span.start, 0, mat_left(active, grad_low).astype(BF))
        grad_normed = part if grad_normed is None else grad_normed + part
    hand_out(plain, (keep, send), flags, PLAIN)
    send.send()
    keep.send()
    unit, scale = centre(after[...])
    mlp_tail(
        0, grad, grad_normed, unit, scale, gain, mixed, w_out, split, DOWN_ROWS + 2 * place, out_grad, out_mixed, small
    )
    split[:, DOWN_ROWS + 3 * place :, :] = later[...]
    hand_out(split, (split_keep, split_send), flags, SPLIT)


def descend(
    flags, state, gain, normed, grad, query, kv, fars, owns, w_attn, feats, lang_normed, language, w_lang,
    after, mixed, low_normed, active, slope, w_up, w_down, later, follows,
):
    rows, width = state.shape
    hidden = w_up.shape[2]
    place = width // SLICES
    plain, split = hidden // SLICES + 2 * place, DOWN_ROWS + 4 * place
    fetches = []
    for span in chunks(hidden):
        fetches += [(13, (0, span)), (14, (slice(None), span)), (12, (0, slice(None), span)), (15, (slice(None), span))]
    head, foot = slice(0, LPAD), slice(ROWS, ROWS + LONE)
    done = dense_call(
        descend_kernel, "descend",
        (query, normed, state, kv, *fars, *owns, w_attn, gain, grad, low_normed)
        + (w_up, w_down, slope, active, after, mixed, lang_normed, feats, language, w_lang, later),
        [(at, None) for at in range(6)]
        + [(at, (head,)) for at in range(6, 8)]
        + [(at, (foot,)) for at in range(6, 8)]
        + [(8, (1, QKV)), (9, None), (10, None), (11, None)]
        + fetches
        + [(16, None), (17, None), (8, (0, 3)), (18, None), (19, None), (20, None), (21, None), (22, None)],
        [((rows, width), F32), ((rows, width), BF), ((LPAD, width), F32)]
        + part_shapes(PLAIN, plain, width)
        + part_shapes(SPLIT, split, width)
        + [((8, hidden), F32), ((8, 2 * width), F32)],
        LONG,
        [
            pltpu.VMEM((rows, 2 * width), BF),
            pltpu.VMEM((LPAD, 2 * width), BF),
            pltpu.VMEM((SLICES, plain, width), BF),
            pltpu.VMEM((SLICES, split, width), BF),
        ],
        flags,
        follows,
        lead=6,
    )
    return (done[0], done[1], done[2], done[3:5], done[5:7], done[7], done[8])


def pair_swap(block):
    count = lax.axis_size("wide")
    return lax.ppermute(block, "wide", [(at, at ^ 1) for at in range(count)])


class Flow:
    def __init__(self, route, parts):
        self.route, self.step = route, 0
        self.units = route.units
        self.keep = [parts[0]]
        self.send(parts)

    def send(self, parts):
        self.got = []
        if self.step < len(self.route.steps):
            bits = self.route.steps[self.step]
            self.units //= 1 << len(bits)
            for at, part in enumerate(parts[1:], 1):
                found = [bit for place, bit in enumerate(bits) if at >> (len(bits) - 1 - place) & 1]
                self.got.append(self.move(part, found))
        else:
            self.keep = [parts[0]]
            self.got.append(self.move(parts[0], [0] if self.route.halves else None))

    def move(self, part, bits):
        shift = 1 if self.route.halves else 0
        if bits is None or bits == [0] and shift:
            return lax.ppermute(part, "narrow", [(0, 1), (1, 0)])
        count = lax.axis_size("wide")
        stride = sum((count // SLICES) << (bit - shift) for bit in bits)
        return lax.ppermute(part, "wide", [(p, p ^ stride) for p in range(count)])


def step_kernel(layout, ins, outs):
    at = 0
    for out, (count, rows) in zip(outs, layout):
        total = None
        for term in ins[at : at + count]:
            part = term[rows] if rows is not None else term[...]
            total = part.astype(F32) if total is None else total + part.astype(F32)
        out[...] = total.astype(BF)
        if isinstance(out, Store):
            out.send()
        at += count


def step(flows, after=(), near=False, cost=SHORT, lazy=False):
    operands, fetches, layout, outs, plan = [], [], [], [], []
    for flow in flows:
        flow.step += 1
        terms = flow.keep + flow.got
        last = flow.step == len(flow.route.steps)
        count = 1 if last else flow.route.parts(flow.step)
        each = flow.units // count
        made = [part for part in range(count) if part or last or not lazy]
        for part in reversed(made):
            rows = slice(part * each, (part + 1) * each)
            for term in terms:
                fetches.append((len(operands), rows))
                operands.append(term)
            layout.append((len(terms), rows))
            outs.append(((each,) + terms[0].shape[1:], BF))
        plan.append((flow, terms, count, made))
    if near:
        done = near_call(
            lambda *refs: step_kernel(layout, refs[: len(operands)], refs[len(operands) :]),
            "step", outs, operands, after=after, cost=cost,
        )
    else:
        done = dense_call(
            lambda ins, stores: step_kernel([(count, None) for count, rows in layout], ins, stores),
            "step", operands, fetches, outs, cost, after=after, lead=len(fetches), room=STEP_VMEM,
        )
    at = 0
    for flow, terms, count, made in plan:
        parts = [None] * count
        for part in reversed(made):
            parts[part] = done[at]
            at += 1
        flow.keep = terms if parts[0] is None else [parts[0]]
        flow.send(parts)
    return done


def split_low(buffer):
    count = lax.axis_size("wide")
    position = lax.axis_index("wide")
    half = count // SLICES
    while half > 1:
        half //= 2
        mine = position // half % 2
        size = buffer.shape[0] // 2
        send = lax.dynamic_slice_in_dim(buffer, (1 - mine) * size, size, 0)
        keep = lax.dynamic_slice_in_dim(buffer, mine * size, size, 0)
        buffer = keep + lax.ppermute(send.astype(BF), "wide", [(p, p ^ half) for p in range(count)])
    return buffer


def finish_kernel(
    flags, first, first_got, plain, plain_got, split, split_got, attn_one, attn_one_got,
    lang, attn, ups, downs, gains, biases, ff_biases, out_biases, whole, last,
):
    rows, width = attn.shape[2:]
    up_rows, down_rows = ups.shape[2] // width * rows, downs.shape[1]

    def both(buffer, got):
        return buffer[0].astype(F32) + got[0].astype(F32)

    def put_ups(layer, found):
        for at in range(ups.shape[2] // width):
            ups[layer, :, at * width : (at + 1) * width] = found[at * rows : (at + 1) * rows]

    found = both(first, first_got)
    put_ups(1, found)
    downs[1] = found[up_rows:]
    found = both(plain, plain_got)
    put_ups(0, found)
    attn[1, 0] = found[up_rows : up_rows + rows]
    attn[1, 1] = found[up_rows + rows :]
    whole[flags[3]] = split[0].astype(F32)
    whole[1 - flags[3]] = split_got[0].astype(F32)
    found = jnp.concatenate([whole[0], whole[1]], axis=0)
    downs[0] = found[:down_rows]
    attn[1, 2] = found[down_rows : down_rows + rows]
    lang[...] = found[down_rows + rows : down_rows + 2 * rows]
    attn[0, 3] = found[down_rows + 2 * rows : down_rows + 3 * rows]
    attn[1, 3] = found[down_rows + 3 * rows :]
    last[flags[3]] = attn_one[0].astype(F32)
    last[1 - flags[3]] = attn_one_got[0].astype(F32)
    found = jnp.concatenate([last[0], last[1]], axis=0)
    for at in range(3):
        attn[0, at] = found[at * rows : (at + 1) * rows]
    small = found[3 * rows :]
    for layer in range(2):
        gains[layer] = small[2 * layer : 2 * layer + 2, :rows]
        biases[layer] = small[4 + 2 * layer : 6 + 2 * layer, :rows]
    out_biases[...] = small[8:10, :rows]
    ff_biases[...] = small[10:12, : ff_biases.shape[1]]


def finish(flags, flows, width, hidden):
    rows = width // SLICES
    args = []
    for flow in flows:
        args += flow.keep + flow.got
    return near_call(
        finish_kernel, "finish",
        [
            ((rows, width), F32),
            ((2, 4, rows, width), F32),
            ((2, rows, hidden), F32),
            ((2, hidden // SLICES, width), F32),
            ((2, 2, rows), F32),
            ((2, 2, rows), F32),
            ((2, hidden // SLICES), F32),
            ((2, rows), F32),
        ],
        args,
        [
            pltpu.VMEM((2, (DOWN_ROWS + 4 * rows) // 2, width), F32),
            pltpu.VMEM((2, (3 * rows + SMALL_ROWS) // 2, width), F32),
        ],
        flags,
    )


def body(
    patches,
    language,
    w_lang,
    w_attn,
    w_up,
    w_down,
    norm_gain,
    norm_bias,
    ff_bias,
    out_bias,
    cotangent,
    classes,
):
    position = lax.axis_index("wide")
    wide = lax.axis_size("wide")
    side = position % 2
    klass = lax.dynamic_index_in_dim(classes[0], position // 2, 0, keepdims=False)
    high = position // (wide // SLICES)
    flags = jnp.stack([klass, side, high, lax.axis_index("narrow")]).astype(jnp.int32)
    width = w_lang.shape[0]
    hidden = w_up.shape[2]
    start = patches[0]
    lang_low = jnp.pad(language[0], ((0, LPAD - language.shape[1]), (0, 0)))

    other = pair_swap(start)
    normed_a, query_a, key_a, value_a, mixed_a, weights_a, share_a, *rest = climb(
        flags, start, other, norm_gain, norm_bias, w_attn, w_up, ff_bias, w_down, out_bias, lang_low, w_lang
    )
    after_a, normed_b, active_b, slope_b, state_b, normed_c, query_c, kv_c, feats, lang_normed, lang_kv = rest
    far_c = pair_swap(kv_c)
    mixed_c, weights_c, share_c, grad, grad_mixed_c, parts, small_two, outs_two = crest(
        flags, query_c, kv_c, far_c, lang_kv, state_b, norm_gain, norm_bias, w_attn, w_up, ff_bias, w_down,
        cotangent[0],
    )
    first = Flow(PLAIN, parts)
    joint = (flags, query_c, kv_c, far_c, lang_kv, mixed_c, weights_c, share_c, grad_mixed_c)
    query, kv, *edges, token = joint_backward(*joint, 0, HEADS // 2)
    fars = [pair_swap(part) for part in edges]
    done = step([first], [token], lazy=True)
    grad, grad_mixed_a, grad_language, plain_parts, split_parts, small_one, small_mid = descend(
        flags, state_b, norm_gain, normed_c, grad, query, kv, fars, edges, w_attn, feats, lang_normed, lang_low,
        w_lang, after_a, mixed_a, normed_b, active_b, slope_b, w_up, w_down, outs_two, done,
    )
    plain, split = Flow(PLAIN, plain_parts), Flow(SPLIT, split_parts)

    done = step([first], [small_mid], lazy=True, cost=30.0)
    done = step([plain, split], [done[0]])
    view = (flags, query_a, key_a, value_a, mixed_a, weights_a, share_a, grad_mixed_a)
    query, kv, edge, token = view_backward(*view, 0, HEADS // 2, done)
    far = pair_swap(edge)
    done = step([first], [token])
    grad, attn_parts, token = leave(
        flags, start, norm_gain, normed_a, grad, query, kv, far, w_attn, (small_one, small_two, small_mid), done
    )
    attn_one = Flow(LAST, attn_parts)

    done = step([plain, split], [token], near=True, cost=LONG)
    done = step([attn_one], [done[0]], near=True)
    done = step([first], [done[0]], near=True, cost=5.0)
    done = step([plain, split], [done[0]], near=True)
    done = step([attn_one], [done[0]], near=True)
    done = step([plain, split], [done[0], first.got[0]], near=True)
    done = step([attn_one], [done[0]], near=True)
    done = step([split], [done[0]], near=True)
    done = step([attn_one], [done[0], plain.got[0]], near=True)
    flows = (first, plain, split, attn_one)
    grad_w_lang, grad_w_attn, grad_w_up, grad_w_down, *vectors = finish(flags, flows, width, hidden)
    gains, biases, ff_biases, out_biases = vectors

    def own(values, dim):
        if wide == SLICES:
            return values
        values = jnp.moveaxis(values, dim, 0)
        return jnp.moveaxis(split_low(values), 0, dim)

    return (
        grad[None],
        grad_language[None, : language.shape[1]],
        own(grad_w_lang, 0),
        own(grad_w_attn, 2),
        own(grad_w_up, 1),
        own(grad_w_down, 1),
        own(gains, 2),
        own(biases, 2),
        own(ff_biases, 1),
        own(out_biases, 1),
    )


def solution(mesh):
    in_specs = (
        P("narrow", "wide", None),
        P("narrow", "wide", None),
        P(),
        P(),
        P(),
        P(),
        P(),
        P(),
        P(),
        P(),
        P("narrow", "wide", None),
        P("narrow", None),
    )
    out_specs = (
        P("narrow", "wide", None),
        P("narrow", "wide", None),
        P("wide", None),
        P(None, None, "wide", None),
        P(None, "wide", None),
        P(None, "wide", None),
        P(None, None, "wide"),
        P(None, None, "wide"),
        P(None, "wide"),
        P(None, "wide"),
    )
    return jax.shard_map(body, mesh=mesh, in_specs=in_specs, out_specs=out_specs, check_vma=False)
```

```python
import functools

import jax
import jax.numpy as jnp
from jax import lax
from jax.experimental import pallas as pl
from jax.experimental.pallas import tpu as pltpu
from jax.sharding import PartitionSpec as P

HEADS = 8
HD = 64
LANG = 77
VB = 288
VS = 72
ROWS = 720
EDGE = VB // 2
PADDED = ROWS + EDGE
LPAD = 160
LONE = 96
KEYS = 2 * ROWS + LONE
PAIR = 2 * HD
SLICES = 16
ROWS_UP = 768
VB_UP = 384
STEP_VMEM = 20 * 2**20
LONG, SHORT = 60.0, 0.5
JOINT_VMEM = 60 * 2**20
JOINT_BACK_VMEM = 60 * 2**20
VIEW_VMEM = 36 * 2**20
DENSE_VMEM = 60 * 2**20
NEAR_VMEM = 16 * 2**20

epsilon = 1e-05
masked_out = -1e30
BF = jnp.bfloat16
F32 = jnp.float32


def matmul(left, right):
    return jnp.dot(left, right, preferred_element_type=F32)


def mat_left(left, right):
    return lax.dot_general(left, right, (((0,), (0,)), ((), ())), preferred_element_type=F32)


def mat_right(left, right):
    return lax.dot_general(left, right, (((1,), (1,)), ((), ())), preferred_element_type=F32)


def cost_of(microseconds):
    return pl.CostEstimate(flops=int(microseconds * 1e9), bytes_accessed=1, transcendentals=0)


def waiting(kernel, inputs, more):
    if not more:
        return kernel

    def without(*refs):
        return kernel(*refs[:inputs], *refs[inputs + more :])

    return without


def lane_mask(head):
    lanes = lax.broadcasted_iota(jnp.int32, (1, PAIR), 1)
    return jnp.where(lanes // HD == head, 1.0, 0.0).astype(BF)


def in_half(shape):
    return lax.broadcasted_iota(jnp.int32, shape, 1) % HD


def row_of(shape):
    return lax.broadcasted_iota(jnp.int32, shape, 0)


def key_marks(allowed, items):
    lane = in_half(allowed.shape)
    marks = jnp.where(lane < items, jnp.where(allowed, 0.0, masked_out), 0.0)
    return jnp.where((lane >= 4) & (lane < 7), 1.0, marks).astype(BF)


def joint_key_marks(klass):
    shape = (KEYS, PAIR)
    row, lane = row_of(shape), in_half(shape)
    first = (row < ROWS // 2) | ((row >= ROWS) & (row < ROWS + LANG))
    second = ((row >= ROWS // 2) & (row < ROWS)) | ((row >= ROWS + LANG) & (row < ROWS + 2 * LANG))
    fine = jnp.where(row < 2 * ROWS + LANG, 1, 0)
    coarse = jnp.where(lane == 0, jnp.where(first, 1, 0), jnp.where(second, 1, 0))
    return key_marks(jnp.where(klass == 1, fine, coarse) == 1, 2)


def joint_row_marks():
    shape = (ROWS, PAIR)
    row, lane = row_of(shape), in_half(shape)
    return jnp.where(lane == row // (ROWS // 2), 1.0, 0.0).astype(BF)


def view_key_marks(klass):
    shape = (PADDED, PAIR)
    row, lane = row_of(shape), in_half(shape)
    same = jnp.where(lane == row % VB // VS, 1, 0)
    return key_marks(jnp.where(klass == 1, 1, same) == 1, 4)


def view_row_marks():
    shape = (PADDED, PAIR)
    row, lane = row_of(shape), in_half(shape)
    return jnp.where(lane == row % VB // VS, 1.0, 0.0).astype(BF)


def with_parts(values):
    lane = in_half(values.shape)
    high = values.astype(BF).astype(F32)
    rest = values - high
    middle = rest.astype(BF).astype(F32)
    low = rest - middle
    picked = jnp.where(lane == 4, -high, jnp.where(lane == 5, -middle, jnp.where(lane == 6, -low, 0.0)))
    return picked.astype(BF)


def attend_heads(units):
    scores = [mat_right(keys, right) for right, keys, across in units]
    weights = [jnp.exp(part - jnp.max(part, axis=0, keepdims=True)).astype(BF) for part in scores]
    outs = [matmul(unit[2], part) for unit, part in zip(units, weights)]
    shares = [1.0 / out[HD : HD + 1] for out in outs]
    return [(part, out[:HD] * share, share) for part, out, share in zip(weights, outs, shares)]


def score_side(query, marks, head):
    mask = lane_mask(head)
    return jnp.concatenate([query * mask, marks * mask], axis=1)


def joint_place(klass, side, kv_ref, far_ref, lang_ref, put):
    put(slice(0, ROWS), kv_ref[:ROWS])

    @pl.when(klass == 1)
    def fine():
        put(slice(ROWS, 2 * ROWS), far_ref[:ROWS])

        @pl.when(side == 0)
        def own():
            put(slice(2 * ROWS, KEYS), lang_ref[:LONE])

        @pl.when(side == 1)
        def partner():
            put(slice(2 * ROWS, KEYS), far_ref[ROWS:])

    @pl.when(klass != 1)
    def coarse():
        put(slice(ROWS, ROWS + LPAD), lang_ref[...])


def inner_marks(grad, mixed):
    lanes = lax.broadcasted_iota(jnp.int32, (1, PAIR), 1)
    product = grad.astype(F32) * mixed.astype(F32)
    first = jnp.sum(jnp.where(lanes < HD, product, 0.0), axis=1, keepdims=True)
    second = jnp.sum(jnp.where(lanes < HD, 0.0, product), axis=1, keepdims=True)
    return with_parts(jnp.where(lanes < HD, first, second))


def attend_back(units):
    inner = [mat_right(unit[0], unit[5]) for unit in units]
    probs = [unit[2].astype(F32) * unit[3] for unit in units]
    grad_scores = [(left * right).astype(BF) for left, right in zip(probs, inner)]
    grad_values = [matmul(part.astype(BF), unit[5][:, :PAIR]) for part, unit in zip(probs, units)]
    grad_keys = [matmul(part, unit[4]) for part, unit in zip(grad_scores, units)]
    across = [matmul(unit[1], part) for part, unit in zip(grad_scores, units)]
    return list(zip(grad_keys, grad_values, across))


def fill_rows(left, grads, rows, query, grad, mixed):
    inner = inner_marks(grad, mixed)
    for head in range(2):
        mask = lane_mask(head)
        left[head, rows, :] = query * mask
        grads[head, rows, :PAIR] = grad * mask
        grads[head, rows, PAIR:] = inner * mask


def joint_backward_kernel(
    flags, q_ref, kv_ref, far_ref, lang_ref, mixed_ref, weights_ref, share_ref, grad_ref, dq_ref, dkv_ref,
    dfar_key, dfar_value, token, keys, values, across, left, grads,
):
    klass, side = flags[0], flags[1]

    @pl.when(pl.program_id(0) == 0)
    def prepare():
        keys[...] = jnp.zeros_like(keys)
        values[...] = jnp.zeros_like(values)
        values[:, PAIR:] = joint_key_marks(klass)

    def put(rows, block):
        keys[rows, :] = block[:, :PAIR]
        values[rows, :PAIR] = block[:, PAIR:]

    joint_place(klass, side, kv_ref, far_ref, lang_ref, put)
    token[...] = jnp.zeros_like(token)
    across[...] = keys[...].T
    fill_rows(left, grads, slice(0, ROWS), q_ref[...], grad_ref[...], mixed_ref[...])
    units = [
        (
            values[...],
            across[head * HD : (head + 1) * HD, :],
            weights_ref[head, :, :ROWS],
            share_ref[0, head : head + 1, :],
            left[head],
            grads[head],
        )
        for head in range(2)
    ]
    first, second = attend_back(units)
    for span, at, far in ((slice(0, PAIR), 0, dfar_key), (slice(PAIR, 2 * PAIR), 1, dfar_value)):
        both = (first[at] + second[at]).astype(BF)
        dkv_ref[:, span] = both[:ROWS]
        far[...] = both[ROWS:]
    dq_ref[...] = jnp.concatenate([first[2], second[2]], axis=0).T.astype(BF)


def joint_backward(flags, query, kv, far, lang, mixed, weights, share, grad, base, pairs, after=(), cost=LONG):
    rows = query.shape[0]
    one = pl.BlockSpec((rows, PAIR), lambda i, f: (0, i + base))
    return pl.pallas_call(
        waiting(joint_backward_kernel, 9, len(after)),
        grid_spec=pltpu.PrefetchScalarGridSpec(
            num_scalar_prefetch=1,
            grid=(pairs,),
            in_specs=[
                one,
                pl.BlockSpec((rows, 2 * PAIR), lambda i, f: (0, i + base)),
                pl.BlockSpec((ROWS + LONE, 2 * PAIR), lambda i, f: (0, i + base)),
                pl.BlockSpec((LPAD, 2 * PAIR), lambda i, f: (0, i + base)),
                one,
                pl.BlockSpec((2, KEYS, ROWS_UP), lambda i, f: (i + base, 0, 0)),
                pl.BlockSpec((1, 8, rows), lambda i, f: (i + base, 0, 0)),
                one,
            ]
            + [pl.BlockSpec(memory_space=pltpu.HBM)] * len(after),
            out_specs=[
                pl.BlockSpec((rows, PAIR), lambda i, f: (0, i)),
                pl.BlockSpec((rows, 2 * PAIR), lambda i, f: (0, i)),
                pl.BlockSpec((ROWS + LONE, PAIR), lambda i, f: (0, i)),
                pl.BlockSpec((ROWS + LONE, PAIR), lambda i, f: (0, i)),
                pl.BlockSpec((8, PAIR), lambda i, f: (0, 0)),
            ],
            scratch_shapes=[
                pltpu.VMEM((KEYS, PAIR), BF),
                pltpu.VMEM((KEYS, 2 * PAIR), BF),
                pltpu.VMEM((PAIR, KEYS), BF),
                pltpu.VMEM((2, ROWS, PAIR), BF),
                pltpu.VMEM((2, ROWS, 2 * PAIR), BF),
            ],
        ),
        out_shape=[
            jax.ShapeDtypeStruct((rows, pairs * PAIR), BF),
            jax.ShapeDtypeStruct((rows, 2 * pairs * PAIR), BF),
            jax.ShapeDtypeStruct((ROWS + LONE, pairs * PAIR), BF),
            jax.ShapeDtypeStruct((ROWS + LONE, pairs * PAIR), BF),
            jax.ShapeDtypeStruct((8, PAIR), F32),
        ],
        compiler_params=pltpu.CompilerParams(vmem_limit_bytes=JOINT_BACK_VMEM),
        cost_estimate=cost_of(cost),
        name="joint_backward",
    )(flags, query, kv, far, lang, mixed, weights, share, grad, *after)


def view_spots(side):
    own = pl.ds(pl.multiple_of(side * EDGE, 16), ROWS)
    far = pl.ds(pl.multiple_of((1 - side) * ROWS, 16), EDGE)
    return (own, far)


def view_backward_kernel(
    flags, q_ref, key_ref, value_ref, mixed_ref, weights_ref, share_ref, grad_ref, dq_ref, dkv_ref, dfar_ref,
    token, values, left, grads, back, dkv,
):
    klass, side = flags[0], flags[1]
    own, far = view_spots(side)

    @pl.when(pl.program_id(0) == 0)
    def prepare():
        for p in range(2):
            values[p, :, PAIR:] = view_key_marks(klass)
        left[...] = jnp.zeros_like(left)
        grads[...] = jnp.zeros_like(grads)

    units = []
    for p in range(2):
        lanes = slice(p * PAIR, (p + 1) * PAIR)
        values[p, :, :PAIR] = value_ref[:, lanes]
        fill_rows(left.at[p], grads.at[p], own, q_ref[own, lanes], grad_ref[:, lanes], mixed_ref[:, lanes])
    for p in range(2):
        lanes = slice(p * PAIR, (p + 1) * PAIR)
        for index in range(PADDED // VB):
            rows = slice(index * VB, (index + 1) * VB)
            across = key_ref[rows, lanes].T
            for head in range(2):
                units.append(
                    (
                        values[p, rows, :],
                        across[head * HD : (head + 1) * HD, :],
                        weights_ref[index, 2 * p + head, :, :VB],
                        share_ref[index, p, head : head + 1, :],
                        left[p, head, rows, :],
                        grads[p, head, rows, :],
                    )
                )
    done = attend_back(units)
    for p in range(2):
        for index in range(PADDED // VB):
            rows = slice(index * VB, (index + 1) * VB)
            at = 2 * (p * (PADDED // VB) + index)
            first, second = done[at], done[at + 1]
            dkv[rows, 2 * p * PAIR : (2 * p + 1) * PAIR] = (first[0] + second[0]).astype(BF)
            dkv[rows, (2 * p + 1) * PAIR : (2 * p + 2) * PAIR] = (first[1] + second[1]).astype(BF)
            back[rows, p * PAIR : (p + 1) * PAIR] = jnp.concatenate([first[2], second[2]], axis=0).T.astype(BF)

    dq_ref[...] = back[own, :]
    dkv_ref[...] = dkv[own, :]
    dfar_ref[...] = dkv[far, :]
    token[...] = jnp.zeros_like(token)


def view_backward(flags, query, key, value, mixed, weights, share, grad, base, pairs, after=(), cost=LONG):
    rows = mixed.shape[0]
    blocks = PADDED // VB
    one = pl.BlockSpec((rows, 2 * PAIR), lambda i, f: (0, i + base))
    tall = pl.BlockSpec((PADDED, 2 * PAIR), lambda i, f: (0, i + base))
    return pl.pallas_call(
        waiting(view_backward_kernel, 8, len(after)),
        grid_spec=pltpu.PrefetchScalarGridSpec(
            num_scalar_prefetch=1,
            grid=(pairs // 2,),
            in_specs=[
                tall,
                tall,
                tall,
                one,
                pl.BlockSpec((blocks, 4, VB, VB_UP), lambda i, f: (0, i + base, 0, 0)),
                pl.BlockSpec((blocks, 2, 8, VB), lambda i, f: (0, i + base, 0, 0)),
                one,
            ]
            + [pl.BlockSpec(memory_space=pltpu.HBM)] * len(after),
            out_specs=[
                pl.BlockSpec((rows, 2 * PAIR), lambda i, f: (0, i)),
                pl.BlockSpec((rows, 4 * PAIR), lambda i, f: (0, i)),
                pl.BlockSpec((EDGE, 4 * PAIR), lambda i, f: (0, i)),
                pl.BlockSpec((8, PAIR), lambda i, f: (0, 0)),
            ],
            scratch_shapes=[
                pltpu.VMEM((2, PADDED, 2 * PAIR), BF),
                pltpu.VMEM((2, 2, PADDED, PAIR), BF),
                pltpu.VMEM((2, 2, PADDED, 2 * PAIR), BF),
                pltpu.VMEM((PADDED, 2 * PAIR), BF),
                pltpu.VMEM((PADDED, 4 * PAIR), BF),
            ],
        ),
        out_shape=[
            jax.ShapeDtypeStruct((rows, pairs * PAIR), BF),
            jax.ShapeDtypeStruct((rows, 2 * pairs * PAIR), BF),
            jax.ShapeDtypeStruct((EDGE, 2 * pairs * PAIR), BF),
            jax.ShapeDtypeStruct((8, PAIR), F32),
        ],
        compiler_params=pltpu.CompilerParams(vmem_limit_bytes=VIEW_VMEM),
        cost_estimate=cost_of(cost),
        name="view_backward",
    )(flags, query, key, value, mixed, weights, share, grad, *after)


CHUNK = 1024
SHORT_CHUNK = 512
DOWN_ROWS = 128
BITS = SLICES.bit_length() - 1


class Route:
    def __init__(self, steps, halves):
        self.steps = steps
        self.halves = halves
        self.order = [bit for step in steps for bit in step]
        self.units = 1 << len(self.order)

    def unit(self, position):
        last = len(self.order) - 1
        return sum((position >> (last - at) & 1) << bit for at, bit in enumerate(self.order))

    def parts(self, step):
        return 1 << len(self.steps[step])

    def rows(self, rows):
        return rows // 2 if self.halves else rows


PLAIN = Route(((0,), (1,), (2,), (3,)), False)
SPLIT = Route(((1,), (0,), (2,), (3,), (4,)), True)
LAST = Route(((1,), (0,), (2,), (3, 4)), True)


def hand_out(held, parts, flags, route, span=slice(None)):
    each = route.units // len(parts)
    rows = route.rows(held.shape[1])
    for position in range(route.units):
        if route.halves:
            unit = jnp.bitwise_xor(route.unit(position), flags[2] * 2 + flags[3])
            block = held[unit // 2, pl.ds(pl.multiple_of(unit % 2 * rows, 16), rows), :]
        else:
            block = held[jnp.bitwise_xor(route.unit(position), flags[2]), span]
        parts[position // each][position % each, span] = block


def part_shapes(route, rows, width):
    each = route.units // route.parts(0)
    return [((each, route.rows(rows), width), BF)] * route.parts(0)


def centre(values):
    mean = jnp.mean(values, axis=-1, keepdims=True)
    centered = values - mean
    variance = jnp.mean(centered * centered, axis=-1, keepdims=True)
    scale = lax.rsqrt(variance + epsilon)
    return (centered * scale, scale)


def norm_back(grad, unit, scale, gain):
    grad_gain = jnp.sum(grad * unit, axis=0, keepdims=True)
    grad_bias = jnp.sum(grad, axis=0, keepdims=True)
    scaled = grad * gain
    level = jnp.mean(scaled, axis=-1, keepdims=True)
    along = jnp.mean(scaled * unit, axis=-1, keepdims=True)
    return ((scaled - level - unit * along) * scale, grad_gain, grad_bias)


def gelu_both(hidden):
    root, cubic = 0.7978845608028654, 0.044715
    square = hidden * hidden
    bend = jnp.tanh(hidden * (root + (root * cubic) * square))
    half = 0.5 + 0.5 * bend
    slope = (0.5 * hidden) * (1.0 - bend * bend) * (root + (3.0 * root * cubic) * square)
    return (hidden * half, half + slope)


def mix(keys, values):
    parts = []
    for at in range(0, keys.shape[1], PAIR):
        parts += [keys[:, at : at + PAIR], values[:, at : at + PAIR]]
    return jnp.concatenate(parts, axis=1)


def unmix(both):
    blocks = [both[:, at : at + PAIR] for at in range(0, both.shape[1], PAIR)]
    return (jnp.concatenate(blocks[0::2], axis=1), jnp.concatenate(blocks[1::2], axis=1))


class Fetch:
    def __init__(self, source, buffer, semaphore, more):
        self.copy = pltpu.make_async_copy(source, buffer, semaphore)
        self.buffer, self.more, self.here = buffer, more, False

    def ref(self):
        if not self.here:
            self.more(0, self)
            self.copy.wait()
            self.here = True
            self.more(2)
        return self.buffer

    def __getitem__(self, index):
        return self.ref()[index]


class Store:
    def __init__(self, buffer, target, semaphores, pieces):
        self.buffer, self.copies, self.gone = buffer, [], []
        for at, piece in enumerate(pieces):
            source = buffer if piece is None else buffer.at[piece]
            place = target if piece is None else target.at[piece]
            self.copies.append(pltpu.make_async_copy(source, place, semaphores.at[at]))
            self.gone.append(False)

    def __setitem__(self, index, value):
        self.buffer[index] = value

    def __getitem__(self, index):
        return self.buffer[index]

    def send(self, at=None):
        for place, copy in enumerate(self.copies):
            if not self.gone[place] and at in (None, place):
                copy.start()
                self.gone[place] = True


LEAD = 4
QKV = slice(0, 3)


def dense_call(kernel, name, operands, fetches, outs, cost, scratch=(), flags=None, after=(), pieces=None, lead=LEAD, room=DENSE_VMEM, raw=()):
    shapes = [
        jax.eval_shape(lambda array, index=index: array[:EDGE] if callable(index) else array[index or ...], operands[at])
        for at, index in fetches
    ]
    count, first = len(operands), 0 if flags is None else 1
    pieces = [(pieces or {}).get(at, (None,)) for at in range(len(outs))]

    def run(*refs):
        inputs = refs[first : first + count]
        rest = refs[first + count + len(after) :]
        targets, rest = rest[: len(outs)], rest[len(outs) :]
        straight, rest = rest[: len(raw)], rest[len(raw) :]
        buffers, rest = rest[: len(fetches)], rest[len(fetches) :]
        held, rest = rest[: len(outs)], rest[len(outs) :]
        came, went, own = rest[0], rest[1 : 1 + len(outs)], rest[1 + len(outs) :]
        fetched, started = [], [0]

        def more(number, wanted=None):
            if wanted is not None:
                number = fetched.index(wanted) + 1 - started[0]
            for fetch in fetched[started[0] : started[0] + max(number, 0)]:
                fetch.copy.start()
            started[0] += max(number, 0)

        for place, (at, index) in enumerate(fetches):
            index = index(refs[0]) if callable(index) else index
            source = inputs[at] if index is None else inputs[at].at[index]
            fetched.append(Fetch(source, buffers[place], came.at[place], more))
        more(lead)
        stores = [Store(*parts) for parts in zip(held, targets, went, pieces)]
        kernel(*([refs[0]] if first else []), fetched, stores, *straight, *own)
        for fetch in fetched:
            fetch.ref()
        for store in stores:
            store.send()
        for store in stores:
            for copy in store.copies:
                copy.wait()

    anywhere = pl.BlockSpec(memory_space=pl.ANY)
    return pl.pallas_call(
        run,
        in_specs=[pl.BlockSpec(memory_space=pltpu.SMEM)] * first
        + [anywhere] * count
        + [pl.BlockSpec(memory_space=pltpu.HBM)] * len(after),
        out_specs=[anywhere] * (len(outs) + len(raw)),
        out_shape=[jax.ShapeDtypeStruct(shape, kind) for shape, kind in (*outs, *raw)],
        scratch_shapes=[pltpu.VMEM(part.shape, part.dtype) for part in shapes]
        + [pltpu.VMEM(shape, kind) for shape, kind in outs]
        + [pltpu.SemaphoreType.DMA((len(fetches),))]
        + [pltpu.SemaphoreType.DMA((len(piece),)) for piece in pieces]
        + list(scratch),
        compiler_params=pltpu.CompilerParams(vmem_limit_bytes=room),
        cost_estimate=cost_of(cost),
        name=name,
    )(*([flags] if first else []), *operands, *after)


def near_call(kernel, name, outs, args, scratch=(), flags=None, after=(), cost=SHORT):
    vmem = pl.BlockSpec(memory_space=pltpu.VMEM)
    specs = [vmem] * len(args)
    if flags is not None:
        specs = [pl.BlockSpec(memory_space=pltpu.SMEM)] + specs
        args = [flags] + list(args)
    return pl.pallas_call(
        waiting(kernel, len(args), len(after)),
        in_specs=specs + [pl.BlockSpec(memory_space=pl.ANY)] * len(after),
        out_specs=[vmem] * len(outs),
        out_shape=[jax.ShapeDtypeStruct(shape, kind) for shape, kind in outs],
        scratch_shapes=list(scratch),
        compiler_params=pltpu.CompilerParams(vmem_limit_bytes=NEAR_VMEM),
        cost_estimate=cost_of(cost),
        name=name,
    )(*args, *after)


QKV = slice(0, 3)


def chunks(hidden, size=CHUNK):
    return [slice(at, at + size) for at in range(0, hidden, size)]


def wide_pieces(hidden):
    return [(slice(None), span) for span in chunks(hidden)]


def mlp_fetches(layer, up_at, down_at, hidden, size=CHUNK):
    found = []
    for span in chunks(hidden, size):
        found += [(up_at, (layer, slice(None), span)), (down_at, (layer, span))]
    return found


def attend_views(pairs, query, key, value, row_marks, key_marks, weights, share, mixed):
    places = [(p, index) for p in pairs for index in range(PADDED // VB)]
    units = []
    for p, index in places:
        lanes = pl.ds(pl.multiple_of(p * PAIR, PAIR), PAIR)
        rows = slice(index * VB, (index + 1) * VB)
        keys = jnp.concatenate([key[rows, lanes], key_marks[rows, :]], axis=1)
        turned = value[rows, lanes].T
        for head in range(2):
            across = jnp.concatenate([turned[head * HD : (head + 1) * HD], jnp.ones((16, VB), BF)], axis=0)
            units.append((score_side(query[rows, lanes], row_marks[rows, :], head), keys, across))
    done = attend_heads(units)
    for at, (p, index) in enumerate(places):
        lanes = pl.ds(pl.multiple_of(p * PAIR, PAIR), PAIR)
        rows = slice(index * VB, (index + 1) * VB)
        for head in range(2):
            weights[index, 2 * p + head, :, :VB] = done[2 * at + head][0]
            share[index, p, head : head + 1, :] = done[2 * at + head][2]
        pair = [done[2 * at + head][1] for head in range(2)]
        mixed[rows, lanes] = jnp.concatenate(pair, axis=0).T.astype(BF)


def climb_kernel(flags, fetched, stores, rows_all, mixed_all, row_marks, key_marks):
    x, edge, gain, bias, w_first, w_out, ff_bias, out_bias = fetched[:8]
    mlp, (language, w_lang, w_qkv) = fetched[8:-3], fetched[-3:]
    first, rest = stores[:7], stores[7:]
    normed_one, query_all, key_all, value_all, mixed, weights, share = first
    after, normed, active, slope, state, next_normed, query, kv, feats, lang_normed, lang_kv = rest
    klass, side = flags[0], flags[1]
    own, far = view_spots(side)
    rows_all[own, :] = x[...]
    rows_all[far, :] = edge[...]
    row_marks[...] = view_row_marks()
    key_marks[...] = view_key_marks(klass)
    unit, scale = centre(rows_all[...].astype(F32))
    low = (unit * gain[0, 0:1] + bias[0, 0:1]).astype(BF)
    key_all[...] = matmul(low, w_first[1]).astype(BF)
    key_all.send()
    value_all[...] = matmul(low, w_first[2]).astype(BF)
    value_all.send()
    query_all[...] = (matmul(low, w_first[0]) * 0.125).astype(BF)
    query_all.send()
    rows_all[...] = low
    normed_one[...] = rows_all[own, :]
    normed_one.send()

    def pair(p, carry):
        attend_views(
            tuple(range(HEADS // 2)), query_all.buffer, key_all.buffer, value_all.buffer, row_marks, key_marks, weights.buffer,
            share.buffer, mixed_all,
        )
        return carry

    pair(0, 0)
    weights.send()
    share.send()
    mixed[...] = mixed_all[own, :]
    mixed.send()

    total = x[...].astype(F32) + matmul(mixed[...], w_out[...])
    after[...] = total
    after.send()
    unit, scale = centre(total)
    low = (unit * gain[0, 1:2] + bias[0, 1:2]).astype(BF)
    normed[...] = low
    normed.send()
    total = total + out_bias[0:1, :]
    for at in range(0, len(mlp), 2):
        span = slice(at // 2 * CHUNK, (at // 2 + 1) * CHUNK)
        grown, rise = gelu_both(matmul(low, mlp[at][...]) + ff_bias[0:1, span])
        grown = grown.astype(BF)
        active[:, span] = grown
        active.send(at // 2)
        slope[:, span] = rise.astype(BF)
        slope.send(at // 2)
        total = total + matmul(grown, mlp[at + 1][...])
    found = matmul(language[...], w_lang[...])
    feats[...] = found
    feats.send()
    unit, scale = centre(found)
    low = (unit * gain[1, 0:1] + bias[1, 0:1]).astype(BF)
    lang_normed[...] = low
    lang_normed.send()
    both = mix(matmul(low, w_qkv[1]).astype(BF), matmul(low, w_qkv[2]).astype(BF))
    lang_kv[...] = both
    lang_kv.send()
    kv[ROWS:] = both[:LONE]
    state[...] = total
    state.send()
    unit, scale = centre(total)
    low = (unit * gain[1, 0:1] + bias[1, 0:1]).astype(BF)
    next_normed[...] = low
    next_normed.send()
    kv[:ROWS] = mix(matmul(low, w_qkv[1]).astype(BF), matmul(low, w_qkv[2]).astype(BF))
    kv.send()
    query[...] = (matmul(low, w_qkv[0]) * 0.125).astype(BF)


def far_rows(flags):
    return (pl.ds(pl.multiple_of(flags[1] * (ROWS - EDGE), 16), EDGE),)


def climb(flags, x, edge, gain, bias, w_attn, w_up, ff_bias, w_down, out_bias, language, w_lang):
    rows, width = x.shape
    hidden = w_up.shape[2]
    blocks = PADDED // VB
    return dense_call(
        climb_kernel,
        "climb",
        (x, edge, gain, bias, w_attn, ff_bias, out_bias, w_up, w_down, language, w_lang),
        [(0, None), (1, far_rows), (2, None), (3, None), (4, (0, QKV)), (4, (0, 3)), (5, None), (6, None)]
        + mlp_fetches(0, 7, 8, hidden)
        + [(9, None), (10, None), (4, (1, QKV))],
        [
            ((rows, width), BF),
            ((PADDED, width), BF),
            ((PADDED, width), BF),
            ((PADDED, width), BF),
            ((rows, width), BF),
            ((blocks, HEADS, VB, VB_UP), BF),
            ((blocks, HEADS // 2, 8, VB), F32),
            ((rows, width), F32),
            ((rows, width), BF),
            ((rows, hidden), BF),
            ((rows, hidden), BF),
            ((rows, width), F32),
            ((rows, width), BF),
            ((rows, width), BF),
            ((rows + LONE, 2 * width), BF),
            ((LPAD, width), F32),
            ((LPAD, width), BF),
            ((LPAD, 2 * width), BF),
        ],
        LONG,
        [
            pltpu.VMEM((PADDED, width), BF),
            pltpu.VMEM((PADDED, width), BF),
            pltpu.VMEM((PADDED, PAIR), BF),
            pltpu.VMEM((PADDED, PAIR), BF),
        ],
        flags,
        pieces={9: wide_pieces(hidden), 10: wide_pieces(hidden)},
        lead=5,
        room=DENSE_VMEM,
    )


def put_up(held, at, grad):
    width = grad.shape[0]
    rows = width // SLICES
    for place in range(0, grad.shape[1], width):
        put_rows(held, (at + place) // width * rows, grad[:, place : place + width])


def put_down(held, at, start, grad):
    rows = DOWN_ROWS
    for piece in range(grad.shape[0] // rows):
        held[at // rows + piece, start : start + rows, :] = grad[piece * rows : (piece + 1) * rows]


def put_rows(held, place, grad):
    rows = grad.shape[0] // SLICES
    for piece in range(SLICES):
        held[piece, place : place + rows, :] = grad[piece * rows : (piece + 1) * rows]


def mlp_tail(layer, grad, grad_normed, unit, scale, gain, mixed, w_out, ups, place, out_grad, out_mixed, small):
    width = unit.shape[1]
    grad_state, grad_gain, grad_bias = norm_back(grad_normed, unit, scale, gain[layer, 1:2])
    grad = grad + grad_state
    out_grad[...] = grad
    out_grad.send()
    small[1:2, :width] = grad_gain
    small[1:2, width : 2 * width] = grad_bias
    low = grad.astype(BF)
    out_mixed[...] = mat_right(low, w_out[...]).astype(BF)
    out_mixed.send()
    put_rows(ups, place, mat_left(mixed[...], low).astype(BF))


def mlp_chunk(span, low, grad_low, slope, w_up, w_down, ups, small):
    grad_hidden = slope * mat_right(grad_low, w_down)
    hidden_low = grad_hidden.astype(BF)
    put_up(ups, span.start, mat_left(low, hidden_low).astype(BF))
    small[0:1, span] = jnp.sum(hidden_low.astype(F32), axis=0, keepdims=True)
    return mat_right(hidden_low, w_up)


def joint_scores(query, marks, keys, key_marks, p, head):
    lanes = pl.ds(pl.multiple_of(p * PAIR, PAIR), PAIR)
    return mat_right(
        jnp.concatenate([keys[:, lanes], key_marks[...]], axis=1), score_side(query[:, lanes], marks[...], head)
    )


def crest_kernel(
    flags, fetched, stores, probs, weights, keys, values, key_marks, marks, scores, peaks, held, copied
):
    query, kv, far, lang, x, w_out, gain, bias, ff_bias, cotangent = fetched[:10]
    mlp = fetched[10:]
    mixed, share, out_grad, out_mixed, keep, send, small, outs = stores
    klass, side = flags[0], flags[1]
    query, kv, far, lang = query.ref(), kv.ref(), far.ref(), lang.ref()
    x.more(len(fetched))

    @pl.when(klass != 1)
    def empty():
        keys[ROWS:] = jnp.zeros((KEYS - ROWS, keys.shape[1]), BF)
        values[ROWS:] = jnp.zeros((KEYS - ROWS, values.shape[1]), BF)

    key_marks[...] = joint_key_marks(klass)
    marks[...] = joint_row_marks()

    def put(rows, block):
        for p in range(HEADS // 2):
            lanes = slice(p * PAIR, (p + 1) * PAIR)
            keys[rows, lanes] = block[:, 2 * p * PAIR : (2 * p + 1) * PAIR]
            values[rows, lanes] = block[:, (2 * p + 1) * PAIR : (2 * p + 2) * PAIR]

    joint_place(klass, side, kv, far, lang, put)

    def copy_out(p, head):
        return pltpu.make_async_copy(held.at[head], probs.at[2 * p + head], copied.at[head])

    def one(p, head, turned):
        across = jnp.concatenate([turned[head * HD : (head + 1) * HD], jnp.ones((16, KEYS), BF)], axis=0)
        found = jnp.exp(scores[head, :, :ROWS] - peaks[head]).astype(BF)
        held[head, :, :ROWS] = found
        copy_out(p, head).start()
        out = matmul(across, found)
        part = 1.0 / out[HD : HD + 1]
        share[p, head : head + 1, :] = part
        return out[:HD] * part

    for head in range(2):
        copy_out(0, head).start()
    def form(p, head):
        found = joint_scores(query, marks, keys, key_marks, p, head)
        scores[head, :, :ROWS] = found
        peaks[head] = jnp.max(found, axis=0, keepdims=True)

    form(0, 0)

    def pair(p, carry, last=False):
        lanes = pl.ds(pl.multiple_of(p * PAIR, PAIR), PAIR)
        turned = values[:, lanes].T
        copy_out(p, 0).wait()
        form(p, 1)
        first = one(p, 0, turned)
        copy_out(p, 1).wait()
        if not last:
            form(p + 1, 0)
        second = one(p, 1, turned)
        mixed.buffer[:, lanes] = jnp.concatenate([first, second], axis=0).T.astype(BF)
        return carry

    lax.fori_loop(0, HEADS // 2 - 1, pair, 0)
    pair(HEADS // 2 - 1, 0, True)
    mixed.send()
    share.send()

    small[...] = jnp.zeros(small.buffer.shape, F32)
    total = x[...] + matmul(mixed[...], w_out[...])
    width = total.shape[1]
    hidden = len(mlp) // 2 * SHORT_CHUNK
    unit, scale = centre(total)
    low = (unit * gain[1, 1:2] + bias[1, 1:2]).astype(BF)
    grad_low = cotangent[...]
    grad = grad_low.astype(F32)
    small[1:2, 2 * width : 3 * width] = jnp.sum(grad, axis=0, keepdims=True)
    grad_normed = None
    for at, span in enumerate(chunks(hidden, SHORT_CHUNK)):
        w_up, w_down = mlp[2 * at][...], mlp[2 * at + 1][...]
        value, rise = gelu_both(matmul(low, w_up) + ff_bias[1:2, span])
        part = mlp_chunk(span, low, grad_low, rise, w_up, w_down, weights, small)
        put_down(weights, span.start, DOWN_ROWS, mat_left(value.astype(BF), grad_low).astype(BF))
        grad_normed = part if grad_normed is None else grad_normed + part
    hand_out(weights, (keep, send), flags, PLAIN)
    send.send()
    keep.send()
    mlp_tail(1, grad, grad_normed, unit, scale, gain, mixed, w_out, outs.buffer, 0, out_grad, out_mixed, small)
    for head in range(2):
        copy_out(HEADS // 2 - 1, head).wait()


def crest(flags, query, kv, far, lang, x, gain, bias, w_attn, w_up, ff_bias, w_down, cotangent):
    rows, width = x.shape
    hidden = w_up.shape[2]
    held = 2 * hidden // SLICES
    done = dense_call(
        crest_kernel, "crest",
        (query, kv, far, lang, x, w_attn, gain, bias, ff_bias, cotangent, w_up, w_down),
        [(0, None), (1, None), (2, None), (3, None), (4, None), (5, (1, 3))]
        + [(at, None) for at in range(6, 10)]
        + mlp_fetches(1, 10, 11, hidden, SHORT_CHUNK),
        [((rows, width), BF), ((HEADS // 2, 8, rows), F32), ((rows, width), F32), ((rows, width), BF)]
        + part_shapes(PLAIN, held, width)
        + [((8, hidden), F32), ((SLICES, width // SLICES, width), BF)],
        LONG,
        [
            pltpu.VMEM((SLICES, held, width), BF),
            pltpu.VMEM((KEYS, width), BF),
            pltpu.VMEM((KEYS, width), BF),
            pltpu.VMEM((KEYS, PAIR), BF),
            pltpu.VMEM((rows, PAIR), BF),
            pltpu.VMEM((2, KEYS, ROWS_UP), F32),
            pltpu.VMEM((2, 1, rows), F32),
            pltpu.VMEM((2, KEYS, ROWS_UP), BF),
            pltpu.SemaphoreType.DMA((2,)),
        ],
        flags,
        lead=4,
        room=DENSE_VMEM,
        raw=[((HEADS, KEYS, ROWS_UP), BF)],
    )
    return (done[0], done[8], done[1], done[2], done[3], done[4:6], done[6], done[7])


def leave_grad(unit, scale, gain, grad, grad_query, grad_key, grad_value, w_qkv):
    grad_normed = mat_right(grad_query, w_qkv[0]) * 0.125
    grad_normed = grad_normed + mat_right(grad_key, w_qkv[1]) + mat_right(grad_value, w_qkv[2])
    grad_state, grad_gain, grad_bias = norm_back(grad_normed, unit, scale, gain)
    return (grad + grad_state, grad_gain, grad_bias)


def leave_kernel(flags, fetched, stores, sums, held):
    query, normed, kv, far, x, gain, w_qkv, grad = fetched[:8]
    out, keep, send, token = stores
    token[...] = jnp.zeros(token.buffer.shape, F32)
    grad_query, low = query[...], normed[...]
    width = low.shape[1]
    place = width // SLICES
    put_rows(held, 0, (mat_left(low, grad_query) * 0.125).astype(BF))
    sums[...] = kv[...].astype(F32)
    rows = pl.ds(pl.multiple_of((1 - flags[1]) * (ROWS - EDGE), 16), EDGE)
    sums[rows, :] += far[...].astype(F32)
    grad_key, grad_value = unmix(sums[...].astype(BF))
    unit, scale = centre(x[...].astype(F32))
    total, grad_gain, grad_bias = leave_grad(
        unit, scale, gain[0, 0:1], grad[...], grad_query, grad_key, grad_value, w_qkv
    )
    out[...] = total
    out.send()
    put_rows(held, place, mat_left(low, grad_key).astype(BF))
    put_rows(held, 2 * place, mat_left(low, grad_value).astype(BF))
    put_small(held, 3 * place, fetched[8:], grad_gain, grad_bias)
    hand_out(held, (keep, send), flags, LAST)


SMALL_ROWS = 32


def put_small(held, place, small, grad_gain, grad_bias):
    width = grad_gain.shape[1]
    rows = [grad_gain, small[0][1:2, :width], small[2][0:1, :width], small[1][1:2, :width]]
    rows += [grad_bias, small[0][1:2, width : 2 * width], small[2][0:1, width : 2 * width]]
    rows += [small[1][1:2, width : 2 * width]]
    rows += [small[at][1:2, 2 * width : 3 * width] for at in range(2)]
    block = jnp.concatenate(rows, axis=0)
    long = jnp.concatenate([small[at][0:1, :] for at in range(2)], axis=0)
    each, more = width // SLICES, long.shape[1] // SLICES
    for piece in range(SLICES):
        head = jnp.pad(block[:, piece * each : (piece + 1) * each], ((0, 0), (0, more - each)))
        tail = long[:, piece * more : (piece + 1) * more]
        rest = jnp.zeros((SMALL_ROWS - head.shape[0] - tail.shape[0], more), F32)
        both = jnp.concatenate([head, tail, rest], axis=0).astype(BF)
        held[piece, place : place + SMALL_ROWS, :] = jnp.pad(both, ((0, 0), (0, width - more)))


def leave(flags, x, gain, normed, grad, query, kv, far, w_attn, smalls, after):
    rows, width = x.shape
    held = 3 * (width // SLICES) + SMALL_ROWS
    done = dense_call(
        leave_kernel, "leave",
        (query, normed, kv, far, x, gain, w_attn, grad, *smalls),
        [(at, None) for at in range(6)] + [(6, (0, QKV))] + [(at, None) for at in range(7, 11)],
        [((rows, width), F32)] + part_shapes(LAST, held, width) + [((8, PAIR), F32)],
        4.0,
        [pltpu.VMEM((rows, 2 * width), F32), pltpu.VMEM((SLICES, held, width), BF)],
        flags,
        after,
        lead=8,
        room=30 * 2**20,
    )
    return (done[0], done[1:3], done[3])


def put_sums(klass, side, sums, lang_sums, kv, here, far, own, lone, there):
    @pl.when(klass == 1)
    def fine():
        sums[:, here] = (kv[:, here].astype(F32) + far[:ROWS, there].astype(F32)).astype(BF)

        @pl.when(side == 0)
        def owner():
            lang_sums[:LONE, here] = (lone[:, there].astype(F32) + far[ROWS:, there].astype(F32)).astype(BF)

    @pl.when(klass != 1)
    def coarse():
        sums[:, here] = kv[:, here]
        lang_sums[:, here] = own[:, there]


def descend_kernel(flags, fetched, stores, sums, lang_sums, plain, split):
    query, normed, x, kv = fetched[:4]
    fars, owns, lones = fetched[4:6], fetched[6:8], fetched[8:10]
    w_qkv, gain, grad, low_normed = fetched[10:14]
    mlp, (after, mixed, w_out, lang_normed, feats, language, w_lang, later) = fetched[14:-8], fetched[-8:]
    out_grad, out_mixed, grad_language, keep, send, split_keep, split_send, small, small_mid = stores
    klass, side = flags[0], flags[1]
    small[...] = jnp.zeros(small.buffer.shape, F32)
    small_mid[...] = jnp.zeros(small_mid.buffer.shape, F32)
    lang_sums[...] = jnp.zeros_like(lang_sums)
    grad_query, low = query[...], normed[...]
    width = low.shape[1]
    place = width // SLICES
    hidden = len(mlp) // 4 * CHUNK
    up_rows = hidden // SLICES
    put_rows(plain, up_rows, (mat_left(low, grad_query) * 0.125).astype(BF))
    unit, scale = centre(x[...])
    kv = kv.ref()
    fars, owns, lones = [[part.ref() for part in parts] for parts in (fars, owns, lones)]
    for pair in range(HEADS // 2):
        for which in range(2):
            there = slice(pair * PAIR, (pair + 1) * PAIR)
            here = slice((2 * pair + which) * PAIR, (2 * pair + which + 1) * PAIR)
            put_sums(klass, side, sums, lang_sums, kv, here, fars[which], owns[which], lones[which], there)

    grad_key, grad_value = unmix(sums[...])
    grad, grad_gain, grad_bias = leave_grad(
        unit, scale, gain[1, 0:1], grad[...], grad_query, grad_key, grad_value, w_qkv
    )
    lang_key, lang_value = unmix(lang_sums[...])
    lang_low = lang_normed[...]
    put_rows(plain, up_rows + place, (mat_left(low, grad_key) + mat_left(lang_low, lang_key)).astype(BF))
    put_rows(split, DOWN_ROWS, (mat_left(low, grad_value) + mat_left(lang_low, lang_value)).astype(BF))
    lang_grad = mat_right(lang_key, w_qkv[1]) + mat_right(lang_value, w_qkv[2])
    unit, scale = centre(feats[...])
    grad_feats, lang_gain, lang_bias = norm_back(lang_grad, unit, scale, gain[1, 0:1])
    feats_low = grad_feats.astype(BF)
    put_rows(split, DOWN_ROWS + place, mat_left(language[...], feats_low).astype(BF))
    grad_language[...] = mat_right(feats_low, w_lang[...])
    grad_language.send()
    small_mid[0:1, :width] = grad_gain + lang_gain
    small_mid[0:1, width : 2 * width] = grad_bias + lang_bias

    grad_low = grad.astype(BF)
    small[1:2, 2 * width : 3 * width] = jnp.sum(grad_low.astype(F32), axis=0, keepdims=True)
    low = low_normed[...]
    grad_normed = None
    for at, span in enumerate(chunks(hidden)):
        w_down, rise, w_up, active = [part[...] for part in mlp[4 * at : 4 * at + 4]]
        part = mlp_chunk(span, low, grad_low, rise.astype(F32), w_up, w_down, plain, small)
        put_down(split, span.start, 0, mat_left(active, grad_low).astype(BF))
        grad_normed = part if grad_normed is None else grad_normed + part
    hand_out(plain, (keep, send), flags, PLAIN)
    send.send()
    keep.send()
    unit, scale = centre(after[...])
    mlp_tail(
        0, grad, grad_normed, unit, scale, gain, mixed, w_out, split, DOWN_ROWS + 2 * place, out_grad, out_mixed, small
    )
    split[:, DOWN_ROWS + 3 * place :, :] = later[...]
    hand_out(split, (split_keep, split_send), flags, SPLIT)


def descend(
    flags, state, gain, normed, grad, query, kv, fars, owns, w_attn, feats, lang_normed, language, w_lang,
    after, mixed, low_normed, active, slope, w_up, w_down, later, follows,
):
    rows, width = state.shape
    hidden = w_up.shape[2]
    place = width // SLICES
    plain, split = hidden // SLICES + 2 * place, DOWN_ROWS + 4 * place
    fetches = []
    for span in chunks(hidden):
        fetches += [(13, (0, span)), (14, (slice(None), span)), (12, (0, slice(None), span)), (15, (slice(None), span))]
    head, foot = slice(0, LPAD), slice(ROWS, ROWS + LONE)
    done = dense_call(
        descend_kernel, "descend",
        (query, normed, state, kv, *fars, *owns, w_attn, gain, grad, low_normed)
        + (w_up, w_down, slope, active, after, mixed, lang_normed, feats, language, w_lang, later),
        [(at, None) for at in range(6)]
        + [(at, (head,)) for at in range(6, 8)]
        + [(at, (foot,)) for at in range(6, 8)]
        + [(8, (1, QKV)), (9, None), (10, None), (11, None)]
        + fetches
        + [(16, None), (17, None), (8, (0, 3)), (18, None), (19, None), (20, None), (21, None), (22, None)],
        [((rows, width), F32), ((rows, width), BF), ((LPAD, width), F32)]
        + part_shapes(PLAIN, plain, width)
        + part_shapes(SPLIT, split, width)
        + [((8, hidden), F32), ((8, 2 * width), F32)],
        LONG,
        [
            pltpu.VMEM((rows, 2 * width), BF),
            pltpu.VMEM((LPAD, 2 * width), BF),
            pltpu.VMEM((SLICES, plain, width), BF),
            pltpu.VMEM((SLICES, split, width), BF),
        ],
        flags,
        follows,
        lead=6,
    )
    return (done[0], done[1], done[2], done[3:5], done[5:7], done[7], done[8])


def pair_swap(block):
    count = lax.axis_size("wide")
    return lax.ppermute(block, "wide", [(at, at ^ 1) for at in range(count)])


class Flow:
    def __init__(self, route, parts):
        self.route, self.step = route, 0
        self.units = route.units
        self.keep = [parts[0]]
        self.send(parts)

    def send(self, parts):
        self.got = []
        if self.step < len(self.route.steps):
            bits = self.route.steps[self.step]
            self.units //= 1 << len(bits)
            for at, part in enumerate(parts[1:], 1):
                found = [bit for place, bit in enumerate(bits) if at >> (len(bits) - 1 - place) & 1]
                self.got.append(self.move(part, found))
        else:
            self.keep = [parts[0]]
            self.got.append(self.move(parts[0], [0] if self.route.halves else None))

    def move(self, part, bits):
        shift = 1 if self.route.halves else 0
        if bits is None or bits == [0] and shift:
            return lax.ppermute(part, "narrow", [(0, 1), (1, 0)])
        count = lax.axis_size("wide")
        stride = sum((count // SLICES) << (bit - shift) for bit in bits)
        return lax.ppermute(part, "wide", [(p, p ^ stride) for p in range(count)])


def step_kernel(layout, ins, outs):
    at = 0
    for out, (count, rows) in zip(outs, layout):
        total = None
        for term in ins[at : at + count]:
            part = term[rows] if rows is not None else term[...]
            total = part.astype(F32) if total is None else total + part.astype(F32)
        out[...] = total.astype(BF)
        if isinstance(out, Store):
            out.send()
        at += count


def step(flows, after=(), near=False, cost=SHORT, lazy=False):
    operands, fetches, layout, outs, plan = [], [], [], [], []
    for flow in flows:
        flow.step += 1
        terms = flow.keep + flow.got
        last = flow.step == len(flow.route.steps)
        count = 1 if last else flow.route.parts(flow.step)
        each = flow.units // count
        made = [part for part in range(count) if part or last or not lazy]
        for part in reversed(made):
            rows = slice(part * each, (part + 1) * each)
            for term in terms:
                fetches.append((len(operands), rows))
                operands.append(term)
            layout.append((len(terms), rows))
            outs.append(((each,) + terms[0].shape[1:], BF))
        plan.append((flow, terms, count, made))
    if near:
        done = near_call(
            lambda *refs: step_kernel(layout, refs[: len(operands)], refs[len(operands) :]),
            "step", outs, operands, after=after, cost=cost,
        )
    else:
        done = dense_call(
            lambda ins, stores: step_kernel([(count, None) for count, rows in layout], ins, stores),
            "step", operands, fetches, outs, cost, after=after, lead=len(fetches), room=STEP_VMEM,
        )
    at = 0
    for flow, terms, count, made in plan:
        parts = [None] * count
        for part in reversed(made):
            parts[part] = done[at]
            at += 1
        flow.keep = terms if parts[0] is None else [parts[0]]
        flow.send(parts)
    return done


def split_low(buffer):
    count = lax.axis_size("wide")
    position = lax.axis_index("wide")
    half = count // SLICES
    while half > 1:
        half //= 2
        mine = position // half % 2
        size = buffer.shape[0] // 2
        send = lax.dynamic_slice_in_dim(buffer, (1 - mine) * size, size, 0)
        keep = lax.dynamic_slice_in_dim(buffer, mine * size, size, 0)
        buffer = keep + lax.ppermute(send.astype(BF), "wide", [(p, p ^ half) for p in range(count)])
    return buffer


def finish_kernel(
    flags, first, first_got, plain, plain_got, split, split_got, attn_one, attn_one_got,
    lang, attn, ups, downs, gains, biases, ff_biases, out_biases, whole, last,
):
    rows, width = attn.shape[2:]
    up_rows, down_rows = ups.shape[2] // width * rows, downs.shape[1]

    def both(buffer, got):
        return buffer[0].astype(F32) + got[0].astype(F32)

    def put_ups(layer, found):
        for at in range(ups.shape[2] // width):
            ups[layer, :, at * width : (at + 1) * width] = found[at * rows : (at + 1) * rows]

    found = both(first, first_got)
    put_ups(1, found)
    downs[1] = found[up_rows:]
    found = both(plain, plain_got)
    put_ups(0, found)
    attn[1, 0] = found[up_rows : up_rows + rows]
    attn[1, 1] = found[up_rows + rows :]
    whole[flags[3]] = split[0].astype(F32)
    whole[1 - flags[3]] = split_got[0].astype(F32)
    found = jnp.concatenate([whole[0], whole[1]], axis=0)
    downs[0] = found[:down_rows]
    attn[1, 2] = found[down_rows : down_rows + rows]
    lang[...] = found[down_rows + rows : down_rows + 2 * rows]
    attn[0, 3] = found[down_rows + 2 * rows : down_rows + 3 * rows]
    attn[1, 3] = found[down_rows + 3 * rows :]
    last[flags[3]] = attn_one[0].astype(F32)
    last[1 - flags[3]] = attn_one_got[0].astype(F32)
    found = jnp.concatenate([last[0], last[1]], axis=0)
    for at in range(3):
        attn[0, at] = found[at * rows : (at + 1) * rows]
    small = found[3 * rows :]
    for layer in range(2):
        gains[layer] = small[2 * layer : 2 * layer + 2, :rows]
        biases[layer] = small[4 + 2 * layer : 6 + 2 * layer, :rows]
    out_biases[...] = small[8:10, :rows]
    ff_biases[...] = small[10:12, : ff_biases.shape[1]]


def finish(flags, flows, width, hidden):
    rows = width // SLICES
    args = []
    for flow in flows:
        args += flow.keep + flow.got
    return near_call(
        finish_kernel, "finish",
        [
            ((rows, width), F32),
            ((2, 4, rows, width), F32),
            ((2, rows, hidden), F32),
            ((2, hidden // SLICES, width), F32),
            ((2, 2, rows), F32),
            ((2, 2, rows), F32),
            ((2, hidden // SLICES), F32),
            ((2, rows), F32),
        ],
        args,
        [
            pltpu.VMEM((2, (DOWN_ROWS + 4 * rows) // 2, width), F32),
            pltpu.VMEM((2, (3 * rows + SMALL_ROWS) // 2, width), F32),
        ],
        flags,
    )


def body(
    patches,
    language,
    w_lang,
    w_attn,
    w_up,
    w_down,
    norm_gain,
    norm_bias,
    ff_bias,
    out_bias,
    cotangent,
    classes,
):
    position = lax.axis_index("wide")
    wide = lax.axis_size("wide")
    side = position % 2
    klass = lax.dynamic_index_in_dim(classes[0], position // 2, 0, keepdims=False)
    high = position // (wide // SLICES)
    flags = jnp.stack([klass, side, high, lax.axis_index("narrow")]).astype(jnp.int32)
    width = w_lang.shape[0]
    hidden = w_up.shape[2]
    start = patches[0]
    lang_low = jnp.pad(language[0], ((0, LPAD - language.shape[1]), (0, 0)))

    other = pair_swap(start)
    normed_a, query_a, key_a, value_a, mixed_a, weights_a, share_a, *rest = climb(
        flags, start, other, norm_gain, norm_bias, w_attn, w_up, ff_bias, w_down, out_bias, lang_low, w_lang
    )
    after_a, normed_b, active_b, slope_b, state_b, normed_c, query_c, kv_c, feats, lang_normed, lang_kv = rest
    far_c = pair_swap(kv_c)
    mixed_c, weights_c, share_c, grad, grad_mixed_c, parts, small_two, outs_two = crest(
        flags, query_c, kv_c, far_c, lang_kv, state_b, norm_gain, norm_bias, w_attn, w_up, ff_bias, w_down,
        cotangent[0],
    )
    first = Flow(PLAIN, parts)
    joint = (flags, query_c, kv_c, far_c, lang_kv, mixed_c, weights_c, share_c, grad_mixed_c)
    query, kv, *edges, token = joint_backward(*joint, 0, HEADS // 2)
    fars = [pair_swap(part) for part in edges]
    done = step([first], [token], lazy=True)
    grad, grad_mixed_a, grad_language, plain_parts, split_parts, small_one, small_mid = descend(
        flags, state_b, norm_gain, normed_c, grad, query, kv, fars, edges, w_attn, feats, lang_normed, lang_low,
        w_lang, after_a, mixed_a, normed_b, active_b, slope_b, w_up, w_down, outs_two, done,
    )
    plain, split = Flow(PLAIN, plain_parts), Flow(SPLIT, split_parts)

    done = step([first], [small_mid], lazy=True, cost=30.0)
    done = step([plain, split], [done[0]])
    view = (flags, query_a, key_a, value_a, mixed_a, weights_a, share_a, grad_mixed_a)
    query, kv, edge, token = view_backward(*view, 0, HEADS // 2, done)
    far = pair_swap(edge)
    done = step([first], [token])
    grad, attn_parts, token = leave(
        flags, start, norm_gain, normed_a, grad, query, kv, far, w_attn, (small_one, small_two, small_mid), done
    )
    attn_one = Flow(LAST, attn_parts)

    done = step([plain, split], [token], near=True, cost=LONG)
    done = step([attn_one], [done[0]], near=True)
    done = step([first], [done[0]], near=True, cost=5.0)
    done = step([plain, split], [done[0]], near=True)
    done = step([attn_one], [done[0]], near=True)
    done = step([plain, split], [done[0], first.got[0]], near=True)
    done = step([attn_one], [done[0]], near=True)
    done = step([split], [done[0]], near=True)
    done = step([attn_one], [done[0], plain.got[0]], near=True)
    flows = (first, plain, split, attn_one)
    grad_w_lang, grad_w_attn, grad_w_up, grad_w_down, *vectors = finish(flags, flows, width, hidden)
    gains, biases, ff_biases, out_biases = vectors

    def own(values, dim):
        if wide == SLICES:
            return values
        values = jnp.moveaxis(values, dim, 0)
        return jnp.moveaxis(split_low(values), 0, dim)

    return (
        grad[None],
        grad_language[None, : language.shape[1]],
        own(grad_w_lang, 0),
        own(grad_w_attn, 2),
        own(grad_w_up, 1),
        own(grad_w_down, 1),
        own(gains, 2),
        own(biases, 2),
        own(ff_biases, 1),
        own(out_biases, 1),
    )


def solution(mesh):
    in_specs = (
        P("narrow", "wide", None),
        P("narrow", "wide", None),
        P(),
        P(),
        P(),
        P(),
        P(),
        P(),
        P(),
        P(),
        P("narrow", "wide", None),
        P("narrow", None),
    )
    out_specs = (
        P("narrow", "wide", None),
        P("narrow", "wide", None),
        P("wide", None),
        P(None, None, "wide", None),
        P(None, "wide", None),
        P(None, "wide", None),
        P(None, None, "wide"),
        P(None, None, "wide"),
        P(None, "wide"),
        P(None, "wide"),
    )
    return jax.shard_map(body, mesh=mesh, in_specs=in_specs, out_specs=out_specs, check_vma=False)
```
